32 devices in a mesh: group: 2 (over x), space: 16 (over z, y, core).
Axes of the slice: x: 2, y: 2, z: 4, core: 2. Of those that a mesh axis runs over, the one named last changes fastest.
Arguments:
- probes: float32 [32, 64, 32, 128], P('group', 'space'), parts along dimension 0, may hold values from -4 to 4
- sources: float32 [3, 128, 32, 128], P(None, ('group', 'space')), parts along dimension 1, may hold values from -6 to 6
- kappa: float32 [128, 32, 128], P(('group', 'space')), parts along dimension 0, may hold values from 0.05 to 0.3
- prior: float32 [128, 32, 128], P(('group', 'space')), parts along dimension 0, may hold values from 0.1 to 1
- basis: float32 [128, 64, 32, 128], P('group', 'space'), parts along dimension 0, may hold values from -0.0078125 to 0.0078125
- entry_cell: int32 [16384], P(('group', 'space')), parts along dimension 0, may hold values from 0 to 16383
- entry_owner: int32 [16384], P(('group', 'space')), parts along dimension 0, may hold values from 0 to 15, as said below
- entry_slot: int32 [16384], P(('group', 'space')), parts along dimension 0, may hold values from 0 to 127
- entry_weight: float32 [16384], P(('group', 'space')), parts along dimension 0, may hold values from 0.05 to 1
- entry_count: int32 [32], P(('group', 'space')), parts along dimension 0, may hold values from 384 to 512, as said below
- trace_weight: float32 [4096], P(('group', 'space')), parts along dimension 0, may hold values from 0.3 to 3
Outputs:
- hess_probe: float32 [32, 64, 32, 128], P('group', 'space'), parts along dimension 0
- coeffs: float32 [128, 16], P('group'), parts along dimension 0
The draws below stay inside these ranges and needn't reach their ends.
There are 2 independent parts, one for each index of `group`. The reference program is written for one: setup_inputs(seed, part) draws one part's arguments, and reference() takes and returns one part's arrays. A program takes and returns all parts, laid end to end along the dimension named above; each array names one. Nothing has to cross between parts.
Inputs may be any that keep to these rules, and one draw needn't show every extreme that they name: `entry_owner`: among the entries of one tile at most 64 name the same owner, and the first 64 entries of every tile name one owner. `entry_count`: some tile has all 512 entries live.
All inputs are finite; a program needn't handle non-finite values.
Results may differ from the reference program's by a relative error of at most 0.00012.
Values sent between devices are 32-bit elements; how exact they have to be, the bound alone decides.
No kernel may reach another device: no remote copies, remote signals or barrier semaphores. Data moves between devices by JAX's collectives and lax.ppermute only.
A program may use at most 64 MiB of HBM per device.

```python
import math
import jax
import jax.numpy as jnp
from jax import lax

PROBES = 16
RANK = 64
CX = 4
CY = 32
CZ = 128
E_DEV = 512
R_DEV = 128
CAP = 64
NX = 64
N_SPACE = 16


def shared_columns(key):
    return jnp.clip(jax.random.normal(key, (RANK, NX, CY, CZ), jnp.float32), -4.0, 4.0)


def draw_basis(key, part):
    columns = shared_columns(key)
    scale = float(NX * CY * CZ) ** (-0.5)
    return (columns * scale).astype(jnp.float32)


def draw_probes(key, part):
    columns = shared_columns(key)
    key = jax.random.fold_in(key, 13)
    sign_key, half_key, noise_key = jax.random.split(key, 3)
    signs = jnp.where(jax.random.bernoulli(sign_key, 0.5, (RANK, PROBES)), 1.0, -1.0)
    halves = jnp.where(jax.random.bernoulli(half_key, 0.5, (RANK, PROBES)), 1.0, 0.5)
    mixing = (signs * halves).astype(jnp.float32)

    def add_column(index, total):
        return total + mixing[index][:, None, None, None] * columns[index][None]
    structured = lax.fori_loop(0, RANK, add_column, jnp.zeros((PROBES, NX, CY, CZ), jnp.float32))
    structured = structured * float(RANK) ** (-0.5)
    noise = jax.random.normal(noise_key, (PROBES, NX, CY, CZ), jnp.float32)
    total = 0.6 * noise + structured
    return jnp.clip(total, -4.0, 4.0).astype(jnp.float32)


def draw_entry_owner(key, part):
    key = jax.random.fold_in(key, 11)
    half = CAP // 2

    def one_tile(tile_key):
        pick_key, gap_key, mix_key = jax.random.split(tile_key, 3)
        heavy = jax.random.randint(pick_key, (), 0, N_SPACE)
        spacing = jax.random.randint(gap_key, (), 1, N_SPACE)
        index = jnp.arange(N_SPACE - 2, dtype=jnp.int32)
        chosen = index + (index >= spacing - 1).astype(jnp.int32)
        others = (heavy + 1 + chosen) % N_SPACE
        spread = jax.random.permutation(mix_key, jnp.repeat(others, half))
        return jnp.concatenate([jnp.full((CAP,), heavy, jnp.int32), spread.astype(jnp.int32)])
    keys = jax.random.split(key, N_SPACE)
    return jax.vmap(one_tile)(keys).reshape(-1).astype(jnp.int32)


def draw_entry_count(key, part):
    key = jax.random.fold_in(key, 12)
    level_key, full_key = jax.random.split(key)
    levels = jax.random.randint(level_key, (N_SPACE,), 0, 2).astype(jnp.int32)
    counts = E_DEV - levels * (E_DEV // 4)
    full_at = jax.random.randint(full_key, (), 0, N_SPACE)
    counts = jnp.where(jnp.arange(N_SPACE) == full_at, E_DEV, counts)
    return counts.astype(jnp.int32)


def with_ends(drawn, own_key, low, high):
    longest = drawn.shape.index(max(drawn.shape))
    spots = []
    for shift in (0, 1):
        where = [jax.random.randint(jax.random.fold_in(own_key, axis), (), 0, length) for axis, length in enumerate(drawn.shape)]
        where[longest] = (where[longest] + shift) % drawn.shape[longest]
        spots.append(tuple(where))
    return drawn.at[spots[0]].set(low).at[spots[1]].set(high)


def level_of(key, shape, cuts, low, high):
    def one(dim, parts):
        draws = jax.random.uniform(jax.random.fold_in(jax.random.fold_in(key, 6), dim), (parts,), jnp.float32, low / len(cuts), high / len(cuts))
        return jnp.repeat(jnp.exp(draws), shape[dim] // parts).reshape((-1,) + (1,) * (len(shape) - dim - 1))

    factor_of = one(*cuts[0])
    for cut in cuts[1:]:
        factor_of = factor_of * one(*cut)
    return factor_of


def gaussian(key, shape, scale, limit, cuts=(), held_as=jnp.bfloat16):
    result = scale * jax.random.normal(key, shape, jnp.float32)
    if cuts:
        result = result * level_of(key, shape, cuts, -0.22, 0.18)
    return jnp.clip(result, -limit, limit).astype(held_as)


def setup_inputs(seed: int = 0, part: int = 0) -> dict:
    key_of = jax.random.split(jax.random.key(seed), 12)
    part_keys = jax.random.split(jax.random.fold_in(key_of[11], part), 12)
    return {
        "probes": draw_probes(jax.random.fold_in(jax.random.fold_in(key_of[11], part), 71), part),
        "sources": gaussian(part_keys[1], (3, NX, CY, CZ), 1.0, 6.0, ((1, 16),), jnp.float32),
        "kappa": jnp.clip(0.05 + 0.25 * jax.random.uniform(part_keys[2], (NX, CY, CZ), jnp.float32) ** level_of(part_keys[2], (NX, CY, CZ), ((0, 16),), -0.2, 0.2), 0.05, 0.3),
        "prior": jnp.clip(jnp.exp(math.log(1.0) - 2.3025851 * jax.random.uniform(part_keys[3], (NX, CY, CZ), jnp.float32) ** level_of(part_keys[3], (NX, CY, CZ), ((0, 16),), -0.2, 0.2)), 0.1, 1.0),
        "basis": draw_basis(jax.random.fold_in(jax.random.fold_in(key_of[11], part), 71), part),
        "entry_cell": with_ends(jax.random.randint(part_keys[5], (N_SPACE * E_DEV,), 0, CX * CY * CZ), jax.random.fold_in(part_keys[5], 1), 0, (CX * CY * CZ) - 1).astype(jnp.int32),
        "entry_owner": draw_entry_owner(jax.random.fold_in(jax.random.fold_in(key_of[11], part), 71), part),
        "entry_slot": with_ends(jax.random.randint(part_keys[7], (N_SPACE * E_DEV,), 0, R_DEV), jax.random.fold_in(part_keys[7], 1), 0, R_DEV - 1).astype(jnp.int32),
        "entry_weight": jnp.clip(0.05 + 0.95 * jax.random.uniform(part_keys[8], (N_SPACE * E_DEV,), jnp.float32) ** level_of(part_keys[8], (N_SPACE * E_DEV,), ((0, 16),), -0.2, 0.2), 0.05, 1.0),
        "entry_count": draw_entry_count(jax.random.fold_in(jax.random.fold_in(key_of[11], part), 71), part),
        "trace_weight": jnp.clip(jnp.exp(math.log(3.0) - 2.3025851 * jax.random.uniform(part_keys[10], (N_SPACE * R_DEV,), jnp.float32) ** level_of(part_keys[10], (N_SPACE * R_DEV,), ((0, 16),), -0.2, 0.2)), 0.3, 3.0),
    }


STENCIL = (-205.0 / 72.0, 8.0 / 5.0, -1.0 / 5.0, 8.0 / 315.0, -1.0 / 560.0)


def second_difference(padded, length_x, length_y, length_z):
    def part(shift_x, shift_y, shift_z):
        return padded[:, 4 + shift_x:4 + shift_x + length_x, 4 + shift_y:4 + shift_y + length_y, 4 + shift_z:4 + shift_z + length_z]
    total = 3.0 * STENCIL[0] * part(0, 0, 0)
    for reach in range(1, 5):
        pair = part(reach, 0, 0) + part(-reach, 0, 0) + part(0, reach, 0) + part(0, -reach, 0)
        pair = pair + part(0, 0, reach) + part(0, 0, -reach)
        total = total + STENCIL[reach] * pair
    return total


def stencil(field):
    padded = jnp.pad(field, ((0, 0), (4, 4), (4, 4), (4, 4)))
    return second_difference(padded, field.shape[1], field.shape[2], field.shape[3])


def reference(probes, sources, kappa, prior, basis, entry_cell, entry_owner, entry_slot, entry_weight, entry_count, trace_weight):
    first = probes * sources[0]
    second = 2.0 * first + kappa * stencil(first) + probes * sources[1]
    third = 2.0 * second - first + kappa * stencil(second) + probes * sources[2]
    position = jnp.arange(N_SPACE * E_DEV, dtype=jnp.int32)
    tile = position // E_DEV
    live = (position % E_DEV) < entry_count[tile]
    weight = jnp.where(live, entry_weight, jnp.zeros_like(entry_weight))
    global_cell = tile * (CX * CY * CZ) + entry_cell
    flat = third.reshape(PROBES, -1)
    values = flat[:, global_cell] * weight[None, :]
    trace_id = entry_owner * R_DEV + entry_slot
    traces = jnp.zeros((PROBES, N_SPACE * R_DEV), flat.dtype).at[:, trace_id].add(values)
    weighted = traces * trace_weight[None, :]
    returned = weighted[:, trace_id] * weight[None, :]
    adjoint_two = jnp.zeros_like(flat).at[:, global_cell].add(returned).reshape(third.shape)
    adjoint_one = 2.0 * adjoint_two + stencil(kappa * adjoint_two)
    adjoint_zero = 2.0 * adjoint_one - adjoint_two + stencil(kappa * adjoint_one)
    image = sources[0] * adjoint_zero + sources[1] * adjoint_one + sources[2] * adjoint_two + prior * probes
    coeffs = jnp.einsum("rxyz,pxyz->rp", basis, image, precision=lax.Precision.HIGHEST)
    hess_probe = image - jnp.einsum("rxyz,rp->pxyz", basis, coeffs, precision=lax.Precision.HIGHEST)
    return hess_probe, coeffs
```

```python
import functools

import jax
import jax.numpy as jnp
import ml_dtypes
import numpy as np
from jax import lax
from jax.experimental import pallas as pl
from jax.experimental.pallas import tpu as pltpu
from jax.sharding import PartitionSpec as P

STENCIL = (-205.0 / 72.0, 8.0 / 5.0, -1.0 / 5.0, 8.0 / 315.0, -1.0 / 560.0)
CENTER = 3.0 * STENCIL[0]
REACH = 4
LAYERS = 4
PADDED = 40
HALF = 128
F32 = jnp.float32
BF16 = jnp.bfloat16
NT = (((1,), (1,)), ((), ()))


def band():
    place = np.arange(HALF)
    apart = np.abs(place[:, None] - place[None, :])
    full = np.zeros((HALF, HALF), np.float32)
    for reach in range(1, REACH + 1):
        full[apart == reach] = STENCIL[reach]
    high = full.astype(ml_dtypes.bfloat16)
    low = (full - high.astype(np.float32)).astype(ml_dtypes.bfloat16)
    return np.block([[high, low], [high, np.zeros_like(low)]])


def split(value):
    high = value.astype(BF16)
    low = (value - high.astype(F32)).astype(BF16)
    return high, low


def at(row, count=16):
    return pl.ds(pl.multiple_of(row, 16), count)


def spread(ref, row, fields):
    return jnp.broadcast_to(ref[pl.ds(row, 1), :], (fields, HALF))


def clear_margins(ref, layers, fields):
    margin = jnp.zeros((REACH * fields, HALF), F32)
    for layer in range(layers):
        start = layer * PADDED * fields
        ref[start : start + REACH * fields, :] = margin
        start += (PADDED - REACH) * fields
        ref[start : start + REACH * fields, :] = margin


def along_z(ref, first, chunk, fields, band_ref, out_ref):
    count = 8 * fields
    pieces = [ref[at(((first + x) * PADDED + REACH + chunk * 8) * fields, count), :] for x in range(LAYERS)]
    high, low = split(jnp.concatenate(pieces, axis=0))
    both = jnp.dot(jnp.concatenate([high, low], axis=1), band_ref[...], preferred_element_type=F32)
    out_ref[...] = both[:, :HALF] + both[:, HALF:]


def laplacian(get, x, y, z_term, lowest, highest):
    total = CENTER * get(x, y) + z_term
    for k in range(1, REACH + 1):
        ring = get(x, y + k) + get(x, y - k)
        if x + k <= highest:
            ring = ring + get(x + k, y)
        if x - k >= lowest:
            ring = ring + get(x - k, y)
        total = total + STENCIL[k] * ring
    return total


def forward_own(fields, probes, sources, kappa, band_ref, turned, first, second, third, z_term):
    clear_margins(first, LAYERS, fields)
    clear_margins(second, LAYERS, fields)

    def load(chunk, carry):
        for x in range(LAYERS):
            for step in range(8):
                y = chunk * 8 + step
                cell = x * 32 + y
                value = probes[pl.ds(cell, fields, stride=HALF), :]
                turned[at(cell * fields, fields), :] = value
                first[at((x * PADDED + REACH + y) * fields, fields), :] = value * spread(sources, cell, fields)
        return carry

    lax.fori_loop(0, 4, load, 0)

    def sweep(field, chunk, emit):
        along_z(field, 0, chunk, fields, band_ref, z_term)
        for x in range(LAYERS):
            for step in range(8):
                y = chunk * 8 + step

                def get(layer, row):
                    return field[at((layer * PADDED + REACH + row) * fields, fields), :]

                z_part = z_term[at((x * 8 + step) * fields, fields), :]
                total = laplacian(get, x, y, z_part, 0, LAYERS - 1)
                emit(x, y, get(x, y), spread(kappa, x * 32 + y, fields) * total)

    def step_one(chunk, carry):
        def emit(x, y, now, change):
            cell = x * 32 + y
            push = turned[at(cell * fields, fields), :] * spread(sources, 128 + cell, fields)
            second[at((x * PADDED + REACH + y) * fields, fields), :] = 2.0 * now + change + push

        sweep(first, chunk, emit)
        return carry

    lax.fori_loop(0, 4, step_one, 0)

    def step_two(chunk, carry):
        def emit(x, y, now, change):
            cell = x * 32 + y
            push = turned[at(cell * fields, fields), :] * spread(sources, 256 + cell, fields)
            before = first[at((x * PADDED + REACH + y) * fields, fields), :]
            third[at(cell * fields, fields), :] = 2.0 * now - before + change + push

        sweep(second, chunk, emit)
        return carry

    lax.fori_loop(0, 4, step_two, 0)


def entry_row(ref, row):
    return jnp.concatenate([ref[row + i : row + i + 1, :] for i in range(4)], axis=1)


def describe(statics, fields, pair, cell_ref, line_ref, owner_ref, slot_ref, weight_ref):
    entries = pair.shape[1]
    place = lax.broadcasted_iota(jnp.int32, (256, entries), 0)
    slot_place = lax.broadcasted_iota(jnp.int32, (HALF, entries), 0)
    for tile, ref in enumerate(statics):
        cell = entry_row(ref, 128).astype(jnp.int32)
        owner = entry_row(ref, 132).astype(jnp.int32)
        slot = entry_row(ref, 136).astype(jnp.int32)
        weight = entry_row(ref, 140)
        hot = jnp.where(place == jnp.bitwise_and(cell, 255), 1.0, 0.0)
        cell_ref[tile * 256 : (tile + 1) * 256, :] = hot.astype(BF16)
        hot = jnp.where(slot_place == slot, 1.0, 0.0)
        slot_ref[tile * HALF : (tile + 1) * HALF, :] = hot.astype(BF16)
        rows = slice(tile * fields, (tile + 1) * fields)
        line_ref[rows, :] = jnp.broadcast_to(lax.shift_right_logical(cell, 8), (fields, entries))
        owner_ref[rows, :] = jnp.broadcast_to(owner, (fields, entries))
        weight_ref[rows, :] = jnp.broadcast_to(weight, (fields, entries))


def forward_window(
    fields, peers, me, first, second, third, kappa_mm, kappa_m, kappa, kappa_p, kappa_pp, band_ref, own_scale,
    table, cell_ref, slot_ref, below, above, z_term, sample, total_ref, line_ref, owner_ref, weight_ref,
):
    statics = (kappa_mm, kappa_m, kappa, kappa_p, kappa_pp)
    entries = line_ref.shape[1]
    describe(statics, fields, cell_ref, cell_ref, line_ref, owner_ref, slot_ref, weight_ref)
    clear_margins(below, LAYERS, fields)
    clear_margins(above, LAYERS, fields)
    total_ref[...] = jnp.zeros_like(total_ref)

    def outward(chunk, carry):
        for step in range(8):
            y = chunk * 8 + step
            own = [first[at((x * PADDED + REACH + y) * fields, fields), :] for x in range(LAYERS)]
            for x in range(LAYERS):
                up = sum(STENCIL[4 + x - other] * own[other] for other in range(x, LAYERS))
                down = sum(STENCIL[4 + other - x] * own[other] for other in range(x + 1))
                row = at((x * PADDED + REACH + y) * fields, fields)
                above[row, :] = spread(kappa_p, x * 32 + y, fields) * up
                below[row, :] = spread(kappa_m, x * 32 + y, fields) * down
        return carry

    lax.fori_loop(0, 4, outward, 0)

    def read(layer, y):
        ref = (below, second, above)[(layer + LAYERS) // LAYERS]
        return ref[at((layer % LAYERS * PADDED + REACH + y) * fields, fields), :]

    def far(x, y, lowest, highest):
        total = None
        for other in range(lowest, highest + 1):
            if 1 <= abs(x - other) <= REACH:
                term = STENCIL[abs(x - other)] * read(other, y)
                total = term if total is None else total + term
        return total

    def sampling(chunk, carry):
        for tile in range(5):
            if tile in (1, 3):
                along_z((below, above)[tile // 2], 0, chunk, fields, band_ref, z_term)
            for x in range(LAYERS):
                for step in range(8):
                    y = chunk * 8 + step
                    cell = x * 32 + y
                    layer = (tile - 2) * LAYERS + x
                    speed = spread(statics[tile], cell, fields)
                    if tile in (0, 4):
                        value = speed * far(layer, y, -4, 7)
                    elif tile == 2:
                        outside = far(layer, y, -4, -1) + far(layer, y, 4, 7)
                        value = third[at(cell * fields, fields), :] + speed * outside
                    else:
                        z_part = z_term[at((x * 8 + step) * fields, fields), :]
                        value = 2.0 * read(layer, y) + speed * laplacian(read, layer, y, z_part, -4, 7)
                    row = (x * 4 + step // 2) * fields
                    side = step % 2 * HALF
                    sample[row : row + fields, side : side + HALF] = value
            high, low = split(sample[...])
            hot = cell_ref[tile * 256 : (tile + 1) * 256, :]
            picked = jnp.dot(high, hot, preferred_element_type=F32) + jnp.dot(low, hot, preferred_element_type=F32)
            rows = slice(tile * fields, (tile + 1) * fields)
            line = line_ref[rows, :]
            total = total_ref[rows, :]
            for x in range(LAYERS):
                for pair in range(4):
                    row = (x * 4 + pair) * fields
                    chosen = line == x * 16 + chunk * 4 + pair
                    total = total + jnp.where(chosen, picked[row : row + fields, :], 0.0)
            total_ref[rows, :] = total
        return carry

    lax.fori_loop(0, 4, sampling, 0)

    for group in range(peers // 16):
        result = jnp.zeros((16 * fields, HALF), F32)
        for tile in range(5):
            rows = slice(tile * fields, (tile + 1) * fields)
            high, low = split(total_ref[rows, :] * weight_ref[rows, :])
            high, low = high.astype(F32), low.astype(F32)
            owner = owner_ref[rows, :]
            hot = slot_ref[tile * HALF : (tile + 1) * HALF, :]
            for part in (high, low):
                pieces = [jnp.where(owner == group * 16 + i, part, 0.0).astype(BF16) for i in range(16)]
                result = result + lax.dot_general(
                    jnp.concatenate(pieces, axis=0), hot, NT, preferred_element_type=F32
                )
        table[group * 16 * fields : (group + 1) * 16 * fields, :] = result
    place = lax.broadcasted_iota(jnp.int32, (peers, HALF), 0)
    own = jnp.broadcast_to(own_scale[...], (peers, HALF))
    table[peers * fields : peers * fields + peers, :] = jnp.where(place == me[0], own, 0.0)


def basis_parts(basis, out):
    rank = basis.shape[0] // HALF

    def body(group, carry):
        for step in range(8):
            high, low = split(basis[pl.ds(group * 8 + step, rank, stride=HALF), :])
            rows = at(group * rank, rank)
            out[rows, step * 256 : step * 256 + HALF] = high
            out[rows, step * 256 + HALF : (step + 1) * 256] = low
        return carry

    lax.fori_loop(0, 16, body, 0)


def adjoint(
    fields, peers, table, statics_mm, statics_m, statics, statics_p, statics_pp, cell_ref, slot_ref, turned, sources,
    prior, band_ref, basis, image, coeffs, speed_ref, line_ref, high_ref, low_ref, left, inner_two, outer_two,
    inner_one, outer_one, z_term, image_parts, scaled,
):
    tiles = (statics_mm, statics_m, statics, statics_p, statics_pp)
    entries = line_ref.shape[1]
    clear_margins(inner_two, 5 * LAYERS, fields)
    clear_margins(inner_one, 3 * LAYERS, fields)
    for owner in range(peers):
        rows = slice(owner * fields, (owner + 1) * fields)
        scaled[rows, :] = table[rows, :] * table[peers * fields + owner : peers * fields + owner + 1, :]
    for tile, ref in enumerate(tiles):
        speed_ref[tile * HALF : (tile + 1) * HALF, :] = ref[0:HALF, :]
        rows = slice(tile * fields, (tile + 1) * fields)
        cell = entry_row(ref, 128).astype(jnp.int32)
        owner = jnp.broadcast_to(entry_row(ref, 132).astype(jnp.int32), (fields, entries))
        line_ref[rows, :] = jnp.broadcast_to(lax.shift_right_logical(cell, 8), (fields, entries))
        hot = slot_ref[tile * HALF : (tile + 1) * HALF, :]
        total = jnp.zeros((fields, entries), F32)
        for group in range(peers // 16):
            high, low = split(scaled[group * 16 * fields : (group + 1) * 16 * fields, :])
            read = jnp.dot(high, hot, preferred_element_type=F32) + jnp.dot(low, hot, preferred_element_type=F32)
            for i in range(16):
                total = total + jnp.where(owner == group * 16 + i, read[i * fields : (i + 1) * fields, :], 0.0)
        high, low = split(total * entry_row(ref, 140))
        high_ref[rows, :] = high.astype(F32)
        low_ref[rows, :] = low.astype(F32)

    def inject(index, carry):
        tile, chunk = index // 4, index % 4
        rows = at(tile * fields, fields)
        line, high, low = line_ref[rows, :], high_ref[rows, :], low_ref[rows, :]
        for x in range(LAYERS):
            for pair in range(4):
                row = (x * 4 + pair) * fields
                chosen = line == x * 16 + chunk * 4 + pair
                left[row : row + fields, :entries] = jnp.where(chosen, high, 0.0).astype(BF16)
                left[row : row + fields, entries:] = jnp.where(chosen, low, 0.0).astype(BF16)
        hot = cell_ref[pl.ds(pl.multiple_of(tile * 256, 256), 256), :]
        value = lax.dot_general(left[:, :entries], hot, NT, preferred_element_type=F32)
        value = value + lax.dot_general(left[:, entries:], hot, NT, preferred_element_type=F32)
        for x in range(LAYERS):
            for step in range(8):
                y = chunk * 8 + step
                row = (x * 4 + step // 2) * fields
                side = step % 2 * HALF
                now = value[row : row + fields, side : side + HALF]
                layer = tile * LAYERS + x
                outer_two[at((layer * 32 + y) * fields, fields), :] = now
                speed = spread(speed_ref, layer * 32 + y, fields)
                inner_two[at((layer * PADDED + REACH + y) * fields, fields), :] = speed * now
        return carry

    lax.fori_loop(0, 20, inject, 0)

    def step_one(index, carry):
        tile, chunk = index // 4 + 1, index % 4
        along_z(inner_two, tile * LAYERS, chunk, fields, band_ref, z_term)
        for x in range(LAYERS):
            for step in range(8):
                y = chunk * 8 + step

                def get(layer, row):
                    return inner_two[at(((tile * LAYERS + layer) * PADDED + REACH + row) * fields, fields), :]

                z_part = z_term[at((x * 8 + step) * fields, fields), :]
                layer = tile * LAYERS + x
                now = 2.0 * outer_two[at((layer * 32 + y) * fields, fields), :]
                now = now + laplacian(get, x, y, z_part, -4, 7)
                speed = spread(speed_ref, layer * 32 + y, fields)
                layer = layer - LAYERS
                outer_one[at((layer * 32 + y) * fields, fields), :] = now
                inner_one[at((layer * PADDED + REACH + y) * fields, fields), :] = speed * now
        return carry

    lax.fori_loop(0, 12, step_one, 0)

    def get_one(layer, row):
        return inner_one[at(((LAYERS + layer) * PADDED + REACH + row) * fields, fields), :]

    def step_two(chunk, total):
        along_z(inner_one, LAYERS, chunk, fields, band_ref, z_term)
        for x in range(LAYERS):
            for step in range(8):
                y = chunk * 8 + step
                cell = x * 32 + y
                z_part = z_term[at((x * 8 + step) * fields, fields), :]
                two = outer_two[at((2 * LAYERS * 32 + cell) * fields, fields), :]
                one = outer_one[at((LAYERS * 32 + cell) * fields, fields), :]
                zero = 2.0 * one - two + laplacian(get_one, x, y, z_part, -4, 7)
                value = spread(sources, cell, fields) * zero
                value = value + spread(sources, 128 + cell, fields) * one
                value = value + spread(sources, 256 + cell, fields) * two
                value = value + spread(prior, cell, fields) * turned[at(cell * fields, fields), :]
                image[at(cell * fields, fields), :] = value
                high, low = split(value)
                side = step * 256
                image_parts[0:fields, side : side + HALF] = high
                image_parts[0:fields, side + HALF : side + 256] = high
                image_parts[fields : 2 * fields, side : side + HALF] = low
                image_parts[fields : 2 * fields, side + HALF : side + 256] = jnp.zeros_like(low)
            rank = coeffs.shape[1]
            columns = basis[at((x * 4 + chunk) * rank, rank), :]
            total = total + lax.dot_general(image_parts[...], columns, NT, preferred_element_type=F32)
        return total

    total = lax.fori_loop(0, 4, step_two, jnp.zeros((2 * fields, coeffs.shape[1]), F32))
    coeffs[...] = total[:fields, :] + total[fields:, :]


def remainder(fields, image, basis, coeffs, out):
    rank = coeffs.shape[1]
    high, low = split(coeffs[...])
    parts = jnp.concatenate([high, low], axis=0)

    def body(group, carry):
        columns = basis[at(group * rank, rank), :]
        both = jnp.dot(parts, columns, preferred_element_type=F32)
        for step in range(8):
            cell = group * 8 + step
            side = step * 256
            along = both[:fields, side : side + HALF] + both[:fields, side + HALF : side + 256]
            along = along + both[fields:, side : side + HALF]
            out[pl.ds(cell, fields, stride=HALF), :] = image[at(cell * fields, fields), :] - along
        return carry

    lax.fori_loop(0, 16, body, 0)


def call(kernel, inputs, out_shape, scratch, flops, size, scalars=0):
    smem = pl.BlockSpec(memory_space=pltpu.SMEM)
    vmem = pl.BlockSpec(memory_space=pltpu.VMEM)
    return pl.pallas_call(
        kernel,
        out_shape=out_shape,
        in_specs=[smem] * scalars + [vmem] * (len(inputs) - scalars),
        out_specs=[vmem] * len(out_shape),
        scratch_shapes=scratch,
        cost_estimate=pl.CostEstimate(flops=flops, bytes_accessed=size, transcendentals=0),
        compiler_params=pltpu.CompilerParams(vmem_limit_bytes=44 * 2**20),
    )(*inputs)


def struct(*shape, dtype=F32):
    return jax.ShapeDtypeStruct(shape, dtype)


def shifted(array, axis, by):
    count = lax.axis_size(axis)
    pairs = [(i, i + by) for i in range(count) if 0 <= i + by < count]
    return lax.ppermute(array, axis, pairs)


def summed(array, axis):
    count = lax.axis_size(axis)
    if count & (count - 1):
        return lax.psum(array, axis)
    bit = 1
    while bit < count:
        array = array + lax.ppermute(array, axis, [(i, i ^ bit) for i in range(count)])
        bit *= 2
    return array


def local(
    probes,
    sources,
    kappa,
    prior,
    basis,
    entry_cell,
    entry_owner,
    entry_slot,
    entry_weight,
    entry_count,
    trace_weight,
):
    fields, rank = probes.shape[0], basis.shape[0]
    entries = entry_cell.shape[0]
    peers = lax.axis_size("space")
    padded = LAYERS * PADDED * fields
    cells = LAYERS * 32
    live = jnp.arange(entries, dtype=jnp.int32) < entry_count[0]
    weight = jnp.where(live, entry_weight, jnp.zeros_like(entry_weight))
    numbers = [array.astype(F32).reshape(-1, HALF) for array in (entry_cell, entry_owner, entry_slot)]
    own = jnp.concatenate([kappa.reshape(cells, HALF)] + numbers + [weight.reshape(-1, HALF)], axis=0)
    near = [shifted(own, "space", by) for by in (2, 1, -1, -2)]
    statics = [near[0], near[1], own, near[2], near[3]]
    matrix = jnp.asarray(band())
    sources = sources.reshape(3 * cells, HALF)

    turned, first, second, third = call(
        functools.partial(forward_own, fields),
        (probes.reshape(fields * cells, HALF), sources, kappa.reshape(cells, HALF), matrix),
        [struct(cells * fields, HALF), struct(padded, HALF), struct(padded, HALF), struct(cells * fields, HALF)],
        [pltpu.VMEM((32 * fields, HALF), F32)],
        600_000_000,
        6 * 2**20,
    )
    me = lax.axis_index("space").astype(jnp.int32).reshape(1)
    table, cell_hot, slot_hot = call(
        functools.partial(forward_window, fields, peers),
        (me, first, second, third, *statics, matrix, trace_weight.reshape(1, HALF)),
        [
            struct(peers * (fields + 1), HALF),
            struct(5 * 256, entries, dtype=BF16),
            struct(5 * HALF, entries, dtype=BF16),
        ],
        [
            pltpu.VMEM((padded, HALF), F32),
            pltpu.VMEM((padded, HALF), F32),
            pltpu.VMEM((32 * fields, HALF), F32),
            pltpu.VMEM((16 * fields, 256), F32),
            pltpu.VMEM((5 * fields, entries), F32),
            pltpu.VMEM((5 * fields, entries), jnp.int32),
            pltpu.VMEM((5 * fields, entries), jnp.int32),
            pltpu.VMEM((5 * fields, entries), F32),
        ],
        3_000_000_000,
        6 * 2**20,
        scalars=1,
    )
    table = summed(table, "space")
    (columns,) = call(
        basis_parts,
        (basis.reshape(rank * cells, HALF),),
        [struct(16 * rank, 2048, dtype=BF16)],
        [],
        10_000_000,
        8 * 2**20,
    )
    image, coeffs = call(
        functools.partial(adjoint, fields, peers),
        (table, *statics, cell_hot, slot_hot, turned, sources, prior.reshape(cells, HALF), matrix, columns),
        [struct(cells * fields, HALF), struct(fields, rank)],
        [
            pltpu.VMEM((5 * HALF, HALF), F32),
            pltpu.VMEM((5 * fields, entries), jnp.int32),
            pltpu.VMEM((5 * fields, entries), F32),
            pltpu.VMEM((5 * fields, entries), F32),
            pltpu.VMEM((16 * fields, 2 * entries), BF16),
            pltpu.VMEM((5 * padded, HALF), F32),
            pltpu.VMEM((5 * cells * fields, HALF), F32),
            pltpu.VMEM((3 * padded, HALF), F32),
            pltpu.VMEM((3 * cells * fields, HALF), F32),
            pltpu.VMEM((32 * fields, HALF), F32),
            pltpu.VMEM((2 * fields, 2048), BF16),
            pltpu.VMEM((peers * fields, HALF), F32),
        ],
        5_000_000_000,
        10 * 2**20,
    )
    coeffs = summed(coeffs, "space")
    (hess_probe,) = call(
        functools.partial(remainder, fields),
        (image, columns, coeffs),
        [struct(fields * cells, HALF)],
        [],
        200_000_000,
        6 * 2**20,
    )
    return hess_probe.reshape(probes.shape), coeffs.T


def solution(mesh):
    return jax.shard_map(
        local,
        mesh=mesh,
        in_specs=(
            P("group", "space", None, None),
            P(None, ("group", "space"), None, None),
            P(("group", "space"), None, None),
            P(("group", "space"), None, None),
            P("group", "space", None, None),
            P(("group", "space")),
            P(("group", "space")),
            P(("group", "space")),
            P(("group", "space")),
            P(("group", "space")),
            P(("group", "space")),
        ),
        out_specs=(P("group", "space", None, None), P("group", None)),
        check_vma=False,
    )
```

```python
import functools

import jax
import jax.numpy as jnp
import ml_dtypes
import numpy as np
from jax import lax
from jax.experimental import pallas as pl
from jax.experimental.pallas import tpu as pltpu
from jax.sharding import PartitionSpec as P

STENCIL = (-205.0 / 72.0, 8.0 / 5.0, -1.0 / 5.0, 8.0 / 315.0, -1.0 / 560.0)
CENTER = 3.0 * STENCIL[0]
REACH = 4
LAYERS = 4
PADDED = 40
HALF = 128
F32 = jnp.float32
BF16 = jnp.bfloat16
NT = (((1,), (1,)), ((), ()))


def band():
    place = np.arange(HALF)
    apart = np.abs(place[:, None] - place[None, :])
    full = np.zeros((HALF, HALF), np.float32)
    for reach in range(1, REACH + 1):
        full[apart == reach] = STENCIL[reach]
    high = full.astype(ml_dtypes.bfloat16)
    low = (full - high.astype(np.float32)).astype(ml_dtypes.bfloat16)
    return np.block([[high, low], [high, np.zeros_like(low)]])


def split(value):
    high = value.astype(BF16)
    low = (value - high.astype(F32)).astype(BF16)
    return high, low


def at(row, count=16):
    return pl.ds(pl.multiple_of(row, 16), count)


def spread(ref, row, fields):
    return jnp.broadcast_to(ref[pl.ds(row, 1), :], (fields, HALF))


def clear_margins(ref, layers, fields):
    margin = jnp.zeros((REACH * fields, HALF), F32)
    for layer in range(layers):
        start = layer * PADDED * fields
        ref[start : start + REACH * fields, :] = margin
        start += (PADDED - REACH) * fields
        ref[start : start + REACH * fields, :] = margin


def along_z(ref, first, chunk, fields, band_ref, out_ref):
    count = 8 * fields
    pieces = [ref[at(((first + x) * PADDED + REACH + chunk * 8) * fields, count), :] for x in range(LAYERS)]
    high, low = split(jnp.concatenate(pieces, axis=0))
    both = jnp.dot(jnp.concatenate([high, low], axis=1), band_ref[...], preferred_element_type=F32)
    out_ref[...] = both[:, :HALF] + both[:, HALF:]


def laplacian(get, x, y, z_term, lowest, highest):
    total = CENTER * get(x, y) + z_term
    for k in range(1, REACH + 1):
        ring = get(x, y + k) + get(x, y - k)
        if x + k <= highest:
            ring = ring + get(x + k, y)
        if x - k >= lowest:
            ring = ring + get(x - k, y)
        total = total + STENCIL[k] * ring
    return total


def forward_own(fields, probes, sources, kappa, band_ref, turned, first, second, third, z_term):
    clear_margins(first, LAYERS, fields)
    clear_margins(second, LAYERS, fields)

    def load(chunk, carry):
        for x in range(LAYERS):
            for step in range(8):
                y = chunk * 8 + step
                cell = x * 32 + y
                value = probes[pl.ds(cell, fields, stride=HALF), :]
                turned[at(cell * fields, fields), :] = value
                first[at((x * PADDED + REACH + y) * fields, fields), :] = value * spread(sources, cell, fields)
        return carry

    lax.fori_loop(0, 4, load, 0)

    def sweep(field, chunk, emit):
        along_z(field, 0, chunk, fields, band_ref, z_term)
        for x in range(LAYERS):
            for step in range(8):
                y = chunk * 8 + step

                def get(layer, row):
                    return field[at((layer * PADDED + REACH + row) * fields, fields), :]

                z_part = z_term[at((x * 8 + step) * fields, fields), :]
                total = laplacian(get, x, y, z_part, 0, LAYERS - 1)
                emit(x, y, get(x, y), spread(kappa, x * 32 + y, fields) * total)

    def step_one(chunk, carry):
        def emit(x, y, now, change):
            cell = x * 32 + y
            push = turned[at(cell * fields, fields), :] * spread(sources, 128 + cell, fields)
            second[at((x * PADDED + REACH + y) * fields, fields), :] = 2.0 * now + change + push

        sweep(first, chunk, emit)
        return carry

    lax.fori_loop(0, 4, step_one, 0)

    def step_two(chunk, carry):
        def emit(x, y, now, change):
            cell = x * 32 + y
            push = turned[at(cell * fields, fields), :] * spread(sources, 256 + cell, fields)
            before = first[at((x * PADDED + REACH + y) * fields, fields), :]
            third[at(cell * fields, fields), :] = 2.0 * now - before + change + push

        sweep(second, chunk, emit)
        return carry

    lax.fori_loop(0, 4, step_two, 0)


def entry_row(ref, row):
    return jnp.concatenate([ref[row + i : row + i + 1, :] for i in range(4)], axis=1)


def describe(statics, fields, pair, cell_ref, line_ref, owner_ref, slot_ref, weight_ref):
    entries = pair.shape[1]
    place = lax.broadcasted_iota(jnp.int32, (256, entries), 0)
    slot_place = lax.broadcasted_iota(jnp.int32, (HALF, entries), 0)
    for tile, ref in enumerate(statics):
        cell = entry_row(ref, 128).astype(jnp.int32)
        owner = entry_row(ref, 132).astype(jnp.int32)
        slot = entry_row(ref, 136).astype(jnp.int32)
        weight = entry_row(ref, 140)
        hot = jnp.where(place == jnp.bitwise_and(cell, 255), 1.0, 0.0)
        cell_ref[tile * 256 : (tile + 1) * 256, :] = hot.astype(BF16)
        hot = jnp.where(slot_place == slot, 1.0, 0.0)
        slot_ref[tile * HALF : (tile + 1) * HALF, :] = hot.astype(BF16)
        rows = slice(tile * fields, (tile + 1) * fields)
        line_ref[rows, :] = jnp.broadcast_to(lax.shift_right_logical(cell, 8), (fields, entries))
        owner_ref[rows, :] = jnp.broadcast_to(owner, (fields, entries))
        weight_ref[rows, :] = jnp.broadcast_to(weight, (fields, entries))


def forward_window(
    fields, peers, first, second, third, kappa_mm, kappa_m, kappa, kappa_p, kappa_pp, band_ref,
    table, cell_ref, slot_ref, below, above, z_term, sample, total_ref, line_ref, owner_ref, weight_ref,
):
    statics = (kappa_mm, kappa_m, kappa, kappa_p, kappa_pp)
    entries = line_ref.shape[1]
    describe(statics, fields, cell_ref, cell_ref, line_ref, owner_ref, slot_ref, weight_ref)
    clear_margins(below, LAYERS, fields)
    clear_margins(above, LAYERS, fields)
    total_ref[...] = jnp.zeros_like(total_ref)

    def outward(chunk, carry):
        for step in range(8):
            y = chunk * 8 + step
            own = [first[at((x * PADDED + REACH + y) * fields, fields), :] for x in range(LAYERS)]
            for x in range(LAYERS):
                up = sum(STENCIL[4 + x - other] * own[other] for other in range(x, LAYERS))
                down = sum(STENCIL[4 + other - x] * own[other] for other in range(x + 1))
                row = at((x * PADDED + REACH + y) * fields, fields)
                above[row, :] = spread(kappa_p, x * 32 + y, fields) * up
                below[row, :] = spread(kappa_m, x * 32 + y, fields) * down
        return carry

    lax.fori_loop(0, 4, outward, 0)

    def read(layer, y):
        ref = (below, second, above)[(layer + LAYERS) // LAYERS]
        return ref[at((layer % LAYERS * PADDED + REACH + y) * fields, fields), :]

    def far(x, y, lowest, highest):
        total = None
        for other in range(lowest, highest + 1):
            if 1 <= abs(x - other) <= REACH:
                term = STENCIL[abs(x - other)] * read(other, y)
                total = term if total is None else total + term
        return total

    def sampling(chunk, carry):
        for tile in range(5):
            if tile in (1, 3):
                along_z((below, above)[tile // 2], 0, chunk, fields, band_ref, z_term)
            for x in range(LAYERS):
                for step in range(8):
                    y = chunk * 8 + step
                    cell = x * 32 + y
                    layer = (tile - 2) * LAYERS + x
                    speed = spread(statics[tile], cell, fields)
                    if tile in (0, 4):
                        value = speed * far(layer, y, -4, 7)
                    elif tile == 2:
                        outside = far(layer, y, -4, -1) + far(layer, y, 4, 7)
                        value = third[at(cell * fields, fields), :] + speed * outside
                    else:
                        z_part = z_term[at((x * 8 + step) * fields, fields), :]
                        value = 2.0 * read(layer, y) + speed * laplacian(read, layer, y, z_part, -4, 7)
                    row = (x * 4 + step // 2) * fields
                    side = step % 2 * HALF
                    sample[row : row + fields, side : side + HALF] = value
            high, low = split(sample[...])
            hot = cell_ref[tile * 256 : (tile + 1) * 256, :]
            picked = jnp.dot(high, hot, preferred_element_type=F32) + jnp.dot(low, hot, preferred_element_type=F32)
            rows = slice(tile * fields, (tile + 1) * fields)
            line = line_ref[rows, :]
            total = total_ref[rows, :]
            for x in range(LAYERS):
                for pair in range(4):
                    row = (x * 4 + pair) * fields
                    chosen = line == x * 16 + chunk * 4 + pair
                    total = total + jnp.where(chosen, picked[row : row + fields, :], 0.0)
            total_ref[rows, :] = total
        return carry

    lax.fori_loop(0, 4, sampling, 0)

    for group in range(peers // 16):
        result = jnp.zeros((16 * fields, HALF), F32)
        for tile in range(5):
            rows = slice(tile * fields, (tile + 1) * fields)
            high, low = split(total_ref[rows, :] * weight_ref[rows, :])
            high, low = high.astype(F32), low.astype(F32)
            owner = owner_ref[rows, :]
            hot = slot_ref[tile * HALF : (tile + 1) * HALF, :]
            for part in (high, low):
                pieces = [jnp.where(owner == group * 16 + i, part, 0.0).astype(BF16) for i in range(16)]
                result = result + lax.dot_general(
                    jnp.concatenate(pieces, axis=0), hot, NT, preferred_element_type=F32
                )
        table[group * 16 * fields : (group + 1) * 16 * fields, :] = result


def basis_parts(basis, out):
    rank = basis.shape[0] // HALF

    def body(group, carry):
        for step in range(8):
            high, low = split(basis[pl.ds(group * 8 + step, rank, stride=HALF), :])
            rows = at(group * rank, rank)
            out[rows, step * 256 : step * 256 + HALF] = high
            out[rows, step * 256 + HALF : (step + 1) * 256] = low
        return carry

    lax.fori_loop(0, 16, body, 0)


def adjoint(
    fields, peers, table, statics_mm, statics_m, statics, statics_p, statics_pp, cell_ref, slot_ref, turned, sources,
    prior, band_ref, basis, image, coeffs, speed_ref, line_ref, high_ref, low_ref, left, inner_two, outer_two,
    inner_one, outer_one, z_term, image_parts,
):
    rank = basis.shape[0] // 16
    tiles = (statics_mm, statics_m, statics, statics_p, statics_pp)
    entries = line_ref.shape[1]
    clear_margins(inner_two, 5 * LAYERS, fields)
    clear_margins(inner_one, 3 * LAYERS, fields)
    for tile, ref in enumerate(tiles):
        speed_ref[tile * HALF : (tile + 1) * HALF, :] = ref[0:HALF, :]
        rows = slice(tile * fields, (tile + 1) * fields)
        cell = entry_row(ref, 128).astype(jnp.int32)
        owner = jnp.broadcast_to(entry_row(ref, 132).astype(jnp.int32), (fields, entries))
        line_ref[rows, :] = jnp.broadcast_to(lax.shift_right_logical(cell, 8), (fields, entries))
        hot = slot_ref[tile * HALF : (tile + 1) * HALF, :]
        total = jnp.zeros((fields, entries), F32)
        for group in range(peers // 16):
            high, low = split(table[group * 16 * fields : (group + 1) * 16 * fields, :])
            read = jnp.dot(high, hot, preferred_element_type=F32) + jnp.dot(low, hot, preferred_element_type=F32)
            for i in range(16):
                total = total + jnp.where(owner == group * 16 + i, read[i * fields : (i + 1) * fields, :], 0.0)
        high, low = split(total * entry_row(ref, 140))
        high_ref[rows, :] = high.astype(F32)
        low_ref[rows, :] = low.astype(F32)

    def inject(index, carry):
        tile, chunk = index // 4, index % 4
        rows = at(tile * fields, fields)
        line, high, low = line_ref[rows, :], high_ref[rows, :], low_ref[rows, :]
        for x in range(LAYERS):
            for pair in range(4):
                row = (x * 4 + pair) * fields
                chosen = line == x * 16 + chunk * 4 + pair
                left[row : row + fields, :entries] = jnp.where(chosen, high, 0.0).astype(BF16)
                left[row : row + fields, entries:] = jnp.where(chosen, low, 0.0).astype(BF16)
        hot = cell_ref[pl.ds(pl.multiple_of(tile * 256, 256), 256), :]
        value = lax.dot_general(left[:, :entries], hot, NT, preferred_element_type=F32)
        value = value + lax.dot_general(left[:, entries:], hot, NT, preferred_element_type=F32)
        for x in range(LAYERS):
            for step in range(8):
                y = chunk * 8 + step
                row = (x * 4 + step // 2) * fields
                side = step % 2 * HALF
                now = value[row : row + fields, side : side + HALF]
                layer = tile * LAYERS + x
                outer_two[at((layer * 32 + y) * fields, fields), :] = now
                speed = spread(speed_ref, layer * 32 + y, fields)
                inner_two[at((layer * PADDED + REACH + y) * fields, fields), :] = speed * now
        return carry

    lax.fori_loop(0, 20, inject, 0)

    def step_one(index, carry):
        tile, chunk = index // 4 + 1, index % 4
        along_z(inner_two, tile * LAYERS, chunk, fields, band_ref, z_term)
        for x in range(LAYERS):
            for step in range(8):
                y = chunk * 8 + step

                def get(layer, row):
                    return inner_two[at(((tile * LAYERS + layer) * PADDED + REACH + row) * fields, fields), :]

                z_part = z_term[at((x * 8 + step) * fields, fields), :]
                layer = tile * LAYERS + x
                now = 2.0 * outer_two[at((layer * 32 + y) * fields, fields), :]
                now = now + laplacian(get, x, y, z_part, -4, 7)
                speed = spread(speed_ref, layer * 32 + y, fields)
                layer = layer - LAYERS
                outer_one[at((layer * 32 + y) * fields, fields), :] = now
                inner_one[at((layer * PADDED + REACH + y) * fields, fields), :] = speed * now
        return carry

    lax.fori_loop(0, 12, step_one, 0)

    def get_one(layer, row):
        return inner_one[at(((LAYERS + layer) * PADDED + REACH + row) * fields, fields), :]

    def step_two(chunk, total):
        along_z(inner_one, LAYERS, chunk, fields, band_ref, z_term)
        for x in range(LAYERS):
            for step in range(8):
                y = chunk * 8 + step
                cell = x * 32 + y
                z_part = z_term[at((x * 8 + step) * fields, fields), :]
                two = outer_two[at((2 * LAYERS * 32 + cell) * fields, fields), :]
                one = outer_one[at((LAYERS * 32 + cell) * fields, fields), :]
                zero = 2.0 * one - two + laplacian(get_one, x, y, z_part, -4, 7)
                value = spread(sources, cell, fields) * zero
                value = value + spread(sources, 128 + cell, fields) * one
                value = value + spread(sources, 256 + cell, fields) * two
                value = value + spread(prior, cell, fields) * turned[at(cell * fields, fields), :]
                image[at(cell * fields, fields), :] = value
                high, low = split(value)
                side = step * 256
                image_parts[0:fields, side : side + HALF] = high
                image_parts[0:fields, side + HALF : side + 256] = high
                image_parts[fields : 2 * fields, side : side + HALF] = low
                image_parts[fields : 2 * fields, side + HALF : side + 256] = jnp.zeros_like(low)
            columns = basis[at((x * 4 + chunk) * rank, rank), :]
            total = total + lax.dot_general(image_parts[...], columns, NT, preferred_element_type=F32)
        return total

    total = lax.fori_loop(0, 4, step_two, jnp.zeros((2 * fields, rank), F32))
    part = total[:fields, :] + total[fields:, :]
    part = jnp.concatenate([part, jnp.zeros((fields, coeffs.shape[1] - rank), F32)], axis=1)
    for peer in range(peers):
        coeffs[peer * fields : (peer + 1) * fields, :] = part


def weigh(fields, peers, arrived, scale, out):
    total = arrived[0:fields, :]
    for peer in range(1, peers):
        total = total + arrived[peer * fields : (peer + 1) * fields, :]
    total = total * scale[...]
    for peer in range(peers):
        out[peer * fields : (peer + 1) * fields, :] = total


def remainder(fields, peers, image, basis, arrived, out, coeffs):
    rank = coeffs.shape[1]
    total = arrived[0:fields, :rank]
    for peer in range(1, peers):
        total = total + arrived[peer * fields : (peer + 1) * fields, :rank]
    coeffs[...] = total
    high, low = split(total)
    parts = jnp.concatenate([high, low], axis=0)

    def body(group, carry):
        columns = basis[at(group * rank, rank), :]
        both = jnp.dot(parts, columns, preferred_element_type=F32)
        for step in range(8):
            cell = group * 8 + step
            side = step * 256
            along = both[:fields, side : side + HALF] + both[:fields, side + HALF : side + 256]
            along = along + both[fields:, side : side + HALF]
            out[pl.ds(cell, fields, stride=HALF), :] = image[at(cell * fields, fields), :] - along
        return carry

    lax.fori_loop(0, 16, body, 0)


def call(kernel, inputs, out_shape, scratch, flops, size, scalars=0):
    smem = pl.BlockSpec(memory_space=pltpu.SMEM)
    vmem = pl.BlockSpec(memory_space=pltpu.VMEM)
    return pl.pallas_call(
        kernel,
        out_shape=out_shape,
        in_specs=[smem] * scalars + [vmem] * (len(inputs) - scalars),
        out_specs=[vmem] * len(out_shape),
        scratch_shapes=scratch,
        cost_estimate=pl.CostEstimate(flops=flops, bytes_accessed=size, transcendentals=0),
        compiler_params=pltpu.CompilerParams(vmem_limit_bytes=44 * 2**20),
    )(*inputs)


def struct(*shape, dtype=F32):
    return jax.ShapeDtypeStruct(shape, dtype)


def shifted(array, axis, by):
    count = lax.axis_size(axis)
    pairs = [(i, i + by) for i in range(count) if 0 <= i + by < count]
    return lax.ppermute(array, axis, pairs)


def exchanged(array, axis):
    return lax.all_to_all(array, axis, split_axis=0, concat_axis=0, tiled=True)


def local(
    probes,
    sources,
    kappa,
    prior,
    basis,
    entry_cell,
    entry_owner,
    entry_slot,
    entry_weight,
    entry_count,
    trace_weight,
):
    fields, rank = probes.shape[0], basis.shape[0]
    entries = entry_cell.shape[0]
    peers = lax.axis_size("space")
    padded = LAYERS * PADDED * fields
    cells = LAYERS * 32
    live = jnp.arange(entries, dtype=jnp.int32) < entry_count[0]
    weight = jnp.where(live, entry_weight, jnp.zeros_like(entry_weight))
    numbers = [array.astype(F32).reshape(-1, HALF) for array in (entry_cell, entry_owner, entry_slot)]
    own = jnp.concatenate([kappa.reshape(cells, HALF)] + numbers + [weight.reshape(-1, HALF)], axis=0)
    near = [shifted(own, "space", by) for by in (2, 1, -1, -2)]
    statics = [near[0], near[1], own, near[2], near[3]]
    matrix = jnp.asarray(band())
    sources = sources.reshape(3 * cells, HALF)

    turned, first, second, third = call(
        functools.partial(forward_own, fields),
        (probes.reshape(fields * cells, HALF), sources, kappa.reshape(cells, HALF), matrix),
        [struct(cells * fields, HALF), struct(padded, HALF), struct(padded, HALF), struct(cells * fields, HALF)],
        [pltpu.VMEM((32 * fields, HALF), F32)],
        600_000_000,
        6 * 2**20,
    )
    table, cell_hot, slot_hot = call(
        functools.partial(forward_window, fields, peers),
        (first, second, third, *statics, matrix),
        [
            struct(peers * fields, HALF),
            struct(5 * 256, entries, dtype=BF16),
            struct(5 * HALF, entries, dtype=BF16),
        ],
        [
            pltpu.VMEM((padded, HALF), F32),
            pltpu.VMEM((padded, HALF), F32),
            pltpu.VMEM((32 * fields, HALF), F32),
            pltpu.VMEM((16 * fields, 256), F32),
            pltpu.VMEM((5 * fields, entries), F32),
            pltpu.VMEM((5 * fields, entries), jnp.int32),
            pltpu.VMEM((5 * fields, entries), jnp.int32),
            pltpu.VMEM((5 * fields, entries), F32),
        ],
        3_000_000_000,
        6 * 2**20,
    )
    arrived = exchanged(table, "space")
    (weighted,) = call(
        functools.partial(weigh, fields, peers),
        (arrived, trace_weight.reshape(1, HALF)),
        [struct(peers * fields, HALF)],
        [],
        1_000_000,
        2**18,
    )
    table = exchanged(weighted, "space")
    (columns,) = call(
        basis_parts,
        (basis.reshape(rank * cells, HALF),),
        [struct(16 * rank, 2048, dtype=BF16)],
        [],
        10_000_000,
        8 * 2**20,
    )
    image, coeffs = call(
        functools.partial(adjoint, fields, peers),
        (table, *statics, cell_hot, slot_hot, turned, sources, prior.reshape(cells, HALF), matrix, columns),
        [struct(cells * fields, HALF), struct(peers * fields, -(-rank // HALF) * HALF)],
        [
            pltpu.VMEM((5 * HALF, HALF), F32),
            pltpu.VMEM((5 * fields, entries), jnp.int32),
            pltpu.VMEM((5 * fields, entries), F32),
            pltpu.VMEM((5 * fields, entries), F32),
            pltpu.VMEM((16 * fields, 2 * entries), BF16),
            pltpu.VMEM((5 * padded, HALF), F32),
            pltpu.VMEM((5 * cells * fields, HALF), F32),
            pltpu.VMEM((3 * padded, HALF), F32),
            pltpu.VMEM((3 * cells * fields, HALF), F32),
            pltpu.VMEM((32 * fields, HALF), F32),
            pltpu.VMEM((2 * fields, 2048), BF16),
        ],
        5_000_000_000,
        10 * 2**20,
    )
    arrived = exchanged(coeffs, "space")
    hess_probe, coeffs = call(
        functools.partial(remainder, fields, peers),
        (image, columns, arrived),
        [struct(fields * cells, HALF), struct(fields, rank)],
        [],
        200_000_000,
        6 * 2**20,
    )
    return hess_probe.reshape(probes.shape), coeffs.T


def solution(mesh):
    return jax.shard_map(
        local,
        mesh=mesh,
        in_specs=(
            P("group", "space", None, None),
            P(None, ("group", "space"), None, None),
            P(("group", "space"), None, None),
            P(("group", "space"), None, None),
            P("group", "space", None, None),
            P(("group", "space")),
            P(("group", "space")),
            P(("group", "space")),
            P(("group", "space")),
            P(("group", "space")),
            P(("group", "space")),
        ),
        out_specs=(P("group", "space", None, None), P("group", None)),
        check_vma=False,
    )
```

```python
import functools

import jax
import jax.numpy as jnp
from jax import lax
from jax.experimental import pallas as pl
from jax.experimental.pallas import tpu as pltpu
from jax.sharding import PartitionSpec as P

STENCIL = (-205.0 / 72.0, 8.0 / 5.0, -1.0 / 5.0, 8.0 / 315.0, -1.0 / 560.0)
CENTER = 3.0 * STENCIL[0]
REACH = 4
LAYERS = 4
PADDED = 40
HALF = 128
F32 = jnp.float32
BF16 = jnp.bfloat16
NT = (((1,), (1,)), ((), ()))


def split(value):
    high = value.astype(BF16)
    low = (value - high.astype(F32)).astype(BF16)
    return high, low


def at(row, count=16):
    return pl.ds(pl.multiple_of(row, 16), count)


def spread(ref, row, fields):
    return jnp.broadcast_to(ref[pl.ds(row, 1), :], (fields, HALF))


def clear_margins(ref, layers, fields):
    margin = jnp.zeros((REACH * fields, HALF), F32)
    for layer in range(layers):
        start = layer * PADDED * fields
        ref[start : start + REACH * fields, :] = margin
        start += (PADDED - REACH) * fields
        ref[start : start + REACH * fields, :] = margin


def along_z(ref, first, fields, band_ref, out_ref, row=0):
    pieces = [ref[at(((first + x) * PADDED + REACH) * fields, 32 * fields), :] for x in range(LAYERS)]
    high, low = split(jnp.concatenate(pieces, axis=0))
    both = jnp.dot(jnp.concatenate([high, low], axis=1), band_ref[...], preferred_element_type=F32)
    out_ref[at(row, LAYERS * 32 * fields), :] = both[:, :HALF] + both[:, HALF:]


def laplacian(get, x, y, z_term, lowest, highest):
    total = CENTER * get(x, y) + z_term
    for k in range(1, REACH + 1):
        ring = get(x, y + k) + get(x, y - k)
        if x + k <= highest:
            ring = ring + get(x + k, y)
        if x - k >= lowest:
            ring = ring + get(x - k, y)
        total = total + STENCIL[k] * ring
    return total


def pack(
    count, probes, sources, prior, kappa, cell, owner, slot, weight,
    statics, probes_out, sources_out, prior_out, band_ref, small_int, small_float, sem,
):
    rows = cell.shape[0]
    cells = kappa.shape[0]
    small = [
        pltpu.make_async_copy(kappa, statics.at[pl.ds(0, cells)], sem.at[0]),
        pltpu.make_async_copy(cell, small_int.at[0], sem.at[1]),
        pltpu.make_async_copy(owner, small_int.at[1], sem.at[2]),
        pltpu.make_async_copy(slot, small_int.at[2], sem.at[3]),
        pltpu.make_async_copy(weight, small_float, sem.at[4]),
    ]
    large = [
        pltpu.make_async_copy(probes, probes_out, sem.at[5]),
        pltpu.make_async_copy(sources, sources_out, sem.at[6]),
        pltpu.make_async_copy(prior, prior_out, sem.at[7]),
    ]
    for copy in small + large:
        copy.start()
    apart = lax.broadcasted_iota(jnp.int32, (HALF, HALF), 0) - lax.broadcasted_iota(jnp.int32, (HALF, HALF), 1)
    full = jnp.zeros((HALF, HALF), F32)
    for reach in range(1, REACH + 1):
        full = jnp.where(jnp.abs(apart) == reach, STENCIL[reach], full)
    high, low = split(full)
    band_ref[0:HALF, 0:HALF] = high
    band_ref[HALF:, 0:HALF] = high
    band_ref[0:HALF, HALF:] = low
    band_ref[HALF:, HALF:] = jnp.zeros_like(low)
    for copy in small:
        copy.wait()
    for i in range(3):
        statics[cells + i * rows : cells + (i + 1) * rows, :] = small_int[i].astype(F32)
    place = lax.broadcasted_iota(jnp.int32, (rows, HALF), 0) * HALF
    place = place + lax.broadcasted_iota(jnp.int32, (rows, HALF), 1)
    live = jnp.where(place < count[0], small_float[...], 0.0)
    statics[cells + 3 * rows : cells + 4 * rows, :] = live
    for copy in large:
        copy.wait()


def forward_own(fields, probes, sources, statics, band_ref, turned, first, second, third, z_term):
    clear_margins(first, LAYERS, fields)
    clear_margins(second, LAYERS, fields)

    def load(chunk, carry):
        for x in range(LAYERS):
            for step in range(8):
                y = chunk * 8 + step
                cell = x * 32 + y
                value = probes[pl.ds(cell, fields, stride=HALF), :]
                turned[at(cell * fields, fields), :] = value
                first[at((x * PADDED + REACH + y) * fields, fields), :] = value * spread(sources, cell, fields)
        return carry

    lax.fori_loop(0, 4, load, 0)

    def sweep(field, emit):
        along_z(field, 0, fields, band_ref, z_term)

        def body(chunk, carry):
            for x in range(LAYERS):
                for step in range(8):
                    y = chunk * 8 + step
                    cell = x * 32 + y

                    def get(layer, row):
                        return field[at((layer * PADDED + REACH + row) * fields, fields), :]

                    z_part = z_term[at(cell * fields, fields), :]
                    total = laplacian(get, x, y, z_part, 0, LAYERS - 1)
                    emit(x, y, get(x, y), spread(statics, cell, fields) * total)
            return carry

        lax.fori_loop(0, 4, body, 0)

    def step_one(x, y, now, change):
        cell = x * 32 + y
        push = turned[at(cell * fields, fields), :] * spread(sources, 128 + cell, fields)
        second[at((x * PADDED + REACH + y) * fields, fields), :] = 2.0 * now + change + push

    sweep(first, step_one)

    def step_two(x, y, now, change):
        cell = x * 32 + y
        push = turned[at(cell * fields, fields), :] * spread(sources, 256 + cell, fields)
        before = first[at((x * PADDED + REACH + y) * fields, fields), :]
        third[at(cell * fields, fields), :] = 2.0 * now - before + change + push

    sweep(second, step_two)


def entry_row(value, row):
    return jnp.concatenate([value[row + i : row + i + 1, :] for i in range(4)], axis=1)


def forward_window(
    fields, peers, me, first, second, third, own, partner, before, after, band_ref, own_scale,
    kept, sent, cell_ref, slot_ref, speed_ref, line_ref, owner_ref, weight_ref,
    below, above, z_term, sample, total_ref, table,
):
    entries = line_ref.shape[1]
    cells = LAYERS * 32
    length = own.shape[0]
    odd = me[0] % 2 == 1
    clear_margins(below, LAYERS, fields)
    clear_margins(above, LAYERS, fields)
    total_ref[...] = jnp.zeros_like(total_ref)
    tiles = (
        before[0:length, :],
        jnp.where(odd, partner[...], before[length:, :]),
        own[...],
        jnp.where(odd, after[length:, :], partner[...]),
        after[0:length, :],
    )
    place = lax.broadcasted_iota(jnp.int32, (256, entries), 0)
    slot_place = lax.broadcasted_iota(jnp.int32, (HALF, entries), 0)
    for tile, value in enumerate(tiles):
        speed_ref[tile * cells : (tile + 1) * cells, :] = value[0:cells, :]
        cell = entry_row(value, cells).astype(jnp.int32)
        owner = entry_row(value, cells + 4).astype(jnp.int32)
        slot = entry_row(value, cells + 8).astype(jnp.int32)
        weight = entry_row(value, cells + 12)
        hot = jnp.where(place == jnp.bitwise_and(cell, 255), 1.0, 0.0)
        cell_ref[tile * 256 : (tile + 1) * 256, :] = hot.astype(BF16)
        hot = jnp.where(slot_place == slot, 1.0, 0.0)
        slot_ref[tile * HALF : (tile + 1) * HALF, :] = hot.astype(BF16)
        rows = slice(tile * fields, (tile + 1) * fields)
        line_ref[rows, :] = jnp.broadcast_to(lax.shift_right_logical(cell, 8), (fields, entries))
        owner_ref[rows, :] = jnp.broadcast_to(owner, (fields, entries))
        weight_ref[rows, :] = jnp.broadcast_to(weight, (fields, entries))

    def outward(chunk, carry):
        for step in range(8):
            y = chunk * 8 + step
            mine = [first[at((x * PADDED + REACH + y) * fields, fields), :] for x in range(LAYERS)]
            for x in range(LAYERS):
                up = sum(STENCIL[4 + x - other] * mine[other] for other in range(x, LAYERS))
                down = sum(STENCIL[4 + other - x] * mine[other] for other in range(x + 1))
                row = at((x * PADDED + REACH + y) * fields, fields)
                above[row, :] = spread(speed_ref, 3 * cells + x * 32 + y, fields) * up
                below[row, :] = spread(speed_ref, cells + x * 32 + y, fields) * down
        return carry

    lax.fori_loop(0, 4, outward, 0)
    along_z(below, 0, fields, band_ref, z_term, 0)
    along_z(above, 0, fields, band_ref, z_term, cells * fields)

    def read(layer, y):
        ref = (below, second, above)[(layer + LAYERS) // LAYERS]
        return ref[at((layer % LAYERS * PADDED + REACH + y) * fields, fields), :]

    def far(x, y, lowest, highest):
        total = None
        for other in range(lowest, highest + 1):
            if 1 <= abs(x - other) <= REACH:
                term = STENCIL[abs(x - other)] * read(other, y)
                total = term if total is None else total + term
        return total

    def respond(chunk, carry):
        for tile in range(5):
            for x in range(LAYERS):
                for pair in range(4):
                    halves = []
                    for step in range(2):
                        y = chunk * 8 + pair * 2 + step
                        cell = x * 32 + y
                        layer = (tile - 2) * LAYERS + x
                        speed = spread(speed_ref, tile * cells + cell, fields)
                        if tile in (0, 4):
                            value = speed * far(layer, y, -4, 7)
                        elif tile == 2:
                            outside = far(layer, y, -4, -1) + far(layer, y, 4, 7)
                            value = third[at(cell * fields, fields), :] + speed * outside
                        else:
                            z_part = z_term[at((tile // 2 * cells + cell) * fields, fields), :]
                            value = 2.0 * read(layer, y) + speed * laplacian(read, layer, y, z_part, -4, 7)
                        halves.append(split(value))
                    row = at((tile * 64 + x * 16 + chunk * 4 + pair) * fields, fields)
                    for step, (high, low) in enumerate(halves):
                        sample[row, step * HALF : (step + 1) * HALF] = high
                        sample[row, 256 + step * HALF : 256 + (step + 1) * HALF] = low
        return carry

    lax.fori_loop(0, 4, respond, 0)

    def pick(tile, carry):
        hot = cell_ref[at(tile * 256, 256), :]
        parts = sample[at(tile * 64 * fields, 64 * fields), :]
        picked = jnp.dot(parts, jnp.concatenate([hot, hot], axis=0), preferred_element_type=F32)
        rows = at(tile * fields, fields)
        line = line_ref[rows, :]
        total = jnp.zeros((fields, entries), F32)
        for i in range(64):
            total = total + jnp.where(line == i, picked[i * fields : (i + 1) * fields, :], 0.0)
        total_ref[rows, :] = total
        return carry

    lax.fori_loop(0, 5, pick, 0)

    for group in range(peers // 16):
        lefts, rights = [], []
        for tile in range(5):
            rows = slice(tile * fields, (tile + 1) * fields)
            high, low = split(total_ref[rows, :] * weight_ref[rows, :])
            high, low = high.astype(F32), low.astype(F32)
            owner = owner_ref[rows, :]
            for part in (high, low):
                pieces = [jnp.where(owner == group * 16 + i, part, 0.0).astype(BF16) for i in range(16)]
                lefts.append(jnp.concatenate(pieces, axis=0))
                rights.append(slot_ref[tile * HALF : (tile + 1) * HALF, :])
        result = lax.dot_general(
            jnp.concatenate(lefts, axis=1), jnp.concatenate(rights, axis=1), NT, preferred_element_type=F32
        )
        table[group * 16 * fields : (group + 1) * 16 * fields, :] = result
    count = peers // 2
    mine = me[0] % 2
    place = lax.broadcasted_iota(jnp.int32, (count, HALF), 0)
    scale = jnp.broadcast_to(own_scale[...], (count, HALF))
    for out, side in ((kept, mine), (sent, 1 - mine)):
        out[0 : count * fields, :] = table[at(side * count * fields, count * fields), :]
        out[count * fields :, :] = jnp.where(place == me[0] - side * count, scale, 0.0)


def basis_parts(basis, out):
    rank = basis.shape[0] // HALF

    def body(group, carry):
        for step in range(8):
            high, low = split(basis[pl.ds(group * 8 + step, rank, stride=HALF), :])
            rows = at(group * rank, rank)
            out[rows, step * 256 : step * 256 + HALF] = high
            out[rows, step * 256 + HALF : (step + 1) * 256] = low
        return carry

    lax.fori_loop(0, 16, body, 0)


def adjoint(
    fields, peers, me, half, other, cell_ref, slot_ref, speed_ref, line_ref, owner_ref, weight_ref, turned, sources,
    prior, band_ref, basis, image, coeffs, high_ref, low_ref, left, inner_two, outer_two,
    inner_one, outer_one, z_term, image_parts, scaled,
):
    entries = line_ref.shape[1]
    cells = LAYERS * 32
    rank = basis.shape[0] // 16
    clear_margins(inner_two, 5 * LAYERS, fields)
    clear_margins(inner_one, 3 * LAYERS, fields)
    count = peers // 2
    mine = me[0] % 2
    for ref, side in ((half, mine), (other, 1 - mine)):
        for i in range(count):
            scale = ref[count * fields + i : count * fields + i + 1, :]
            scaled[at((side * count + i) * fields, fields), :] = ref[i * fields : (i + 1) * fields, :] * scale
    for tile in range(5):
        rows = slice(tile * fields, (tile + 1) * fields)
        owner = owner_ref[rows, :]
        hot = slot_ref[tile * HALF : (tile + 1) * HALF, :]
        hot = jnp.concatenate([hot, hot], axis=0)
        total = jnp.zeros((fields, entries), F32)
        for group in range(peers // 16):
            parts = split(scaled[group * 16 * fields : (group + 1) * 16 * fields, :])
            found = jnp.dot(jnp.concatenate(parts, axis=1), hot, preferred_element_type=F32)
            for i in range(16):
                total = total + jnp.where(owner == group * 16 + i, found[i * fields : (i + 1) * fields, :], 0.0)
        high, low = split(total * weight_ref[rows, :])
        high_ref[rows, :] = high.astype(F32)
        low_ref[rows, :] = low.astype(F32)

    def inject(tile, carry):
        rows = at(tile * fields, fields)
        line, high, low = line_ref[rows, :], high_ref[rows, :], low_ref[rows, :]
        for i in range(64):
            chosen = line == i
            left[i * fields : (i + 1) * fields, :entries] = jnp.where(chosen, high, 0.0).astype(BF16)
            left[i * fields : (i + 1) * fields, entries:] = jnp.where(chosen, low, 0.0).astype(BF16)
        hot = cell_ref[at(tile * 256, 256), :]
        value = lax.dot_general(left[...], jnp.concatenate([hot, hot], axis=1), NT, preferred_element_type=F32)
        for i in range(64):
            x, pair = i // 16, i % 16
            for step in range(2):
                y = pair * 2 + step
                now = value[i * fields : (i + 1) * fields, step * HALF : (step + 1) * HALF]
                layer = tile * LAYERS + x
                outer_two[at((layer * 32 + y) * fields, fields), :] = now
                speed = spread(speed_ref, layer * 32 + y, fields)
                inner_two[at((layer * PADDED + REACH + y) * fields, fields), :] = speed * now
        return carry

    lax.fori_loop(0, 5, inject, 0)

    def terms(index, carry):
        along_z(inner_two, (index + 1) * LAYERS, fields, band_ref, z_term, index * cells * fields)
        return carry

    lax.fori_loop(0, 3, terms, 0)

    def step_one(index, carry):
        tile, chunk = index // 4 + 1, index % 4
        for x in range(LAYERS):
            for step in range(8):
                y = chunk * 8 + step

                def get(layer, row):
                    return inner_two[at(((tile * LAYERS + layer) * PADDED + REACH + row) * fields, fields), :]

                layer = tile * LAYERS + x
                speed = spread(speed_ref, layer * 32 + y, fields)
                now = 2.0 * outer_two[at((layer * 32 + y) * fields, fields), :]
                layer = layer - LAYERS
                z_part = z_term[at((layer * 32 + y) * fields, fields), :]
                now = now + laplacian(get, x, y, z_part, -4, 7)
                outer_one[at((layer * 32 + y) * fields, fields), :] = now
                inner_one[at((layer * PADDED + REACH + y) * fields, fields), :] = speed * now
        return carry

    lax.fori_loop(0, 12, step_one, 0)

    def get_one(layer, row):
        return inner_one[at(((LAYERS + layer) * PADDED + REACH + row) * fields, fields), :]

    along_z(inner_one, LAYERS, fields, band_ref, z_term)

    def step_two(chunk, total):
        for x in range(LAYERS):
            for step in range(8):
                y = chunk * 8 + step
                cell = x * 32 + y
                z_part = z_term[at(cell * fields, fields), :]
                two = outer_two[at((2 * LAYERS * 32 + cell) * fields, fields), :]
                one = outer_one[at((LAYERS * 32 + cell) * fields, fields), :]
                zero = 2.0 * one - two + laplacian(get_one, x, y, z_part, -4, 7)
                value = spread(sources, cell, fields) * zero
                value = value + spread(sources, 128 + cell, fields) * one
                value = value + spread(sources, 256 + cell, fields) * two
                value = value + spread(prior, cell, fields) * turned[at(cell * fields, fields), :]
                image[at(cell * fields, fields), :] = value
                high, low = split(value)
                side = step * 256
                rows = slice(x * 2 * fields, x * 2 * fields + fields)
                image_parts[rows, side : side + HALF] = high
                image_parts[rows, side + HALF : side + 256] = high
                rows = slice(x * 2 * fields + fields, (x + 1) * 2 * fields)
                image_parts[rows, side : side + HALF] = low
                image_parts[rows, side + HALF : side + 256] = jnp.zeros_like(low)
        for x in range(LAYERS):
            columns = basis[at((x * 4 + chunk) * rank, rank), :]
            parts = image_parts[x * 2 * fields : (x + 1) * 2 * fields, :]
            total = total + lax.dot_general(parts, columns, NT, preferred_element_type=F32)
        return total

    total = lax.fori_loop(0, 4, step_two, jnp.zeros((2 * fields, rank), F32))
    coeffs[...] = total[:fields, :] + total[fields:, :]


def remainder(fields, image, basis, *rest):
    *shares, out, coeffs, natural, sem = rest
    rank = coeffs.shape[1]
    while len(shares) > 1:
        shares = [shares[i][...] + shares[i + 1][...] for i in range(0, len(shares), 2)]
    total = shares[0][...]
    coeffs[...] = total
    parts = jnp.concatenate(split(total), axis=0)
    whole = natural.reshape(out.shape)

    def leave(x):
        return pltpu.make_async_copy(whole.at[:, x], out.at[:, x], sem.at[x])

    def body(x, carry):
        for part in range(4):
            columns = basis[at((x * 4 + part) * rank, rank), :]
            both = jnp.dot(parts, columns, preferred_element_type=F32)
            for step in range(8):
                cell = x * 32 + part * 8 + step
                side = step * 256
                along = both[:fields, side : side + HALF] + both[:fields, side + HALF : side + 256]
                along = along + both[fields:, side : side + HALF]
                natural[pl.ds(cell, fields, stride=HALF), :] = image[at(cell * fields, fields), :] - along
        leave(x).start()
        return carry

    lax.fori_loop(0, LAYERS, body, 0)
    for x in range(LAYERS):
        leave(x).wait()


def call(kernel, inputs, out_shape, scratch, flops, size, scalars=0, far=0, far_out=0):
    smem = pl.BlockSpec(memory_space=pltpu.SMEM)
    vmem = pl.BlockSpec(memory_space=pltpu.VMEM)
    hbm = pl.BlockSpec(memory_space=pltpu.HBM)
    return pl.pallas_call(
        kernel,
        out_shape=out_shape,
        in_specs=[smem] * scalars + [hbm] * far + [vmem] * (len(inputs) - scalars - far),
        out_specs=[hbm] * far_out + [vmem] * (len(out_shape) - far_out),
        scratch_shapes=scratch,
        cost_estimate=pl.CostEstimate(flops=flops, bytes_accessed=size, transcendentals=0),
        compiler_params=pltpu.CompilerParams(vmem_limit_bytes=44 * 2**20),
    )(*inputs)


def struct(*shape, dtype=F32):
    return jax.ShapeDtypeStruct(shape, dtype)


def shifted(array, axis, by):
    count = lax.axis_size(axis)
    return lax.ppermute(array, axis, [(i, i + by) for i in range(count) if 0 <= i + by < count])


def swapped(array, axis, bits):
    count = lax.axis_size(axis)
    return lax.ppermute(array, axis, [(i, i ^ bits) for i in range(count)])


def local(
    probes,
    sources,
    kappa,
    prior,
    basis,
    entry_cell,
    entry_owner,
    entry_slot,
    entry_weight,
    entry_count,
    trace_weight,
):
    fields, rank = probes.shape[0], basis.shape[0]
    entries = entry_cell.shape[0]
    peers = lax.axis_size("space")
    padded = LAYERS * PADDED * fields
    cells = LAYERS * 32
    rows = entries // HALF
    me = lax.axis_index("space").astype(jnp.int32).reshape(1)

    own, probes_near, sources_near, prior_near, matrix = call(
        pack,
        (
            entry_count,
            probes.reshape(fields * cells, HALF),
            sources.reshape(3 * cells, HALF),
            prior.reshape(cells, HALF),
            kappa.reshape(cells, HALF),
            entry_cell.reshape(rows, HALF),
            entry_owner.reshape(rows, HALF),
            entry_slot.reshape(rows, HALF),
            entry_weight.reshape(rows, HALF),
        ),
        [
            struct(cells + 4 * rows, HALF),
            struct(fields * cells, HALF),
            struct(3 * cells, HALF),
            struct(cells, HALF),
            struct(256, 256, dtype=BF16),
        ],
        [pltpu.VMEM((3, rows, HALF), jnp.int32), pltpu.VMEM((rows, HALF), F32), pltpu.SemaphoreType.DMA((8,))],
        100_000,
        2 * 2**20,
        scalars=1,
        far=8,
    )
    partner = swapped(own, "space", 1)
    both = jnp.concatenate([own, partner], axis=0)
    before = shifted(both, "space", 2)
    after = shifted(both, "space", -2)

    turned, first, second, third = call(
        functools.partial(forward_own, fields),
        (probes_near, sources_near, own, matrix),
        [struct(cells * fields, HALF), struct(padded, HALF), struct(padded, HALF), struct(cells * fields, HALF)],
        [pltpu.VMEM((cells * fields, HALF), F32)],
        600_000_000,
        6 * 2**20,
    )
    half_rows = peers // 2 * (fields + 1)
    kept, sent, cell_hot, slot_hot, speed, line, owner, weight = call(
        functools.partial(forward_window, fields, peers),
        (me, first, second, third, own, partner, before, after, matrix, trace_weight.reshape(1, HALF)),
        [
            struct(half_rows, HALF),
            struct(half_rows, HALF),
            struct(5 * 256, entries, dtype=BF16),
            struct(5 * HALF, entries, dtype=BF16),
            struct(5 * cells, HALF),
            struct(5 * fields, entries, dtype=jnp.int32),
            struct(5 * fields, entries, dtype=jnp.int32),
            struct(5 * fields, entries),
        ],
        [
            pltpu.VMEM((padded, HALF), F32),
            pltpu.VMEM((padded, HALF), F32),
            pltpu.VMEM((2 * cells * fields, HALF), F32),
            pltpu.VMEM((5 * 64 * fields, 512), BF16),
            pltpu.VMEM((5 * fields, entries), F32),
            pltpu.VMEM((peers * fields, HALF), F32),
        ],
        3_000_000_000,
        6 * 2**20,
        scalars=1,
    )
    half = kept + swapped(sent, "space", 1)
    bits = 2
    while bits < peers:
        half = half + swapped(half, "space", bits)
        bits *= 2
    other = swapped(half, "space", 1)
    (columns,) = call(
        basis_parts,
        (basis.reshape(rank * cells, HALF),),
        [struct(16 * rank, 2048, dtype=BF16)],
        [],
        10_000_000,
        8 * 2**20,
    )
    image, coeffs = call(
        functools.partial(adjoint, fields, peers),
        (
            me, half, other, cell_hot, slot_hot, speed, line, owner, weight,
            turned, sources_near, prior_near, matrix, columns,
        ),
        [struct(cells * fields, HALF), struct(fields, rank)],
        [
            pltpu.VMEM((5 * fields, entries), F32),
            pltpu.VMEM((5 * fields, entries), F32),
            pltpu.VMEM((64 * fields, 2 * entries), BF16),
            pltpu.VMEM((5 * padded, HALF), F32),
            pltpu.VMEM((5 * cells * fields, HALF), F32),
            pltpu.VMEM((3 * padded, HALF), F32),
            pltpu.VMEM((3 * cells * fields, HALF), F32),
            pltpu.VMEM((3 * cells * fields, HALF), F32),
            pltpu.VMEM((8 * fields, 2048), BF16),
            pltpu.VMEM((peers * fields, HALF), F32),
        ],
        5_000_000_000,
        10 * 2**20,
        scalars=1,
    )
    bits = 1
    while bits * 4 < peers:
        coeffs = coeffs + swapped(coeffs, "space", bits)
        bits *= 2
    shares = [coeffs] + [swapped(coeffs, "space", bits * i) for i in range(1, peers // bits)]
    hess_probe, coeffs = call(
        functools.partial(remainder, fields),
        (image, columns, *shares),
        [struct(*probes.shape), struct(fields, rank)],
        [pltpu.VMEM((fields * cells, HALF), F32), pltpu.SemaphoreType.DMA((LAYERS,))],
        200_000_000,
        6 * 2**20,
        far_out=1,
    )
    return hess_probe, coeffs.T


def solution(mesh):
    return jax.shard_map(
        local,
        mesh=mesh,
        in_specs=(
            P("group", "space", None, None),
            P(None, ("group", "space"), None, None),
            P(("group", "space"), None, None),
            P(("group", "space"), None, None),
            P("group", "space", None, None),
            P(("group", "space")),
            P(("group", "space")),
            P(("group", "space")),
            P(("group", "space")),
            P(("group", "space")),
            P(("group", "space")),
        ),
        out_specs=(P("group", "space", None, None), P("group", None)),
        check_vma=False,
    )
```

```python
import functools

import jax
import jax.numpy as jnp
from jax import lax
from jax.experimental import pallas as pl
from jax.experimental.pallas import tpu as pltpu
from jax.sharding import PartitionSpec as P

STENCIL = (-205.0 / 72.0, 8.0 / 5.0, -1.0 / 5.0, 8.0 / 315.0, -1.0 / 560.0)
CENTER = 3.0 * STENCIL[0]
REACH = 4
LAYERS = 4
PADDED = 40
HALF = 128
PLACES = 512
F32 = jnp.float32
BF16 = jnp.bfloat16
NT = (((1,), (1,)), ((), ()))


def split(value):
    high = value.astype(BF16)
    low = (value - high.astype(F32)).astype(BF16)
    return high, low


def at(row, count=16):
    return pl.ds(pl.multiple_of(row, 16), count)


def spread(ref, row, fields):
    return jnp.broadcast_to(ref[pl.ds(row, 1), :], (fields, HALF))


def clear_margins(ref, layers, fields):
    margin = jnp.zeros((REACH * fields, HALF), F32)
    for layer in range(layers):
        start = layer * PADDED * fields
        ref[start : start + REACH * fields, :] = margin
        start += (PADDED - REACH) * fields
        ref[start : start + REACH * fields, :] = margin


def along_z(ref, first, fields, band_ref, out_ref, row=0):
    pieces = [ref[at(((first + x) * PADDED + REACH) * fields, 32 * fields), :] for x in range(LAYERS)]
    high, low = split(jnp.concatenate(pieces, axis=0))
    both = jnp.dot(jnp.concatenate([high, low], axis=1), band_ref[...], preferred_element_type=F32)
    out_ref[at(row, LAYERS * 32 * fields), :] = both[:, :HALF] + both[:, HALF:]


def laplacian(get, x, y, z_term, lowest, highest):
    total = z_term
    for k in range(1, REACH + 1):
        ring = get(x, y + k) + get(x, y - k)
        if x + k <= highest:
            ring = ring + get(x + k, y)
        if x - k >= lowest:
            ring = ring + get(x - k, y)
        total = total + STENCIL[k] * ring
    return total


def pack(
    count, probes, sources, prior, kappa, cell, owner, slot, weight,
    statics, probes_out, sources_out, prior_out, band_ref, small_int, small_float, sem,
):
    rows = cell.shape[0]
    cells = kappa.shape[0]
    small = [
        pltpu.make_async_copy(kappa, statics.at[pl.ds(0, cells)], sem.at[0]),
        pltpu.make_async_copy(cell, small_int.at[0], sem.at[1]),
        pltpu.make_async_copy(owner, small_int.at[1], sem.at[2]),
        pltpu.make_async_copy(slot, small_int.at[2], sem.at[3]),
        pltpu.make_async_copy(weight, small_float, sem.at[4]),
    ]
    large = [
        pltpu.make_async_copy(probes, probes_out, sem.at[5]),
        pltpu.make_async_copy(sources, sources_out, sem.at[6]),
        pltpu.make_async_copy(prior, prior_out, sem.at[7]),
    ]
    for copy in small + large:
        copy.start()
    apart = lax.broadcasted_iota(jnp.int32, (HALF, HALF), 0) - lax.broadcasted_iota(jnp.int32, (HALF, HALF), 1)
    full = jnp.where(apart == 0, CENTER, jnp.zeros((HALF, HALF), F32))
    for reach in range(1, REACH + 1):
        full = jnp.where(jnp.abs(apart) == reach, STENCIL[reach], full)
    high, low = split(full)
    band_ref[0:HALF, 0:HALF] = high
    band_ref[HALF:, 0:HALF] = high
    band_ref[0:HALF, HALF:] = low
    band_ref[HALF:, HALF:] = jnp.zeros_like(low)
    for copy in small:
        copy.wait()
    for i in range(3):
        statics[cells + i * rows : cells + (i + 1) * rows, :] = small_int[i].astype(F32)
    place = lax.broadcasted_iota(jnp.int32, (rows, HALF), 0) * HALF
    place = place + lax.broadcasted_iota(jnp.int32, (rows, HALF), 1)
    live = jnp.where(place < count[0], small_float[...], 0.0)
    statics[cells + 3 * rows : cells + 4 * rows, :] = live
    for copy in large:
        copy.wait()


def forward_own(fields, probes, sources, statics, band_ref, turned, first, second, third, z_term):
    clear_margins(first, LAYERS, fields)
    clear_margins(second, LAYERS, fields)

    def load(chunk, carry):
        for x in range(LAYERS):
            for step in range(8):
                y = chunk * 8 + step
                cell = x * 32 + y
                value = probes[pl.ds(cell, fields, stride=HALF), :]
                turned[at(cell * fields, fields), :] = value
                first[at((x * PADDED + REACH + y) * fields, fields), :] = value * spread(sources, cell, fields)
        return carry

    lax.fori_loop(0, 4, load, 0)

    def sweep(field, emit):
        along_z(field, 0, fields, band_ref, z_term)

        def body(chunk, carry):
            for x in range(LAYERS):
                for step in range(8):
                    y = chunk * 8 + step
                    cell = x * 32 + y

                    def get(layer, row):
                        return field[at((layer * PADDED + REACH + row) * fields, fields), :]

                    z_part = z_term[at(cell * fields, fields), :]
                    total = laplacian(get, x, y, z_part, 0, LAYERS - 1)
                    emit(x, y, get(x, y), spread(statics, cell, fields) * total)
            return carry

        lax.fori_loop(0, 4, body, 0)

    def step_one(x, y, now, change):
        cell = x * 32 + y
        push = turned[at(cell * fields, fields), :] * spread(sources, 128 + cell, fields)
        second[at((x * PADDED + REACH + y) * fields, fields), :] = 2.0 * now + change + push

    sweep(first, step_one)

    def step_two(x, y, now, change):
        cell = x * 32 + y
        push = turned[at(cell * fields, fields), :] * spread(sources, 256 + cell, fields)
        before = first[at((x * PADDED + REACH + y) * fields, fields), :]
        third[at(cell * fields, fields), :] = 2.0 * now - before + change + push

    sweep(second, step_two)


def entry_row(value, row):
    return jnp.concatenate([value[row + i : row + i + 1, :] for i in range(4)], axis=1)


def forward_window(
    fields, peers, me, first, second, third, own, partner, before, after, band_ref, own_scale,
    kept, sent, cell_ref, slot_ref, speed_ref, line_ref, owner_ref, weight_ref,
    below, above, z_term, total_ref, table, *samples,
):
    entries = line_ref.shape[1]
    cells = LAYERS * 32
    length = own.shape[0]
    odd = me[0] % 2 == 1
    clear_margins(below, LAYERS, fields)
    clear_margins(above, LAYERS, fields)
    total_ref[...] = jnp.zeros_like(total_ref)
    tiles = (
        before[...],
        jnp.where(odd, partner[0:length, :], partner[length:, :]),
        own[...],
        jnp.where(odd, partner[length:, :], partner[0:length, :]),
        after[...],
    )
    place = lax.broadcasted_iota(jnp.int32, (PLACES, entries), 0)
    slot_place = lax.broadcasted_iota(jnp.int32, (HALF, entries), 0)
    for tile, value in enumerate(tiles):
        speed_ref[tile * cells : (tile + 1) * cells, :] = value[0:cells, :]
        cell = entry_row(value, cells).astype(jnp.int32)
        owner = entry_row(value, cells + 4).astype(jnp.int32)
        slot = entry_row(value, cells + 8).astype(jnp.int32)
        weight = entry_row(value, cells + 12)
        hot = jnp.where(place == jnp.bitwise_and(cell, PLACES - 1), 1.0, 0.0)
        cell_ref[tile * PLACES : (tile + 1) * PLACES, :] = hot.astype(BF16)
        hot = jnp.where(slot_place == slot, 1.0, 0.0)
        slot_ref[tile * HALF : (tile + 1) * HALF, :] = hot.astype(BF16)
        rows = slice(tile * fields, (tile + 1) * fields)
        line_ref[rows, :] = jnp.broadcast_to(lax.shift_right_logical(cell, 9), (fields, entries))
        owner_ref[rows, :] = jnp.broadcast_to(owner, (fields, entries))
        weight_ref[rows, :] = jnp.broadcast_to(weight, (fields, entries))

    def outward(chunk, carry):
        for step in range(8):
            y = chunk * 8 + step
            mine = [first[at((x * PADDED + REACH + y) * fields, fields), :] for x in range(LAYERS)]
            for x in range(LAYERS):
                up = sum(STENCIL[4 + x - other] * mine[other] for other in range(x, LAYERS))
                down = sum(STENCIL[4 + other - x] * mine[other] for other in range(x + 1))
                row = at((x * PADDED + REACH + y) * fields, fields)
                above[row, :] = spread(speed_ref, 3 * cells + x * 32 + y, fields) * up
                below[row, :] = spread(speed_ref, cells + x * 32 + y, fields) * down
        return carry

    lax.fori_loop(0, 4, outward, 0)
    along_z(below, 0, fields, band_ref, z_term, 0)
    along_z(above, 0, fields, band_ref, z_term, cells * fields)

    def read(layer, y):
        ref = (below, second, above)[(layer + LAYERS) // LAYERS]
        return ref[at((layer % LAYERS * PADDED + REACH + y) * fields, fields), :]

    def far(x, y, lowest, highest):
        total = None
        for other in range(lowest, highest + 1):
            if 1 <= abs(x - other) <= REACH:
                term = STENCIL[abs(x - other)] * read(other, y)
                total = term if total is None else total + term
        return total

    def respond(chunk, carry):
        for tile in range(5):
            sample = samples[tile]
            for x in range(LAYERS):
                for step in range(8):
                    y = chunk * 8 + step
                    cell = x * 32 + y
                    layer = (tile - 2) * LAYERS + x
                    speed = spread(speed_ref, tile * cells + cell, fields)
                    if tile in (0, 4):
                        value = speed * far(layer, y, -4, 7)
                    elif tile == 2:
                        outside = far(layer, y, -4, -1) + far(layer, y, 4, 7)
                        value = third[at(cell * fields, fields), :] + speed * outside
                    else:
                        z_part = z_term[at((tile // 2 * cells + cell) * fields, fields), :]
                        value = 2.0 * read(layer, y) + speed * laplacian(read, layer, y, z_part, -4, 7)
                    row = (x * 2 + step // 4) * fields
                    side = step % 4 * HALF
                    high, low = split(value)
                    sample[row : row + fields, side : side + HALF] = high
                    row = row + 8 * fields
                    sample[row : row + fields, side : side + HALF] = low
            hot = cell_ref[tile * PLACES : (tile + 1) * PLACES, :]
            picked = jnp.dot(sample[...], hot, preferred_element_type=F32)
            picked = picked[: 8 * fields, :] + picked[8 * fields :, :]
            for part in range(fields // 8):
                rows = slice(tile * fields + part * 8, tile * fields + part * 8 + 8)
                line = line_ref[rows, :]
                total = total_ref[rows, :]
                for i in range(8):
                    chosen = line == i // 2 * 8 + chunk * 2 + i % 2
                    row = i * fields + part * 8
                    total = total + jnp.where(chosen, picked[row : row + 8, :], 0.0)
                total_ref[rows, :] = total
        return carry

    lax.fori_loop(0, 4, respond, 0)

    for group in range(peers // 16):
        lefts, rights = [], []
        for tile in range(5):
            rows = slice(tile * fields, (tile + 1) * fields)
            high, low = split(total_ref[rows, :] * weight_ref[rows, :])
            high, low = high.astype(F32), low.astype(F32)
            owner = owner_ref[rows, :]
            for part in (high, low):
                pieces = [jnp.where(owner == group * 16 + i, part, 0.0).astype(BF16) for i in range(16)]
                lefts.append(jnp.concatenate(pieces, axis=0))
                rights.append(slot_ref[tile * HALF : (tile + 1) * HALF, :])
        result = lax.dot_general(
            jnp.concatenate(lefts, axis=1), jnp.concatenate(rights, axis=1), NT, preferred_element_type=F32
        )
        table[group * 16 * fields : (group + 1) * 16 * fields, :] = result
    count = peers // 2
    mine = me[0] % 2
    place = lax.broadcasted_iota(jnp.int32, (count, HALF), 0)
    scale = jnp.broadcast_to(own_scale[...], (count, HALF))
    for out, side in ((kept, mine), (sent, 1 - mine)):
        out[0 : count * fields, :] = table[at(side * count * fields, count * fields), :]
        out[count * fields :, :] = jnp.where(place == me[0] - side * count, scale, 0.0)


def basis_parts(basis, when, out):
    rank = basis.shape[0] // HALF

    def body(group, carry):
        for step in range(8):
            high, low = split(basis[pl.ds(group * 8 + step, rank, stride=HALF), :])
            rows = at(group * rank, rank)
            out[rows, step * 256 : step * 256 + HALF] = high
            out[rows, step * 256 + HALF : (step + 1) * 256] = low
        return carry

    lax.fori_loop(0, 16, body, 0)


def adjoint(
    fields, peers, me, half, other, cell_ref, slot_ref, speed_ref, line_ref, owner_ref, weight_ref, turned, sources,
    prior, band_ref, basis, image, coeffs, high_ref, low_ref, inner_two, outer_two,
    inner_one, outer_one, z_term, image_parts, scaled, *lefts,
):
    entries = line_ref.shape[1]
    cells = LAYERS * 32
    rank = basis.shape[0] // 16
    clear_margins(inner_two, 5 * LAYERS, fields)
    clear_margins(inner_one, 3 * LAYERS, fields)
    count = peers // 2
    mine = me[0] % 2
    for ref, side in ((half, mine), (other, 1 - mine)):
        for i in range(count):
            scale = ref[count * fields + i : count * fields + i + 1, :]
            scaled[at((side * count + i) * fields, fields), :] = ref[i * fields : (i + 1) * fields, :] * scale
    for tile in range(5):
        rows = slice(tile * fields, (tile + 1) * fields)
        owner = owner_ref[rows, :]
        hot = slot_ref[tile * HALF : (tile + 1) * HALF, :]
        hot = jnp.concatenate([hot, hot], axis=0)
        total = jnp.zeros((fields, entries), F32)
        for group in range(peers // 16):
            parts = split(scaled[group * 16 * fields : (group + 1) * 16 * fields, :])
            found = jnp.dot(jnp.concatenate(parts, axis=1), hot, preferred_element_type=F32)
            for i in range(16):
                total = total + jnp.where(owner == group * 16 + i, found[i * fields : (i + 1) * fields, :], 0.0)
        high, low = split(total * weight_ref[rows, :])
        high_ref[rows, :] = high.astype(F32)
        low_ref[rows, :] = low.astype(F32)

    for tile in range(5):
        left = lefts[tile]
        for part in range(fields // 16):
            rows = slice(tile * fields + part * 16, tile * fields + part * 16 + 16)
            line, high, low = line_ref[rows, :], high_ref[rows, :], low_ref[rows, :]
            for i in range(32):
                chosen = line == i
                row = i * fields + part * 16
                left[row : row + 16, :entries] = jnp.where(chosen, high, 0.0).astype(BF16)
                left[row : row + 16, entries:] = jnp.where(chosen, low, 0.0).astype(BF16)
        hot = cell_ref[tile * PLACES : (tile + 1) * PLACES, :]
        value = lax.dot_general(left[...], jnp.concatenate([hot, hot], axis=1), NT, preferred_element_type=F32)
        for i in range(32):
            for step in range(4):
                layer, y = tile * LAYERS + i // 8, i % 8 * 4 + step
                now = value[i * fields : (i + 1) * fields, step * HALF : (step + 1) * HALF]
                if 1 <= tile <= 3:
                    outer_two[at(((layer - LAYERS) * 32 + y) * fields, fields), :] = now
                speed = spread(speed_ref, layer * 32 + y, fields)
                inner_two[at((layer * PADDED + REACH + y) * fields, fields), :] = speed * now

    def terms(index, carry):
        along_z(inner_two, (index + 1) * LAYERS, fields, band_ref, z_term, index * cells * fields)
        return carry

    lax.fori_loop(0, 3, terms, 0)

    def step_one(index, carry):
        tile, chunk = index // 4 + 1, index % 4
        for x in range(LAYERS):
            for step in range(8):
                y = chunk * 8 + step

                def get(layer, row):
                    return inner_two[at(((tile * LAYERS + layer) * PADDED + REACH + row) * fields, fields), :]

                layer = tile * LAYERS + x
                speed = spread(speed_ref, layer * 32 + y, fields)
                layer = layer - LAYERS
                now = 2.0 * outer_two[at((layer * 32 + y) * fields, fields), :]
                z_part = z_term[at((layer * 32 + y) * fields, fields), :]
                now = now + laplacian(get, x, y, z_part, -4, 7)
                outer_one[at((layer * 32 + y) * fields, fields), :] = now
                inner_one[at((layer * PADDED + REACH + y) * fields, fields), :] = speed * now
        return carry

    lax.fori_loop(0, 12, step_one, 0)

    def get_one(layer, row):
        return inner_one[at(((LAYERS + layer) * PADDED + REACH + row) * fields, fields), :]

    along_z(inner_one, LAYERS, fields, band_ref, z_term)

    def step_two(chunk, total):
        for x in range(LAYERS):
            for step in range(8):
                y = chunk * 8 + step
                cell = x * 32 + y
                z_part = z_term[at(cell * fields, fields), :]
                two = outer_two[at((LAYERS * 32 + cell) * fields, fields), :]
                one = outer_one[at((LAYERS * 32 + cell) * fields, fields), :]
                zero = 2.0 * one - two + laplacian(get_one, x, y, z_part, -4, 7)
                value = spread(sources, cell, fields) * zero
                value = value + spread(sources, 128 + cell, fields) * one
                value = value + spread(sources, 256 + cell, fields) * two
                value = value + spread(prior, cell, fields) * turned[at(cell * fields, fields), :]
                image[at(cell * fields, fields), :] = value
                high, low = split(value)
                side = step * 256
                rows = slice(x * 2 * fields, x * 2 * fields + fields)
                image_parts[rows, side : side + HALF] = high
                image_parts[rows, side + HALF : side + 256] = high
                rows = slice(x * 2 * fields + fields, (x + 1) * 2 * fields)
                image_parts[rows, side : side + HALF] = low
                image_parts[rows, side + HALF : side + 256] = jnp.zeros_like(low)
        for x in range(LAYERS):
            columns = basis[at((x * 4 + chunk) * rank, rank), :]
            parts = image_parts[x * 2 * fields : (x + 1) * 2 * fields, :]
            total = total + lax.dot_general(parts, columns, NT, preferred_element_type=F32)
        return total

    total = lax.fori_loop(0, 4, step_two, jnp.zeros((2 * fields, rank), F32))
    coeffs[...] = total[:fields, :] + total[fields:, :]


def remainder(fields, image, basis, *rest):
    *shares, out, coeffs, natural, sem = rest
    rank = coeffs.shape[1]
    while len(shares) > 1:
        shares = [shares[i][...] + shares[i + 1][...] for i in range(0, len(shares), 2)]
    total = shares[0][...]
    coeffs[...] = total
    parts = jnp.concatenate(split(total), axis=0)
    whole = natural.reshape(out.shape)

    def leave(x):
        return pltpu.make_async_copy(whole.at[:, x], out.at[:, x], sem.at[x])

    def body(x, carry):
        for part in range(4):
            columns = basis[at((x * 4 + part) * rank, rank), :]
            both = jnp.dot(parts, columns, preferred_element_type=F32)
            for step in range(8):
                cell = x * 32 + part * 8 + step
                side = step * 256
                along = both[:fields, side : side + HALF] + both[:fields, side + HALF : side + 256]
                along = along + both[fields:, side : side + HALF]
                natural[pl.ds(cell, fields, stride=HALF), :] = image[at(cell * fields, fields), :] - along
        leave(x).start()
        return carry

    lax.fori_loop(0, LAYERS, body, 0)
    for x in range(LAYERS):
        leave(x).wait()


def call(kernel, inputs, out_shape, scratch, flops, size, scalars=0, far=0, far_out=0, room=16):
    smem = pl.BlockSpec(memory_space=pltpu.SMEM)
    vmem = pl.BlockSpec(memory_space=pltpu.VMEM)
    hbm = pl.BlockSpec(memory_space=pltpu.HBM)
    inputs = [
        pltpu.with_memory_space_constraint(array, pltpu.HBM) if scalars <= i < scalars + far else array
        for i, array in enumerate(inputs)
    ]
    return pl.pallas_call(
        kernel,
        out_shape=out_shape,
        in_specs=[smem] * scalars + [hbm] * far + [vmem] * (len(inputs) - scalars - far),
        out_specs=[hbm] * far_out + [vmem] * (len(out_shape) - far_out),
        scratch_shapes=scratch,
        cost_estimate=pl.CostEstimate(flops=flops, bytes_accessed=size, transcendentals=0),
        compiler_params=pltpu.CompilerParams(vmem_limit_bytes=room * 2**20),
    )(*inputs)


def struct(*shape, dtype=F32):
    return jax.ShapeDtypeStruct(shape, dtype)


def shifted(array, axis, by):
    count = lax.axis_size(axis)
    return lax.ppermute(array, axis, [(i, i + by) for i in range(count) if 0 <= i + by < count])


def swapped(array, axis, bits):
    count = lax.axis_size(axis)
    return lax.ppermute(array, axis, [(i, i ^ bits) for i in range(count)])


def local(
    probes,
    sources,
    kappa,
    prior,
    basis,
    entry_cell,
    entry_owner,
    entry_slot,
    entry_weight,
    entry_count,
    trace_weight,
):
    fields, rank = probes.shape[0], basis.shape[0]
    entries = entry_cell.shape[0]
    peers = lax.axis_size("space")
    padded = LAYERS * PADDED * fields
    cells = LAYERS * 32
    rows = entries // HALF
    me = lax.axis_index("space").astype(jnp.int32).reshape(1)

    own, probes_near, sources_near, prior_near, matrix = call(
        pack,
        (
            entry_count,
            probes.reshape(fields * cells, HALF),
            sources.reshape(3 * cells, HALF),
            prior.reshape(cells, HALF),
            kappa.reshape(cells, HALF),
            entry_cell.reshape(rows, HALF),
            entry_owner.reshape(rows, HALF),
            entry_slot.reshape(rows, HALF),
            entry_weight.reshape(rows, HALF),
        ),
        [
            struct(cells + 4 * rows, HALF),
            struct(fields * cells, HALF),
            struct(3 * cells, HALF),
            struct(cells, HALF),
            struct(256, 256, dtype=BF16),
        ],
        [pltpu.VMEM((3, rows, HALF), jnp.int32), pltpu.VMEM((rows, HALF), F32), pltpu.SemaphoreType.DMA((8,))],
        100_000,
        2 * 2**20,
        scalars=1,
        far=8,
    )
    before = shifted(own, "space", 2)
    after = shifted(own, "space", -2)

    turned, first, second, third = call(
        functools.partial(forward_own, fields),
        (probes_near, sources_near, own, matrix),
        [struct(cells * fields, HALF), struct(padded, HALF), struct(padded, HALF), struct(cells * fields, HALF)],
        [pltpu.VMEM((cells * fields, HALF), F32)],
        600_000_000,
        6 * 2**20,
    )
    half_rows = peers // 2 * (fields + 1)
    before, after, second = lax.optimization_barrier((before, after, second))
    relayed = jnp.where(jnp.bitwise_and(me, 1)[0] == 1, before, after)
    partner = swapped(jnp.concatenate([own, relayed], axis=0), "space", 1)
    kept, sent, cell_hot, slot_hot, speed, line, owner, weight = call(
        functools.partial(forward_window, fields, peers),
        (me, first, second, third, own, partner, before, after, matrix, trace_weight.reshape(1, HALF)),
        [
            struct(half_rows, HALF),
            struct(half_rows, HALF),
            struct(5 * PLACES, entries, dtype=BF16),
            struct(5 * HALF, entries, dtype=BF16),
            struct(5 * cells, HALF),
            struct(5 * fields, entries, dtype=jnp.int32),
            struct(5 * fields, entries, dtype=jnp.int32),
            struct(5 * fields, entries),
        ],
        [
            pltpu.VMEM((padded, HALF), F32),
            pltpu.VMEM((padded, HALF), F32),
            pltpu.VMEM((2 * cells * fields, HALF), F32),
            pltpu.VMEM((5 * fields, entries), F32),
            pltpu.VMEM((peers * fields, HALF), F32),
        ]
        + [pltpu.VMEM((16 * fields, PLACES), BF16)] * 5,
        3_000_000_000,
        6 * 2**20,
        scalars=1,
        room=20,
    )
    half = kept + swapped(sent, "space", 1)
    bits = 2
    while bits * 2 < peers:
        half = half + swapped(half, "space", bits)
        bits *= 2
    arrived = swapped(half, "space", bits)
    (columns,) = call(
        basis_parts,
        (basis.reshape(rank * cells, HALF), half),
        [struct(16 * rank, 2048, dtype=BF16)],
        [],
        10_000_000,
        8 * 2**20,
    )
    arrived, columns = lax.optimization_barrier((arrived, columns))
    half = half + arrived
    other = swapped(half, "space", 1)
    image, coeffs = call(
        functools.partial(adjoint, fields, peers),
        (
            me, half, other, cell_hot, slot_hot, speed, line, owner, weight,
            turned, sources_near, prior_near, matrix, columns,
        ),
        [struct(cells * fields, HALF), struct(fields, rank)],
        [
            pltpu.VMEM((5 * fields, entries), F32),
            pltpu.VMEM((5 * fields, entries), F32),
            pltpu.VMEM((5 * padded, HALF), F32),
            pltpu.VMEM((3 * cells * fields, HALF), F32),
            pltpu.VMEM((3 * padded, HALF), F32),
            pltpu.VMEM((3 * cells * fields, HALF), F32),
            pltpu.VMEM((3 * cells * fields, HALF), F32),
            pltpu.VMEM((8 * fields, 2048), BF16),
            pltpu.VMEM((peers * fields, HALF), F32),
        ]
        + [pltpu.VMEM((32 * fields, 2 * entries), BF16)] * 5,
        5_000_000_000,
        10 * 2**20,
        scalars=1,
        room=34,
    )
    bits = 1
    while bits * 4 < peers:
        coeffs = coeffs + swapped(coeffs, "space", bits)
        bits *= 2
    shares = [coeffs] + [swapped(coeffs, "space", bits * i) for i in range(1, peers // bits)]
    hess_probe, coeffs = call(
        functools.partial(remainder, fields),
        (image, columns, *shares),
        [struct(*probes.shape), struct(fields, rank)],
        [pltpu.VMEM((fields * cells, HALF), F32), pltpu.SemaphoreType.DMA((LAYERS,))],
        200_000_000,
        6 * 2**20,
        far_out=1,
    )
    return hess_probe, coeffs.T


def solution(mesh):
    return jax.shard_map(
        local,
        mesh=mesh,
        in_specs=(
            P("group", "space", None, None),
            P(None, ("group", "space"), None, None),
            P(("group", "space"), None, None),
            P(("group", "space"), None, None),
            P("group", "space", None, None),
            P(("group", "space")),
            P(("group", "space")),
            P(("group", "space")),
            P(("group", "space")),
            P(("group", "space")),
            P(("group", "space")),
        ),
        out_specs=(P("group", "space", None, None), P("group", None)),
        check_vma=False,
    )
```

```python
import functools

import jax
import jax.numpy as jnp
from jax import lax
from jax.experimental import pallas as pl
from jax.experimental.pallas import tpu as pltpu
from jax.sharding import PartitionSpec as P

STENCIL = (-205.0 / 72.0, 8.0 / 5.0, -1.0 / 5.0, 8.0 / 315.0, -1.0 / 560.0)
CENTER = 3.0 * STENCIL[0]
REACH = 4
LAYERS = 4
PADDED = 40
HALF = 128
PLACES = 512
F32 = jnp.float32
BF16 = jnp.bfloat16
NT = (((1,), (1,)), ((), ()))


def split(value):
    high = value.astype(BF16)
    low = (value - high.astype(F32)).astype(BF16)
    return high, low


def at(row, count=16):
    return pl.ds(pl.multiple_of(row, 8), count)


def kept_rows(load):
    rows = {}

    def get(layer, y):
        if (layer, y) not in rows:
            rows[layer, y] = load(layer, y)
        return rows[layer, y]

    return get


def spread(ref, row, fields):
    return jnp.broadcast_to(ref[pl.ds(row, 1), :], (fields, HALF))


def clear_margins(ref, layers, fields):
    margin = jnp.zeros((REACH * fields, HALF), F32)
    for layer in range(layers):
        start = layer * PADDED * fields
        ref[start : start + REACH * fields, :] = margin
        start += (PADDED - REACH) * fields
        ref[start : start + REACH * fields, :] = margin


def along_z(ref, first, fields, band_ref, out_ref, row=0):
    pieces = [ref[at(((first + x) * PADDED + REACH) * fields, 32 * fields), :] for x in range(LAYERS)]
    high, low = split(jnp.concatenate(pieces, axis=0))
    both = jnp.dot(jnp.concatenate([high, low], axis=1), band_ref[...], preferred_element_type=F32)
    out_ref[at(row, LAYERS * 32 * fields), :] = both[:, :HALF] + both[:, HALF:]


def laplacian(get, x, y, z_term, lowest, highest):
    total = z_term
    for k in range(1, REACH + 1):
        ring = get(x, y + k) + get(x, y - k)
        if x + k <= highest:
            ring = ring + get(x + k, y)
        if x - k >= lowest:
            ring = ring + get(x - k, y)
        total = total + STENCIL[k] * ring
    return total


def pack(
    count, probes, sources, prior, kappa, cell, owner, slot, weight,
    statics, probes_out, sources_out, prior_out, band_ref, small_int, small_float, sem,
):
    rows = cell.shape[0]
    cells = kappa.shape[0]
    small = [
        pltpu.make_async_copy(kappa, statics.at[pl.ds(0, cells)], sem.at[0]),
        pltpu.make_async_copy(cell, small_int.at[0], sem.at[1]),
        pltpu.make_async_copy(owner, small_int.at[1], sem.at[2]),
        pltpu.make_async_copy(slot, small_int.at[2], sem.at[3]),
        pltpu.make_async_copy(weight, small_float, sem.at[4]),
    ]
    large = [
        pltpu.make_async_copy(probes, probes_out, sem.at[5]),
        pltpu.make_async_copy(sources, sources_out, sem.at[6]),
        pltpu.make_async_copy(prior, prior_out, sem.at[7]),
    ]
    for copy in small + large:
        copy.start()
    apart = lax.broadcasted_iota(jnp.int32, (HALF, HALF), 0) - lax.broadcasted_iota(jnp.int32, (HALF, HALF), 1)
    full = jnp.where(apart == 0, CENTER, jnp.zeros((HALF, HALF), F32))
    for reach in range(1, REACH + 1):
        full = jnp.where(jnp.abs(apart) == reach, STENCIL[reach], full)
    high, low = split(full)
    band_ref[0:HALF, 0:HALF] = high
    band_ref[HALF:, 0:HALF] = high
    band_ref[0:HALF, HALF:] = low
    band_ref[HALF:, HALF:] = jnp.zeros_like(low)
    for copy in small:
        copy.wait()
    for i in range(3):
        statics[cells + i * rows : cells + (i + 1) * rows, :] = small_int[i].astype(F32)
    place = lax.broadcasted_iota(jnp.int32, (rows, HALF), 0) * HALF
    place = place + lax.broadcasted_iota(jnp.int32, (rows, HALF), 1)
    live = jnp.where(place < count[0], small_float[...], 0.0)
    statics[cells + 3 * rows : cells + 4 * rows, :] = live
    for copy in large:
        copy.wait()


def forward_own(fields, probes, sources, statics, band_ref, turned, first, second, third, z_term):
    clear_margins(first, LAYERS, fields)
    clear_margins(second, LAYERS, fields)

    def load(chunk, carry):
        for x in range(LAYERS):
            for step in range(8):
                y = chunk * 8 + step
                cell = x * 32 + y
                value = probes[pl.ds(cell, fields, stride=HALF), :]
                turned[at(cell * fields, fields), :] = value
                first[at((x * PADDED + REACH + y) * fields, fields), :] = value * spread(sources, cell, fields)
        return carry

    lax.fori_loop(0, 4, load, 0)

    def sweep(field, emit):
        along_z(field, 0, fields, band_ref, z_term)

        def body(chunk, carry):
            for part in range(0, fields, 8):

                def load(layer, y):
                    return field[at((layer * PADDED + REACH + chunk * 8 + y) * fields + part, 8), :]

                get = kept_rows(load)
                for y in range(8):
                    for x in range(LAYERS):
                        cell = x * 32 + chunk * 8 + y
                        z_part = z_term[at(cell * fields + part, 8), :]
                        total = laplacian(get, x, y, z_part, 0, LAYERS - 1)
                        emit(x, chunk * 8 + y, part, get(x, y), spread(statics, cell, 8) * total)
            return carry

        lax.fori_loop(0, 4, body, 0)

    def step_one(x, y, part, now, change):
        cell = x * 32 + y
        push = turned[at(cell * fields + part, 8), :] * spread(sources, 128 + cell, 8)
        second[at((x * PADDED + REACH + y) * fields + part, 8), :] = 2.0 * now + change + push

    sweep(first, step_one)

    def step_two(x, y, part, now, change):
        cell = x * 32 + y
        push = turned[at(cell * fields + part, 8), :] * spread(sources, 256 + cell, 8)
        before = first[at((x * PADDED + REACH + y) * fields + part, 8), :]
        third[at(cell * fields + part, 8), :] = 2.0 * now - before + change + push

    sweep(second, step_two)


def entry_row(value, row):
    return jnp.concatenate([value[row + i : row + i + 1, :] for i in range(4)], axis=1)


def forward_window(
    fields, peers, me, first, second, third, own, partner, passed, across, band_ref, own_scale,
    kept, sent, cell_ref, slot_ref, speed_ref, line_ref, owner_ref, weight_ref,
    below, above, z_term, total_ref, table, *samples,
):
    entries = line_ref.shape[1]
    cells = LAYERS * 32
    length = own.shape[0]
    odd = me[0] % 2 == 1
    clear_margins(below, LAYERS, fields)
    clear_margins(above, LAYERS, fields)
    total_ref[...] = jnp.zeros_like(total_ref)
    near, next_one, far_one, side_one = passed[0:length, :], passed[length:, :], across[...], partner[...]
    tiles = (
        jnp.where(odd, far_one, next_one),
        jnp.where(odd, side_one, near),
        own[...],
        jnp.where(odd, near, side_one),
        jnp.where(odd, next_one, far_one),
    )
    place = lax.broadcasted_iota(jnp.int32, (PLACES, entries), 0)
    slot_place = lax.broadcasted_iota(jnp.int32, (HALF, entries), 0)
    for tile, value in enumerate(tiles):
        speed_ref[tile * cells : (tile + 1) * cells, :] = value[0:cells, :]
        cell = entry_row(value, cells).astype(jnp.int32)
        owner = entry_row(value, cells + 4).astype(jnp.int32)
        slot = entry_row(value, cells + 8).astype(jnp.int32)
        weight = entry_row(value, cells + 12)
        hot = jnp.where(place == jnp.bitwise_and(cell, PLACES - 1), 1.0, 0.0)
        cell_ref[tile * PLACES : (tile + 1) * PLACES, :] = hot.astype(BF16)
        hot = jnp.where(slot_place == slot, 1.0, 0.0)
        slot_ref[tile * HALF : (tile + 1) * HALF, :] = hot.astype(BF16)
        rows = slice(tile * fields, (tile + 1) * fields)
        line_ref[rows, :] = jnp.broadcast_to(lax.shift_right_logical(cell, 9), (fields, entries))
        owner_ref[rows, :] = jnp.broadcast_to(owner, (fields, entries))
        weight_ref[rows, :] = jnp.broadcast_to(weight, (fields, entries))

    def outward(chunk, carry):
        for step in range(8):
            y = chunk * 8 + step
            mine = [first[at((x * PADDED + REACH + y) * fields, fields), :] for x in range(LAYERS)]
            for x in range(LAYERS):
                up = sum(STENCIL[4 + x - other] * mine[other] for other in range(x, LAYERS))
                down = sum(STENCIL[4 + other - x] * mine[other] for other in range(x + 1))
                row = at((x * PADDED + REACH + y) * fields, fields)
                above[row, :] = spread(speed_ref, 3 * cells + x * 32 + y, fields) * up
                below[row, :] = spread(speed_ref, cells + x * 32 + y, fields) * down
        return carry

    lax.fori_loop(0, 4, outward, 0)
    along_z(below, 0, fields, band_ref, z_term, 0)
    along_z(above, 0, fields, band_ref, z_term, cells * fields)

    def far(read, x, y, lowest, highest):
        total = None
        for other in range(lowest, highest + 1):
            if 1 <= abs(x - other) <= REACH:
                term = STENCIL[abs(x - other)] * read(other, y)
                total = term if total is None else total + term
        return total

    def respond(chunk, carry):
        for tile in range(5):
            sample = samples[tile]
            for part in range(0, fields, 8):

                def load(layer, y):
                    ref = (below, second, above)[(layer + LAYERS) // LAYERS]
                    return ref[at((layer % LAYERS * PADDED + REACH + chunk * 8 + y) * fields + part, 8), :]

                read = kept_rows(load)
                for y in range(8):
                    for x in range(LAYERS):
                        cell = x * 32 + chunk * 8 + y
                        layer = (tile - 2) * LAYERS + x
                        speed = spread(speed_ref, tile * cells + cell, 8)
                        if tile in (0, 4):
                            value = speed * far(read, layer, y, -4, 7)
                        elif tile == 2:
                            outside = far(read, layer, y, -4, -1) + far(read, layer, y, 4, 7)
                            value = third[at(cell * fields + part, 8), :] + speed * outside
                        else:
                            z_part = z_term[at((tile // 2 * cells + cell) * fields + part, 8), :]
                            value = 2.0 * read(layer, y) + speed * laplacian(read, layer, y, z_part, -4, 7)
                        row = (x * 2 + y // 4) * fields + part
                        side = y % 4 * HALF
                        sample[row : row + 8, side : side + HALF] = value
            hot = cell_ref[tile * PLACES : (tile + 1) * PLACES, :]
            picked = jnp.dot(jnp.concatenate(split(sample[...]), axis=0), hot, preferred_element_type=F32)
            picked = picked[: 8 * fields, :] + picked[8 * fields :, :]
            for part in range(fields // 8):
                rows = slice(tile * fields + part * 8, tile * fields + part * 8 + 8)
                line = line_ref[rows, :]
                total = total_ref[rows, :]
                for i in range(8):
                    chosen = line == i // 2 * 8 + chunk * 2 + i % 2
                    row = i * fields + part * 8
                    total = total + jnp.where(chosen, picked[row : row + 8, :], 0.0)
                total_ref[rows, :] = total
        return carry

    lax.fori_loop(0, 4, respond, 0)

    for group in range(peers // 16):
        lefts, rights = [], []
        for tile in range(5):
            rows = slice(tile * fields, (tile + 1) * fields)
            high, low = split(total_ref[rows, :] * weight_ref[rows, :])
            high, low = high.astype(F32), low.astype(F32)
            owner = owner_ref[rows, :]
            for part in (high, low):
                pieces = [jnp.where(owner == group * 16 + i, part, 0.0).astype(BF16) for i in range(16)]
                lefts.append(jnp.concatenate(pieces, axis=0))
                rights.append(slot_ref[tile * HALF : (tile + 1) * HALF, :])
        result = lax.dot_general(
            jnp.concatenate(lefts, axis=1), jnp.concatenate(rights, axis=1), NT, preferred_element_type=F32
        )
        table[group * 16 * fields : (group + 1) * 16 * fields, :] = result
    count = peers // 2
    mine = me[0] % 2
    place = lax.broadcasted_iota(jnp.int32, (count, HALF), 0)
    scale = jnp.broadcast_to(own_scale[...], (count, HALF))
    for out, side in ((kept, mine), (sent, 1 - mine)):
        out[0 : count * fields, :] = table[at(side * count * fields, count * fields), :]
        out[count * fields :, :] = jnp.where(place == me[0] - side * count, scale, 0.0)


def basis_parts(basis, when, out):
    rank = basis.shape[0] // HALF

    def body(group, carry):
        for step in range(8):
            high, low = split(basis[pl.ds(group * 8 + step, rank, stride=HALF), :])
            rows = at(group * rank, rank)
            out[rows, step * 256 : step * 256 + HALF] = high
            out[rows, step * 256 + HALF : (step + 1) * 256] = low
        return carry

    lax.fori_loop(0, 16, body, 0)


def adjoint(
    fields, peers, me, half, other, cell_ref, slot_ref, speed_ref, line_ref, owner_ref, weight_ref, turned, sources,
    prior, band_ref, basis, image, coeffs, high_ref, low_ref, inner_two, outer_two,
    inner_one, outer_one, z_term, image_parts, scaled, *lefts,
):
    entries = line_ref.shape[1]
    cells = LAYERS * 32
    rank = basis.shape[0] // 16
    clear_margins(inner_two, 5 * LAYERS, fields)
    clear_margins(inner_one, 3 * LAYERS, fields)
    count = peers // 2
    mine = me[0] % 2
    for ref, side in ((half, mine), (other, 1 - mine)):
        for i in range(count):
            scale = ref[count * fields + i : count * fields + i + 1, :]
            scaled[at((side * count + i) * fields, fields), :] = ref[i * fields : (i + 1) * fields, :] * scale
    for tile in range(5):
        rows = slice(tile * fields, (tile + 1) * fields)
        owner = owner_ref[rows, :]
        hot = slot_ref[tile * HALF : (tile + 1) * HALF, :]
        hot = jnp.concatenate([hot, hot], axis=0)
        total = jnp.zeros((fields, entries), F32)
        for group in range(peers // 16):
            parts = split(scaled[group * 16 * fields : (group + 1) * 16 * fields, :])
            found = jnp.dot(jnp.concatenate(parts, axis=1), hot, preferred_element_type=F32)
            for i in range(16):
                total = total + jnp.where(owner == group * 16 + i, found[i * fields : (i + 1) * fields, :], 0.0)
        high, low = split(total * weight_ref[rows, :])
        high_ref[rows, :] = high.astype(F32)
        low_ref[rows, :] = low.astype(F32)

    for tile in range(5):
        left = lefts[tile]
        for part in range(fields // 16):
            rows = slice(tile * fields + part * 16, tile * fields + part * 16 + 16)
            line, high, low = line_ref[rows, :], high_ref[rows, :], low_ref[rows, :]
            for i in range(32):
                chosen = line == i
                row = i * fields + part * 16
                left[row : row + 16, :entries] = jnp.where(chosen, high, 0.0).astype(BF16)
                left[row : row + 16, entries:] = jnp.where(chosen, low, 0.0).astype(BF16)
        hot = cell_ref[tile * PLACES : (tile + 1) * PLACES, :]
        value = lax.dot_general(left[...], jnp.concatenate([hot, hot], axis=1), NT, preferred_element_type=F32)
        for i in range(32):
            for step in range(4):
                layer, y = tile * LAYERS + i // 8, i % 8 * 4 + step
                now = value[i * fields : (i + 1) * fields, step * HALF : (step + 1) * HALF]
                if 1 <= tile <= 3:
                    outer_two[at(((layer - LAYERS) * 32 + y) * fields, fields), :] = now
                speed = spread(speed_ref, layer * 32 + y, fields)
                inner_two[at((layer * PADDED + REACH + y) * fields, fields), :] = speed * now

    def terms(index, carry):
        along_z(inner_two, (index + 1) * LAYERS, fields, band_ref, z_term, index * cells * fields)
        return carry

    lax.fori_loop(0, 3, terms, 0)

    def step_one(index, carry):
        tile, chunk = index // 4 + 1, index % 4
        for part in range(0, fields, 8):

            def load(layer, y):
                row = (tile * LAYERS + layer) * PADDED + REACH + chunk * 8 + y
                return inner_two[at(row * fields + part, 8), :]

            get = kept_rows(load)
            for y in range(8):
                for x in range(LAYERS):
                    layer = tile * LAYERS + x
                    speed = spread(speed_ref, layer * 32 + chunk * 8 + y, 8)
                    layer = layer - LAYERS
                    row = at((layer * 32 + chunk * 8 + y) * fields + part, 8)
                    now = 2.0 * outer_two[row, :] + laplacian(get, x, y, z_term[row, :], -4, 7)
                    outer_one[row, :] = now
                    inner_one[at((layer * PADDED + REACH + chunk * 8 + y) * fields + part, 8), :] = speed * now
        return carry

    lax.fori_loop(0, 12, step_one, 0)
    along_z(inner_one, LAYERS, fields, band_ref, z_term)

    def step_two(chunk, total):
        for part in range(0, fields, 8):

            def load(layer, y):
                row = (LAYERS + layer) * PADDED + REACH + chunk * 8 + y
                return inner_one[at(row * fields + part, 8), :]

            get = kept_rows(load)
            for y in range(8):
                for x in range(LAYERS):
                    cell = x * 32 + chunk * 8 + y
                    row = at(cell * fields + part, 8)
                    own_row = at((cells + cell) * fields + part, 8)
                    two = outer_two[own_row, :]
                    one = outer_one[own_row, :]
                    zero = 2.0 * one - two + laplacian(get, x, y, z_term[row, :], -4, 7)
                    value = spread(sources, cell, 8) * zero
                    value = value + spread(sources, 128 + cell, 8) * one
                    value = value + spread(sources, 256 + cell, 8) * two
                    image[row, :] = value + spread(prior, cell, 8) * turned[row, :]
        for x in range(LAYERS):
            for y in range(8):
                high, low = split(image[at((x * 32 + chunk * 8 + y) * fields, fields), :])
                side = y * 256
                rows = slice(x * 2 * fields, x * 2 * fields + fields)
                image_parts[rows, side : side + HALF] = high
                image_parts[rows, side + HALF : side + 256] = high
                rows = slice(x * 2 * fields + fields, (x + 1) * 2 * fields)
                image_parts[rows, side : side + HALF] = low
                image_parts[rows, side + HALF : side + 256] = jnp.zeros_like(low)
        for x in range(LAYERS):
            columns = basis[at((x * 4 + chunk) * rank, rank), :]
            parts = image_parts[x * 2 * fields : (x + 1) * 2 * fields, :]
            total = total + lax.dot_general(parts, columns, NT, preferred_element_type=F32)
        return total

    total = lax.fori_loop(0, 4, step_two, jnp.zeros((2 * fields, rank), F32))
    coeffs[...] = total[:fields, :] + total[fields:, :]


def remainder(fields, image, basis, *rest):
    *shares, out, coeffs, natural, sem = rest
    rank = coeffs.shape[1]
    while len(shares) > 1:
        shares = [shares[i][...] + shares[i + 1][...] for i in range(0, len(shares), 2)]
    total = shares[0][...]
    coeffs[...] = total
    parts = jnp.concatenate(split(total), axis=0)
    whole = natural.reshape(out.shape)

    def leave(x):
        return pltpu.make_async_copy(whole.at[:, x], out.at[:, x], sem.at[x])

    for x in range(LAYERS):
        for part in range(4):
            columns = basis[(x * 4 + part) * rank : (x * 4 + part + 1) * rank, :]
            both = jnp.dot(parts, columns, preferred_element_type=F32)
            for step in range(8):
                cell = x * 32 + part * 8 + step
                side = step * 256
                along = both[:fields, side : side + HALF] + both[:fields, side + HALF : side + 256]
                along = along + both[fields:, side : side + HALF]
                natural[pl.ds(cell, fields, stride=HALF), :] = image[cell * fields : (cell + 1) * fields, :] - along
        leave(x).start()
    for x in range(LAYERS):
        leave(x).wait()


def call(kernel, inputs, out_shape, scratch, flops, size, scalars=0, far=0, far_out=0, room=16):
    smem = pl.BlockSpec(memory_space=pltpu.SMEM)
    vmem = pl.BlockSpec(memory_space=pltpu.VMEM)
    hbm = pl.BlockSpec(memory_space=pltpu.HBM)
    inputs = [
        pltpu.with_memory_space_constraint(array, pltpu.HBM) if scalars <= i < scalars + far else array
        for i, array in enumerate(inputs)
    ]
    return pl.pallas_call(
        kernel,
        out_shape=out_shape,
        in_specs=[smem] * scalars + [hbm] * far + [vmem] * (len(inputs) - scalars - far),
        out_specs=[hbm] * far_out + [vmem] * (len(out_shape) - far_out),
        scratch_shapes=scratch,
        cost_estimate=pl.CostEstimate(flops=flops, bytes_accessed=size, transcendentals=0),
        compiler_params=pltpu.CompilerParams(vmem_limit_bytes=room * 2**20),
    )(*inputs)


def struct(*shape, dtype=F32):
    return jax.ShapeDtypeStruct(shape, dtype)


def swapped(array, axis, bits):
    count = lax.axis_size(axis)
    return lax.ppermute(array, axis, [(i, i ^ bits) for i in range(count)])


def local(
    probes,
    sources,
    kappa,
    prior,
    basis,
    entry_cell,
    entry_owner,
    entry_slot,
    entry_weight,
    entry_count,
    trace_weight,
):
    fields, rank = probes.shape[0], basis.shape[0]
    entries = entry_cell.shape[0]
    peers = lax.axis_size("space")
    padded = LAYERS * PADDED * fields
    cells = LAYERS * 32
    rows = entries // HALF
    me = lax.axis_index("space").astype(jnp.int32).reshape(1)

    own, probes_near, sources_near, prior_near, matrix = call(
        pack,
        (
            entry_count,
            probes.reshape(fields * cells, HALF),
            sources.reshape(3 * cells, HALF),
            prior.reshape(cells, HALF),
            kappa.reshape(cells, HALF),
            entry_cell.reshape(rows, HALF),
            entry_owner.reshape(rows, HALF),
            entry_slot.reshape(rows, HALF),
            entry_weight.reshape(rows, HALF),
        ),
        [
            struct(cells + 4 * rows, HALF),
            struct(fields * cells, HALF),
            struct(3 * cells, HALF),
            struct(cells, HALF),
            struct(256, 256, dtype=BF16),
        ],
        [pltpu.VMEM((3, rows, HALF), jnp.int32), pltpu.VMEM((rows, HALF), F32), pltpu.SemaphoreType.DMA((8,))],
        100_000,
        2 * 2**20,
        scalars=1,
        far=8,
    )
    partner = swapped(own, "space", 1)
    passed = lax.ppermute(
        jnp.concatenate([own, partner], axis=0),
        "space",
        [pair for i in range(1, peers - 1, 2) for pair in ((i, i + 1), (i + 1, i))],
    )

    turned, first, second, third = call(
        functools.partial(forward_own, fields),
        (probes_near, sources_near, own, matrix),
        [struct(cells * fields, HALF), struct(padded, HALF), struct(padded, HALF), struct(cells * fields, HALF)],
        [pltpu.VMEM((cells * fields, HALF), F32)],
        600_000_000,
        6 * 2**20,
    )
    half_rows = peers // 2 * (fields + 1)
    passed, second = lax.optimization_barrier((passed, second))
    across = swapped(passed[: own.shape[0]], "space", 1)
    kept, sent, cell_hot, slot_hot, speed, line, owner, weight = call(
        functools.partial(forward_window, fields, peers),
        (me, first, second, third, own, partner, passed, across, matrix, trace_weight.reshape(1, HALF)),
        [
            struct(half_rows, HALF),
            struct(half_rows, HALF),
            struct(5 * PLACES, entries, dtype=BF16),
            struct(5 * HALF, entries, dtype=BF16),
            struct(5 * cells, HALF),
            struct(5 * fields, entries, dtype=jnp.int32),
            struct(5 * fields, entries, dtype=jnp.int32),
            struct(5 * fields, entries),
        ],
        [
            pltpu.VMEM((padded, HALF), F32),
            pltpu.VMEM((padded, HALF), F32),
            pltpu.VMEM((2 * cells * fields, HALF), F32),
            pltpu.VMEM((5 * fields, entries), F32),
            pltpu.VMEM((peers * fields, HALF), F32),
        ]
        + [pltpu.VMEM((8 * fields, PLACES), F32)] * 5,
        3_000_000_000,
        6 * 2**20,
        scalars=1,
        room=20,
    )
    half = kept + swapped(sent, "space", 1)
    bits = 2
    while bits * 2 < peers:
        half = half + swapped(half, "space", bits)
        bits *= 2
    arrived = swapped(half, "space", bits)
    (columns,) = call(
        basis_parts,
        (basis.reshape(rank * cells, HALF), half),
        [struct(16 * rank, 2048, dtype=BF16)],
        [],
        10_000_000,
        8 * 2**20,
    )
    arrived, columns = lax.optimization_barrier((arrived, columns))
    half = half + arrived
    other = swapped(half, "space", 1)
    image, coeffs = call(
        functools.partial(adjoint, fields, peers),
        (
            me, half, other, cell_hot, slot_hot, speed, line, owner, weight,
            turned, sources_near, prior_near, matrix, columns,
        ),
        [struct(cells * fields, HALF), struct(fields, rank)],
        [
            pltpu.VMEM((5 * fields, entries), F32),
            pltpu.VMEM((5 * fields, entries), F32),
            pltpu.VMEM((5 * padded, HALF), F32),
            pltpu.VMEM((3 * cells * fields, HALF), F32),
            pltpu.VMEM((3 * padded, HALF), F32),
            pltpu.VMEM((3 * cells * fields, HALF), F32),
            pltpu.VMEM((3 * cells * fields, HALF), F32),
            pltpu.VMEM((8 * fields, 2048), BF16),
            pltpu.VMEM((peers * fields, HALF), F32),
        ]
        + [pltpu.VMEM((32 * fields, 2 * entries), BF16)] * 5,
        5_000_000_000,
        10 * 2**20,
        scalars=1,
        room=34,
    )
    bits = 1
    while bits * 4 < peers:
        coeffs = coeffs + swapped(coeffs, "space", bits)
        bits *= 2
    shares = [coeffs] + [swapped(coeffs, "space", bits * i) for i in range(1, peers // bits)]
    hess_probe, coeffs = call(
        functools.partial(remainder, fields),
        (image, columns, *shares),
        [struct(*probes.shape), struct(fields, rank)],
        [pltpu.VMEM((fields * cells, HALF), F32), pltpu.SemaphoreType.DMA((LAYERS,))],
        200_000_000,
        6 * 2**20,
        far_out=1,
    )
    return hess_probe, coeffs.T


def solution(mesh):
    return jax.shard_map(
        local,
        mesh=mesh,
        in_specs=(
            P("group", "space", None, None),
            P(None, ("group", "space"), None, None),
            P(("group", "space"), None, None),
            P(("group", "space"), None, None),
            P("group", "space", None, None),
            P(("group", "space")),
            P(("group", "space")),
            P(("group", "space")),
            P(("group", "space")),
            P(("group", "space")),
            P(("group", "space")),
        ),
        out_specs=(P("group", "space", None, None), P("group", None)),
        check_vma=False,
    )
```

```python
import functools

import jax
import jax.numpy as jnp
from jax import lax
from jax.experimental import pallas as pl
from jax.experimental.pallas import tpu as pltpu
from jax.sharding import PartitionSpec as P

STENCIL = (-205.0 / 72.0, 8.0 / 5.0, -1.0 / 5.0, 8.0 / 315.0, -1.0 / 560.0)
CENTER = 3.0 * STENCIL[0]
REACH = 4
LAYERS = 4
PADDED = 40
HALF = 128
PLACES = 512
F32 = jnp.float32
BF16 = jnp.bfloat16
NT = (((1,), (1,)), ((), ()))


def split(value):
    high = value.astype(BF16)
    low = (value - high.astype(F32)).astype(BF16)
    return high, low


def at(row, count=16):
    return pl.ds(pl.multiple_of(row, 8), count)


def window(ref, start, size):
    return ref.at[pl.ds(pl.multiple_of(start, 8), size)]


def kept_rows(load):
    rows = {}

    def get(layer, y):
        if (layer, y) not in rows:
            rows[layer, y] = load(layer, y)
        return rows[layer, y]

    return get


def spread(ref, row, fields):
    return jnp.broadcast_to(ref[pl.ds(row, 1), :], (fields, HALF))


def clear_margins(ref, layers, fields):
    margin = jnp.zeros((REACH * fields, HALF), F32)
    for layer in range(layers):
        start = layer * PADDED * fields
        ref[start : start + REACH * fields, :] = margin
        start += (PADDED - REACH) * fields
        ref[start : start + REACH * fields, :] = margin


def along_z(ref, first, fields, band_ref, out_ref, row=0):
    pieces = [ref[at(((first + x) * PADDED + REACH) * fields, 32 * fields), :] for x in range(LAYERS)]
    high, low = split(jnp.concatenate(pieces, axis=0))
    both = jnp.dot(jnp.concatenate([high, low], axis=1), band_ref[...], preferred_element_type=F32)
    out_ref[at(row, LAYERS * 32 * fields), :] = both[:, :HALF] + both[:, HALF:]


def laplacian(get, x, y, z_term, lowest, highest):
    total = z_term
    for k in range(1, REACH + 1):
        ring = get(x, y + k) + get(x, y - k)
        if x + k <= highest:
            ring = ring + get(x + k, y)
        if x - k >= lowest:
            ring = ring + get(x - k, y)
        total = total + STENCIL[k] * ring
    return total


def pack(
    count, probes, sources, prior, kappa, cell, owner, slot, weight,
    statics, probes_out, sources_out, prior_out, band_ref, small_int, small_float, sem,
):
    rows = cell.shape[0]
    cells = kappa.shape[0]
    small = [
        pltpu.make_async_copy(kappa, statics.at[pl.ds(0, cells)], sem.at[0]),
        pltpu.make_async_copy(cell, small_int.at[0], sem.at[1]),
        pltpu.make_async_copy(owner, small_int.at[1], sem.at[2]),
        pltpu.make_async_copy(slot, small_int.at[2], sem.at[3]),
        pltpu.make_async_copy(weight, small_float, sem.at[4]),
    ]
    large = [
        pltpu.make_async_copy(probes, probes_out, sem.at[5]),
        pltpu.make_async_copy(sources, sources_out, sem.at[6]),
        pltpu.make_async_copy(prior, prior_out, sem.at[7]),
    ]
    for copy in small + large:
        copy.start()
    apart = lax.broadcasted_iota(jnp.int32, (HALF, HALF), 0) - lax.broadcasted_iota(jnp.int32, (HALF, HALF), 1)
    full = jnp.where(apart == 0, CENTER, jnp.zeros((HALF, HALF), F32))
    for reach in range(1, REACH + 1):
        full = jnp.where(jnp.abs(apart) == reach, STENCIL[reach], full)
    high, low = split(full)
    band_ref[0:HALF, 0:HALF] = high
    band_ref[HALF:, 0:HALF] = high
    band_ref[0:HALF, HALF:] = low
    band_ref[HALF:, HALF:] = jnp.zeros_like(low)
    for copy in small:
        copy.wait()
    for i in range(3):
        statics[cells + i * rows : cells + (i + 1) * rows, :] = small_int[i].astype(F32)
    place = lax.broadcasted_iota(jnp.int32, (rows, HALF), 0) * HALF
    place = place + lax.broadcasted_iota(jnp.int32, (rows, HALF), 1)
    live = jnp.where(place < count[0], small_float[...], 0.0)
    statics[cells + 3 * rows : cells + 4 * rows, :] = live
    for copy in large:
        copy.wait()


def forward_own(fields, probes, sources, statics, band_ref, turned, first, second, third, z_term):
    clear_margins(first, LAYERS, fields)
    clear_margins(second, LAYERS, fields)

    slab, flat = PADDED * fields, 32 * fields
    ahead = 24 * fields

    def load(chunk, carry):
        there = window(turned, chunk * 8 * fields, LAYERS * flat - ahead)
        padded = window(first, chunk * 8 * fields, LAYERS * slab - ahead)
        here = window(probes, chunk * 8, LAYERS * flat - 24)
        push = window(sources, chunk * 8, 3 * LAYERS * 32 - 24)
        for x in range(LAYERS):
            for y in range(8):
                cell = x * 32 + y
                value = here[pl.ds(cell, fields, stride=HALF), :]
                there[cell * fields : (cell + 1) * fields, :] = value
                row = x * slab + (REACH + y) * fields
                padded[row : row + fields, :] = value * spread(push, cell, fields)
        return carry

    lax.fori_loop(0, 4, load, 0)

    def sweep(field, emit):
        along_z(field, 0, fields, band_ref, z_term)

        def body(chunk, carry):
            padded = window(field, chunk * 8 * fields, LAYERS * slab - ahead)
            z_part = window(z_term, chunk * 8 * fields, LAYERS * flat - ahead)
            speed = window(statics, chunk * 8, LAYERS * 32 - 24)
            put = emit(chunk)
            for part in range(0, fields, 8):

                def load(layer, y):
                    row = layer * slab + (REACH + y) * fields + part
                    return padded[row : row + 8, :]

                get = kept_rows(load)
                for y in range(8):
                    for x in range(LAYERS):
                        cell = x * 32 + y
                        row = cell * fields + part
                        total = laplacian(get, x, y, z_part[row : row + 8, :], 0, LAYERS - 1)
                        put(x, y, part, get(x, y), spread(speed, cell, 8) * total)
            return carry

        lax.fori_loop(0, 4, body, 0)

    def step_one(chunk):
        push = window(sources, chunk * 8, 3 * LAYERS * 32 - 24)
        there = window(turned, chunk * 8 * fields, LAYERS * flat - ahead)
        out = window(second, chunk * 8 * fields, LAYERS * slab - ahead)

        def put(x, y, part, now, change):
            cell = x * 32 + y
            row = cell * fields + part
            change = change + there[row : row + 8, :] * spread(push, 128 + cell, 8)
            row = x * slab + (REACH + y) * fields + part
            out[row : row + 8, :] = 2.0 * now + change

        return put

    sweep(first, step_one)

    def step_two(chunk):
        push = window(sources, chunk * 8, 3 * LAYERS * 32 - 24)
        there = window(turned, chunk * 8 * fields, LAYERS * flat - ahead)
        before = window(first, chunk * 8 * fields, LAYERS * slab - ahead)
        out = window(third, chunk * 8 * fields, LAYERS * flat - ahead)

        def put(x, y, part, now, change):
            cell = x * 32 + y
            row = x * slab + (REACH + y) * fields + part
            change = change - before[row : row + 8, :]
            row = cell * fields + part
            change = change + there[row : row + 8, :] * spread(push, 256 + cell, 8)
            out[row : row + 8, :] = 2.0 * now + change

        return put

    sweep(second, step_two)


def entry_row(value, row):
    return jnp.concatenate([value[row + i : row + i + 1, :] for i in range(4)], axis=1)


def forward_window(
    fields, peers, me, first, second, third, own, partner, passed, across, band_ref, own_scale,
    kept, sent, cell_ref, slot_ref, speed_ref, line_ref, owner_ref, weight_ref,
    below, above, z_term, total_ref, table, *samples,
):
    entries = line_ref.shape[1]
    cells = LAYERS * 32
    length = own.shape[0]
    odd = me[0] % 2 == 1
    clear_margins(below, LAYERS, fields)
    clear_margins(above, LAYERS, fields)
    total_ref[...] = jnp.zeros_like(total_ref)
    near, next_one, far_one, side_one = passed[0:length, :], passed[length:, :], across[0:length, :], partner[...]
    tiles = (
        jnp.where(odd, far_one, next_one),
        jnp.where(odd, side_one, near),
        own[...],
        jnp.where(odd, near, side_one),
        jnp.where(odd, next_one, far_one),
    )
    place = lax.broadcasted_iota(jnp.int32, (PLACES, entries), 0)
    slot_place = lax.broadcasted_iota(jnp.int32, (HALF, entries), 0)
    for tile, value in enumerate(tiles):
        speed_ref[tile * cells : (tile + 1) * cells, :] = value[0:cells, :]
        cell = entry_row(value, cells).astype(jnp.int32)
        owner = entry_row(value, cells + 4).astype(jnp.int32)
        slot = entry_row(value, cells + 8).astype(jnp.int32)
        weight = entry_row(value, cells + 12)
        hot = jnp.where(place == jnp.bitwise_and(cell, PLACES - 1), 1.0, 0.0)
        cell_ref[tile * PLACES : (tile + 1) * PLACES, :] = hot.astype(BF16)
        hot = jnp.where(slot_place == slot, 1.0, 0.0)
        slot_ref[tile * HALF : (tile + 1) * HALF, :] = hot.astype(BF16)
        rows = slice(tile * fields, (tile + 1) * fields)
        line_ref[rows, :] = jnp.broadcast_to(lax.shift_right_logical(cell, 9), (fields, entries))
        owner_ref[rows, :] = jnp.broadcast_to(owner, (fields, entries))
        weight_ref[rows, :] = jnp.broadcast_to(weight, (fields, entries))

    slab, flat = PADDED * fields, 32 * fields
    ahead = 24 * fields

    def outward(chunk, carry):
        speed = window(speed_ref, chunk * 8, 5 * cells - 24)
        here, low, high = (window(ref, chunk * 8 * fields, LAYERS * slab - ahead) for ref in (first, below, above))
        for y in range(8):
            rows = [slice(x * slab + (REACH + y) * fields, x * slab + (REACH + y + 1) * fields) for x in range(LAYERS)]
            mine = [here[row, :] for row in rows]
            for x in range(LAYERS):
                up = sum(STENCIL[4 + x - other] * mine[other] for other in range(x, LAYERS))
                down = sum(STENCIL[4 + other - x] * mine[other] for other in range(x + 1))
                high[rows[x], :] = spread(speed, 3 * cells + x * 32 + y, fields) * up
                low[rows[x], :] = spread(speed, cells + x * 32 + y, fields) * down
        return carry

    lax.fori_loop(0, 4, outward, 0)
    along_z(below, 0, fields, band_ref, z_term, 0)
    along_z(above, 0, fields, band_ref, z_term, cells * fields)

    def far(read, x, y, lowest, highest):
        total = None
        for other in range(lowest, highest + 1):
            if 1 <= abs(x - other) <= REACH:
                term = STENCIL[abs(x - other)] * read(other, y)
                total = term if total is None else total + term
        return total

    def respond(chunk, carry):
        speeds = window(speed_ref, chunk * 8, 5 * cells - 24)
        sides = [window(ref, chunk * 8 * fields, LAYERS * slab - ahead) for ref in (below, second, above)]
        base = window(third, chunk * 8 * fields, LAYERS * flat - ahead)
        z_parts = window(z_term, chunk * 8 * fields, 2 * LAYERS * flat - ahead)
        for tile in range(5):
            sample = samples[tile]
            for part in range(0, fields, 8):

                def load(layer, y):
                    row = layer % LAYERS * slab + (REACH + y) * fields + part
                    return sides[(layer + LAYERS) // LAYERS][row : row + 8, :]

                read = kept_rows(load)
                for y in range(8):
                    for x in range(LAYERS):
                        cell = x * 32 + y
                        row = cell * fields + part
                        layer = (tile - 2) * LAYERS + x
                        speed = spread(speeds, tile * cells + cell, 8)
                        if tile in (0, 4):
                            value = speed * far(read, layer, y, -4, 7)
                        elif tile == 2:
                            outside = far(read, layer, y, -4, -1) + far(read, layer, y, 4, 7)
                            value = base[row : row + 8, :] + speed * outside
                        else:
                            row = row + tile // 2 * cells * fields
                            z_part = z_parts[row : row + 8, :]
                            value = 2.0 * read(layer, y) + speed * laplacian(read, layer, y, z_part, -4, 7)
                        row = (x * 2 + y // 4) * fields + part
                        side = y % 4 * HALF
                        sample[row : row + 8, side : side + HALF] = value
            hot = cell_ref[tile * PLACES : (tile + 1) * PLACES, :]
            picked = jnp.dot(jnp.concatenate(split(sample[...]), axis=0), hot, preferred_element_type=F32)
            picked = picked[: 8 * fields, :] + picked[8 * fields :, :]
            for part in range(fields // 8):
                rows = slice(tile * fields + part * 8, tile * fields + part * 8 + 8)
                line = line_ref[rows, :]
                total = total_ref[rows, :]
                for i in range(8):
                    chosen = line == i // 2 * 8 + chunk * 2 + i % 2
                    row = i * fields + part * 8
                    total = total + jnp.where(chosen, picked[row : row + 8, :], 0.0)
                total_ref[rows, :] = total
        return carry

    lax.fori_loop(0, 4, respond, 0)

    for group in range(peers // 16):
        lefts, rights = [], []
        for tile in range(5):
            rows = slice(tile * fields, (tile + 1) * fields)
            high, low = split(total_ref[rows, :] * weight_ref[rows, :])
            high, low = high.astype(F32), low.astype(F32)
            owner = owner_ref[rows, :]
            for part in (high, low):
                pieces = [jnp.where(owner == group * 16 + i, part, 0.0).astype(BF16) for i in range(16)]
                lefts.append(jnp.concatenate(pieces, axis=0))
                rights.append(slot_ref[tile * HALF : (tile + 1) * HALF, :])
        result = lax.dot_general(
            jnp.concatenate(lefts, axis=1), jnp.concatenate(rights, axis=1), NT, preferred_element_type=F32
        )
        table[group * 16 * fields : (group + 1) * 16 * fields, :] = result
    count = peers // 2
    mine = me[0] % 2
    place = lax.broadcasted_iota(jnp.int32, (count, HALF), 0)
    scale = jnp.broadcast_to(own_scale[...], (count, HALF))
    for out, side in ((kept, mine), (sent, 1 - mine)):
        out[0 : count * fields, :] = table[at(side * count * fields, count * fields), :]
        out[count * fields :, :] = jnp.where(place == me[0] - side * count, scale, 0.0)


def basis_parts(first, basis, when, out):
    rank = basis.shape[0] // HALF

    def body(group, carry):
        here = window(basis, (first + group) * 8, basis.shape[0] - 15 * 8)
        there = window(out, group * rank, rank)
        for step in range(8):
            high, low = split(here[pl.ds(step, rank, stride=HALF), :])
            there[:, step * 256 : step * 256 + HALF] = high
            there[:, step * 256 + HALF : (step + 1) * 256] = low
        return carry

    lax.fori_loop(0, 8, body, 0)


def adjoint(
    fields, peers, me, half, other, cell_ref, slot_ref, speed_ref, line_ref, owner_ref, weight_ref, turned, sources,
    prior, band_ref, basis, basis_two, image, coeffs, high_ref, low_ref, inner_two, outer_two,
    inner_one, outer_one, z_term, image_parts, scaled, *lefts,
):
    entries = line_ref.shape[1]
    cells = LAYERS * 32
    rank = basis.shape[0] // 8
    clear_margins(inner_two, 5 * LAYERS, fields)
    clear_margins(inner_one, 3 * LAYERS, fields)
    count = peers // 2
    mine = me[0] % 2
    for ref, side in ((half, mine), (other, 1 - mine)):
        for i in range(count):
            scale = ref[count * fields + i : count * fields + i + 1, :]
            scaled[at((side * count + i) * fields, fields), :] = ref[i * fields : (i + 1) * fields, :] * scale
    for tile in range(5):
        rows = slice(tile * fields, (tile + 1) * fields)
        owner = owner_ref[rows, :]
        hot = slot_ref[tile * HALF : (tile + 1) * HALF, :]
        hot = jnp.concatenate([hot, hot], axis=0)
        total = jnp.zeros((fields, entries), F32)
        for group in range(peers // 16):
            parts = split(scaled[group * 16 * fields : (group + 1) * 16 * fields, :])
            found = jnp.dot(jnp.concatenate(parts, axis=1), hot, preferred_element_type=F32)
            for i in range(16):
                total = total + jnp.where(owner == group * 16 + i, found[i * fields : (i + 1) * fields, :], 0.0)
        high, low = split(total * weight_ref[rows, :])
        high_ref[rows, :] = high.astype(F32)
        low_ref[rows, :] = low.astype(F32)

    for tile in range(5):
        left = lefts[tile]
        for part in range(fields // 16):
            rows = slice(tile * fields + part * 16, tile * fields + part * 16 + 16)
            line, high, low = line_ref[rows, :], high_ref[rows, :], low_ref[rows, :]
            for i in range(32):
                chosen = line == i
                row = i * fields + part * 16
                left[row : row + 16, :entries] = jnp.where(chosen, high, 0.0).astype(BF16)
                left[row : row + 16, entries:] = jnp.where(chosen, low, 0.0).astype(BF16)
        hot = cell_ref[tile * PLACES : (tile + 1) * PLACES, :]
        value = lax.dot_general(left[...], jnp.concatenate([hot, hot], axis=1), NT, preferred_element_type=F32)
        for i in range(32):
            for step in range(4):
                layer, y = tile * LAYERS + i // 8, i % 8 * 4 + step
                now = value[i * fields : (i + 1) * fields, step * HALF : (step + 1) * HALF]
                if 1 <= tile <= 3:
                    outer_two[at(((layer - LAYERS) * 32 + y) * fields, fields), :] = now
                speed = spread(speed_ref, layer * 32 + y, fields)
                inner_two[at((layer * PADDED + REACH + y) * fields, fields), :] = speed * now

    def terms(index, carry):
        along_z(inner_two, (index + 1) * LAYERS, fields, band_ref, z_term, index * cells * fields)
        return carry

    lax.fori_loop(0, 3, terms, 0)

    slab, flat = PADDED * fields, 32 * fields
    ahead = 24 * fields

    def step_one(index, carry):
        tile, chunk = index // 4, index % 4
        start, skip = tile * LAYERS * slab + chunk * 8 * fields, tile * LAYERS * flat + chunk * 8 * fields
        here = window(inner_two, start, 3 * LAYERS * slab - ahead)
        two, one, z_part = (window(ref, skip, LAYERS * flat - ahead) for ref in (outer_two, outer_one, z_term))
        out = window(inner_one, start, LAYERS * slab - ahead)
        speed = window(speed_ref, (tile + 1) * cells + chunk * 8, cells - 24)
        for part in range(0, fields, 8):

            def load(layer, y):
                row = (layer + LAYERS) * slab + (REACH + y) * fields + part
                return here[row : row + 8, :]

            get = kept_rows(load)
            for y in range(8):
                for x in range(LAYERS):
                    cell = x * 32 + y
                    row = slice(cell * fields + part, cell * fields + part + 8)
                    now = 2.0 * two[row, :] + laplacian(get, x, y, z_part[row, :], -4, 7)
                    one[row, :] = now
                    row = x * slab + (REACH + y) * fields + part
                    out[row : row + 8, :] = spread(speed, cell, 8) * now
        return carry

    lax.fori_loop(0, 12, step_one, 0)
    along_z(inner_one, LAYERS, fields, band_ref, z_term)

    def step_two(chunk, total):
        skip = chunk * 8 * fields
        here = window(inner_one, skip, 3 * LAYERS * slab - ahead)
        two_rows, one_rows = (window(ref, LAYERS * flat + skip, LAYERS * flat - ahead) for ref in (outer_two, outer_one))
        z_part, there, out = (window(ref, skip, LAYERS * flat - ahead) for ref in (z_term, turned, image))
        push = window(sources, chunk * 8, 3 * cells - 24)
        damping = window(prior, chunk * 8, cells - 24)
        for part in range(0, fields, 8):

            def load(layer, y):
                row = (layer + LAYERS) * slab + (REACH + y) * fields + part
                return here[row : row + 8, :]

            get = kept_rows(load)
            for y in range(8):
                for x in range(LAYERS):
                    cell = x * 32 + y
                    row = slice(cell * fields + part, cell * fields + part + 8)
                    two, one = two_rows[row, :], one_rows[row, :]
                    zero = 2.0 * one - two + laplacian(get, x, y, z_part[row, :], -4, 7)
                    value = spread(push, cell, 8) * zero
                    value = value + spread(push, 128 + cell, 8) * one
                    value = value + spread(push, 256 + cell, 8) * two
                    out[row, :] = value + spread(damping, cell, 8) * there[row, :]
        for x in range(LAYERS):
            for y in range(8):
                cell = x * 32 + y
                high, low = split(out[cell * fields : (cell + 1) * fields, :])
                side = y * 256
                rows = slice(x * 2 * fields, x * 2 * fields + fields)
                image_parts[rows, side : side + HALF] = high
                image_parts[rows, side + HALF : side + 256] = high
                rows = slice(x * 2 * fields + fields, (x + 1) * 2 * fields)
                image_parts[rows, side : side + HALF] = low
                image_parts[rows, side + HALF : side + 256] = jnp.zeros_like(low)
        for x in range(LAYERS):
            columns = (basis, basis_two)[x // 2][at((x % 2 * 4 + chunk) * rank, rank), :]
            parts = image_parts[x * 2 * fields : (x + 1) * 2 * fields, :]
            total = total + lax.dot_general(parts, columns, NT, preferred_element_type=F32)
        return total

    total = lax.fori_loop(0, 4, step_two, jnp.zeros((2 * fields, rank), F32))
    coeffs[...] = total[:fields, :] + total[fields:, :]


def remainder(fields, image, basis, basis_two, *rest):
    *shares, out, coeffs, natural, sem = rest
    rank = coeffs.shape[1]
    while len(shares) > 1:
        shares = [shares[i][...] + shares[i + 1][...] for i in range(0, len(shares), 2)]
    total = shares[0][...]
    coeffs[...] = total
    parts = jnp.concatenate(split(total), axis=0)
    whole = natural.reshape(out.shape)

    def leave(x):
        return pltpu.make_async_copy(whole.at[:, x], out.at[:, x], sem.at[x])

    for x in range(LAYERS):
        for part in range(4):
            columns = (basis, basis_two)[x // 2][(x % 2 * 4 + part) * rank : (x % 2 * 4 + part + 1) * rank, :]
            both = jnp.dot(parts, columns, preferred_element_type=F32)
            for step in range(8):
                cell = x * 32 + part * 8 + step
                side = step * 256
                along = both[:fields, side : side + HALF] + both[:fields, side + HALF : side + 256]
                along = along + both[fields:, side : side + HALF]
                natural[pl.ds(cell, fields, stride=HALF), :] = image[cell * fields : (cell + 1) * fields, :] - along
        leave(x).start()
    for x in range(LAYERS):
        leave(x).wait()


def call(kernel, inputs, out_shape, scratch, flops, size, scalars=0, far=0, far_out=0, room=16):
    smem = pl.BlockSpec(memory_space=pltpu.SMEM)
    vmem = pl.BlockSpec(memory_space=pltpu.VMEM)
    hbm = pl.BlockSpec(memory_space=pltpu.HBM)
    inputs = [
        pltpu.with_memory_space_constraint(array, pltpu.HBM) if scalars <= i < scalars + far else array
        for i, array in enumerate(inputs)
    ]
    return pl.pallas_call(
        kernel,
        out_shape=out_shape,
        in_specs=[smem] * scalars + [hbm] * far + [vmem] * (len(inputs) - scalars - far),
        out_specs=[hbm] * far_out + [vmem] * (len(out_shape) - far_out),
        scratch_shapes=scratch,
        cost_estimate=pl.CostEstimate(flops=flops, bytes_accessed=size, transcendentals=0),
        compiler_params=pltpu.CompilerParams(vmem_limit_bytes=room * 2**20),
    )(*inputs)


def struct(*shape, dtype=F32):
    return jax.ShapeDtypeStruct(shape, dtype)


def swapped(array, axis, bits):
    count = lax.axis_size(axis)
    return lax.ppermute(array, axis, [(i, i ^ bits) for i in range(count)])


def local(
    probes,
    sources,
    kappa,
    prior,
    basis,
    entry_cell,
    entry_owner,
    entry_slot,
    entry_weight,
    entry_count,
    trace_weight,
):
    fields, rank = probes.shape[0], basis.shape[0]
    entries = entry_cell.shape[0]
    peers = lax.axis_size("space")
    padded = LAYERS * PADDED * fields
    cells = LAYERS * 32
    rows = entries // HALF
    me = lax.axis_index("space").astype(jnp.int32).reshape(1)

    own, probes_near, sources_near, prior_near, matrix = call(
        pack,
        (
            entry_count,
            probes.reshape(fields * cells, HALF),
            sources.reshape(3 * cells, HALF),
            prior.reshape(cells, HALF),
            kappa.reshape(cells, HALF),
            entry_cell.reshape(rows, HALF),
            entry_owner.reshape(rows, HALF),
            entry_slot.reshape(rows, HALF),
            entry_weight.reshape(rows, HALF),
        ),
        [
            struct(cells + 4 * rows, HALF),
            struct(fields * cells, HALF),
            struct(3 * cells, HALF),
            struct(cells, HALF),
            struct(256, 256, dtype=BF16),
        ],
        [pltpu.VMEM((3, rows, HALF), jnp.int32), pltpu.VMEM((rows, HALF), F32), pltpu.SemaphoreType.DMA((8,))],
        100_000,
        2 * 2**20,
        scalars=1,
        far=8,
    )
    partner = swapped(own, "space", 1)
    passed = lax.ppermute(
        jnp.concatenate([own, partner], axis=0),
        "space",
        [pair for i in range(1, peers - 1, 2) for pair in ((i, i + 1), (i + 1, i))],
    )

    turned, first, second, third = call(
        functools.partial(forward_own, fields),
        (probes_near, sources_near, own, matrix),
        [struct(cells * fields, HALF), struct(padded, HALF), struct(padded, HALF), struct(cells * fields, HALF)],
        [pltpu.VMEM((cells * fields, HALF), F32)],
        600_000_000,
        6 * 2**20,
    )
    half_rows = peers // 2 * (fields + 1)
    passed, second = lax.optimization_barrier((passed, second))
    across = swapped(passed, "space", 1)
    kept, sent, cell_hot, slot_hot, speed, line, owner, weight = call(
        functools.partial(forward_window, fields, peers),
        (me, first, second, third, own, partner, passed, across, matrix, trace_weight.reshape(1, HALF)),
        [
            struct(half_rows, HALF),
            struct(half_rows, HALF),
            struct(5 * PLACES, entries, dtype=BF16),
            struct(5 * HALF, entries, dtype=BF16),
            struct(5 * cells, HALF),
            struct(5 * fields, entries, dtype=jnp.int32),
            struct(5 * fields, entries, dtype=jnp.int32),
            struct(5 * fields, entries),
        ],
        [
            pltpu.VMEM((padded, HALF), F32),
            pltpu.VMEM((padded, HALF), F32),
            pltpu.VMEM((2 * cells * fields, HALF), F32),
            pltpu.VMEM((5 * fields, entries), F32),
            pltpu.VMEM((peers * fields, HALF), F32),
        ]
        + [pltpu.VMEM((8 * fields, PLACES), F32)] * 5,
        3_000_000_000,
        6 * 2**20,
        scalars=1,
        room=20,
    )
    half = kept + swapped(sent, "space", 1)
    columns = []
    bits = 2
    while bits < peers:
        arrived = swapped(half, "space", bits)
        if len(columns) < 2:
            (some,) = call(
                functools.partial(basis_parts, 8 * len(columns)),
                (basis.reshape(rank * cells, HALF), half),
                [struct(8 * rank, 2048, dtype=BF16)],
                [],
                10_000_000,
                4 * 2**20,
            )
            arrived, some = lax.optimization_barrier((arrived, some))
            columns.append(some)
        half = half + arrived
        bits *= 2
    other = swapped(half, "space", 1)
    image, coeffs = call(
        functools.partial(adjoint, fields, peers),
        (
            me, half, other, cell_hot, slot_hot, speed, line, owner, weight,
            turned, sources_near, prior_near, matrix, *columns,
        ),
        [struct(cells * fields, HALF), struct(fields, rank)],
        [
            pltpu.VMEM((5 * fields, entries), F32),
            pltpu.VMEM((5 * fields, entries), F32),
            pltpu.VMEM((5 * padded, HALF), F32),
            pltpu.VMEM((3 * cells * fields, HALF), F32),
            pltpu.VMEM((3 * padded, HALF), F32),
            pltpu.VMEM((3 * cells * fields, HALF), F32),
            pltpu.VMEM((3 * cells * fields, HALF), F32),
            pltpu.VMEM((8 * fields, 2048), BF16),
            pltpu.VMEM((peers * fields, HALF), F32),
        ]
        + [pltpu.VMEM((32 * fields, 2 * entries), BF16)] * 5,
        5_000_000_000,
        10 * 2**20,
        scalars=1,
        room=34,
    )
    bits = 1
    while bits * 4 < peers:
        coeffs = coeffs + swapped(coeffs, "space", bits)
        bits *= 2
    shares = [coeffs] + [swapped(coeffs, "space", bits * i) for i in range(1, peers // bits)]
    hess_probe, coeffs = call(
        functools.partial(remainder, fields),
        (image, *columns, *shares),
        [struct(*probes.shape), struct(fields, rank)],
        [pltpu.VMEM((fields * cells, HALF), F32), pltpu.SemaphoreType.DMA((LAYERS,))],
        200_000_000,
        6 * 2**20,
        far_out=1,
    )
    return hess_probe, coeffs.T


def solution(mesh):
    return jax.shard_map(
        local,
        mesh=mesh,
        in_specs=(
            P("group", "space", None, None),
            P(None, ("group", "space"), None, None),
            P(("group", "space"), None, None),
            P(("group", "space"), None, None),
            P("group", "space", None, None),
            P(("group", "space")),
            P(("group", "space")),
            P(("group", "space")),
            P(("group", "space")),
            P(("group", "space")),
            P(("group", "space")),
        ),
        out_specs=(P("group", "space", None, None), P("group", None)),
        check_vma=False,
    )
```

```python
import functools

import jax
import jax.numpy as jnp
from jax import lax
from jax.experimental import pallas as pl
from jax.experimental.pallas import tpu as pltpu
from jax.sharding import PartitionSpec as P

STENCIL = (-205.0 / 72.0, 8.0 / 5.0, -1.0 / 5.0, 8.0 / 315.0, -1.0 / 560.0)
CENTER = 3.0 * STENCIL[0]
REACH = 4
LAYERS = 4
PADDED = 40
HALF = 128
PLACES = 512
F32 = jnp.float32
BF16 = jnp.bfloat16
NT = (((1,), (1,)), ((), ()))


def split(value):
    high = value.astype(BF16)
    low = (value - high.astype(F32)).astype(BF16)
    return high, low


def at(row, count=16):
    return pl.ds(pl.multiple_of(row, 8), count)


def window(ref, start, size):
    return ref.at[pl.ds(pl.multiple_of(start, 8), size)]


def kept_rows(load):
    rows = {}

    def get(layer, y):
        if (layer, y) not in rows:
            rows[layer, y] = load(layer, y)
        return rows[layer, y]

    return get


def spread(ref, row, fields):
    return jnp.broadcast_to(ref[pl.ds(row, 1), :], (fields, HALF))


def clear_margins(ref, layers, fields):
    margin = jnp.zeros((REACH * fields, HALF), F32)
    for layer in range(layers):
        start = layer * PADDED * fields
        ref[start : start + REACH * fields, :] = margin
        start += (PADDED - REACH) * fields
        ref[start : start + REACH * fields, :] = margin


def along_z(ref, first, fields, band_ref, out_ref, row=0):
    pieces = [ref[at(((first + x) * PADDED + REACH) * fields, 32 * fields), :] for x in range(LAYERS)]
    high, low = split(jnp.concatenate(pieces, axis=0))
    both = jnp.dot(jnp.concatenate([high, low], axis=1), band_ref[...], preferred_element_type=F32)
    out_ref[at(row, LAYERS * 32 * fields), :] = both[:, :HALF] + both[:, HALF:]


def laplacian(get, x, y, z_term, lowest, highest):
    total = z_term
    for k in range(1, REACH + 1):
        ring = get(x, y + k) + get(x, y - k)
        if x + k <= highest:
            ring = ring + get(x + k, y)
        if x - k >= lowest:
            ring = ring + get(x - k, y)
        total = total + STENCIL[k] * ring
    return total


def pack(
    count, me, probes, sources, prior, kappa, cell, owner, slot, weight,
    statics, probes_out, sources_out, prior_out, band_ref, small_int, small_float, sem,
):
    rows = cell.shape[0]
    cells = kappa.shape[0]
    small = [
        pltpu.make_async_copy(kappa, statics.at[pl.ds(0, cells)], sem.at[0]),
        pltpu.make_async_copy(cell, small_int.at[0], sem.at[1]),
        pltpu.make_async_copy(owner, small_int.at[1], sem.at[2]),
        pltpu.make_async_copy(slot, small_int.at[2], sem.at[3]),
        pltpu.make_async_copy(weight, small_float, sem.at[4]),
    ]
    large = [
        pltpu.make_async_copy(probes, probes_out, sem.at[5]),
        pltpu.make_async_copy(sources, sources_out, sem.at[6]),
        pltpu.make_async_copy(prior, prior_out, sem.at[7]),
    ]
    for copy in small + large:
        copy.start()
    apart = lax.broadcasted_iota(jnp.int32, (HALF, HALF), 0) - lax.broadcasted_iota(jnp.int32, (HALF, HALF), 1)
    full = jnp.where(apart == 0, CENTER, jnp.zeros((HALF, HALF), F32))
    for reach in range(1, REACH + 1):
        full = jnp.where(jnp.abs(apart) == reach, STENCIL[reach], full)
    high, low = split(full)
    band_ref[0:HALF, 0:HALF] = high
    band_ref[HALF:, 0:HALF] = high
    band_ref[0:HALF, HALF:] = low
    band_ref[HALF:, HALF:] = jnp.zeros_like(low)
    for copy in small:
        copy.wait()
    for i in range(3):
        statics[cells + i * rows : cells + (i + 1) * rows, :] = small_int[i].astype(F32)
    place = lax.broadcasted_iota(jnp.int32, (rows, HALF), 0) * HALF
    place = place + lax.broadcasted_iota(jnp.int32, (rows, HALF), 1)
    live = jnp.where(place < count[0], small_float[...], 0.0)
    statics[cells + 3 * rows : cells + 4 * rows, :] = live
    for copy in large:
        copy.wait()


def forward_own(fields, probes, sources, statics, band_ref, turned, first, second, third, z_term):
    clear_margins(first, LAYERS, fields)
    clear_margins(second, LAYERS, fields)

    slab, flat = PADDED * fields, 32 * fields
    ahead = 24 * fields

    def load(chunk, carry):
        there = window(turned, chunk * 8 * fields, LAYERS * flat - ahead)
        padded = window(first, chunk * 8 * fields, LAYERS * slab - ahead)
        here = window(probes, chunk * 8, LAYERS * flat - 24)
        push = window(sources, chunk * 8, 3 * LAYERS * 32 - 24)
        for x in range(LAYERS):
            for y in range(8):
                cell = x * 32 + y
                value = here[pl.ds(cell, fields, stride=HALF), :]
                there[cell * fields : (cell + 1) * fields, :] = value
                row = x * slab + (REACH + y) * fields
                padded[row : row + fields, :] = value * spread(push, cell, fields)
        return carry

    lax.fori_loop(0, 4, load, 0)

    def sweep(field, emit):
        along_z(field, 0, fields, band_ref, z_term)

        def body(chunk, carry):
            padded = window(field, chunk * 8 * fields, LAYERS * slab - ahead)
            z_part = window(z_term, chunk * 8 * fields, LAYERS * flat - ahead)
            speed = window(statics, chunk * 8, LAYERS * 32 - 24)
            put = emit(chunk)
            for part in range(0, fields, 8):

                def load(layer, y):
                    row = layer * slab + (REACH + y) * fields + part
                    return padded[row : row + 8, :]

                get = kept_rows(load)
                for y in range(8):
                    for x in range(LAYERS):
                        cell = x * 32 + y
                        row = cell * fields + part
                        total = laplacian(get, x, y, z_part[row : row + 8, :], 0, LAYERS - 1)
                        put(x, y, part, get(x, y), spread(speed, cell, 8) * total)
            return carry

        lax.fori_loop(0, 4, body, 0)

    def step_one(chunk):
        push = window(sources, chunk * 8, 3 * LAYERS * 32 - 24)
        there = window(turned, chunk * 8 * fields, LAYERS * flat - ahead)
        out = window(second, chunk * 8 * fields, LAYERS * slab - ahead)

        def put(x, y, part, now, change):
            cell = x * 32 + y
            row = cell * fields + part
            change = change + there[row : row + 8, :] * spread(push, 128 + cell, 8)
            row = x * slab + (REACH + y) * fields + part
            out[row : row + 8, :] = 2.0 * now + change

        return put

    sweep(first, step_one)

    def step_two(chunk):
        push = window(sources, chunk * 8, 3 * LAYERS * 32 - 24)
        there = window(turned, chunk * 8 * fields, LAYERS * flat - ahead)
        before = window(first, chunk * 8 * fields, LAYERS * slab - ahead)
        out = window(third, chunk * 8 * fields, LAYERS * flat - ahead)

        def put(x, y, part, now, change):
            cell = x * 32 + y
            row = x * slab + (REACH + y) * fields + part
            change = change - before[row : row + 8, :]
            row = cell * fields + part
            change = change + there[row : row + 8, :] * spread(push, 256 + cell, 8)
            out[row : row + 8, :] = 2.0 * now + change

        return put

    sweep(second, step_two)


def entry_row(value, row):
    return jnp.concatenate([value[row + i : row + i + 1, :] for i in range(4)], axis=1)


def forward_window(
    fields, peers, me, first, second, third, own, partner, passed, across, band_ref, own_scale,
    kept, sent, cell_ref, slot_ref, speed_ref, line_ref, owner_ref, weight_ref,
    below, above, z_term, total_ref, table, *samples,
):
    entries = line_ref.shape[1]
    cells = LAYERS * 32
    length = own.shape[0]
    odd = me[0] % 2 == 1
    clear_margins(below, LAYERS, fields)
    clear_margins(above, LAYERS, fields)
    total_ref[...] = jnp.zeros_like(total_ref)
    near, next_one, far_one, side_one = passed[0:length, :], passed[length:, :], across[0:length, :], partner[...]
    tiles = (
        jnp.where(odd, far_one, next_one),
        jnp.where(odd, side_one, near),
        own[...],
        jnp.where(odd, near, side_one),
        jnp.where(odd, next_one, far_one),
    )
    place = lax.broadcasted_iota(jnp.int32, (PLACES, entries), 0)
    slot_place = lax.broadcasted_iota(jnp.int32, (HALF, entries), 0)
    for tile, value in enumerate(tiles):
        speed_ref[tile * cells : (tile + 1) * cells, :] = value[0:cells, :]
        cell = entry_row(value, cells).astype(jnp.int32)
        owner = entry_row(value, cells + 4).astype(jnp.int32)
        slot = entry_row(value, cells + 8).astype(jnp.int32)
        weight = entry_row(value, cells + 12)
        hot = jnp.where(place == jnp.bitwise_and(cell, PLACES - 1), 1.0, 0.0)
        cell_ref[tile * PLACES : (tile + 1) * PLACES, :] = hot.astype(BF16)
        hot = jnp.where(slot_place == slot, 1.0, 0.0)
        slot_ref[tile * HALF : (tile + 1) * HALF, :] = hot.astype(BF16)
        rows = slice(tile * fields, (tile + 1) * fields)
        line_ref[rows, :] = jnp.broadcast_to(lax.shift_right_logical(cell, 9), (fields, entries))
        owner_ref[rows, :] = jnp.broadcast_to(owner, (fields, entries))
        weight_ref[rows, :] = jnp.broadcast_to(weight, (fields, entries))

    slab, flat = PADDED * fields, 32 * fields
    ahead = 24 * fields

    def outward(chunk, carry):
        speed = window(speed_ref, chunk * 8, 5 * cells - 24)
        here, low, high = (window(ref, chunk * 8 * fields, LAYERS * slab - ahead) for ref in (first, below, above))
        for y in range(8):
            rows = [slice(x * slab + (REACH + y) * fields, x * slab + (REACH + y + 1) * fields) for x in range(LAYERS)]
            mine = [here[row, :] for row in rows]
            for x in range(LAYERS):
                up = sum(STENCIL[4 + x - other] * mine[other] for other in range(x, LAYERS))
                down = sum(STENCIL[4 + other - x] * mine[other] for other in range(x + 1))
                high[rows[x], :] = spread(speed, 3 * cells + x * 32 + y, fields) * up
                low[rows[x], :] = spread(speed, cells + x * 32 + y, fields) * down
        return carry

    lax.fori_loop(0, 4, outward, 0)
    along_z(below, 0, fields, band_ref, z_term, 0)
    along_z(above, 0, fields, band_ref, z_term, cells * fields)

    def far(read, x, y, lowest, highest):
        total = None
        for other in range(lowest, highest + 1):
            if 1 <= abs(x - other) <= REACH:
                term = STENCIL[abs(x - other)] * read(other, y)
                total = term if total is None else total + term
        return total

    def respond(chunk, carry):
        speeds = window(speed_ref, chunk * 8, 5 * cells - 24)
        sides = [window(ref, chunk * 8 * fields, LAYERS * slab - ahead) for ref in (below, second, above)]
        base = window(third, chunk * 8 * fields, LAYERS * flat - ahead)
        z_parts = window(z_term, chunk * 8 * fields, 2 * LAYERS * flat - ahead)
        for tile in range(5):
            sample = samples[tile]
            for part in range(0, fields, 8):

                def load(layer, y):
                    row = layer % LAYERS * slab + (REACH + y) * fields + part
                    return sides[(layer + LAYERS) // LAYERS][row : row + 8, :]

                read = kept_rows(load)
                for y in range(8):
                    for x in range(LAYERS):
                        cell = x * 32 + y
                        row = cell * fields + part
                        layer = (tile - 2) * LAYERS + x
                        speed = spread(speeds, tile * cells + cell, 8)
                        if tile in (0, 4):
                            value = speed * far(read, layer, y, -4, 7)
                        elif tile == 2:
                            outside = far(read, layer, y, -4, -1) + far(read, layer, y, 4, 7)
                            value = base[row : row + 8, :] + speed * outside
                        else:
                            row = row + tile // 2 * cells * fields
                            z_part = z_parts[row : row + 8, :]
                            value = 2.0 * read(layer, y) + speed * laplacian(read, layer, y, z_part, -4, 7)
                        row = (x * 2 + y // 4) * fields + part
                        side = y % 4 * HALF
                        sample[row : row + 8, side : side + HALF] = value
            hot = cell_ref[tile * PLACES : (tile + 1) * PLACES, :]
            picked = jnp.dot(jnp.concatenate(split(sample[...]), axis=0), hot, preferred_element_type=F32)
            picked = picked[: 8 * fields, :] + picked[8 * fields :, :]
            for part in range(fields // 8):
                rows = slice(tile * fields + part * 8, tile * fields + part * 8 + 8)
                line = line_ref[rows, :]
                total = total_ref[rows, :]
                for i in range(8):
                    chosen = line == i // 2 * 8 + chunk * 2 + i % 2
                    row = i * fields + part * 8
                    total = total + jnp.where(chosen, picked[row : row + 8, :], 0.0)
                total_ref[rows, :] = total
        return carry

    lax.fori_loop(0, 4, respond, 0)

    for group in range(peers // 16):
        lefts, rights = [], []
        for tile in range(5):
            rows = slice(tile * fields, (tile + 1) * fields)
            high, low = split(total_ref[rows, :] * weight_ref[rows, :])
            high, low = high.astype(F32), low.astype(F32)
            owner = owner_ref[rows, :]
            for part in (high, low):
                pieces = [jnp.where(owner == group * 16 + i, part, 0.0).astype(BF16) for i in range(16)]
                lefts.append(jnp.concatenate(pieces, axis=0))
                rights.append(slot_ref[tile * HALF : (tile + 1) * HALF, :])
        result = lax.dot_general(
            jnp.concatenate(lefts, axis=1), jnp.concatenate(rights, axis=1), NT, preferred_element_type=F32
        )
        table[group * 16 * fields : (group + 1) * 16 * fields, :] = result
    count = peers // 2
    mine = me[0] % 2
    place = lax.broadcasted_iota(jnp.int32, (count, HALF), 0)
    scale = jnp.broadcast_to(own_scale[...], (count, HALF))
    for out, side in ((kept, mine), (sent, 1 - mine)):
        out[0 : count * fields, :] = table[at(side * count * fields, count * fields), :]
        out[count * fields :, :] = jnp.where(place == me[0] - side * count, scale, 0.0)


def basis_parts(first, basis, when, out):
    rank = basis.shape[0] // HALF

    def body(group, carry):
        here = window(basis, (first + group) * 8, basis.shape[0] - 15 * 8)
        there = window(out, group * rank, rank)
        for step in range(8):
            high, low = split(here[pl.ds(step, rank, stride=HALF), :])
            there[:, step * 256 : step * 256 + HALF] = high
            there[:, step * 256 + HALF : (step + 1) * 256] = low
        return carry

    lax.fori_loop(0, 8, body, 0)


def adjoint(
    fields, peers, me, half, other, cell_ref, slot_ref, speed_ref, line_ref, owner_ref, weight_ref, turned, sources,
    prior, band_ref, basis, basis_two, image, coeffs, high_ref, low_ref, inner_two, outer_two,
    inner_one, outer_one, z_term, image_parts, scaled, *lefts,
):
    entries = line_ref.shape[1]
    cells = LAYERS * 32
    rank = basis.shape[0] // 8
    clear_margins(inner_two, 5 * LAYERS, fields)
    clear_margins(inner_one, 3 * LAYERS, fields)
    count = peers // 2
    mine = me[0] % 2
    for ref, side in ((half, mine), (other, 1 - mine)):
        for i in range(count):
            scale = ref[count * fields + i : count * fields + i + 1, :]
            scaled[at((side * count + i) * fields, fields), :] = ref[i * fields : (i + 1) * fields, :] * scale
    for tile in range(5):
        rows = slice(tile * fields, (tile + 1) * fields)
        owner = owner_ref[rows, :]
        hot = slot_ref[tile * HALF : (tile + 1) * HALF, :]
        hot = jnp.concatenate([hot, hot], axis=0)
        total = jnp.zeros((fields, entries), F32)
        for group in range(peers // 16):
            parts = split(scaled[group * 16 * fields : (group + 1) * 16 * fields, :])
            found = jnp.dot(jnp.concatenate(parts, axis=1), hot, preferred_element_type=F32)
            for i in range(16):
                total = total + jnp.where(owner == group * 16 + i, found[i * fields : (i + 1) * fields, :], 0.0)
        high, low = split(total * weight_ref[rows, :])
        high_ref[rows, :] = high.astype(F32)
        low_ref[rows, :] = low.astype(F32)

    for tile in range(5):
        left = lefts[tile]
        for part in range(fields // 16):
            rows = slice(tile * fields + part * 16, tile * fields + part * 16 + 16)
            line, high, low = line_ref[rows, :], high_ref[rows, :], low_ref[rows, :]
            for i in range(32):
                chosen = line == i
                row = i * fields + part * 16
                left[row : row + 16, :entries] = jnp.where(chosen, high, 0.0).astype(BF16)
                left[row : row + 16, entries:] = jnp.where(chosen, low, 0.0).astype(BF16)
        hot = cell_ref[tile * PLACES : (tile + 1) * PLACES, :]
        value = lax.dot_general(left[...], jnp.concatenate([hot, hot], axis=1), NT, preferred_element_type=F32)
        for i in range(32):
            for step in range(4):
                layer, y = tile * LAYERS + i // 8, i % 8 * 4 + step
                now = value[i * fields : (i + 1) * fields, step * HALF : (step + 1) * HALF]
                if 1 <= tile <= 3:
                    outer_two[at(((layer - LAYERS) * 32 + y) * fields, fields), :] = now
                speed = spread(speed_ref, layer * 32 + y, fields)
                inner_two[at((layer * PADDED + REACH + y) * fields, fields), :] = speed * now

    def terms(index, carry):
        along_z(inner_two, (index + 1) * LAYERS, fields, band_ref, z_term, index * cells * fields)
        return carry

    lax.fori_loop(0, 3, terms, 0)

    slab, flat = PADDED * fields, 32 * fields
    ahead = 24 * fields

    def step_one(index, carry):
        tile, chunk = index // 4, index % 4
        start, skip = tile * LAYERS * slab + chunk * 8 * fields, tile * LAYERS * flat + chunk * 8 * fields
        here = window(inner_two, start, 3 * LAYERS * slab - ahead)
        two, one, z_part = (window(ref, skip, LAYERS * flat - ahead) for ref in (outer_two, outer_one, z_term))
        out = window(inner_one, start, LAYERS * slab - ahead)
        speed = window(speed_ref, (tile + 1) * cells + chunk * 8, cells - 24)
        for part in range(0, fields, 8):

            def load(layer, y):
                row = (layer + LAYERS) * slab + (REACH + y) * fields + part
                return here[row : row + 8, :]

            get = kept_rows(load)
            for y in range(8):
                for x in range(LAYERS):
                    cell = x * 32 + y
                    row = slice(cell * fields + part, cell * fields + part + 8)
                    now = 2.0 * two[row, :] + laplacian(get, x, y, z_part[row, :], -4, 7)
                    one[row, :] = now
                    row = x * slab + (REACH + y) * fields + part
                    out[row : row + 8, :] = spread(speed, cell, 8) * now
        return carry

    lax.fori_loop(0, 12, step_one, 0)
    along_z(inner_one, LAYERS, fields, band_ref, z_term)

    def step_two(chunk, total):
        skip = chunk * 8 * fields
        here = window(inner_one, skip, 3 * LAYERS * slab - ahead)
        two_rows, one_rows = (window(ref, LAYERS * flat + skip, LAYERS * flat - ahead) for ref in (outer_two, outer_one))
        z_part, there, out = (window(ref, skip, LAYERS * flat - ahead) for ref in (z_term, turned, image))
        push = window(sources, chunk * 8, 3 * cells - 24)
        damping = window(prior, chunk * 8, cells - 24)
        for part in range(0, fields, 8):

            def load(layer, y):
                row = (layer + LAYERS) * slab + (REACH + y) * fields + part
                return here[row : row + 8, :]

            get = kept_rows(load)
            for y in range(8):
                for x in range(LAYERS):
                    cell = x * 32 + y
                    row = slice(cell * fields + part, cell * fields + part + 8)
                    two, one = two_rows[row, :], one_rows[row, :]
                    zero = 2.0 * one - two + laplacian(get, x, y, z_part[row, :], -4, 7)
                    value = spread(push, cell, 8) * zero
                    value = value + spread(push, 128 + cell, 8) * one
                    value = value + spread(push, 256 + cell, 8) * two
                    out[row, :] = value + spread(damping, cell, 8) * there[row, :]
        for x in range(LAYERS):
            for y in range(8):
                cell = x * 32 + y
                high, low = split(out[cell * fields : (cell + 1) * fields, :])
                side = y * 256
                rows = slice(x * 2 * fields, x * 2 * fields + fields)
                image_parts[rows, side : side + HALF] = high
                image_parts[rows, side + HALF : side + 256] = high
                rows = slice(x * 2 * fields + fields, (x + 1) * 2 * fields)
                image_parts[rows, side : side + HALF] = low
                image_parts[rows, side + HALF : side + 256] = jnp.zeros_like(low)
        for x in range(LAYERS):
            columns = (basis, basis_two)[x // 2][at((x % 2 * 4 + chunk) * rank, rank), :]
            parts = image_parts[x * 2 * fields : (x + 1) * 2 * fields, :]
            total = total + lax.dot_general(parts, columns, NT, preferred_element_type=F32)
        return total

    total = lax.fori_loop(0, 4, step_two, jnp.zeros((2 * fields, rank), F32))
    coeffs[...] = total[:fields, :] + total[fields:, :]


def remainder(fields, image, basis, basis_two, *rest):
    *shares, out, coeffs, natural, sem = rest
    rank = coeffs.shape[1]
    while len(shares) > 1:
        shares = [shares[i][...] + shares[i + 1][...] for i in range(0, len(shares), 2)]
    total = shares[0][...]
    coeffs[...] = total
    parts = jnp.concatenate(split(total), axis=0)
    whole = natural.reshape(out.shape)

    def leave(x):
        return pltpu.make_async_copy(whole.at[:, x], out.at[:, x], sem.at[x])

    for x in range(LAYERS):
        for part in range(4):
            columns = (basis, basis_two)[x // 2][(x % 2 * 4 + part) * rank : (x % 2 * 4 + part + 1) * rank, :]
            both = jnp.dot(parts, columns, preferred_element_type=F32)
            for step in range(8):
                cell = x * 32 + part * 8 + step
                side = step * 256
                along = both[:fields, side : side + HALF] + both[:fields, side + HALF : side + 256]
                along = along + both[fields:, side : side + HALF]
                natural[pl.ds(cell, fields, stride=HALF), :] = image[cell * fields : (cell + 1) * fields, :] - along
        leave(x).start()
    for x in range(LAYERS):
        leave(x).wait()


def call(kernel, inputs, out_shape, scratch, flops, size, scalars=0, far=0, far_out=0, room=16):
    smem = pl.BlockSpec(memory_space=pltpu.SMEM)
    vmem = pl.BlockSpec(memory_space=pltpu.VMEM)
    hbm = pl.BlockSpec(memory_space=pltpu.HBM)
    inputs = [
        pltpu.with_memory_space_constraint(array, pltpu.HBM) if scalars <= i < scalars + far else array
        for i, array in enumerate(inputs)
    ]
    return pl.pallas_call(
        kernel,
        out_shape=out_shape,
        in_specs=[smem] * scalars + [hbm] * far + [vmem] * (len(inputs) - scalars - far),
        out_specs=[hbm] * far_out + [vmem] * (len(out_shape) - far_out),
        scratch_shapes=scratch,
        cost_estimate=pl.CostEstimate(flops=flops, bytes_accessed=size, transcendentals=0),
        compiler_params=pltpu.CompilerParams(vmem_limit_bytes=room * 2**20),
    )(*inputs)


def struct(*shape, dtype=F32):
    return jax.ShapeDtypeStruct(shape, dtype)


def swapped(array, axis, bits):
    count = lax.axis_size(axis)
    return lax.ppermute(array, axis, [(i, i ^ bits) for i in range(count)])


def local(
    probes,
    sources,
    kappa,
    prior,
    basis,
    entry_cell,
    entry_owner,
    entry_slot,
    entry_weight,
    entry_count,
    trace_weight,
):
    fields, rank = probes.shape[0], basis.shape[0]
    entries = entry_cell.shape[0]
    peers = lax.axis_size("space")
    padded = LAYERS * PADDED * fields
    cells = LAYERS * 32
    rows = entries // HALF
    me = lax.axis_index("space").astype(jnp.int32).reshape(1)

    own, probes_near, sources_near, prior_near, matrix = call(
        pack,
        (
            entry_count,
            me,
            probes.reshape(fields * cells, HALF),
            sources.reshape(3 * cells, HALF),
            prior.reshape(cells, HALF),
            kappa.reshape(cells, HALF),
            entry_cell.reshape(rows, HALF),
            entry_owner.reshape(rows, HALF),
            entry_slot.reshape(rows, HALF),
            entry_weight.reshape(rows, HALF),
        ),
        [
            struct(cells + 4 * rows, HALF),
            struct(fields * cells, HALF),
            struct(3 * cells, HALF),
            struct(cells, HALF),
            struct(256, 256, dtype=BF16),
        ],
        [pltpu.VMEM((3, rows, HALF), jnp.int32), pltpu.VMEM((rows, HALF), F32), pltpu.SemaphoreType.DMA((8,))],
        100_000,
        2 * 2**20,
        scalars=2,
        far=8,
    )
    partner = swapped(own, "space", 1)
    passed = lax.ppermute(
        jnp.concatenate([own, partner], axis=0),
        "space",
        [pair for i in range(1, peers - 1, 2) for pair in ((i, i + 1), (i + 1, i))],
    )

    turned, first, second, third = call(
        functools.partial(forward_own, fields),
        (probes_near, sources_near, own, matrix),
        [struct(cells * fields, HALF), struct(padded, HALF), struct(padded, HALF), struct(cells * fields, HALF)],
        [pltpu.VMEM((cells * fields, HALF), F32)],
        600_000_000,
        6 * 2**20,
    )
    half_rows = peers // 2 * (fields + 1)
    passed, second = lax.optimization_barrier((passed, second))
    across = swapped(passed, "space", 1)
    kept, sent, cell_hot, slot_hot, speed, line, owner, weight = call(
        functools.partial(forward_window, fields, peers),
        (me, first, second, third, own, partner, passed, across, matrix, trace_weight.reshape(1, HALF)),
        [
            struct(half_rows, HALF),
            struct(half_rows, HALF),
            struct(5 * PLACES, entries, dtype=BF16),
            struct(5 * HALF, entries, dtype=BF16),
            struct(5 * cells, HALF),
            struct(5 * fields, entries, dtype=jnp.int32),
            struct(5 * fields, entries, dtype=jnp.int32),
            struct(5 * fields, entries),
        ],
        [
            pltpu.VMEM((padded, HALF), F32),
            pltpu.VMEM((padded, HALF), F32),
            pltpu.VMEM((2 * cells * fields, HALF), F32),
            pltpu.VMEM((5 * fields, entries), F32),
            pltpu.VMEM((peers * fields, HALF), F32),
        ]
        + [pltpu.VMEM((8 * fields, PLACES), F32)] * 5,
        3_000_000_000,
        6 * 2**20,
        scalars=1,
        room=20,
    )
    half = kept + swapped(sent, "space", 1)
    columns = []
    bits = 2
    while bits < peers:
        arrived = swapped(half, "space", bits)
        if len(columns) < 2:
            (some,) = call(
                functools.partial(basis_parts, 8 * len(columns)),
                (basis.reshape(rank * cells, HALF), half),
                [struct(8 * rank, 2048, dtype=BF16)],
                [],
                10_000_000,
                4 * 2**20,
            )
            arrived, some = lax.optimization_barrier((arrived, some))
            columns.append(some)
        half = half + arrived
        bits *= 2
    other = swapped(half, "space", 1)
    image, coeffs = call(
        functools.partial(adjoint, fields, peers),
        (
            me, half, other, cell_hot, slot_hot, speed, line, owner, weight,
            turned, sources_near, prior_near, matrix, *columns,
        ),
        [struct(cells * fields, HALF), struct(fields, rank)],
        [
            pltpu.VMEM((5 * fields, entries), F32),
            pltpu.VMEM((5 * fields, entries), F32),
            pltpu.VMEM((5 * padded, HALF), F32),
            pltpu.VMEM((3 * cells * fields, HALF), F32),
            pltpu.VMEM((3 * padded, HALF), F32),
            pltpu.VMEM((3 * cells * fields, HALF), F32),
            pltpu.VMEM((3 * cells * fields, HALF), F32),
            pltpu.VMEM((8 * fields, 2048), BF16),
            pltpu.VMEM((peers * fields, HALF), F32),
        ]
        + [pltpu.VMEM((32 * fields, 2 * entries), BF16)] * 5,
        5_000_000_000,
        10 * 2**20,
        scalars=1,
        room=34,
    )
    bits = 1
    while bits * 4 < peers:
        coeffs = coeffs + swapped(coeffs, "space", bits)
        bits *= 2
    shares = [coeffs] + [swapped(coeffs, "space", bits * i) for i in range(1, peers // bits)]
    hess_probe, coeffs = call(
        functools.partial(remainder, fields),
        (image, *columns, *shares),
        [struct(*probes.shape), struct(fields, rank)],
        [pltpu.VMEM((fields * cells, HALF), F32), pltpu.SemaphoreType.DMA((LAYERS,))],
        200_000_000,
        6 * 2**20,
        far_out=1,
    )
    return hess_probe, coeffs.T


def solution(mesh):
    return jax.shard_map(
        local,
        mesh=mesh,
        in_specs=(
            P("group", "space", None, None),
            P(None, ("group", "space"), None, None),
            P(("group", "space"), None, None),
            P(("group", "space"), None, None),
            P("group", "space", None, None),
            P(("group", "space")),
            P(("group", "space")),
            P(("group", "space")),
            P(("group", "space")),
            P(("group", "space")),
            P(("group", "space")),
        ),
        out_specs=(P("group", "space", None, None), P("group", None)),
        check_vma=False,
    )
```

```python
import functools

import jax
import jax.numpy as jnp
from jax import lax
from jax.experimental import pallas as pl
from jax.experimental.pallas import tpu as pltpu
from jax.sharding import PartitionSpec as P

STENCIL = (-205.0 / 72.0, 8.0 / 5.0, -1.0 / 5.0, 8.0 / 315.0, -1.0 / 560.0)
CENTER = 3.0 * STENCIL[0]
REACH = 4
LAYERS = 4
PAIR = 8
TILES = 6
PADDED = 40
HALF = 128
PLACES = 512
F32 = jnp.float32
BF16 = jnp.bfloat16
NT = (((1,), (1,)), ((), ()))


def split(value):
    high = value.astype(BF16)
    low = (value - high.astype(F32)).astype(BF16)
    return high, low


def at(row, count=16):
    return pl.ds(pl.multiple_of(row, 8), count)


def window(ref, start, size):
    return ref.at[pl.ds(pl.multiple_of(start, 8), size)]


def kept_rows(load):
    rows = {}

    def get(layer, y):
        if (layer, y) not in rows:
            rows[layer, y] = load(layer, y)
        return rows[layer, y]

    return get


def spread(ref, row, fields):
    return jnp.broadcast_to(ref[pl.ds(row, 1), :], (fields, HALF))


def clear_margins(ref, layers, fields):
    margin = jnp.zeros((REACH * fields, HALF), F32)
    for layer in range(layers):
        start = layer * PADDED * fields
        ref[start : start + REACH * fields, :] = margin
        start += (PADDED - REACH) * fields
        ref[start : start + REACH * fields, :] = margin


def along_z(ref, first, layers, fields, band_ref, out_ref, row=0):
    pieces = [ref[at(((first + x) * PADDED + REACH) * fields, 32 * fields), :] for x in range(layers)]
    high, low = split(jnp.concatenate(pieces, axis=0))
    both = jnp.dot(jnp.concatenate([high, low], axis=1), band_ref[...], preferred_element_type=F32)
    out_ref[at(row, layers * 32 * fields), :] = both[:, :HALF] + both[:, HALF:]


def laplacian(get, x, y, z_term, lowest, highest):
    total = z_term
    for k in range(1, REACH + 1):
        ring = get(x, y + k) + get(x, y - k)
        if x + k <= highest:
            ring = ring + get(x + k, y)
        if x - k >= lowest:
            ring = ring + get(x - k, y)
        total = total + STENCIL[k] * ring
    return total


def pack(
    count, me, probes, sources, prior, kappa, cell, owner, slot, weight, scale,
    statics, probes_out, sources_out, prior_out, lent, band_ref, small_int, small_float, sem,
):
    rows = cell.shape[0]
    cells = kappa.shape[0]
    half = probes_out.shape[0]
    mine = me[0] % 2
    other = probes.at[pl.ds(pl.multiple_of((1 - mine) * half, 8), half)]
    small = [
        pltpu.make_async_copy(kappa, statics.at[pl.ds(0, cells)], sem.at[0]),
        pltpu.make_async_copy(cell, small_int.at[0], sem.at[1]),
        pltpu.make_async_copy(owner, small_int.at[1], sem.at[2]),
        pltpu.make_async_copy(slot, small_int.at[2], sem.at[3]),
        pltpu.make_async_copy(weight, small_float.at[pl.ds(0, rows)], sem.at[4]),
        pltpu.make_async_copy(scale, small_float.at[pl.ds(8, 1)], sem.at[5]),
    ]
    large = [
        pltpu.make_async_copy(other, lent.at[pl.ds(0, half)], sem.at[6]),
        pltpu.make_async_copy(sources, lent.at[pl.ds(half, 3 * cells)], sem.at[7]),
        pltpu.make_async_copy(prior, lent.at[pl.ds(half + 3 * cells, cells)], sem.at[8]),
        pltpu.make_async_copy(probes.at[pl.ds(pl.multiple_of(mine * half, 8), half)], probes_out, sem.at[9]),
        pltpu.make_async_copy(sources, sources_out, sem.at[10]),
        pltpu.make_async_copy(prior, prior_out, sem.at[11]),
    ]
    for copy in small + large:
        copy.start()
    apart = lax.broadcasted_iota(jnp.int32, (HALF, HALF), 0) - lax.broadcasted_iota(jnp.int32, (HALF, HALF), 1)
    full = jnp.where(apart == 0, CENTER, jnp.zeros((HALF, HALF), F32))
    for reach in range(1, REACH + 1):
        full = jnp.where(jnp.abs(apart) == reach, STENCIL[reach], full)
    high, low = split(full)
    band_ref[0:HALF, 0:HALF] = high
    band_ref[HALF:, 0:HALF] = high
    band_ref[0:HALF, HALF:] = low
    band_ref[HALF:, HALF:] = jnp.zeros_like(low)
    for copy in small:
        copy.wait()
    for i in range(3):
        statics[cells + i * rows : cells + (i + 1) * rows, :] = small_int[i].astype(F32)
    place = lax.broadcasted_iota(jnp.int32, (rows, HALF), 0) * HALF
    place = place + lax.broadcasted_iota(jnp.int32, (rows, HALF), 1)
    live = jnp.where(place < count[0], small_float[0:rows, :], 0.0)
    statics[cells + 3 * rows : cells + 4 * rows, :] = live
    statics[cells + 4 * rows : cells + 4 * rows + 8, :] = jnp.broadcast_to(small_float[8:9, :], (8, HALF))
    for copy in large:
        copy.wait()


def forward_own(
    fields, me, probes, sources, prior, own, partner, borrowed, band_ref,
    turned, first, second, third, push_ref, prior_ref, z_term, speed_ref,
):
    slab, flat, cells = PADDED * fields, 32 * fields, LAYERS * 32
    ahead = 24 * fields
    half = probes.shape[0]
    mine = me[0] % 2
    clear_margins(first, PAIR, fields)
    clear_margins(second, PAIR, fields)
    lent = borrowed.at[pl.ds(half, 4 * cells)]
    for side, pushes, damping, statics in ((mine, sources, prior, own), (1 - mine, lent, None, partner)):
        for i in range(3):
            push_ref[at(i * 2 * cells + side * cells, cells), :] = pushes[i * cells : (i + 1) * cells, :]
        place = at(side * cells, cells)
        prior_ref[place, :] = lent[3 * cells :, :] if damping is None else damping[...]
        speed_ref[place, :] = statics[0:cells, :]

    def load(chunk, carry):
        for side, ref in ((mine, probes), (1 - mine, borrowed)):
            there = window(turned, side * LAYERS * flat + chunk * 8 * fields, LAYERS * flat - ahead)
            padded = window(first, side * LAYERS * slab + chunk * 8 * fields, LAYERS * slab - ahead)
            here = window(ref, chunk * 8, half - 24)
            push = window(push_ref, side * cells + chunk * 8, cells - 24)
            for x in range(LAYERS):
                for y in range(8):
                    cell = x * 32 + y
                    value = here[pl.ds(cell, fields, stride=HALF), :]
                    there[cell * fields : (cell + 1) * fields, :] = value
                    row = x * slab + (REACH + y) * fields
                    padded[row : row + fields, :] = value * spread(push, cell, fields)
        return carry

    lax.fori_loop(0, 4, load, 0)

    def sweep(field, emit):
        along_z(field, 0, PAIR, fields, band_ref, z_term)

        def body(chunk, carry):
            padded = window(field, chunk * 8 * fields, PAIR * slab - ahead)
            z_part = window(z_term, chunk * 8 * fields, PAIR * flat - ahead)
            speed = window(speed_ref, chunk * 8, 2 * cells - 24)
            push = window(push_ref, chunk * 8, 6 * cells - 24)
            there = window(turned, chunk * 8 * fields, PAIR * flat - ahead)
            put = emit(chunk)

            def load(layer, y):
                row = layer * slab + (REACH + y) * fields
                return padded[row : row + fields, :]

            for side in range(2):
                get = kept_rows(load)
                for y in range(8):
                    for x in range(side * LAYERS, (side + 1) * LAYERS):
                        cell = x * 32 + y
                        row = slice(cell * fields, (cell + 1) * fields)
                        change = spread(speed, cell, fields) * laplacian(get, x, y, z_part[row, :], 0, PAIR - 1)
                        put(x, y, get(x, y), change, there[row, :], push)
            return carry

        lax.fori_loop(0, 4, body, 0)

    def step_one(chunk):
        out = window(second, chunk * 8 * fields, PAIR * slab - ahead)

        def put(x, y, now, change, probe, push):
            change = change + probe * spread(push, 2 * cells + x * 32 + y, fields)
            row = x * slab + (REACH + y) * fields
            out[row : row + fields, :] = 2.0 * now + change

        return put

    sweep(first, step_one)

    def step_two(chunk):
        before = window(first, chunk * 8 * fields, PAIR * slab - ahead)
        out = window(third, chunk * 8 * fields, PAIR * flat - ahead)

        def put(x, y, now, change, probe, push):
            row = x * slab + (REACH + y) * fields
            change = change - before[row : row + fields, :]
            cell = x * 32 + y
            change = change + probe * spread(push, 4 * cells + cell, fields)
            out[cell * fields : (cell + 1) * fields, :] = 2.0 * now + change

        return put

    sweep(second, step_two)


def entry_row(value, row):
    return jnp.concatenate([value[row + i : row + i + 1, :] for i in range(4)], axis=1)


def forward_window(
    fields, peers, me, first, second, third, own, partner, passed, across, band_ref,
    table, cell_ref, slot_ref, speed_ref, line_ref, owner_ref, weight_ref,
    below, above, z_term, total_ref, *samples,
):
    entries = line_ref.shape[1]
    cells = LAYERS * 32
    length = own.shape[0]
    odd = me[0] % 2 == 1
    slab, flat = PADDED * fields, 32 * fields
    clear_margins(below, LAYERS, fields)
    clear_margins(above, LAYERS, fields)
    total_ref[...] = jnp.zeros_like(total_ref)
    mine, theirs = own[...], partner[...]
    low = jnp.where(odd, across[...], passed[...])
    high = jnp.where(odd, passed[...], across[...])
    tiles = (
        low[length:, :],
        low[0:length, :],
        jnp.where(odd, theirs, mine),
        jnp.where(odd, mine, theirs),
        high[0:length, :],
        high[length:, :],
    )
    place = lax.broadcasted_iota(jnp.int32, (PLACES, entries), 0)
    slot_place = lax.broadcasted_iota(jnp.int32, (HALF, entries), 0)
    for tile, value in enumerate(tiles):
        speed_ref[tile * cells : (tile + 1) * cells, :] = value[0:cells, :]
        cell = entry_row(value, cells).astype(jnp.int32)
        owner = entry_row(value, cells + 4).astype(jnp.int32)
        slot = entry_row(value, cells + 8).astype(jnp.int32)
        weight = entry_row(value, cells + 12)
        hot = jnp.where(place == jnp.bitwise_and(cell, PLACES - 1), 1.0, 0.0)
        cell_ref[tile * PLACES : (tile + 1) * PLACES, :] = hot.astype(BF16)
        hot = jnp.where(slot_place == slot, 1.0, 0.0)
        slot_ref[tile * HALF : (tile + 1) * HALF, :] = hot.astype(BF16)
        rows = slice(tile * fields, (tile + 1) * fields)
        line_ref[rows, :] = jnp.broadcast_to(lax.shift_right_logical(cell, 9), (fields, entries))
        owner_ref[rows, :] = jnp.broadcast_to(owner, (fields, entries))
        weight_ref[rows, :] = jnp.broadcast_to(weight, (fields, entries))

    def outward(chunk, carry):
        ahead = 24 * fields
        speed = window(speed_ref, chunk * 8, TILES * cells - 24)
        here = window(first, chunk * 8 * fields, PAIR * slab - ahead)
        down_out, up_out = (window(ref, chunk * 8 * fields, LAYERS * slab - ahead) for ref in (below, above))
        for y in range(8):
            rows = [slice(x * slab + (REACH + y) * fields, x * slab + (REACH + y + 1) * fields) for x in range(PAIR)]
            field = [here[row, :] for row in rows]
            for x in range(LAYERS):
                up = sum(STENCIL[4 + x - other] * field[4 + other] for other in range(x, LAYERS))
                down = sum(STENCIL[4 + other - x] * field[other] for other in range(x + 1))
                up_out[rows[x], :] = spread(speed, 4 * cells + x * 32 + y, fields) * up
                down_out[rows[x], :] = spread(speed, cells + x * 32 + y, fields) * down
        return carry

    lax.fori_loop(0, 4, outward, 0)
    along_z(below, 0, LAYERS, fields, band_ref, z_term, 0)
    along_z(above, 0, LAYERS, fields, band_ref, z_term, cells * fields)

    def far(read, x, y, lowest, highest):
        total = None
        for other in range(lowest, highest + 1):
            if 1 <= abs(x - other) <= REACH:
                term = STENCIL[abs(x - other)] * read(other, y)
                total = term if total is None else total + term
        return total

    def respond(chunk, carry):
        ahead = 16 * fields
        speeds = window(speed_ref, chunk * 16, TILES * cells - 16)
        low_side, high_side = (window(ref, chunk * 16 * fields, LAYERS * slab - ahead) for ref in (below, above))
        inside = window(second, chunk * 16 * fields, PAIR * slab - ahead)
        base = window(third, chunk * 16 * fields, PAIR * flat - ahead)
        z_parts = window(z_term, chunk * 16 * fields, PAIR * flat - ahead)

        def load(layer, y):
            if layer < 0:
                ref, layer = low_side, layer + LAYERS
            elif layer >= PAIR:
                ref, layer = high_side, layer - PAIR
            else:
                ref = inside
            row = layer * slab + (REACH + y) * fields
            return ref[row : row + fields, :]

        for tile in range(TILES):
            sample = samples[tile]
            read = kept_rows(load)
            for y in range(16):
                for x in range(LAYERS):
                    cell = x * 32 + y
                    layer = (tile - 2) * LAYERS + x
                    speed = spread(speeds, tile * cells + cell, fields)
                    if tile in (0, 5):
                        value = speed * far(read, layer, y, -4, 11)
                    elif tile in (2, 3):
                        outside = far(read, layer, y, -4, -1) if tile == 2 else far(read, layer, y, 8, 11)
                        row = ((tile - 2) * cells + cell) * fields
                        value = base[row : row + fields, :] + speed * outside
                    else:
                        row = (tile // 4 * cells + cell) * fields
                        lap = laplacian(read, layer, y, z_parts[row : row + fields, :], -4, 11)
                        value = 2.0 * read(layer, y) + speed * lap
                    row = (x * 4 + y // 4) * fields
                    side = y % 4 * HALF
                    sample[row : row + fields, side : side + HALF] = value
            hot = cell_ref[tile * PLACES : (tile + 1) * PLACES, :]
            picked = jnp.dot(jnp.concatenate(split(sample[...]), axis=0), hot, preferred_element_type=F32)
            picked = picked[: 16 * fields, :] + picked[16 * fields :, :]
            rows = slice(tile * fields, (tile + 1) * fields)
            line = line_ref[rows, :]
            total = total_ref[rows, :]
            for i in range(16):
                chosen = line == i // 4 * 8 + chunk * 4 + i % 4
                total = total + jnp.where(chosen, picked[i * fields : (i + 1) * fields, :], 0.0)
            total_ref[rows, :] = total
        return carry

    lax.fori_loop(0, 2, respond, 0)

    for group in range(peers // 16):
        lefts, rights = [], []
        for tile in range(TILES):
            rows = slice(tile * fields, (tile + 1) * fields)
            value = total_ref[rows, :] * weight_ref[rows, :]
            high = value.astype(BF16).astype(F32)
            owner = owner_ref[rows, :]
            for part in (high, value - high):
                pieces = [jnp.where(owner == group * 16 + i, part, 0.0) for i in range(16)]
                lefts.append(jnp.concatenate(pieces, axis=0).astype(BF16))
                rights.append(slot_ref[tile * HALF : (tile + 1) * HALF, :])
        result = lax.dot_general(
            jnp.concatenate(lefts, axis=1), jnp.concatenate(rights, axis=1), NT, preferred_element_type=F32
        )
        table[group * 16 * fields : (group + 1) * 16 * fields, :] = result
    place = lax.broadcasted_iota(jnp.int32, (peers, HALF), 0)
    scales = jnp.zeros((peers, HALF), F32)
    for position, value in ((me[0], mine), (me[0] + 1 - 2 * (me[0] % 2), theirs)):
        scale = jnp.broadcast_to(value[cells + 16 : cells + 17, :], (peers, HALF))
        scales = jnp.where(place == position, scale, scales)
    table[peers * fields :, :] = scales


def basis_parts(first, basis, when, out):
    rank = basis.shape[0] // HALF

    def body(group, carry):
        here = window(basis, (first + group) * 8, basis.shape[0] - 15 * 8)
        there = window(out, group * rank, rank)
        for step in range(8):
            high, low = split(here[pl.ds(step, rank, stride=HALF), :])
            there[:, step * 256 : step * 256 + HALF] = high
            there[:, step * 256 + HALF : (step + 1) * 256] = low
        return carry

    lax.fori_loop(0, 8, body, 0)


def adjoint(
    fields, peers, me, table, cell_ref, slot_ref, speed_ref, line_ref, owner_ref, weight_ref, turned, push_ref,
    prior_ref, band_ref, own_basis, own_basis_two, other_basis, other_basis_two, kept, lent, coeffs,
    high_ref, low_ref, inner_two, outer_two, inner_one, outer_one, z_term, image, image_parts, scaled, *lefts,
):
    entries = line_ref.shape[1]
    cells = LAYERS * 32
    rank = own_basis.shape[0] // 8
    slab, flat = PADDED * fields, 32 * fields
    ahead = 24 * fields
    clear_margins(inner_two, TILES * LAYERS, fields)
    clear_margins(inner_one, 2 * PAIR, fields)
    for owner in range(peers):
        rows = slice(owner * fields, (owner + 1) * fields)
        scaled[rows, :] = table[rows, :] * table[peers * fields + owner : peers * fields + owner + 1, :]
    for tile in range(TILES):
        rows = slice(tile * fields, (tile + 1) * fields)
        owner = owner_ref[rows, :]
        hot = slot_ref[tile * HALF : (tile + 1) * HALF, :]
        hot = jnp.concatenate([hot, hot], axis=0)
        total = jnp.zeros((fields, entries), F32)
        for group in range(peers // 16):
            parts = split(scaled[group * 16 * fields : (group + 1) * 16 * fields, :])
            found = jnp.dot(jnp.concatenate(parts, axis=1), hot, preferred_element_type=F32)
            for i in range(16):
                total = total + jnp.where(owner == group * 16 + i, found[i * fields : (i + 1) * fields, :], 0.0)
        value = total * weight_ref[rows, :]
        high = value.astype(BF16).astype(F32)
        high_ref[rows, :] = high
        low_ref[rows, :] = value - high

    for tile in range(TILES):
        left = lefts[tile]
        rows = slice(tile * fields, (tile + 1) * fields)
        line, high, low = line_ref[rows, :], high_ref[rows, :], low_ref[rows, :]
        for i in range(0, 32, 2):
            chosen = [line == i, line == i + 1]
            row = slice(i * fields, (i + 2) * fields)
            for part, side in ((high, slice(0, entries)), (low, slice(entries, 2 * entries))):
                both = [jnp.where(which, part, 0.0) for which in chosen]
                left[row, side] = jnp.concatenate(both, axis=0).astype(BF16)
        hot = cell_ref[tile * PLACES : (tile + 1) * PLACES, :]
        value = lax.dot_general(left[...], jnp.concatenate([hot, hot], axis=1), NT, preferred_element_type=F32)
        for i in range(32):
            for step in range(4):
                layer, y = tile * LAYERS + i // 8, i % 8 * 4 + step
                now = value[i * fields : (i + 1) * fields, step * HALF : (step + 1) * HALF]
                if 1 <= tile <= 4:
                    row = ((layer - LAYERS) * 32 + y) * fields
                    outer_two[row : row + fields, :] = now
                speed = spread(speed_ref, layer * 32 + y, fields)
                row = layer * slab + (REACH + y) * fields
                inner_two[row : row + fields, :] = speed * now
        if 1 <= tile <= 4:
            along_z(inner_two, tile * LAYERS, LAYERS, fields, band_ref, z_term, (tile - 1) * cells * fields)

    def step_one(index, carry):
        pair, chunk = index // 4, index % 4
        start, skip = pair * PAIR * slab + chunk * 8 * fields, pair * PAIR * flat + chunk * 8 * fields
        here = window(inner_two, start, 2 * PAIR * slab - ahead)
        two, one, z_part = (window(ref, skip, PAIR * flat - ahead) for ref in (outer_two, outer_one, z_term))
        out = window(inner_one, start, PAIR * slab - ahead)
        speed = window(speed_ref, cells + pair * 2 * cells + chunk * 8, 2 * cells - 24)

        def load(layer, y):
            row = (layer + LAYERS) * slab + (REACH + y) * fields
            return here[row : row + fields, :]

        for side in range(2):
            get = kept_rows(load)
            for y in range(8):
                for x in range(side * LAYERS, (side + 1) * LAYERS):
                    cell = x * 32 + y
                    row = slice(cell * fields, (cell + 1) * fields)
                    now = 2.0 * two[row, :] + laplacian(get, x, y, z_part[row, :], -4, 11)
                    one[row, :] = now
                    row = x * slab + (REACH + y) * fields
                    out[row : row + fields, :] = spread(speed, cell, fields) * now
        return carry

    lax.fori_loop(0, 8, step_one, 0)
    along_z(inner_one, LAYERS, PAIR, fields, band_ref, z_term)
    mine = me[0] % 2

    def step_two(chunk, total):
        skip = chunk * 8 * fields
        here = window(inner_one, skip, 2 * PAIR * slab - ahead)
        two_rows, one_rows = (window(ref, LAYERS * flat + skip, PAIR * flat - ahead) for ref in (outer_two, outer_one))
        z_part, there, out = (window(ref, skip, PAIR * flat - ahead) for ref in (z_term, turned, image))
        push = window(push_ref, chunk * 8, 6 * cells - 24)
        damping = window(prior_ref, chunk * 8, 2 * cells - 24)

        def load(layer, y):
            row = (layer + LAYERS) * slab + (REACH + y) * fields
            return here[row : row + fields, :]

        nothing = jnp.zeros((fields, HALF), F32)
        for side in range(2):
            get = kept_rows(load)
            for y in range(8):
                for x in range(side * LAYERS, (side + 1) * LAYERS):
                    cell = x * 32 + y
                    row = slice(cell * fields, (cell + 1) * fields)
                    two, one = two_rows[row, :], one_rows[row, :]
                    zero = 2.0 * one - two + laplacian(get, x, y, z_part[row, :], -4, 11)
                    value = spread(push, cell, fields) * zero
                    value = value + spread(push, 2 * cells + cell, fields) * one
                    value = value + spread(push, 4 * cells + cell, fields) * two
                    value = value + spread(damping, cell, fields) * there[row, :]
                    out[row, :] = value
                    high = value.astype(BF16).astype(F32)
                    rows, lane = slice(x * 2 * fields, (x + 1) * 2 * fields), y * 256
                    image_parts[rows, lane : lane + HALF] = jnp.concatenate([high, value - high], axis=0).astype(BF16)
                    image_parts[rows, lane + HALF : lane + 256] = jnp.concatenate([high, nothing], axis=0).astype(BF16)
        for side, pieces in ((mine, (own_basis, own_basis_two)), (1 - mine, (other_basis, other_basis_two))):
            for x in range(LAYERS):
                columns = pieces[x // 2][at((x % 2 * 4 + chunk) * rank, rank), :]
                parts = image_parts[at((side * LAYERS + x) * 2 * fields, 2 * fields), :]
                total = total + lax.dot_general(parts, columns, NT, preferred_element_type=F32)
        return total

    total = lax.fori_loop(0, 4, step_two, jnp.zeros((2 * fields, rank), F32))
    coeffs[...] = total[:fields, :] + total[fields:, :]
    kept[...] = image[at(mine * LAYERS * flat, LAYERS * flat), :]
    lent[...] = image[at((1 - mine) * LAYERS * flat, LAYERS * flat), :]


def remainder(fields, me, image, borrowed, basis, basis_two, *rest):
    *shares, out, coeffs, natural, sem = rest
    rank = coeffs.shape[1]
    half = fields // 2
    mine = me[0] % 2
    while len(shares) > 1:
        shares = [shares[i][...] + shares[i + 1][...] for i in range(0, len(shares), 2)]
    total = shares[0][...]
    coeffs[at(mine * half, half), :] = total[:half, :]
    coeffs[at((1 - mine) * half, half), :] = total[half:, :]
    parts = jnp.concatenate(split(total), axis=0)
    whole = natural.reshape(out.shape)
    first, second = (window(natural, side * half * HALF, half * HALF) for side in (mine, 1 - mine))

    def leave(x):
        return pltpu.make_async_copy(whole.at[:, x], out.at[:, x], sem.at[x])

    for x in range(LAYERS):
        for part in range(4):
            columns = (basis, basis_two)[x // 2][(x % 2 * 4 + part) * rank : (x % 2 * 4 + part + 1) * rank, :]
            both = jnp.dot(parts, columns, preferred_element_type=F32)
            for step in range(8):
                cell = x * 32 + part * 8 + step
                side = step * 256
                along = both[:fields, side : side + HALF] + both[:fields, side + HALF : side + 256]
                along = along + both[fields:, side : side + HALF]
                row = slice(cell * half, (cell + 1) * half)
                first[pl.ds(cell, half, stride=HALF), :] = image[row, :] - along[:half, :]
                second[pl.ds(cell, half, stride=HALF), :] = borrowed[row, :] - along[half:, :]
        leave(x).start()
    for x in range(LAYERS):
        leave(x).wait()


def call(kernel, inputs, out_shape, scratch, flops, size, scalars=0, far=0, far_out=0, room=16):
    smem = pl.BlockSpec(memory_space=pltpu.SMEM)
    vmem = pl.BlockSpec(memory_space=pltpu.VMEM)
    hbm = pl.BlockSpec(memory_space=pltpu.HBM)
    inputs = [
        pltpu.with_memory_space_constraint(array, pltpu.HBM) if scalars <= i < scalars + far else array
        for i, array in enumerate(inputs)
    ]
    return pl.pallas_call(
        kernel,
        out_shape=out_shape,
        in_specs=[smem] * scalars + [hbm] * far + [vmem] * (len(inputs) - scalars - far),
        out_specs=[hbm] * far_out + [vmem] * (len(out_shape) - far_out),
        scratch_shapes=scratch,
        cost_estimate=pl.CostEstimate(flops=flops, bytes_accessed=size, transcendentals=0),
        compiler_params=pltpu.CompilerParams(vmem_limit_bytes=room * 2**20),
    )(*inputs)


def struct(*shape, dtype=F32):
    return jax.ShapeDtypeStruct(shape, dtype)


def swapped(array, axis, bits):
    count = lax.axis_size(axis)
    return lax.ppermute(array, axis, [(i, i ^ bits) for i in range(count)])


def local(
    probes,
    sources,
    kappa,
    prior,
    basis,
    entry_cell,
    entry_owner,
    entry_slot,
    entry_weight,
    entry_count,
    trace_weight,
):
    rank = basis.shape[0]
    fields = probes.shape[0] // 2
    entries = entry_cell.shape[0]
    peers = lax.axis_size("space")
    slab, flat = PADDED * fields, 32 * fields
    cells = LAYERS * 32
    rows = entries // HALF
    basis = basis.reshape(rank * cells, HALF)
    me = lax.axis_index("space").astype(jnp.int32).reshape(1)

    own, probes_near, sources_near, prior_near, lent, matrix = call(
        pack,
        (
            entry_count,
            me,
            probes.reshape(2 * fields * cells, HALF),
            sources.reshape(3 * cells, HALF),
            prior.reshape(cells, HALF),
            kappa.reshape(cells, HALF),
            entry_cell.reshape(rows, HALF),
            entry_owner.reshape(rows, HALF),
            entry_slot.reshape(rows, HALF),
            entry_weight.reshape(rows, HALF),
            trace_weight.reshape(1, HALF),
        ),
        [
            struct(cells + 4 * rows + 8, HALF),
            struct(fields * cells, HALF),
            struct(3 * cells, HALF),
            struct(cells, HALF),
            struct((fields + 4) * cells, HALF),
            struct(256, 256, dtype=BF16),
        ],
        [pltpu.VMEM((3, rows, HALF), jnp.int32), pltpu.VMEM((16, HALF), F32), pltpu.SemaphoreType.DMA((12,))],
        100_000,
        2 * 2**20,
        scalars=2,
        far=9,
    )
    partner = swapped(own, "space", 1)
    lent, partner = lax.optimization_barrier((lent, partner))
    borrowed = swapped(lent, "space", 1)
    passed = lax.ppermute(
        jnp.concatenate([own, partner], axis=0),
        "space",
        [pair for i in range(1, peers - 1, 2) for pair in ((i, i + 1), (i + 1, i))],
    )

    turned, first, second, third, push, damping = call(
        functools.partial(forward_own, fields),
        (me, probes_near, sources_near, prior_near, own, partner, borrowed, matrix),
        [
            struct(PAIR * flat, HALF),
            struct(PAIR * slab, HALF),
            struct(PAIR * slab, HALF),
            struct(PAIR * flat, HALF),
            struct(6 * cells, HALF),
            struct(2 * cells, HALF),
        ],
        [pltpu.VMEM((PAIR * flat, HALF), F32), pltpu.VMEM((2 * cells, HALF), F32)],
        600_000_000,
        6 * 2**20,
        scalars=1,
    )
    passed, second = lax.optimization_barrier((passed, second))
    across = swapped(passed, "space", 1)
    across, basis_there = lax.optimization_barrier((across, basis))
    basis_there = swapped(basis_there, "space", 1)
    table, cell_hot, slot_hot, speed, line, owner, weight = call(
        functools.partial(forward_window, fields, peers),
        (me, first, second, third, own, partner, passed, across, matrix),
        [
            struct(peers * (fields + 1), HALF),
            struct(TILES * PLACES, entries, dtype=BF16),
            struct(TILES * HALF, entries, dtype=BF16),
            struct(TILES * cells, HALF),
            struct(TILES * fields, entries, dtype=jnp.int32),
            struct(TILES * fields, entries, dtype=jnp.int32),
            struct(TILES * fields, entries),
        ],
        [
            pltpu.VMEM((LAYERS * slab, HALF), F32),
            pltpu.VMEM((LAYERS * slab, HALF), F32),
            pltpu.VMEM((PAIR * flat, HALF), F32),
            pltpu.VMEM((TILES * fields, entries), F32),
        ]
        + [pltpu.VMEM((16 * fields, PLACES), F32)] * TILES,
        3_000_000_000,
        6 * 2**20,
        scalars=1,
        room=20,
    )
    columns = []
    bits = 2
    while bits < peers:
        arrived = swapped(table, "space", bits)
        for i in ((0,), (1,), (2, 3))[len(columns)] if len(columns) < 3 else ():
            (some,) = call(
                functools.partial(basis_parts, 8 * (i % 2)),
                ((basis, basis_there)[i // 2], table),
                [struct(8 * rank, 2048, dtype=BF16)],
                [],
                10_000_000,
                4 * 2**20,
            )
            columns.append(some)
        arrived, columns = lax.optimization_barrier((arrived, columns))
        table = table + arrived
        bits *= 2
    kept, lent, coeffs = call(
        functools.partial(adjoint, fields, peers),
        (me, table, cell_hot, slot_hot, speed, line, owner, weight, turned, push, damping, matrix, *columns),
        [struct(LAYERS * flat, HALF), struct(LAYERS * flat, HALF), struct(fields, rank)],
        [
            pltpu.VMEM((TILES * fields, entries), F32),
            pltpu.VMEM((TILES * fields, entries), F32),
            pltpu.VMEM((TILES * LAYERS * slab, HALF), F32),
            pltpu.VMEM((2 * PAIR * flat, HALF), F32),
            pltpu.VMEM((2 * PAIR * slab, HALF), F32),
            pltpu.VMEM((2 * PAIR * flat, HALF), F32),
            pltpu.VMEM((2 * PAIR * flat, HALF), F32),
            pltpu.VMEM((PAIR * flat, HALF), F32),
            pltpu.VMEM((2 * PAIR * fields, 2048), BF16),
            pltpu.VMEM((peers * fields, HALF), F32),
        ]
        + [pltpu.VMEM((32 * fields, 2 * entries), BF16)] * TILES,
        5_000_000_000,
        10 * 2**20,
        scalars=1,
        room=30,
    )
    coeffs = jnp.concatenate([coeffs, swapped(coeffs, "space", 1)], axis=0)
    lent, coeffs = lax.optimization_barrier((lent, coeffs))
    borrowed = swapped(lent, "space", 1)
    bits = 2
    while bits * 4 < peers:
        coeffs = coeffs + swapped(coeffs, "space", bits)
        bits *= 2
    shares = [coeffs] + [swapped(coeffs, "space", bits * i) for i in range(1, peers // bits)]
    hess_probe, coeffs = call(
        functools.partial(remainder, 2 * fields),
        (me, kept, borrowed, *columns[:2], *shares),
        [struct(*probes.shape), struct(2 * fields, rank)],
        [pltpu.VMEM((2 * fields * cells, HALF), F32), pltpu.SemaphoreType.DMA((LAYERS,))],
        200_000_000,
        6 * 2**20,
        scalars=1,
        far_out=1,
    )
    return hess_probe, coeffs.T


def solution(mesh):
    return jax.shard_map(
        local,
        mesh=mesh,
        in_specs=(
            P("group", "space", None, None),
            P(None, ("group", "space"), None, None),
            P(("group", "space"), None, None),
            P(("group", "space"), None, None),
            P("group", "space", None, None),
            P(("group", "space")),
            P(("group", "space")),
            P(("group", "space")),
            P(("group", "space")),
            P(("group", "space")),
            P(("group", "space")),
        ),
        out_specs=(P("group", "space", None, None), P("group", None)),
        check_vma=False,
    )
```

```python
import functools

import jax
import jax.numpy as jnp
from jax import lax
from jax.experimental import pallas as pl
from jax.experimental.pallas import tpu as pltpu
from jax.sharding import PartitionSpec as P

STENCIL = (-205.0 / 72.0, 8.0 / 5.0, -1.0 / 5.0, 8.0 / 315.0, -1.0 / 560.0)
CENTER = 3.0 * STENCIL[0]
REACH = 4
LAYERS = 4
PAIR = 8
TILES = 6
PADDED = 40
HALF = 128
PLACES = 512
F32 = jnp.float32
BF16 = jnp.bfloat16
NT = (((1,), (1,)), ((), ()))


def split(value):
    high = value.astype(BF16)
    low = (value - high.astype(F32)).astype(BF16)
    return high, low


def at(row, count=16):
    return pl.ds(pl.multiple_of(row, 8), count)


def window(ref, start, size):
    return ref.at[pl.ds(pl.multiple_of(start, 8), size)]


def kept_rows(load):
    rows = {}

    def get(layer, y):
        if (layer, y) not in rows:
            rows[layer, y] = load(layer, y)
        return rows[layer, y]

    return get


def spread(ref, row, fields):
    return jnp.broadcast_to(ref[pl.ds(row, 1), :], (fields, HALF))


def clear_margins(ref, layers, fields):
    margin = jnp.zeros((REACH * fields, HALF), F32)
    for layer in range(layers):
        start = layer * PADDED * fields
        ref[start : start + REACH * fields, :] = margin
        start += (PADDED - REACH) * fields
        ref[start : start + REACH * fields, :] = margin


def along_z(ref, first, layers, fields, band_ref, out_ref, row=0):
    pieces = [ref[at(((first + x) * PADDED + REACH) * fields, 32 * fields), :] for x in range(layers)]
    high, low = split(jnp.concatenate(pieces, axis=0))
    both = jnp.dot(jnp.concatenate([high, low], axis=1), band_ref[...], preferred_element_type=F32)
    out_ref[at(row, layers * 32 * fields), :] = both[:, :HALF] + both[:, HALF:]


def laplacian(get, x, y, z_term, lowest, highest):
    total = z_term
    for k in range(1, REACH + 1):
        ring = get(x, y + k) + get(x, y - k)
        if x + k <= highest:
            ring = ring + get(x + k, y)
        if x - k >= lowest:
            ring = ring + get(x - k, y)
        total = total + STENCIL[k] * ring
    return total


def pack(
    count, me, probes, sources, prior, kappa, cell, owner, slot, weight, scale,
    statics, probes_out, sources_out, prior_out, lent, band_ref, small_int, small_float, sem,
):
    rows = cell.shape[0]
    cells = kappa.shape[0]
    half = probes_out.shape[0]
    mine = me[0] % 2
    other = probes.at[pl.ds(pl.multiple_of((1 - mine) * half, 8), half)]
    small = [
        pltpu.make_async_copy(kappa, statics.at[pl.ds(0, cells)], sem.at[0]),
        pltpu.make_async_copy(cell, small_int.at[0], sem.at[1]),
        pltpu.make_async_copy(owner, small_int.at[1], sem.at[2]),
        pltpu.make_async_copy(slot, small_int.at[2], sem.at[3]),
        pltpu.make_async_copy(weight, small_float.at[pl.ds(0, rows)], sem.at[4]),
        pltpu.make_async_copy(scale, small_float.at[pl.ds(8, 1)], sem.at[5]),
    ]
    large = [
        pltpu.make_async_copy(other, lent.at[pl.ds(0, half)], sem.at[6]),
        pltpu.make_async_copy(sources, lent.at[pl.ds(half, 3 * cells)], sem.at[7]),
        pltpu.make_async_copy(prior, lent.at[pl.ds(half + 3 * cells, cells)], sem.at[8]),
        pltpu.make_async_copy(probes.at[pl.ds(pl.multiple_of(mine * half, 8), half)], probes_out, sem.at[9]),
        pltpu.make_async_copy(sources, sources_out, sem.at[10]),
        pltpu.make_async_copy(prior, prior_out, sem.at[11]),
    ]
    for copy in small + large:
        copy.start()
    apart = lax.broadcasted_iota(jnp.int32, (HALF, HALF), 0) - lax.broadcasted_iota(jnp.int32, (HALF, HALF), 1)
    full = jnp.where(apart == 0, CENTER, jnp.zeros((HALF, HALF), F32))
    for reach in range(1, REACH + 1):
        full = jnp.where(jnp.abs(apart) == reach, STENCIL[reach], full)
    high, low = split(full)
    band_ref[0:HALF, 0:HALF] = high
    band_ref[HALF:, 0:HALF] = high
    band_ref[0:HALF, HALF:] = low
    band_ref[HALF:, HALF:] = jnp.zeros_like(low)
    for copy in small:
        copy.wait()
    for i in range(3):
        statics[cells + i * rows : cells + (i + 1) * rows, :] = small_int[i].astype(F32)
    place = lax.broadcasted_iota(jnp.int32, (rows, HALF), 0) * HALF
    place = place + lax.broadcasted_iota(jnp.int32, (rows, HALF), 1)
    live = jnp.where(place < count[0], small_float[0:rows, :], 0.0)
    statics[cells + 3 * rows : cells + 4 * rows, :] = live
    statics[cells + 4 * rows : cells + 4 * rows + 8, :] = jnp.broadcast_to(small_float[8:9, :], (8, HALF))
    for copy in large:
        copy.wait()


def forward_own(
    fields, me, probes, sources, prior, own, partner, borrowed, band_ref,
    turned, first, second, third, push_ref, prior_ref, z_term, speed_ref,
):
    slab, flat, cells = PADDED * fields, 32 * fields, LAYERS * 32
    ahead = 24 * fields
    half = probes.shape[0]
    mine = me[0] % 2
    clear_margins(first, PAIR, fields)
    clear_margins(second, PAIR, fields)
    lent = borrowed.at[pl.ds(half, 4 * cells)]
    for side, pushes, damping, statics in ((mine, sources, prior, own), (1 - mine, lent, None, partner)):
        for i in range(3):
            push_ref[at(i * 2 * cells + side * cells, cells), :] = pushes[i * cells : (i + 1) * cells, :]
        place = at(side * cells, cells)
        prior_ref[place, :] = lent[3 * cells :, :] if damping is None else damping[...]
        speed_ref[place, :] = statics[0:cells, :]

    def load(chunk, carry):
        for side, ref in ((mine, probes), (1 - mine, borrowed)):
            there = window(turned, side * LAYERS * flat + chunk * 8 * fields, LAYERS * flat - ahead)
            padded = window(first, side * LAYERS * slab + chunk * 8 * fields, LAYERS * slab - ahead)
            here = window(ref, chunk * 8, half - 24)
            push = window(push_ref, side * cells + chunk * 8, cells - 24)
            for x in range(LAYERS):
                rows = [here[p * cells + x * 32 : p * cells + x * 32 + 8, :] for p in range(fields)]
                values = jnp.swapaxes(jnp.stack(rows, axis=0), 0, 1)
                for y in range(8):
                    cell = x * 32 + y
                    there[cell * fields : (cell + 1) * fields, :] = values[y]
                    row = x * slab + (REACH + y) * fields
                    padded[row : row + fields, :] = values[y] * spread(push, cell, fields)
        return carry

    lax.fori_loop(0, 4, load, 0)

    def sweep(field, emit):
        along_z(field, 0, PAIR, fields, band_ref, z_term)

        def body(chunk, carry):
            padded = window(field, chunk * 8 * fields, PAIR * slab - ahead)
            z_part = window(z_term, chunk * 8 * fields, PAIR * flat - ahead)
            speed = window(speed_ref, chunk * 8, 2 * cells - 24)
            push = window(push_ref, chunk * 8, 6 * cells - 24)
            there = window(turned, chunk * 8 * fields, PAIR * flat - ahead)
            put = emit(chunk)

            def load(layer, y):
                row = layer * slab + (REACH + y) * fields
                return padded[row : row + fields, :]

            for side in range(2):
                get = kept_rows(load)
                for y in range(8):
                    for x in range(side * LAYERS, (side + 1) * LAYERS):
                        cell = x * 32 + y
                        row = slice(cell * fields, (cell + 1) * fields)
                        change = spread(speed, cell, fields) * laplacian(get, x, y, z_part[row, :], 0, PAIR - 1)
                        put(x, y, get(x, y), change, there[row, :], push)
            return carry

        lax.fori_loop(0, 4, body, 0)

    def step_one(chunk):
        out = window(second, chunk * 8 * fields, PAIR * slab - ahead)

        def put(x, y, now, change, probe, push):
            change = change + probe * spread(push, 2 * cells + x * 32 + y, fields)
            row = x * slab + (REACH + y) * fields
            out[row : row + fields, :] = 2.0 * now + change

        return put

    sweep(first, step_one)

    def step_two(chunk):
        before = window(first, chunk * 8 * fields, PAIR * slab - ahead)
        out = window(third, chunk * 8 * fields, PAIR * flat - ahead)

        def put(x, y, now, change, probe, push):
            row = x * slab + (REACH + y) * fields
            change = change - before[row : row + fields, :]
            cell = x * 32 + y
            change = change + probe * spread(push, 4 * cells + cell, fields)
            out[cell * fields : (cell + 1) * fields, :] = 2.0 * now + change

        return put

    sweep(second, step_two)


def entry_row(value, row):
    return jnp.concatenate([value[row + i : row + i + 1, :] for i in range(4)], axis=1)


def forward_window(
    fields, peers, me, first, second, third, own, partner, passed, across, band_ref,
    table, cell_ref, slot_ref, speed_ref, line_ref, owner_ref, weight_ref,
    below, above, z_term, total_ref, *samples,
):
    entries = line_ref.shape[1]
    cells = LAYERS * 32
    length = own.shape[0]
    odd = me[0] % 2 == 1
    slab, flat = PADDED * fields, 32 * fields
    clear_margins(below, LAYERS, fields)
    clear_margins(above, LAYERS, fields)
    total_ref[...] = jnp.zeros_like(total_ref)
    mine, theirs = own[...], partner[...]
    low = jnp.where(odd, across[...], passed[...])
    high = jnp.where(odd, passed[...], across[...])
    tiles = (
        low[length:, :],
        low[0:length, :],
        jnp.where(odd, theirs, mine),
        jnp.where(odd, mine, theirs),
        high[0:length, :],
        high[length:, :],
    )
    place = lax.broadcasted_iota(jnp.int32, (PLACES, entries), 0)
    slot_place = lax.broadcasted_iota(jnp.int32, (HALF, entries), 0)
    for tile, value in enumerate(tiles):
        speed_ref[tile * cells : (tile + 1) * cells, :] = value[0:cells, :]
        cell = entry_row(value, cells).astype(jnp.int32)
        owner = entry_row(value, cells + 4).astype(jnp.int32)
        slot = entry_row(value, cells + 8).astype(jnp.int32)
        weight = entry_row(value, cells + 12)
        hot = jnp.where(place == jnp.bitwise_and(cell, PLACES - 1), 1.0, 0.0)
        cell_ref[tile * PLACES : (tile + 1) * PLACES, :] = hot.astype(BF16)
        hot = jnp.where(slot_place == slot, 1.0, 0.0)
        slot_ref[tile * HALF : (tile + 1) * HALF, :] = hot.astype(BF16)
        rows = slice(tile * fields, (tile + 1) * fields)
        line_ref[rows, :] = jnp.broadcast_to(lax.shift_right_logical(cell, 9), (fields, entries))
        owner_ref[rows, :] = jnp.broadcast_to(owner, (fields, entries))
        weight_ref[rows, :] = jnp.broadcast_to(weight, (fields, entries))

    def outward(chunk, carry):
        ahead = 24 * fields
        speed = window(speed_ref, chunk * 8, TILES * cells - 24)
        here = window(first, chunk * 8 * fields, PAIR * slab - ahead)
        down_out, up_out = (window(ref, chunk * 8 * fields, LAYERS * slab - ahead) for ref in (below, above))
        for y in range(8):
            rows = [slice(x * slab + (REACH + y) * fields, x * slab + (REACH + y + 1) * fields) for x in range(PAIR)]
            field = [here[row, :] for row in rows]
            for x in range(LAYERS):
                up = sum(STENCIL[4 + x - other] * field[4 + other] for other in range(x, LAYERS))
                down = sum(STENCIL[4 + other - x] * field[other] for other in range(x + 1))
                up_out[rows[x], :] = spread(speed, 4 * cells + x * 32 + y, fields) * up
                down_out[rows[x], :] = spread(speed, cells + x * 32 + y, fields) * down
        return carry

    lax.fori_loop(0, 4, outward, 0)
    along_z(below, 0, LAYERS, fields, band_ref, z_term, 0)
    along_z(above, 0, LAYERS, fields, band_ref, z_term, cells * fields)

    def far(read, x, y, lowest, highest):
        total = None
        for other in range(lowest, highest + 1):
            if 1 <= abs(x - other) <= REACH:
                term = STENCIL[abs(x - other)] * read(other, y)
                total = term if total is None else total + term
        return total

    def respond(chunk, carry):
        ahead = 16 * fields
        speeds = window(speed_ref, chunk * 16, TILES * cells - 16)
        low_side, high_side = (window(ref, chunk * 16 * fields, LAYERS * slab - ahead) for ref in (below, above))
        inside = window(second, chunk * 16 * fields, PAIR * slab - ahead)
        base = window(third, chunk * 16 * fields, PAIR * flat - ahead)
        z_parts = window(z_term, chunk * 16 * fields, PAIR * flat - ahead)

        def load(layer, y):
            if layer < 0:
                ref, layer = low_side, layer + LAYERS
            elif layer >= PAIR:
                ref, layer = high_side, layer - PAIR
            else:
                ref = inside
            row = layer * slab + (REACH + y) * fields
            return ref[row : row + fields, :]

        for tile in range(TILES):
            sample = samples[tile]
            read = kept_rows(load)
            for y in range(16):
                for x in range(LAYERS):
                    cell = x * 32 + y
                    layer = (tile - 2) * LAYERS + x
                    speed = spread(speeds, tile * cells + cell, fields)
                    if tile in (0, 5):
                        value = speed * far(read, layer, y, -4, 11)
                    elif tile in (2, 3):
                        outside = far(read, layer, y, -4, -1) if tile == 2 else far(read, layer, y, 8, 11)
                        row = ((tile - 2) * cells + cell) * fields
                        value = base[row : row + fields, :] + speed * outside
                    else:
                        row = (tile // 4 * cells + cell) * fields
                        lap = laplacian(read, layer, y, z_parts[row : row + fields, :], -4, 11)
                        value = 2.0 * read(layer, y) + speed * lap
                    row = (x * 4 + y // 4) * fields
                    side = y % 4 * HALF
                    sample[row : row + fields, side : side + HALF] = value
            hot = cell_ref[tile * PLACES : (tile + 1) * PLACES, :]
            picked = jnp.dot(jnp.concatenate(split(sample[...]), axis=0), hot, preferred_element_type=F32)
            picked = picked[: 16 * fields, :] + picked[16 * fields :, :]
            rows = slice(tile * fields, (tile + 1) * fields)
            line = line_ref[rows, :]
            total = total_ref[rows, :]
            for i in range(16):
                chosen = line == i // 4 * 8 + chunk * 4 + i % 4
                total = total + jnp.where(chosen, picked[i * fields : (i + 1) * fields, :], 0.0)
            total_ref[rows, :] = total
        return carry

    lax.fori_loop(0, 2, respond, 0)

    for group in range(peers // 16):
        lefts, rights = [], []
        for tile in range(TILES):
            rows = slice(tile * fields, (tile + 1) * fields)
            value = total_ref[rows, :] * weight_ref[rows, :]
            high = value.astype(BF16).astype(F32)
            owner = owner_ref[rows, :]
            for part in (high, value - high):
                pieces = [jnp.where(owner == group * 16 + i, part, 0.0) for i in range(16)]
                lefts.append(jnp.concatenate(pieces, axis=0).astype(BF16))
                rights.append(slot_ref[tile * HALF : (tile + 1) * HALF, :])
        result = lax.dot_general(
            jnp.concatenate(lefts, axis=1), jnp.concatenate(rights, axis=1), NT, preferred_element_type=F32
        )
        table[group * 16 * fields : (group + 1) * 16 * fields, :] = result
    place = lax.broadcasted_iota(jnp.int32, (peers, HALF), 0)
    scales = jnp.zeros((peers, HALF), F32)
    for position, value in ((me[0], mine), (me[0] + 1 - 2 * (me[0] % 2), theirs)):
        scale = jnp.broadcast_to(value[cells + 16 : cells + 17, :], (peers, HALF))
        scales = jnp.where(place == position, scale, scales)
    table[peers * fields :, :] = scales


def basis_parts(first, basis, when, out):
    rank = basis.shape[0] // HALF

    def body(group, carry):
        here = window(basis, (first + group) * 8, basis.shape[0] - 15 * 8)
        there = window(out, group * rank, rank)
        for step in range(8):
            high, low = split(here[pl.ds(step, rank, stride=HALF), :])
            there[:, step * 256 : step * 256 + HALF] = high
            there[:, step * 256 + HALF : (step + 1) * 256] = low
        return carry

    lax.fori_loop(0, 8, body, 0)


def adjoint(
    fields, peers, me, table, cell_ref, slot_ref, speed_ref, line_ref, owner_ref, weight_ref, turned, push_ref,
    prior_ref, band_ref, own_basis, own_basis_two, other_basis, other_basis_two, kept, lent, coeffs,
    high_ref, low_ref, inner_two, outer_two, inner_one, outer_one, z_term, image, scaled, *scratch,
):
    lefts, image_parts = scratch[:TILES], scratch[TILES:]
    entries = line_ref.shape[1]
    cells = LAYERS * 32
    rank = own_basis.shape[0] // 8
    slab, flat = PADDED * fields, 32 * fields
    ahead = 24 * fields
    clear_margins(inner_two, TILES * LAYERS, fields)
    clear_margins(inner_one, 2 * PAIR, fields)
    for owner in range(peers):
        rows = slice(owner * fields, (owner + 1) * fields)
        scaled[rows, :] = table[rows, :] * table[peers * fields + owner : peers * fields + owner + 1, :]
    for tile in range(TILES):
        rows = slice(tile * fields, (tile + 1) * fields)
        owner = owner_ref[rows, :]
        hot = slot_ref[tile * HALF : (tile + 1) * HALF, :]
        hot = jnp.concatenate([hot, hot], axis=0)
        total = jnp.zeros((fields, entries), F32)
        for group in range(peers // 16):
            parts = split(scaled[group * 16 * fields : (group + 1) * 16 * fields, :])
            found = jnp.dot(jnp.concatenate(parts, axis=1), hot, preferred_element_type=F32)
            for i in range(16):
                total = total + jnp.where(owner == group * 16 + i, found[i * fields : (i + 1) * fields, :], 0.0)
        value = total * weight_ref[rows, :]
        high = value.astype(BF16).astype(F32)
        high_ref[rows, :] = high
        low_ref[rows, :] = value - high

    for tile in range(TILES):
        left = lefts[tile]
        rows = slice(tile * fields, (tile + 1) * fields)
        line, high, low = line_ref[rows, :], high_ref[rows, :], low_ref[rows, :]
        for i in range(0, 32, 2):
            chosen = [line == i, line == i + 1]
            for part, start in ((high, i * fields), (low, (32 + i) * fields)):
                both = [jnp.where(which, part, 0.0) for which in chosen]
                left[start : start + 2 * fields, :] = jnp.concatenate(both, axis=0).astype(BF16)
        hot = cell_ref[tile * PLACES : (tile + 1) * PLACES, :]
        value = lax.dot_general(left[...], hot, NT, preferred_element_type=F32)
        value = value[: 32 * fields, :] + value[32 * fields :, :]
        for i in range(32):
            for step in range(4):
                layer, y = tile * LAYERS + i // 8, i % 8 * 4 + step
                now = value[i * fields : (i + 1) * fields, step * HALF : (step + 1) * HALF]
                if 1 <= tile <= 4:
                    row = ((layer - LAYERS) * 32 + y) * fields
                    outer_two[row : row + fields, :] = now
                speed = spread(speed_ref, layer * 32 + y, fields)
                row = layer * slab + (REACH + y) * fields
                inner_two[row : row + fields, :] = speed * now
        if 1 <= tile <= 4:
            along_z(inner_two, tile * LAYERS, LAYERS, fields, band_ref, z_term, (tile - 1) * cells * fields)

    def step_one(index, carry):
        pair, chunk = index // 4, index % 4
        start, skip = pair * PAIR * slab + chunk * 8 * fields, pair * PAIR * flat + chunk * 8 * fields
        here = window(inner_two, start, 2 * PAIR * slab - ahead)
        two, one, z_part = (window(ref, skip, PAIR * flat - ahead) for ref in (outer_two, outer_one, z_term))
        out = window(inner_one, start, PAIR * slab - ahead)
        speed = window(speed_ref, cells + pair * 2 * cells + chunk * 8, 2 * cells - 24)

        def load(layer, y):
            row = (layer + LAYERS) * slab + (REACH + y) * fields
            return here[row : row + fields, :]

        for side in range(2):
            get = kept_rows(load)
            for y in range(8):
                for x in range(side * LAYERS, (side + 1) * LAYERS):
                    cell = x * 32 + y
                    row = slice(cell * fields, (cell + 1) * fields)
                    now = 2.0 * two[row, :] + laplacian(get, x, y, z_part[row, :], -4, 11)
                    one[row, :] = now
                    row = x * slab + (REACH + y) * fields
                    out[row : row + fields, :] = spread(speed, cell, fields) * now
        return carry

    lax.fori_loop(0, 8, step_one, 0)
    along_z(inner_one, LAYERS, PAIR, fields, band_ref, z_term)
    mine = me[0] % 2

    def step_two(chunk, total, image_parts):
        skip = chunk * 8 * fields
        here = window(inner_one, skip, 2 * PAIR * slab - ahead)
        two_rows, one_rows = (window(ref, LAYERS * flat + skip, PAIR * flat - ahead) for ref in (outer_two, outer_one))
        z_part, there, out = (window(ref, skip, PAIR * flat - ahead) for ref in (z_term, turned, image))
        push = window(push_ref, chunk * 8, 6 * cells - 24)
        damping = window(prior_ref, chunk * 8, 2 * cells - 24)

        def load(layer, y):
            row = (layer + LAYERS) * slab + (REACH + y) * fields
            return here[row : row + fields, :]

        nothing = jnp.zeros((fields, HALF), F32)
        for side in range(2):
            get = kept_rows(load)
            for y in range(8):
                for x in range(side * LAYERS, (side + 1) * LAYERS):
                    cell = x * 32 + y
                    row = slice(cell * fields, (cell + 1) * fields)
                    two, one = two_rows[row, :], one_rows[row, :]
                    zero = 2.0 * one - two + laplacian(get, x, y, z_part[row, :], -4, 11)
                    value = spread(push, cell, fields) * zero
                    value = value + spread(push, 2 * cells + cell, fields) * one
                    value = value + spread(push, 4 * cells + cell, fields) * two
                    value = value + spread(damping, cell, fields) * there[row, :]
                    out[row, :] = value
                    high = value.astype(BF16).astype(F32)
                    rows, lane = slice(x * 2 * fields, (x + 1) * 2 * fields), y * 256
                    image_parts[rows, lane : lane + HALF] = jnp.concatenate([high, value - high], axis=0).astype(BF16)
                    image_parts[rows, lane + HALF : lane + 256] = jnp.concatenate([high, nothing], axis=0).astype(BF16)
        for side, pieces in ((mine, (own_basis, own_basis_two)), (1 - mine, (other_basis, other_basis_two))):
            for x in range(LAYERS):
                columns = pieces[x // 2][(x % 2 * 4 + chunk) * rank : (x % 2 * 4 + chunk + 1) * rank, :]
                parts = image_parts[at((side * LAYERS + x) * 2 * fields, 2 * fields), :]
                total = total + lax.dot_general(parts, columns, NT, preferred_element_type=F32)
        return total

    total = jnp.zeros((2 * fields, rank), F32)
    for chunk in range(4):
        total = step_two(chunk, total, image_parts[chunk])
    coeffs[...] = total[:fields, :] + total[fields:, :]
    kept[...] = image[at(mine * LAYERS * flat, LAYERS * flat), :]
    lent[...] = image[at((1 - mine) * LAYERS * flat, LAYERS * flat), :]


def remainder(fields, me, image, borrowed, basis, basis_two, *rest):
    *shares, out, coeffs, natural, sem = rest
    rank = coeffs.shape[1]
    half = fields // 2
    mine = me[0] % 2
    while len(shares) > 1:
        shares = [shares[i][...] + shares[i + 1][...] for i in range(0, len(shares), 2)]
    total = shares[0][...]
    coeffs[at(mine * half, half), :] = total[:half, :]
    coeffs[at((1 - mine) * half, half), :] = total[half:, :]
    parts = jnp.concatenate(split(total), axis=0)
    whole = natural.reshape(out.shape)
    first, second = (window(natural, side * half * HALF, half * HALF) for side in (mine, 1 - mine))

    def leave(x):
        return pltpu.make_async_copy(whole.at[:, x], out.at[:, x], sem.at[x])

    for x in range(LAYERS):
        for part in range(4):
            columns = (basis, basis_two)[x // 2][(x % 2 * 4 + part) * rank : (x % 2 * 4 + part + 1) * rank, :]
            both = jnp.dot(parts, columns, preferred_element_type=F32)
            cell = x * 32 + part * 8
            results = ([], [])
            for step in range(8):
                side = step * 256
                along = both[:fields, side : side + HALF] + both[:fields, side + HALF : side + 256]
                along = along + both[fields:, side : side + HALF]
                row = slice((cell + step) * half, (cell + step + 1) * half)
                results[0].append(image[row, :] - along[:half, :])
                results[1].append(borrowed[row, :] - along[half:, :])
            for ref, values in zip((first, second), results):
                values = jnp.swapaxes(jnp.stack(values, axis=0), 0, 1)
                for p in range(half):
                    ref[p * HALF + cell : p * HALF + cell + 8, :] = values[p]
        leave(x).start()
    for x in range(LAYERS):
        leave(x).wait()


def call(kernel, inputs, out_shape, scratch, flops, size, scalars=0, far=0, far_out=0, room=16):
    smem = pl.BlockSpec(memory_space=pltpu.SMEM)
    vmem = pl.BlockSpec(memory_space=pltpu.VMEM)
    hbm = pl.BlockSpec(memory_space=pltpu.HBM)
    inputs = [
        pltpu.with_memory_space_constraint(array, pltpu.HBM) if scalars <= i < scalars + far else array
        for i, array in enumerate(inputs)
    ]
    return pl.pallas_call(
        kernel,
        out_shape=out_shape,
        in_specs=[smem] * scalars + [hbm] * far + [vmem] * (len(inputs) - scalars - far),
        out_specs=[hbm] * far_out + [vmem] * (len(out_shape) - far_out),
        scratch_shapes=scratch,
        cost_estimate=pl.CostEstimate(flops=flops, bytes_accessed=size, transcendentals=0),
        compiler_params=pltpu.CompilerParams(vmem_limit_bytes=room * 2**20),
    )(*inputs)


def struct(*shape, dtype=F32):
    return jax.ShapeDtypeStruct(shape, dtype)


def swapped(array, axis, bits):
    count = lax.axis_size(axis)
    return lax.ppermute(array, axis, [(i, i ^ bits) for i in range(count)])


def local(
    probes,
    sources,
    kappa,
    prior,
    basis,
    entry_cell,
    entry_owner,
    entry_slot,
    entry_weight,
    entry_count,
    trace_weight,
):
    rank = basis.shape[0]
    fields = probes.shape[0] // 2
    entries = entry_cell.shape[0]
    peers = lax.axis_size("space")
    slab, flat = PADDED * fields, 32 * fields
    cells = LAYERS * 32
    rows = entries // HALF
    basis = basis.reshape(rank * cells, HALF)
    me = lax.axis_index("space").astype(jnp.int32).reshape(1)

    own, probes_near, sources_near, prior_near, lent, matrix = call(
        pack,
        (
            entry_count,
            me,
            probes.reshape(2 * fields * cells, HALF),
            sources.reshape(3 * cells, HALF),
            prior.reshape(cells, HALF),
            kappa.reshape(cells, HALF),
            entry_cell.reshape(rows, HALF),
            entry_owner.reshape(rows, HALF),
            entry_slot.reshape(rows, HALF),
            entry_weight.reshape(rows, HALF),
            trace_weight.reshape(1, HALF),
        ),
        [
            struct(cells + 4 * rows + 8, HALF),
            struct(fields * cells, HALF),
            struct(3 * cells, HALF),
            struct(cells, HALF),
            struct((fields + 4) * cells, HALF),
            struct(256, 256, dtype=BF16),
        ],
        [pltpu.VMEM((3, rows, HALF), jnp.int32), pltpu.VMEM((16, HALF), F32), pltpu.SemaphoreType.DMA((12,))],
        100_000,
        2 * 2**20,
        scalars=2,
        far=9,
    )
    partner = swapped(own, "space", 1)
    lent, partner = lax.optimization_barrier((lent, partner))
    borrowed = swapped(lent, "space", 1)
    passed = lax.ppermute(
        jnp.concatenate([own, partner], axis=0),
        "space",
        [pair for i in range(1, peers - 1, 2) for pair in ((i, i + 1), (i + 1, i))],
    )

    turned, first, second, third, push, damping = call(
        functools.partial(forward_own, fields),
        (me, probes_near, sources_near, prior_near, own, partner, borrowed, matrix),
        [
            struct(PAIR * flat, HALF),
            struct(PAIR * slab, HALF),
            struct(PAIR * slab, HALF),
            struct(PAIR * flat, HALF),
            struct(6 * cells, HALF),
            struct(2 * cells, HALF),
        ],
        [pltpu.VMEM((PAIR * flat, HALF), F32), pltpu.VMEM((2 * cells, HALF), F32)],
        600_000_000,
        6 * 2**20,
        scalars=1,
    )
    passed, second = lax.optimization_barrier((passed, second))
    across = swapped(passed, "space", 1)
    across, basis_there = lax.optimization_barrier((across, basis))
    basis_there = swapped(basis_there, "space", 1)
    table, cell_hot, slot_hot, speed, line, owner, weight = call(
        functools.partial(forward_window, fields, peers),
        (me, first, second, third, own, partner, passed, across, matrix),
        [
            struct(peers * (fields + 1), HALF),
            struct(TILES * PLACES, entries, dtype=BF16),
            struct(TILES * HALF, entries, dtype=BF16),
            struct(TILES * cells, HALF),
            struct(TILES * fields, entries, dtype=jnp.int32),
            struct(TILES * fields, entries, dtype=jnp.int32),
            struct(TILES * fields, entries),
        ],
        [
            pltpu.VMEM((LAYERS * slab, HALF), F32),
            pltpu.VMEM((LAYERS * slab, HALF), F32),
            pltpu.VMEM((PAIR * flat, HALF), F32),
            pltpu.VMEM((TILES * fields, entries), F32),
        ]
        + [pltpu.VMEM((16 * fields, PLACES), F32)] * TILES,
        3_000_000_000,
        6 * 2**20,
        scalars=1,
        room=20,
    )
    columns = []
    bits = 2
    while bits < peers:
        arrived = swapped(table, "space", bits)
        for i in ((0,), (1,), (2, 3))[len(columns)] if len(columns) < 3 else ():
            (some,) = call(
                functools.partial(basis_parts, 8 * (i % 2)),
                ((basis, basis_there)[i // 2], table),
                [struct(8 * rank, 2048, dtype=BF16)],
                [],
                10_000_000,
                4 * 2**20,
            )
            columns.append(some)
        arrived, columns = lax.optimization_barrier((arrived, columns))
        table = table + arrived
        bits *= 2
    kept, lent, coeffs = call(
        functools.partial(adjoint, fields, peers),
        (me, table, cell_hot, slot_hot, speed, line, owner, weight, turned, push, damping, matrix, *columns),
        [struct(LAYERS * flat, HALF), struct(LAYERS * flat, HALF), struct(fields, rank)],
        [
            pltpu.VMEM((TILES * fields, entries), F32),
            pltpu.VMEM((TILES * fields, entries), F32),
            pltpu.VMEM((TILES * LAYERS * slab, HALF), F32),
            pltpu.VMEM((2 * PAIR * flat, HALF), F32),
            pltpu.VMEM((2 * PAIR * slab, HALF), F32),
            pltpu.VMEM((2 * PAIR * flat, HALF), F32),
            pltpu.VMEM((2 * PAIR * flat, HALF), F32),
            pltpu.VMEM((PAIR * flat, HALF), F32),
            pltpu.VMEM((peers * fields, HALF), F32),
        ]
        + [pltpu.VMEM((64 * fields, entries), BF16)] * TILES
        + [pltpu.VMEM((2 * PAIR * fields, 2048), BF16)] * 4,
        5_000_000_000,
        10 * 2**20,
        scalars=1,
        room=30,
    )
    coeffs = jnp.concatenate([coeffs, swapped(coeffs, "space", 1)], axis=0)
    lent, coeffs = lax.optimization_barrier((lent, coeffs))
    borrowed = swapped(lent, "space", 1)
    bits = 2
    while bits * 4 < peers:
        coeffs = coeffs + swapped(coeffs, "space", bits)
        bits *= 2
    shares = [swapped(coeffs, "space", bits * i) for i in (3, 2, 1)] + [coeffs]
    hess_probe, coeffs = call(
        functools.partial(remainder, 2 * fields),
        (me, kept, borrowed, *columns[:2], *shares),
        [struct(*probes.shape), struct(2 * fields, rank)],
        [pltpu.VMEM((2 * fields * cells, HALF), F32), pltpu.SemaphoreType.DMA((LAYERS,))],
        200_000_000,
        6 * 2**20,
        scalars=1,
        far_out=1,
    )
    return hess_probe, coeffs.T


def solution(mesh):
    return jax.shard_map(
        local,
        mesh=mesh,
        in_specs=(
            P("group", "space", None, None),
            P(None, ("group", "space"), None, None),
            P(("group", "space"), None, None),
            P(("group", "space"), None, None),
            P("group", "space", None, None),
            P(("group", "space")),
            P(("group", "space")),
            P(("group", "space")),
            P(("group", "space")),
            P(("group", "space")),
            P(("group", "space")),
        ),
        out_specs=(P("group", "space", None, None), P("group", None)),
        check_vma=False,
    )
```

```python
import functools

import jax
import jax.numpy as jnp
from jax import lax
from jax.experimental import pallas as pl
from jax.experimental.pallas import tpu as pltpu
from jax.sharding import PartitionSpec as P

STENCIL = (-205.0 / 72.0, 8.0 / 5.0, -1.0 / 5.0, 8.0 / 315.0, -1.0 / 560.0)
CENTER = 3.0 * STENCIL[0]
REACH = 4
LAYERS = 4
PAIR = 8
TILES = 6
PADDED = 40
HALF = 128
PLACES = 512
F32 = jnp.float32
BF16 = jnp.bfloat16
NT = (((1,), (1,)), ((), ()))


def split(value):
    high = value.astype(BF16)
    low = (value - high.astype(F32)).astype(BF16)
    return high, low


def at(row, count=16):
    return pl.ds(pl.multiple_of(row, 8), count)


def window(ref, start, size):
    return ref.at[pl.ds(pl.multiple_of(start, 8), size)]


def kept_rows(load):
    rows = {}

    def get(layer, y):
        if (layer, y) not in rows:
            rows[layer, y] = load(layer, y)
        return rows[layer, y]

    return get


def spread(ref, row, fields):
    return jnp.broadcast_to(ref[pl.ds(row, 1), :], (fields, HALF))


def clear_margins(ref, layers, fields):
    margin = jnp.zeros((REACH * fields, HALF), F32)
    for layer in range(layers):
        start = layer * PADDED * fields
        ref[start : start + REACH * fields, :] = margin
        start += (PADDED - REACH) * fields
        ref[start : start + REACH * fields, :] = margin


def along_z(ref, first, layers, fields, band_ref, out_ref, row=0):
    slab, flat = PADDED * fields, 32 * fields

    def body(index, carry):
        here = window(ref, (first + index * LAYERS) * slab, LAYERS * slab)
        pieces = [here[x * slab + REACH * fields : x * slab + REACH * fields + flat, :] for x in range(LAYERS)]
        high, low = split(jnp.concatenate(pieces, axis=0))
        both = jnp.dot(jnp.concatenate([high, low], axis=1), band_ref[...], preferred_element_type=F32)
        out_ref[at(row + index * LAYERS * flat, LAYERS * flat), :] = both[:, :HALF] + both[:, HALF:]
        return carry

    lax.fori_loop(0, layers // LAYERS, body, 0)


def laplacian(get, x, y, z_term, lowest, highest):
    total = z_term
    for k in range(1, REACH + 1):
        ring = get(x, y + k) + get(x, y - k)
        if x + k <= highest:
            ring = ring + get(x + k, y)
        if x - k >= lowest:
            ring = ring + get(x - k, y)
        total = total + STENCIL[k] * ring
    return total


def pack(
    count, me, probes, sources, prior, kappa, cell, owner, slot, weight, scale,
    statics, probes_out, sources_out, prior_out, lent, band_ref, small_int, small_float, sem,
):
    rows = cell.shape[0]
    cells = kappa.shape[0]
    half = probes_out.shape[0]
    mine = me[0] % 2
    other = probes.at[pl.ds(pl.multiple_of((1 - mine) * half, 8), half)]
    small = [
        pltpu.make_async_copy(kappa, statics.at[pl.ds(0, cells)], sem.at[0]),
        pltpu.make_async_copy(cell, small_int.at[0], sem.at[1]),
        pltpu.make_async_copy(owner, small_int.at[1], sem.at[2]),
        pltpu.make_async_copy(slot, small_int.at[2], sem.at[3]),
        pltpu.make_async_copy(weight, small_float.at[pl.ds(0, rows)], sem.at[4]),
        pltpu.make_async_copy(scale, small_float.at[pl.ds(8, 1)], sem.at[5]),
    ]
    large = [
        pltpu.make_async_copy(other, lent.at[pl.ds(0, half)], sem.at[6]),
        pltpu.make_async_copy(sources, lent.at[pl.ds(half, 3 * cells)], sem.at[7]),
        pltpu.make_async_copy(prior, lent.at[pl.ds(half + 3 * cells, cells)], sem.at[8]),
        pltpu.make_async_copy(probes.at[pl.ds(pl.multiple_of(mine * half, 8), half)], probes_out, sem.at[9]),
        pltpu.make_async_copy(sources, sources_out, sem.at[10]),
        pltpu.make_async_copy(prior, prior_out, sem.at[11]),
    ]
    for copy in small + large:
        copy.start()
    apart = lax.broadcasted_iota(jnp.int32, (HALF, HALF), 0) - lax.broadcasted_iota(jnp.int32, (HALF, HALF), 1)
    full = jnp.where(apart == 0, CENTER, jnp.zeros((HALF, HALF), F32))
    for reach in range(1, REACH + 1):
        full = jnp.where(jnp.abs(apart) == reach, STENCIL[reach], full)
    high, low = split(full)
    band_ref[0:HALF, 0:HALF] = high
    band_ref[HALF:, 0:HALF] = high
    band_ref[0:HALF, HALF:] = low
    band_ref[HALF:, HALF:] = jnp.zeros_like(low)
    for copy in small:
        copy.wait()
    for i in range(3):
        statics[cells + i * rows : cells + (i + 1) * rows, :] = small_int[i].astype(F32)
    place = lax.broadcasted_iota(jnp.int32, (rows, HALF), 0) * HALF
    place = place + lax.broadcasted_iota(jnp.int32, (rows, HALF), 1)
    live = jnp.where(place < count[0], small_float[0:rows, :], 0.0)
    statics[cells + 3 * rows : cells + 4 * rows, :] = live
    statics[cells + 4 * rows : cells + 4 * rows + 8, :] = jnp.broadcast_to(small_float[8:9, :], (8, HALF))
    for copy in large:
        copy.wait()


def forward_own(
    fields, me, probes, sources, prior, own, partner, borrowed, band_ref,
    turned, first, second, third, push_ref, prior_ref, z_term, speed_ref,
):
    slab, flat, cells = PADDED * fields, 32 * fields, LAYERS * 32
    ahead = 24 * fields
    half = probes.shape[0]
    mine = me[0] % 2
    clear_margins(first, PAIR, fields)
    clear_margins(second, PAIR, fields)
    lent = borrowed.at[pl.ds(half, 4 * cells)]
    for side, pushes, damping, statics in ((mine, sources, prior, own), (1 - mine, lent, None, partner)):
        for i in range(3):
            push_ref[at(i * 2 * cells + side * cells, cells), :] = pushes[i * cells : (i + 1) * cells, :]
        place = at(side * cells, cells)
        prior_ref[place, :] = lent[3 * cells :, :] if damping is None else damping[...]
        speed_ref[place, :] = statics[0:cells, :]

    def load(index, carry):
        x, chunk = index // 4, index % 4
        for side, ref in ((mine, probes), (1 - mine, borrowed)):
            there = window(turned, (side * LAYERS + x) * flat + chunk * 8 * fields, 8 * fields)
            padded = window(first, (side * LAYERS + x) * slab + (REACH + chunk * 8) * fields, 8 * fields)
            here = window(ref, x * 32 + chunk * 8, half - cells + 8)
            push = window(push_ref, side * cells + x * 32 + chunk * 8, 8)
            rows = [here[p * cells : p * cells + 8, :] for p in range(fields)]
            values = jnp.swapaxes(jnp.stack(rows, axis=0), 0, 1)
            for y in range(8):
                there[y * fields : (y + 1) * fields, :] = values[y]
                padded[y * fields : (y + 1) * fields, :] = values[y] * spread(push, y, fields)
        return carry

    lax.fori_loop(0, 16, load, 0)

    def sweep(field, emit):
        along_z(field, 0, PAIR, fields, band_ref, z_term)

        def body(chunk, carry):
            ahead = 30 * fields
            padded = window(field, chunk * 2 * fields, PAIR * slab - ahead)
            z_part = window(z_term, chunk * 2 * fields, PAIR * flat - ahead)
            there = window(turned, chunk * 2 * fields, PAIR * flat - ahead)
            put = emit(chunk, ahead)

            def load(layer, y):
                row = layer * slab + (REACH + y) * fields
                return padded[row : row + fields, :]

            get = kept_rows(load)
            for y in range(2):
                for x in range(PAIR):
                    row = slice((x * 32 + y) * fields, (x * 32 + y + 1) * fields)
                    cell = x * 32 + chunk * 2 + y
                    change = spread(speed_ref, cell, fields) * laplacian(get, x, y, z_part[row, :], 0, PAIR - 1)
                    put(x, y, get(x, y), change, there[row, :], cell)
            return carry

        lax.fori_loop(0, 16, body, 0)

    def step_one(chunk, ahead):
        out = window(second, chunk * 2 * fields, PAIR * slab - ahead)

        def put(x, y, now, change, probe, cell):
            change = change + probe * spread(push_ref, 2 * cells + cell, fields)
            row = x * slab + (REACH + y) * fields
            out[row : row + fields, :] = 2.0 * now + change

        return put

    sweep(first, step_one)

    def step_two(chunk, ahead):
        before = window(first, chunk * 2 * fields, PAIR * slab - ahead)
        out = window(third, chunk * 2 * fields, PAIR * flat - ahead)

        def put(x, y, now, change, probe, cell):
            row = x * slab + (REACH + y) * fields
            change = change - before[row : row + fields, :]
            change = change + probe * spread(push_ref, 4 * cells + cell, fields)
            row = (x * 32 + y) * fields
            out[row : row + fields, :] = 2.0 * now + change

        return put

    sweep(second, step_two)


def entry_row(value, row):
    return jnp.concatenate([value[row + i : row + i + 1, :] for i in range(4)], axis=1)


def forward_window(
    fields, peers, me, first, second, third, own, partner, passed, across, band_ref,
    table, cell_ref, slot_ref, speed_ref, line_ref, owner_ref, weight_ref,
    below, above, z_term, total_ref, sample, statics,
):
    entries = line_ref.shape[1]
    cells = LAYERS * 32
    length = own.shape[0]
    odd = me[0] % 2 == 1
    slab, flat = PADDED * fields, 32 * fields
    clear_margins(below, LAYERS, fields)
    clear_margins(above, LAYERS, fields)
    total_ref[...] = jnp.zeros_like(total_ref)
    mine, theirs = own[...], partner[...]
    low = jnp.where(odd, across[...], passed[...])
    high = jnp.where(odd, passed[...], across[...])
    tiles = (
        low[length:, :],
        low[0:length, :],
        jnp.where(odd, theirs, mine),
        jnp.where(odd, mine, theirs),
        high[0:length, :],
        high[length:, :],
    )
    place = lax.broadcasted_iota(jnp.int32, (PLACES, entries), 0)
    slot_place = lax.broadcasted_iota(jnp.int32, (HALF, entries), 0)
    for tile, value in enumerate(tiles):
        speed_ref[tile * cells : (tile + 1) * cells, :] = value[0:cells, :]
        statics[tile * 16 : (tile + 1) * 16, :] = value[cells : cells + 16, :]

    def describe(tile, carry):
        value = statics[at(tile * 16), :]
        cell, owner, slot = (entry_row(value, i * 4).astype(jnp.int32) for i in range(3))
        weight = entry_row(value, 12)
        hot = jnp.where(place == jnp.bitwise_and(cell, PLACES - 1), 1.0, 0.0)
        cell_ref[at(tile * PLACES, PLACES), :] = hot.astype(BF16)
        hot = jnp.where(slot_place == slot, 1.0, 0.0)
        slot_ref[at(tile * HALF, HALF), :] = hot.astype(BF16)
        rows = at(tile * fields, fields)
        line_ref[rows, :] = jnp.broadcast_to(lax.shift_right_logical(cell, 9), (fields, entries))
        owner_ref[rows, :] = jnp.broadcast_to(owner, (fields, entries))
        weight_ref[rows, :] = jnp.broadcast_to(weight, (fields, entries))
        return carry

    lax.fori_loop(0, TILES, describe, 0)

    def outward(chunk, carry):
        ahead = 30 * fields
        here = window(first, chunk * 2 * fields, PAIR * slab - ahead)
        down_out, up_out = (window(ref, chunk * 2 * fields, LAYERS * slab - ahead) for ref in (below, above))
        for y in range(2):
            rows = [slice(x * slab + (REACH + y) * fields, x * slab + (REACH + y + 1) * fields) for x in range(PAIR)]
            field = [here[row, :] for row in rows]
            for x in range(LAYERS):
                up = sum(STENCIL[4 + x - other] * field[4 + other] for other in range(x, LAYERS))
                down = sum(STENCIL[4 + other - x] * field[other] for other in range(x + 1))
                cell = x * 32 + chunk * 2 + y
                up_out[rows[x], :] = spread(speed_ref, 4 * cells + cell, fields) * up
                down_out[rows[x], :] = spread(speed_ref, cells + cell, fields) * down
        return carry

    lax.fori_loop(0, 16, outward, 0)
    along_z(below, 0, LAYERS, fields, band_ref, z_term, 0)
    along_z(above, 0, LAYERS, fields, band_ref, z_term, cells * fields)

    def far(read, x, y, lowest, highest):
        total = None
        for other in range(lowest, highest + 1):
            if 1 <= abs(x - other) <= REACH:
                term = STENCIL[abs(x - other)] * read(other, y)
                total = term if total is None else total + term
        return total

    def respond(chunk, carry):
        ahead = 30 * fields
        low_side, high_side = (window(ref, chunk * 2 * fields, LAYERS * slab - ahead) for ref in (below, above))
        inside = window(second, chunk * 2 * fields, PAIR * slab - ahead)
        base = window(third, chunk * 2 * fields, PAIR * flat - ahead)
        z_parts = window(z_term, chunk * 2 * fields, PAIR * flat - ahead)
        out = window(sample, chunk % 2 * 2 * flat + chunk // 2 * fields, TILES * 4 * flat - 2 * flat - 7 * fields)

        def load(layer, y):
            if layer < 0:
                ref, layer = low_side, layer + LAYERS
            elif layer >= PAIR:
                ref, layer = high_side, layer - PAIR
            else:
                ref = inside
            row = layer * slab + (REACH + y) * fields
            return ref[row : row + fields, :]

        read = kept_rows(load)
        for tile in range(TILES):
            for y in range(2):
                for x in range(LAYERS):
                    cell = x * 32 + y
                    layer = (tile - 2) * LAYERS + x
                    speed = spread(speed_ref, tile * cells + x * 32 + chunk * 2 + y, fields)
                    if tile in (0, 5):
                        value = speed * far(read, layer, y, -4, 11)
                    elif tile in (2, 3):
                        outside = far(read, layer, y, -4, -1) if tile == 2 else far(read, layer, y, 8, 11)
                        row = ((tile - 2) * cells + cell) * fields
                        value = base[row : row + fields, :] + speed * outside
                    else:
                        row = (tile // 4 * cells + cell) * fields
                        lap = laplacian(read, layer, y, z_parts[row : row + fields, :], -4, 11)
                        value = 2.0 * read(layer, y) + speed * lap
                    row = (tile * 4 + y) * flat + x * 8 * fields
                    out[row : row + fields, :] = value
        return carry

    lax.fori_loop(0, 16, respond, 0)

    def pick(index, carry):
        tile, side = index // 2, index % 2
        here = window(sample, tile * 4 * flat + side * 16 * fields, 3 * flat + 16 * fields)
        value = jnp.concatenate([here[i * flat : i * flat + 16 * fields, :] for i in range(4)], axis=1)
        hot = cell_ref[at(tile * PLACES, PLACES), :]
        picked = jnp.dot(jnp.concatenate(split(value), axis=0), hot, preferred_element_type=F32)
        picked = picked[: 16 * fields, :] + picked[16 * fields :, :]
        rows = at(tile * fields, fields)
        line = line_ref[rows, :] - side * 16
        total = total_ref[rows, :]
        for i in range(16):
            total = total + jnp.where(line == i, picked[i * fields : (i + 1) * fields, :], 0.0)
        total_ref[rows, :] = total
        return carry

    lax.fori_loop(0, 2 * TILES, pick, 0)

    for group in range(peers // 16):

        def gather(tile, result):
            rows = at(tile * fields, fields)
            value = total_ref[rows, :] * weight_ref[rows, :]
            high = value.astype(BF16).astype(F32)
            owner = owner_ref[rows, :] - group * 16
            lefts = []
            for part in (high, value - high):
                pieces = [jnp.where(owner == i, part, 0.0) for i in range(16)]
                lefts.append(jnp.concatenate(pieces, axis=0).astype(BF16))
            hot = slot_ref[at(tile * HALF, HALF), :]
            left = jnp.concatenate(lefts, axis=1)
            hots = jnp.concatenate([hot, hot], axis=1)
            return result + lax.dot_general(left, hots, NT, preferred_element_type=F32)

        table[group * 16 * fields : (group + 1) * 16 * fields, :] = lax.fori_loop(
            0, TILES, gather, jnp.zeros((16 * fields, HALF), F32)
        )
    place = lax.broadcasted_iota(jnp.int32, (peers, HALF), 0)
    scales = jnp.zeros((peers, HALF), F32)
    for position, value in ((me[0], mine), (me[0] + 1 - 2 * (me[0] % 2), theirs)):
        scale = jnp.broadcast_to(value[cells + 16 : cells + 17, :], (peers, HALF))
        scales = jnp.where(place == position, scale, scales)
    table[peers * fields :, :] = scales


def basis_parts(first, basis, when, out):
    rank = basis.shape[0] // HALF

    def body(group, carry):
        here = window(basis, (first + group) * 8, basis.shape[0] - 15 * 8)
        there = window(out, group * rank, rank)
        for step in range(8):
            high, low = split(here[pl.ds(step, rank, stride=HALF), :])
            there[:, step * 256 : step * 256 + HALF] = high
            there[:, step * 256 + HALF : (step + 1) * 256] = low
        return carry

    lax.fori_loop(0, 8, body, 0)


def adjoint(
    fields, peers, me, table, cell_ref, slot_ref, speed_ref, line_ref, owner_ref, weight_ref, turned, push_ref,
    prior_ref, band_ref, own_basis, own_basis_two, other_basis, other_basis_two, kept, lent, coeffs,
    high_ref, low_ref, inner_two, outer_two, inner_one, outer_one, z_term, image, scaled, left,
):
    entries = line_ref.shape[1]
    cells = LAYERS * 32
    rank = own_basis.shape[0] // 8
    slab, flat = PADDED * fields, 32 * fields
    ahead = 24 * fields
    clear_margins(inner_two, TILES * LAYERS, fields)
    clear_margins(inner_one, 2 * PAIR, fields)
    for owner in range(peers):
        rows = slice(owner * fields, (owner + 1) * fields)
        scaled[rows, :] = table[rows, :] * table[peers * fields + owner : peers * fields + owner + 1, :]
    def weigh(tile, carry):
        rows = at(tile * fields, fields)
        owner = owner_ref[rows, :]
        hot = slot_ref[at(tile * HALF, HALF), :]
        hot = jnp.concatenate([hot, hot], axis=0)
        total = jnp.zeros((fields, entries), F32)
        for group in range(peers // 16):
            parts = split(scaled[group * 16 * fields : (group + 1) * 16 * fields, :])
            found = jnp.dot(jnp.concatenate(parts, axis=1), hot, preferred_element_type=F32)
            for i in range(16):
                total = total + jnp.where(owner == group * 16 + i, found[i * fields : (i + 1) * fields, :], 0.0)
        value = total * weight_ref[rows, :]
        high = value.astype(BF16).astype(F32)
        high_ref[rows, :] = high
        low_ref[rows, :] = value - high
        return carry

    lax.fori_loop(0, TILES, weigh, 0)

    def inject(index, carry):
        tile, side = index // 2, index % 2
        rows = at(tile * fields, fields)
        line, high, low = line_ref[rows, :] - side * 16, high_ref[rows, :], low_ref[rows, :]
        for i in range(0, 16, 2):
            chosen = [line == i, line == i + 1]
            for part, start in ((high, i * fields), (low, (16 + i) * fields)):
                both = [jnp.where(which, part, 0.0) for which in chosen]
                left[start : start + 2 * fields, :] = jnp.concatenate(both, axis=0).astype(BF16)
        hot = cell_ref[at(tile * PLACES, PLACES), :]
        value = lax.dot_general(left[...], hot, NT, preferred_element_type=F32)
        value = value[: 16 * fields, :] + value[16 * fields :, :]
        layer = tile * LAYERS + side * 2
        two = window(outer_two, layer * flat, 2 * flat)
        out = window(inner_two, layer * slab, 2 * slab)
        speed = window(speed_ref, layer * 32, 64)
        for i in range(16):
            for step in range(4):
                x, y = i // 8, i % 8 * 4 + step
                now = value[i * fields : (i + 1) * fields, step * HALF : (step + 1) * HALF]
                cell = x * 32 + y
                two[cell * fields : (cell + 1) * fields, :] = now
                row = x * slab + (REACH + y) * fields
                out[row : row + fields, :] = spread(speed, cell, fields) * now
        return carry

    lax.fori_loop(0, 2 * TILES, inject, 0)
    along_z(inner_two, LAYERS, 2 * PAIR, fields, band_ref, z_term)

    def step_one(index, carry):
        pair, chunk = index // 16, index % 16
        ahead = 30 * fields
        start, skip = pair * PAIR * slab + chunk * 2 * fields, pair * PAIR * flat + chunk * 2 * fields
        here = window(inner_two, start, 2 * PAIR * slab - ahead)
        two = window(outer_two, LAYERS * flat + skip, PAIR * flat - ahead)
        one, z_part = (window(ref, skip, PAIR * flat - ahead) for ref in (outer_one, z_term))
        out = window(inner_one, start, PAIR * slab - ahead)

        def load(layer, y):
            row = (layer + LAYERS) * slab + (REACH + y) * fields
            return here[row : row + fields, :]

        get = kept_rows(load)
        for y in range(2):
            for x in range(PAIR):
                cell = x * 32 + y
                row = slice(cell * fields, (cell + 1) * fields)
                now = 2.0 * two[row, :] + laplacian(get, x, y, z_part[row, :], -4, 11)
                one[row, :] = now
                row = x * slab + (REACH + y) * fields
                speed = spread(speed_ref, (pair * 2 + 1) * cells + x * 32 + chunk * 2 + y, fields)
                out[row : row + fields, :] = speed * now
        return carry

    lax.fori_loop(0, 32, step_one, 0)
    along_z(inner_one, LAYERS, PAIR, fields, band_ref, z_term)
    mine = me[0] % 2

    def step_two(chunk, carry):
        ahead = 30 * fields
        skip = chunk * 2 * fields
        here = window(inner_one, skip, 2 * PAIR * slab - ahead)
        two_rows = window(outer_two, 2 * LAYERS * flat + skip, PAIR * flat - ahead)
        one_rows = window(outer_one, LAYERS * flat + skip, PAIR * flat - ahead)
        z_part, there, out = (window(ref, skip, PAIR * flat - ahead) for ref in (z_term, turned, image))

        def load(layer, y):
            row = (layer + LAYERS) * slab + (REACH + y) * fields
            return here[row : row + fields, :]

        get = kept_rows(load)
        for y in range(2):
            for x in range(PAIR):
                cell = x * 32 + chunk * 2 + y
                row = slice((x * 32 + y) * fields, (x * 32 + y + 1) * fields)
                two, one = two_rows[row, :], one_rows[row, :]
                zero = 2.0 * one - two + laplacian(get, x, y, z_part[row, :], -4, 11)
                value = spread(push_ref, cell, fields) * zero
                value = value + spread(push_ref, 2 * cells + cell, fields) * one
                value = value + spread(push_ref, 4 * cells + cell, fields) * two
                out[row, :] = value + spread(prior_ref, cell, fields) * there[row, :]
        return carry

    lax.fori_loop(0, 16, step_two, 0)
    nothing = jnp.zeros((fields, HALF), F32)

    def project(chunk, total):
        for side, pieces in ((mine, (own_basis, own_basis_two)), (1 - mine, (other_basis, other_basis_two))):
            for x in range(LAYERS):
                here = window(image, (side * LAYERS + x) * flat + chunk * 8 * fields, 8 * fields)
                parts = []
                for y in range(8):
                    value = here[y * fields : (y + 1) * fields, :]
                    high = value.astype(BF16).astype(F32)
                    parts.append(jnp.concatenate([high, value - high], axis=0))
                    parts.append(jnp.concatenate([high, nothing], axis=0))
                parts = jnp.concatenate(parts, axis=1).astype(BF16)
                columns = pieces[x // 2][at((x % 2 * 4 + chunk) * rank, rank), :]
                total = total + lax.dot_general(parts, columns, NT, preferred_element_type=F32)
        return total

    total = lax.fori_loop(0, 4, project, jnp.zeros((2 * fields, rank), F32))
    coeffs[...] = total[:fields, :] + total[fields:, :]
    kept[...] = image[at(mine * LAYERS * flat, LAYERS * flat), :]
    lent[...] = image[at((1 - mine) * LAYERS * flat, LAYERS * flat), :]


def remainder(fields, me, image, borrowed, basis, basis_two, *rest):
    *shares, out, coeffs, natural, sem = rest
    rank = coeffs.shape[1]
    half = fields // 2
    mine = me[0] % 2
    while len(shares) > 1:
        shares = [shares[i][...] + shares[i + 1][...] for i in range(0, len(shares), 2)]
    total = shares[0][...]
    coeffs[at(mine * half, half), :] = total[:half, :]
    coeffs[at((1 - mine) * half, half), :] = total[half:, :]
    parts = jnp.concatenate(split(total), axis=0)
    whole = natural.reshape(out.shape)
    first, second = (window(natural, side * half * HALF, half * HALF) for side in (mine, 1 - mine))

    def leave(x):
        return pltpu.make_async_copy(whole.at[:, x], out.at[:, x], sem.at[x])

    for x in range(LAYERS):
        for part in range(4):
            columns = (basis, basis_two)[x // 2][(x % 2 * 4 + part) * rank : (x % 2 * 4 + part + 1) * rank, :]
            both = jnp.dot(parts, columns, preferred_element_type=F32)
            cell = x * 32 + part * 8
            results = ([], [])
            for step in range(8):
                side = step * 256
                along = both[:fields, side : side + HALF] + both[:fields, side + HALF : side + 256]
                along = along + both[fields:, side : side + HALF]
                row = slice((cell + step) * half, (cell + step + 1) * half)
                results[0].append(image[row, :] - along[:half, :])
                results[1].append(borrowed[row, :] - along[half:, :])
            for ref, values in zip((first, second), results):
                values = jnp.swapaxes(jnp.stack(values, axis=0), 0, 1)
                for p in range(half):
                    ref[p * HALF + cell : p * HALF + cell + 8, :] = values[p]
        leave(x).start()
    for x in range(LAYERS):
        leave(x).wait()


def call(kernel, inputs, out_shape, scratch, flops, size, scalars=0, far=0, far_out=0, room=16):
    smem = pl.BlockSpec(memory_space=pltpu.SMEM)
    vmem = pl.BlockSpec(memory_space=pltpu.VMEM)
    hbm = pl.BlockSpec(memory_space=pltpu.HBM)
    inputs = [
        pltpu.with_memory_space_constraint(array, pltpu.HBM) if scalars <= i < scalars + far else array
        for i, array in enumerate(inputs)
    ]
    return pl.pallas_call(
        kernel,
        out_shape=out_shape,
        in_specs=[smem] * scalars + [hbm] * far + [vmem] * (len(inputs) - scalars - far),
        out_specs=[hbm] * far_out + [vmem] * (len(out_shape) - far_out),
        scratch_shapes=scratch,
        cost_estimate=pl.CostEstimate(flops=flops, bytes_accessed=size, transcendentals=0),
        compiler_params=pltpu.CompilerParams(vmem_limit_bytes=room * 2**20),
    )(*inputs)


def struct(*shape, dtype=F32):
    return jax.ShapeDtypeStruct(shape, dtype)


def swapped(array, axis, bits):
    count = lax.axis_size(axis)
    return lax.ppermute(array, axis, [(i, i ^ bits) for i in range(count)])


def local(
    probes,
    sources,
    kappa,
    prior,
    basis,
    entry_cell,
    entry_owner,
    entry_slot,
    entry_weight,
    entry_count,
    trace_weight,
):
    rank = basis.shape[0]
    fields = probes.shape[0] // 2
    entries = entry_cell.shape[0]
    peers = lax.axis_size("space")
    slab, flat = PADDED * fields, 32 * fields
    cells = LAYERS * 32
    rows = entries // HALF
    basis = basis.reshape(rank * cells, HALF)
    me = lax.axis_index("space").astype(jnp.int32).reshape(1)

    own, probes_near, sources_near, prior_near, lent, matrix = call(
        pack,
        (
            entry_count,
            me,
            probes.reshape(2 * fields * cells, HALF),
            sources.reshape(3 * cells, HALF),
            prior.reshape(cells, HALF),
            kappa.reshape(cells, HALF),
            entry_cell.reshape(rows, HALF),
            entry_owner.reshape(rows, HALF),
            entry_slot.reshape(rows, HALF),
            entry_weight.reshape(rows, HALF),
            trace_weight.reshape(1, HALF),
        ),
        [
            struct(cells + 4 * rows + 8, HALF),
            struct(fields * cells, HALF),
            struct(3 * cells, HALF),
            struct(cells, HALF),
            struct((fields + 4) * cells, HALF),
            struct(256, 256, dtype=BF16),
        ],
        [pltpu.VMEM((3, rows, HALF), jnp.int32), pltpu.VMEM((16, HALF), F32), pltpu.SemaphoreType.DMA((12,))],
        100_000,
        2 * 2**20,
        scalars=2,
        far=9,
    )
    partner = swapped(own, "space", 1)
    lent, partner = lax.optimization_barrier((lent, partner))
    borrowed = swapped(lent, "space", 1)
    passed = lax.ppermute(
        jnp.concatenate([own, partner], axis=0),
        "space",
        [pair for i in range(1, peers - 1, 2) for pair in ((i, i + 1), (i + 1, i))],
    )

    turned, first, second, third, push, damping = call(
        functools.partial(forward_own, fields),
        (me, probes_near, sources_near, prior_near, own, partner, borrowed, matrix),
        [
            struct(PAIR * flat, HALF),
            struct(PAIR * slab, HALF),
            struct(PAIR * slab, HALF),
            struct(PAIR * flat, HALF),
            struct(6 * cells, HALF),
            struct(2 * cells, HALF),
        ],
        [pltpu.VMEM((PAIR * flat, HALF), F32), pltpu.VMEM((2 * cells, HALF), F32)],
        600_000_000,
        6 * 2**20,
        scalars=1,
    )
    passed, second = lax.optimization_barrier((passed, second))
    across = swapped(passed, "space", 1)
    across, basis_there = lax.optimization_barrier((across, basis))
    basis_there = swapped(basis_there, "space", 1)
    table, cell_hot, slot_hot, speed, line, owner, weight = call(
        functools.partial(forward_window, fields, peers),
        (me, first, second, third, own, partner, passed, across, matrix),
        [
            struct(peers * (fields + 1), HALF),
            struct(TILES * PLACES, entries, dtype=BF16),
            struct(TILES * HALF, entries, dtype=BF16),
            struct(TILES * cells, HALF),
            struct(TILES * fields, entries, dtype=jnp.int32),
            struct(TILES * fields, entries, dtype=jnp.int32),
            struct(TILES * fields, entries),
        ],
        [
            pltpu.VMEM((LAYERS * slab, HALF), F32),
            pltpu.VMEM((LAYERS * slab, HALF), F32),
            pltpu.VMEM((PAIR * flat, HALF), F32),
            pltpu.VMEM((TILES * fields, entries), F32),
        ]
        + [pltpu.VMEM((TILES * 4 * flat, HALF), F32), pltpu.VMEM((TILES * 16, HALF), F32)],
        3_000_000_000,
        6 * 2**20,
        scalars=1,
        room=20,
    )
    columns = []
    bits = 2
    while bits < peers:
        arrived = swapped(table, "space", bits)
        for i in ((0,), (1,), (2, 3))[len(columns)] if len(columns) < 3 else ():
            (some,) = call(
                functools.partial(basis_parts, 8 * (i % 2)),
                ((basis, basis_there)[i // 2], table),
                [struct(8 * rank, 2048, dtype=BF16)],
                [],
                10_000_000,
                4 * 2**20,
            )
            columns.append(some)
        arrived, columns = lax.optimization_barrier((arrived, columns))
        table = table + arrived
        bits *= 2
    kept, lent, coeffs = call(
        functools.partial(adjoint, fields, peers),
        (me, table, cell_hot, slot_hot, speed, line, owner, weight, turned, push, damping, matrix, *columns),
        [struct(LAYERS * flat, HALF), struct(LAYERS * flat, HALF), struct(fields, rank)],
        [
            pltpu.VMEM((TILES * fields, entries), F32),
            pltpu.VMEM((TILES * fields, entries), F32),
            pltpu.VMEM((TILES * LAYERS * slab, HALF), F32),
            pltpu.VMEM((TILES * LAYERS * flat, HALF), F32),
            pltpu.VMEM((2 * PAIR * slab, HALF), F32),
            pltpu.VMEM((2 * PAIR * flat, HALF), F32),
            pltpu.VMEM((2 * PAIR * flat, HALF), F32),
            pltpu.VMEM((PAIR * flat, HALF), F32),
            pltpu.VMEM((peers * fields, HALF), F32),
        ]
        + [pltpu.VMEM((32 * fields, entries), BF16)],
        5_000_000_000,
        10 * 2**20,
        scalars=1,
        room=30,
    )
    coeffs = jnp.concatenate([coeffs, swapped(coeffs, "space", 1)], axis=0)
    lent, coeffs = lax.optimization_barrier((lent, coeffs))
    borrowed = swapped(lent, "space", 1)
    bits = 2
    while bits * 4 < peers:
        coeffs = coeffs + swapped(coeffs, "space", bits)
        bits *= 2
    shares = [swapped(coeffs, "space", bits * i) for i in (3, 2, 1)] + [coeffs]
    hess_probe, coeffs = call(
        functools.partial(remainder, 2 * fields),
        (me, kept, borrowed, *columns[:2], *shares),
        [struct(*probes.shape), struct(2 * fields, rank)],
        [pltpu.VMEM((2 * fields * cells, HALF), F32), pltpu.SemaphoreType.DMA((LAYERS,))],
        200_000_000,
        6 * 2**20,
        scalars=1,
        far_out=1,
    )
    return hess_probe, coeffs.T


def solution(mesh):
    return jax.shard_map(
        local,
        mesh=mesh,
        in_specs=(
            P("group", "space", None, None),
            P(None, ("group", "space"), None, None),
            P(("group", "space"), None, None),
            P(("group", "space"), None, None),
            P("group", "space", None, None),
            P(("group", "space")),
            P(("group", "space")),
            P(("group", "space")),
            P(("group", "space")),
            P(("group", "space")),
            P(("group", "space")),
        ),
        out_specs=(P("group", "space", None, None), P("group", None)),
        check_vma=False,
    )
```

```python
import functools

import jax
import jax.numpy as jnp
from jax import lax
from jax.experimental import pallas as pl
from jax.experimental.pallas import tpu as pltpu
from jax.sharding import PartitionSpec as P

STENCIL = (-205.0 / 72.0, 8.0 / 5.0, -1.0 / 5.0, 8.0 / 315.0, -1.0 / 560.0)
CENTER = 3.0 * STENCIL[0]
REACH = 4
LAYERS = 4
PAIR = 8
TILES = 6
PADDED = 40
HALF = 128
PLACES = 512
F32 = jnp.float32
BF16 = jnp.bfloat16
NT = (((1,), (1,)), ((), ()))


def split(value):
    high = value.astype(BF16)
    low = (value - high.astype(F32)).astype(BF16)
    return high, low


def at(row, count=16):
    return pl.ds(pl.multiple_of(row, 8), count)


def window(ref, start, size):
    return ref.at[pl.ds(pl.multiple_of(start, 8), size)]


def kept_rows(load):
    rows = {}

    def get(layer, y):
        if (layer, y) not in rows:
            rows[layer, y] = load(layer, y)
        return rows[layer, y]

    return get


def spread(ref, row, fields):
    return jnp.broadcast_to(ref[pl.ds(row, 1), :], (fields, HALF))


def clear_margins(ref, layers, fields):
    margin = jnp.zeros((REACH * fields, HALF), F32)
    for layer in range(layers):
        start = layer * PADDED * fields
        ref[start : start + REACH * fields, :] = margin
        start += (PADDED - REACH) * fields
        ref[start : start + REACH * fields, :] = margin


def along_z(ref, first, layers, fields, band_ref, out_ref, row=0):
    pieces = [ref[at(((first + x) * PADDED + REACH) * fields, 32 * fields), :] for x in range(layers)]
    high, low = split(jnp.concatenate(pieces, axis=0))
    both = jnp.dot(jnp.concatenate([high, low], axis=1), band_ref[...], preferred_element_type=F32)
    out_ref[at(row, layers * 32 * fields), :] = both[:, :HALF] + both[:, HALF:]


def laplacian(get, x, y, z_term, lowest, highest):
    total = z_term
    for k in range(1, REACH + 1):
        ring = get(x, y + k) + get(x, y - k)
        if x + k <= highest:
            ring = ring + get(x + k, y)
        if x - k >= lowest:
            ring = ring + get(x - k, y)
        total = total + STENCIL[k] * ring
    return total


def pack(
    count, me, probes, sources, prior, kappa, cell, owner, slot, weight, scale,
    statics, probes_out, sources_out, prior_out, lent, band_ref, small_int, small_float, sem,
):
    rows = cell.shape[0]
    cells = kappa.shape[0]
    half = probes_out.shape[0]
    mine = me[0] % 2
    other = probes.at[pl.ds(pl.multiple_of((1 - mine) * half, 8), half)]
    small = [
        pltpu.make_async_copy(kappa, statics.at[pl.ds(0, cells)], sem.at[0]),
        pltpu.make_async_copy(cell, small_int.at[0], sem.at[1]),
        pltpu.make_async_copy(owner, small_int.at[1], sem.at[2]),
        pltpu.make_async_copy(slot, small_int.at[2], sem.at[3]),
        pltpu.make_async_copy(weight, small_float.at[pl.ds(0, rows)], sem.at[4]),
        pltpu.make_async_copy(scale, small_float.at[pl.ds(8, 1)], sem.at[5]),
    ]
    large = [
        pltpu.make_async_copy(other, lent.at[pl.ds(0, half)], sem.at[6]),
        pltpu.make_async_copy(sources, lent.at[pl.ds(half, 3 * cells)], sem.at[7]),
        pltpu.make_async_copy(prior, lent.at[pl.ds(half + 3 * cells, cells)], sem.at[8]),
        pltpu.make_async_copy(probes.at[pl.ds(pl.multiple_of(mine * half, 8), half)], probes_out, sem.at[9]),
        pltpu.make_async_copy(sources, sources_out, sem.at[10]),
        pltpu.make_async_copy(prior, prior_out, sem.at[11]),
    ]
    for copy in small + large:
        copy.start()
    apart = lax.broadcasted_iota(jnp.int32, (HALF, HALF), 0) - lax.broadcasted_iota(jnp.int32, (HALF, HALF), 1)
    full = jnp.where(apart == 0, CENTER, jnp.zeros((HALF, HALF), F32))
    for reach in range(1, REACH + 1):
        full = jnp.where(jnp.abs(apart) == reach, STENCIL[reach], full)
    high, low = split(full)
    band_ref[0:HALF, 0:HALF] = high
    band_ref[HALF:, 0:HALF] = high
    band_ref[0:HALF, HALF:] = low
    band_ref[HALF:, HALF:] = jnp.zeros_like(low)
    for copy in small:
        copy.wait()
    for i in range(3):
        statics[cells + i * rows : cells + (i + 1) * rows, :] = small_int[i].astype(F32)
    place = lax.broadcasted_iota(jnp.int32, (rows, HALF), 0) * HALF
    place = place + lax.broadcasted_iota(jnp.int32, (rows, HALF), 1)
    live = jnp.where(place < count[0], small_float[0:rows, :], 0.0)
    statics[cells + 3 * rows : cells + 4 * rows, :] = live
    statics[cells + 4 * rows : cells + 4 * rows + 8, :] = jnp.broadcast_to(small_float[8:9, :], (8, HALF))
    for copy in large:
        copy.wait()


def forward_own(
    fields, me, probes, sources, prior, own, partner, borrowed, band_ref,
    turned, first, second, third, push_ref, prior_ref, z_term, speed_ref,
):
    slab, flat, cells = PADDED * fields, 32 * fields, LAYERS * 32
    ahead = 24 * fields
    half = probes.shape[0]
    mine = me[0] % 2
    clear_margins(first, PAIR, fields)
    clear_margins(second, PAIR, fields)
    lent = borrowed.at[pl.ds(half, 4 * cells)]
    for side, pushes, damping, statics in ((mine, sources, prior, own), (1 - mine, lent, None, partner)):
        for i in range(3):
            push_ref[at(i * 2 * cells + side * cells, cells), :] = pushes[i * cells : (i + 1) * cells, :]
        place = at(side * cells, cells)
        prior_ref[place, :] = lent[3 * cells :, :] if damping is None else damping[...]
        speed_ref[place, :] = statics[0:cells, :]

    def load(chunk, carry):
        for side, ref in ((mine, probes), (1 - mine, borrowed)):
            there = window(turned, side * LAYERS * flat + chunk * 8 * fields, LAYERS * flat - ahead)
            padded = window(first, side * LAYERS * slab + chunk * 8 * fields, LAYERS * slab - ahead)
            here = window(ref, chunk * 8, half - 24)
            push = window(push_ref, side * cells + chunk * 8, cells - 24)
            for x in range(LAYERS):
                rows = [here[p * cells + x * 32 : p * cells + x * 32 + 8, :] for p in range(fields)]
                values = jnp.swapaxes(jnp.stack(rows, axis=0), 0, 1)
                for y in range(8):
                    cell = x * 32 + y
                    there[cell * fields : (cell + 1) * fields, :] = values[y]
                    row = x * slab + (REACH + y) * fields
                    padded[row : row + fields, :] = values[y] * spread(push, cell, fields)
        return carry

    lax.fori_loop(0, 4, load, 0)

    def sweep(field, emit):
        along_z(field, 0, PAIR, fields, band_ref, z_term)

        def body(chunk, carry):
            padded = window(field, chunk * 8 * fields, PAIR * slab - ahead)
            z_part = window(z_term, chunk * 8 * fields, PAIR * flat - ahead)
            speed = window(speed_ref, chunk * 8, 2 * cells - 24)
            push = window(push_ref, chunk * 8, 6 * cells - 24)
            there = window(turned, chunk * 8 * fields, PAIR * flat - ahead)
            put = emit(chunk)

            def load(layer, y):
                row = layer * slab + (REACH + y) * fields
                return padded[row : row + fields, :]

            for side in range(2):
                get = kept_rows(load)
                for y in range(8):
                    for x in range(side * LAYERS, (side + 1) * LAYERS):
                        cell = x * 32 + y
                        row = slice(cell * fields, (cell + 1) * fields)
                        change = spread(speed, cell, fields) * laplacian(get, x, y, z_part[row, :], 0, PAIR - 1)
                        put(x, y, get(x, y), change, there[row, :], push)
            return carry

        lax.fori_loop(0, 4, body, 0)

    def step_one(chunk):
        out = window(second, chunk * 8 * fields, PAIR * slab - ahead)

        def put(x, y, now, change, probe, push):
            change = change + probe * spread(push, 2 * cells + x * 32 + y, fields)
            row = x * slab + (REACH + y) * fields
            out[row : row + fields, :] = 2.0 * now + change

        return put

    sweep(first, step_one)

    def step_two(chunk):
        before = window(first, chunk * 8 * fields, PAIR * slab - ahead)
        out = window(third, chunk * 8 * fields, PAIR * flat - ahead)

        def put(x, y, now, change, probe, push):
            row = x * slab + (REACH + y) * fields
            change = change - before[row : row + fields, :]
            cell = x * 32 + y
            change = change + probe * spread(push, 4 * cells + cell, fields)
            out[cell * fields : (cell + 1) * fields, :] = 2.0 * now + change

        return put

    sweep(second, step_two)


def entry_row(value, row):
    return jnp.concatenate([value[row + i : row + i + 1, :] for i in range(4)], axis=1)


def forward_window(
    fields, peers, me, first, second, third, own, partner, passed, across, band_ref,
    table, place_ref, slot_ref, speed_ref, line_ref, owner_ref, weight_ref,
    cell_ref, below, above, z_term, total_ref, *samples,
):
    entries = line_ref.shape[1]
    cells = LAYERS * 32
    length = own.shape[0]
    odd = me[0] % 2 == 1
    slab, flat = PADDED * fields, 32 * fields
    clear_margins(below, LAYERS, fields)
    clear_margins(above, LAYERS, fields)
    total_ref[...] = jnp.zeros_like(total_ref)
    mine, theirs = own[...], partner[...]
    low = jnp.where(odd, across[...], passed[...])
    high = jnp.where(odd, passed[...], across[...])
    tiles = (
        low[length:, :],
        low[0:length, :],
        jnp.where(odd, theirs, mine),
        jnp.where(odd, mine, theirs),
        high[0:length, :],
        high[length:, :],
    )
    place = lax.broadcasted_iota(jnp.int32, (PLACES, entries), 0)
    slot_place = lax.broadcasted_iota(jnp.int32, (HALF, entries), 0)
    for tile, value in enumerate(tiles):
        speed_ref[tile * cells : (tile + 1) * cells, :] = value[0:cells, :]
        cell = entry_row(value, cells).astype(jnp.int32)
        owner = entry_row(value, cells + 4).astype(jnp.int32)
        slot = entry_row(value, cells + 8).astype(jnp.int32)
        weight = entry_row(value, cells + 12)
        hot = jnp.where(place == jnp.bitwise_and(cell, PLACES - 1), 1.0, 0.0)
        cell_ref[tile * PLACES : (tile + 1) * PLACES, :] = hot.astype(BF16)
        hot = jnp.where(slot_place == slot, 1.0, 0.0)
        slot_ref[tile * HALF : (tile + 1) * HALF, :] = hot.astype(BF16)
        rows = slice(tile * fields, (tile + 1) * fields)
        line_ref[rows, :] = jnp.broadcast_to(lax.shift_right_logical(cell, 9), (fields, entries))
        place_ref[rows, :] = jnp.broadcast_to(jnp.bitwise_and(cell, PLACES - 1), (fields, entries)).astype(F32)
        owner_ref[rows, :] = jnp.broadcast_to(owner, (fields, entries))
        weight_ref[rows, :] = jnp.broadcast_to(weight, (fields, entries))

    def outward(chunk, carry):
        ahead = 24 * fields
        speed = window(speed_ref, chunk * 8, TILES * cells - 24)
        here = window(first, chunk * 8 * fields, PAIR * slab - ahead)
        down_out, up_out = (window(ref, chunk * 8 * fields, LAYERS * slab - ahead) for ref in (below, above))
        for y in range(8):
            rows = [slice(x * slab + (REACH + y) * fields, x * slab + (REACH + y + 1) * fields) for x in range(PAIR)]
            field = [here[row, :] for row in rows]
            for x in range(LAYERS):
                up = sum(STENCIL[4 + x - other] * field[4 + other] for other in range(x, LAYERS))
                down = sum(STENCIL[4 + other - x] * field[other] for other in range(x + 1))
                up_out[rows[x], :] = spread(speed, 4 * cells + x * 32 + y, fields) * up
                down_out[rows[x], :] = spread(speed, cells + x * 32 + y, fields) * down
        return carry

    lax.fori_loop(0, 4, outward, 0)
    along_z(below, 0, LAYERS, fields, band_ref, z_term, 0)
    along_z(above, 0, LAYERS, fields, band_ref, z_term, cells * fields)

    def far(read, x, y, lowest, highest):
        total = None
        for other in range(lowest, highest + 1):
            if 1 <= abs(x - other) <= REACH:
                term = STENCIL[abs(x - other)] * read(other, y)
                total = term if total is None else total + term
        return total

    def respond(chunk, carry):
        ahead = 16 * fields
        speeds = window(speed_ref, chunk * 16, TILES * cells - 16)
        low_side, high_side = (window(ref, chunk * 16 * fields, LAYERS * slab - ahead) for ref in (below, above))
        inside = window(second, chunk * 16 * fields, PAIR * slab - ahead)
        base = window(third, chunk * 16 * fields, PAIR * flat - ahead)
        z_parts = window(z_term, chunk * 16 * fields, PAIR * flat - ahead)

        def load(layer, y):
            if layer < 0:
                ref, layer = low_side, layer + LAYERS
            elif layer >= PAIR:
                ref, layer = high_side, layer - PAIR
            else:
                ref = inside
            row = layer * slab + (REACH + y) * fields
            return ref[row : row + fields, :]

        for tile in range(TILES):
            sample = samples[tile]
            read = kept_rows(load)
            for y in range(16):
                for x in range(LAYERS):
                    cell = x * 32 + y
                    layer = (tile - 2) * LAYERS + x
                    speed = spread(speeds, tile * cells + cell, fields)
                    if tile in (0, 5):
                        value = speed * far(read, layer, y, -4, 11)
                    elif tile in (2, 3):
                        outside = far(read, layer, y, -4, -1) if tile == 2 else far(read, layer, y, 8, 11)
                        row = ((tile - 2) * cells + cell) * fields
                        value = base[row : row + fields, :] + speed * outside
                    else:
                        row = (tile // 4 * cells + cell) * fields
                        lap = laplacian(read, layer, y, z_parts[row : row + fields, :], -4, 11)
                        value = 2.0 * read(layer, y) + speed * lap
                    row = (x * 4 + y // 4) * fields
                    side = y % 4 * HALF
                    sample[row : row + fields, side : side + HALF] = value
            hot = cell_ref[tile * PLACES : (tile + 1) * PLACES, :]
            picked = jnp.dot(jnp.concatenate(split(sample[...]), axis=0), hot, preferred_element_type=F32)
            picked = picked[: 16 * fields, :] + picked[16 * fields :, :]
            rows = slice(tile * fields, (tile + 1) * fields)
            line = line_ref[rows, :]
            total = total_ref[rows, :]
            for i in range(16):
                chosen = line == i // 4 * 8 + chunk * 4 + i % 4
                total = total + jnp.where(chosen, picked[i * fields : (i + 1) * fields, :], 0.0)
            total_ref[rows, :] = total
        return carry

    lax.fori_loop(0, 2, respond, 0)

    for group in range(peers // 16):
        lefts, rights = [], []
        for tile in range(TILES):
            rows = slice(tile * fields, (tile + 1) * fields)
            value = total_ref[rows, :] * weight_ref[rows, :]
            high = value.astype(BF16).astype(F32)
            owner = owner_ref[rows, :]
            for part in (high, value - high):
                pieces = [jnp.where(owner == group * 16 + i, part, 0.0) for i in range(16)]
                lefts.append(jnp.concatenate(pieces, axis=0).astype(BF16))
                rights.append(slot_ref[tile * HALF : (tile + 1) * HALF, :])
        result = lax.dot_general(
            jnp.concatenate(lefts, axis=1), jnp.concatenate(rights, axis=1), NT, preferred_element_type=F32
        )
        table[group * 16 * fields : (group + 1) * 16 * fields, :] = result
    place = lax.broadcasted_iota(jnp.int32, (peers, HALF), 0)
    scales = jnp.zeros((peers, HALF), F32)
    for position, value in ((me[0], mine), (me[0] + 1 - 2 * (me[0] % 2), theirs)):
        scale = jnp.broadcast_to(value[cells + 16 : cells + 17, :], (peers, HALF))
        scales = jnp.where(place == position, scale, scales)
    table[peers * fields :, :] = scales


def basis_parts(first, basis, when, out):
    rank = basis.shape[0] // HALF

    def body(group, carry):
        here = window(basis, (first + group) * 8, basis.shape[0] - 15 * 8)
        there = window(out, group * rank, rank)
        for step in range(8):
            high, low = split(here[pl.ds(step, rank, stride=HALF), :])
            there[:, step * 256 : step * 256 + HALF] = high
            there[:, step * 256 + HALF : (step + 1) * 256] = low
        return carry

    lax.fori_loop(0, 8, body, 0)


def turn_places(fields, place_ref, when, hot_ref):
    entries = place_ref.shape[1]
    lane = lax.broadcasted_iota(jnp.int32, (entries, HALF), 1)
    for tile in range(TILES):
        row = place_ref[tile * fields : tile * fields + 1, :]
        column = jnp.transpose(jnp.broadcast_to(row, (HALF, entries))).astype(jnp.int32)
        for part in range(PLACES // HALF):
            hot = jnp.where(column == lane + part * HALF, 1.0, 0.0).astype(BF16)
            hot_ref[tile * entries : (tile + 1) * entries, part * HALF : (part + 1) * HALF] = hot


def adjoint(
    fields, peers, me, table, hot_ref, slot_ref, speed_ref, line_ref, owner_ref, weight_ref, turned, push_ref,
    prior_ref, band_ref, own_basis, own_basis_two, other_basis, other_basis_two, kept, lent, coeffs,
    high_ref, low_ref, inner_two, outer_two, inner_one, outer_one, z_term, image, scaled, *scratch,
):
    *lefts, image_parts = scratch
    entries = line_ref.shape[1]
    cells = LAYERS * 32
    rank = own_basis.shape[0] // 8
    slab, flat = PADDED * fields, 32 * fields
    ahead = 24 * fields
    clear_margins(inner_two, TILES * LAYERS, fields)
    clear_margins(inner_one, 2 * PAIR, fields)
    for owner in range(peers):
        rows = slice(owner * fields, (owner + 1) * fields)
        scaled[rows, :] = table[rows, :] * table[peers * fields + owner : peers * fields + owner + 1, :]
    for tile in range(TILES):
        rows = slice(tile * fields, (tile + 1) * fields)
        owner = owner_ref[rows, :]
        hot = slot_ref[tile * HALF : (tile + 1) * HALF, :]
        hot = jnp.concatenate([hot, hot], axis=0)
        total = jnp.zeros((fields, entries), F32)
        for group in range(peers // 16):
            parts = split(scaled[group * 16 * fields : (group + 1) * 16 * fields, :])
            found = jnp.dot(jnp.concatenate(parts, axis=1), hot, preferred_element_type=F32)
            for i in range(16):
                total = total + jnp.where(owner == group * 16 + i, found[i * fields : (i + 1) * fields, :], 0.0)
        value = total * weight_ref[rows, :]
        high = value.astype(BF16).astype(F32)
        high_ref[rows, :] = high
        low_ref[rows, :] = value - high

    for tile in range(TILES):
        left = lefts[tile]
        rows = slice(tile * fields, (tile + 1) * fields)
        line, high, low = line_ref[rows, :], high_ref[rows, :], low_ref[rows, :]
        for i in range(0, 32, 2):
            chosen = [line == i, line == i + 1]
            row = slice(i * fields, (i + 2) * fields)
            for part, side in ((high, slice(0, entries)), (low, slice(entries, 2 * entries))):
                both = [jnp.where(which, part, 0.0) for which in chosen]
                left[row, side] = jnp.concatenate(both, axis=0).astype(BF16)
        hot = hot_ref[tile * entries : (tile + 1) * entries, :]
        value = jnp.dot(left[...], jnp.concatenate([hot, hot], axis=0), preferred_element_type=F32)
        for i in range(32):
            for step in range(4):
                layer, y = tile * LAYERS + i // 8, i % 8 * 4 + step
                now = value[i * fields : (i + 1) * fields, step * HALF : (step + 1) * HALF]
                if 1 <= tile <= 4:
                    row = ((layer - LAYERS) * 32 + y) * fields
                    outer_two[row : row + fields, :] = now
                speed = spread(speed_ref, layer * 32 + y, fields)
                row = layer * slab + (REACH + y) * fields
                inner_two[row : row + fields, :] = speed * now
        if 1 <= tile <= 4:
            along_z(inner_two, tile * LAYERS, LAYERS, fields, band_ref, z_term, (tile - 1) * cells * fields)

    def step_one(index, carry):
        pair, chunk = index // 4, index % 4
        start, skip = pair * PAIR * slab + chunk * 8 * fields, pair * PAIR * flat + chunk * 8 * fields
        here = window(inner_two, start, 2 * PAIR * slab - ahead)
        two, one, z_part = (window(ref, skip, PAIR * flat - ahead) for ref in (outer_two, outer_one, z_term))
        out = window(inner_one, start, PAIR * slab - ahead)
        speed = window(speed_ref, cells + pair * 2 * cells + chunk * 8, 2 * cells - 24)

        def load(layer, y):
            row = (layer + LAYERS) * slab + (REACH + y) * fields
            return here[row : row + fields, :]

        for side in range(2):
            get = kept_rows(load)
            for y in range(8):
                for x in range(side * LAYERS, (side + 1) * LAYERS):
                    cell = x * 32 + y
                    row = slice(cell * fields, (cell + 1) * fields)
                    now = 2.0 * two[row, :] + laplacian(get, x, y, z_part[row, :], -4, 11)
                    one[row, :] = now
                    row = x * slab + (REACH + y) * fields
                    out[row : row + fields, :] = spread(speed, cell, fields) * now
        return carry

    lax.fori_loop(0, 8, step_one, 0)
    along_z(inner_one, LAYERS, PAIR, fields, band_ref, z_term)
    mine = me[0] % 2

    def step_two(chunk, total):
        skip = chunk * 8 * fields
        here = window(inner_one, skip, 2 * PAIR * slab - ahead)
        two_rows, one_rows = (window(ref, LAYERS * flat + skip, PAIR * flat - ahead) for ref in (outer_two, outer_one))
        z_part, there, out = (window(ref, skip, PAIR * flat - ahead) for ref in (z_term, turned, image))
        push = window(push_ref, chunk * 8, 6 * cells - 24)
        damping = window(prior_ref, chunk * 8, 2 * cells - 24)

        def load(layer, y):
            row = (layer + LAYERS) * slab + (REACH + y) * fields
            return here[row : row + fields, :]

        nothing = jnp.zeros((fields, HALF), F32)
        for side in range(2):
            get = kept_rows(load)
            for y in range(8):
                for x in range(side * LAYERS, (side + 1) * LAYERS):
                    cell = x * 32 + y
                    row = slice(cell * fields, (cell + 1) * fields)
                    two, one = two_rows[row, :], one_rows[row, :]
                    zero = 2.0 * one - two + laplacian(get, x, y, z_part[row, :], -4, 11)
                    value = spread(push, cell, fields) * zero
                    value = value + spread(push, 2 * cells + cell, fields) * one
                    value = value + spread(push, 4 * cells + cell, fields) * two
                    value = value + spread(damping, cell, fields) * there[row, :]
                    out[row, :] = value
                    high = value.astype(BF16).astype(F32)
                    rows, lane = slice(x * 2 * fields, (x + 1) * 2 * fields), y * 256
                    image_parts[rows, lane : lane + HALF] = jnp.concatenate([high, value - high], axis=0).astype(BF16)
                    image_parts[rows, lane + HALF : lane + 256] = jnp.concatenate([high, nothing], axis=0).astype(BF16)
        for side, pieces in ((mine, (own_basis, own_basis_two)), (1 - mine, (other_basis, other_basis_two))):
            for x in range(LAYERS):
                columns = pieces[x // 2][at((x % 2 * 4 + chunk) * rank, rank), :]
                parts = image_parts[at((side * LAYERS + x) * 2 * fields, 2 * fields), :]
                total = total + lax.dot_general(columns, parts, NT, preferred_element_type=F32)
        return total

    total = lax.fori_loop(0, 4, step_two, jnp.zeros((rank, 2 * fields), F32))
    both = jnp.concatenate([total[:, :fields] + total[:, fields:], jnp.zeros((rank, HALF - fields), F32)], axis=1)
    coeffs[...] = jnp.transpose(both)[:fields, :]
    kept[...] = image[at(mine * LAYERS * flat, LAYERS * flat), :]
    lent[...] = image[at((1 - mine) * LAYERS * flat, LAYERS * flat), :]


def remainder(fields, me, image, borrowed, basis, basis_two, *rest):
    *shares, out, coeffs, natural, sem = rest
    rank = coeffs.shape[1]
    half = fields // 2
    mine = me[0] % 2
    while len(shares) > 1:
        shares = [shares[i][...] + shares[i + 1][...] for i in range(0, len(shares), 2)]
    total = shares[0][...]
    coeffs[at(mine * half, half), :] = total[:half, :]
    coeffs[at((1 - mine) * half, half), :] = total[half:, :]
    parts = jnp.concatenate(split(total), axis=0)
    whole = natural.reshape(out.shape)
    first, second = (window(natural, side * half * HALF, half * HALF) for side in (mine, 1 - mine))

    def leave(x):
        return pltpu.make_async_copy(whole.at[:, x], out.at[:, x], sem.at[x])

    for x in range(LAYERS):
        for part in range(4):
            columns = (basis, basis_two)[x // 2][(x % 2 * 4 + part) * rank : (x % 2 * 4 + part + 1) * rank, :]
            both = jnp.dot(parts, columns, preferred_element_type=F32)
            cell = x * 32 + part * 8
            results = ([], [])
            for step in range(8):
                side = step * 256
                along = both[:fields, side : side + HALF] + both[:fields, side + HALF : side + 256]
                along = along + both[fields:, side : side + HALF]
                row = slice((cell + step) * half, (cell + step + 1) * half)
                results[0].append(image[row, :] - along[:half, :])
                results[1].append(borrowed[row, :] - along[half:, :])
            for ref, values in zip((first, second), results):
                values = jnp.swapaxes(jnp.stack(values, axis=0), 0, 1)
                for p in range(half):
                    ref[p * HALF + cell : p * HALF + cell + 8, :] = values[p]
        leave(x).start()
    for x in range(LAYERS):
        leave(x).wait()


def call(kernel, inputs, out_shape, scratch, flops, size, scalars=0, far=0, far_out=0, room=16):
    smem = pl.BlockSpec(memory_space=pltpu.SMEM)
    vmem = pl.BlockSpec(memory_space=pltpu.VMEM)
    hbm = pl.BlockSpec(memory_space=pltpu.HBM)
    inputs = [
        pltpu.with_memory_space_constraint(array, pltpu.HBM) if scalars <= i < scalars + far else array
        for i, array in enumerate(inputs)
    ]
    return pl.pallas_call(
        kernel,
        out_shape=out_shape,
        in_specs=[smem] * scalars + [hbm] * far + [vmem] * (len(inputs) - scalars - far),
        out_specs=[hbm] * far_out + [vmem] * (len(out_shape) - far_out),
        scratch_shapes=scratch,
        cost_estimate=pl.CostEstimate(flops=flops, bytes_accessed=size, transcendentals=0),
        compiler_params=pltpu.CompilerParams(vmem_limit_bytes=room * 2**20),
    )(*inputs)


def struct(*shape, dtype=F32):
    return jax.ShapeDtypeStruct(shape, dtype)


def swapped(array, axis, bits):
    count = lax.axis_size(axis)
    return lax.ppermute(array, axis, [(i, i ^ bits) for i in range(count)])


def local(
    probes,
    sources,
    kappa,
    prior,
    basis,
    entry_cell,
    entry_owner,
    entry_slot,
    entry_weight,
    entry_count,
    trace_weight,
):
    rank = basis.shape[0]
    fields = probes.shape[0] // 2
    entries = entry_cell.shape[0]
    peers = lax.axis_size("space")
    slab, flat = PADDED * fields, 32 * fields
    cells = LAYERS * 32
    rows = entries // HALF
    basis = basis.reshape(rank * cells, HALF)
    me = lax.axis_index("space").astype(jnp.int32).reshape(1)

    own, probes_near, sources_near, prior_near, lent, matrix = call(
        pack,
        (
            entry_count,
            me,
            probes.reshape(2 * fields * cells, HALF),
            sources.reshape(3 * cells, HALF),
            prior.reshape(cells, HALF),
            kappa.reshape(cells, HALF),
            entry_cell.reshape(rows, HALF),
            entry_owner.reshape(rows, HALF),
            entry_slot.reshape(rows, HALF),
            entry_weight.reshape(rows, HALF),
            trace_weight.reshape(1, HALF),
        ),
        [
            struct(cells + 4 * rows + 8, HALF),
            struct(fields * cells, HALF),
            struct(3 * cells, HALF),
            struct(cells, HALF),
            struct((fields + 4) * cells, HALF),
            struct(256, 256, dtype=BF16),
        ],
        [pltpu.VMEM((3, rows, HALF), jnp.int32), pltpu.VMEM((16, HALF), F32), pltpu.SemaphoreType.DMA((12,))],
        100_000,
        2 * 2**20,
        scalars=2,
        far=9,
    )
    partner = swapped(own, "space", 1)
    lent, partner = lax.optimization_barrier((lent, partner))
    borrowed = swapped(lent, "space", 1)
    passed = lax.ppermute(
        jnp.concatenate([own, partner], axis=0),
        "space",
        [pair for i in range(1, peers - 1, 2) for pair in ((i, i + 1), (i + 1, i))],
    )

    turned, first, second, third, push, damping = call(
        functools.partial(forward_own, fields),
        (me, probes_near, sources_near, prior_near, own, partner, borrowed, matrix),
        [
            struct(PAIR * flat, HALF),
            struct(PAIR * slab, HALF),
            struct(PAIR * slab, HALF),
            struct(PAIR * flat, HALF),
            struct(6 * cells, HALF),
            struct(2 * cells, HALF),
        ],
        [pltpu.VMEM((PAIR * flat, HALF), F32), pltpu.VMEM((2 * cells, HALF), F32)],
        600_000_000,
        6 * 2**20,
        scalars=1,
    )
    passed, second = lax.optimization_barrier((passed, second))
    across = swapped(passed, "space", 1)
    across, basis_there = lax.optimization_barrier((across, basis))
    basis_there = swapped(basis_there, "space", 1)
    table, place, slot_hot, speed, line, owner, weight = call(
        functools.partial(forward_window, fields, peers),
        (me, first, second, third, own, partner, passed, across, matrix),
        [
            struct(peers * (fields + 1), HALF),
            struct(TILES * fields, entries),
            struct(TILES * HALF, entries, dtype=BF16),
            struct(TILES * cells, HALF),
            struct(TILES * fields, entries, dtype=jnp.int32),
            struct(TILES * fields, entries, dtype=jnp.int32),
            struct(TILES * fields, entries),
        ],
        [
            pltpu.VMEM((TILES * PLACES, entries), BF16),
            pltpu.VMEM((LAYERS * slab, HALF), F32),
            pltpu.VMEM((LAYERS * slab, HALF), F32),
            pltpu.VMEM((PAIR * flat, HALF), F32),
            pltpu.VMEM((TILES * fields, entries), F32),
        ]
        + [pltpu.VMEM((16 * fields, PLACES), F32)] * TILES,
        3_000_000_000,
        6 * 2**20,
        scalars=1,
        room=20,
    )
    columns = []
    bits = 2
    while bits < peers:
        arrived = swapped(table, "space", bits)
        for i in ((0,), (1,), (2, 3))[len(columns)] if len(columns) < 3 else ():
            (some,) = call(
                functools.partial(basis_parts, 8 * (i % 2)),
                ((basis, basis_there)[i // 2], table),
                [struct(8 * rank, 2048, dtype=BF16)],
                [],
                10_000_000,
                4 * 2**20,
            )
            columns.append(some)
        if bits == 2:
            (turned_hot,) = call(
                functools.partial(turn_places, fields),
                (place, table),
                [struct(TILES * entries, PLACES, dtype=BF16)],
                [],
                10_000_000,
                4 * 2**20,
            )
            arrived, turned_hot = lax.optimization_barrier((arrived, turned_hot))
        arrived, columns = lax.optimization_barrier((arrived, columns))
        table = table + arrived
        bits *= 2
    kept, lent, coeffs = call(
        functools.partial(adjoint, fields, peers),
        (me, table, turned_hot, slot_hot, speed, line, owner, weight, turned, push, damping, matrix, *columns),
        [struct(LAYERS * flat, HALF), struct(LAYERS * flat, HALF), struct(fields, rank)],
        [
            pltpu.VMEM((TILES * fields, entries), F32),
            pltpu.VMEM((TILES * fields, entries), F32),
            pltpu.VMEM((TILES * LAYERS * slab, HALF), F32),
            pltpu.VMEM((2 * PAIR * flat, HALF), F32),
            pltpu.VMEM((2 * PAIR * slab, HALF), F32),
            pltpu.VMEM((2 * PAIR * flat, HALF), F32),
            pltpu.VMEM((2 * PAIR * flat, HALF), F32),
            pltpu.VMEM((PAIR * flat, HALF), F32),
            pltpu.VMEM((peers * fields, HALF), F32),
        ]
        + [pltpu.VMEM((32 * fields, 2 * entries), BF16)] * TILES
        + [pltpu.VMEM((2 * PAIR * fields, 2048), BF16)],
        5_000_000_000,
        10 * 2**20,
        scalars=1,
        room=30,
    )
    coeffs = jnp.concatenate([coeffs, swapped(coeffs, "space", 1)], axis=0)
    lent, coeffs = lax.optimization_barrier((lent, coeffs))
    borrowed = swapped(lent, "space", 1)
    bits = 2
    while bits * 4 < peers:
        coeffs = coeffs + swapped(coeffs, "space", bits)
        bits *= 2
    shares = [swapped(coeffs, "space", bits * i) for i in (3, 2, 1)] + [coeffs]
    hess_probe, coeffs = call(
        functools.partial(remainder, 2 * fields),
        (me, kept, borrowed, *columns[:2], *shares),
        [struct(*probes.shape), struct(2 * fields, rank)],
        [pltpu.VMEM((2 * fields * cells, HALF), F32), pltpu.SemaphoreType.DMA((LAYERS,))],
        200_000_000,
        6 * 2**20,
        scalars=1,
        far_out=1,
    )
    return hess_probe, coeffs.T


def solution(mesh):
    return jax.shard_map(
        local,
        mesh=mesh,
        in_specs=(
            P("group", "space", None, None),
            P(None, ("group", "space"), None, None),
            P(("group", "space"), None, None),
            P(("group", "space"), None, None),
            P("group", "space", None, None),
            P(("group", "space")),
            P(("group", "space")),
            P(("group", "space")),
            P(("group", "space")),
            P(("group", "space")),
            P(("group", "space")),
        ),
        out_specs=(P("group", "space", None, None), P("group", None)),
        check_vma=False,
    )
```

```python
import functools

import jax
import jax.numpy as jnp
from jax import lax
from jax.experimental import pallas as pl
from jax.experimental.pallas import tpu as pltpu
from jax.sharding import PartitionSpec as P

STENCIL = (-205.0 / 72.0, 8.0 / 5.0, -1.0 / 5.0, 8.0 / 315.0, -1.0 / 560.0)
CENTER = 3.0 * STENCIL[0]
REACH = 4
LAYERS = 4
PAIR = 8
TILES = 6
PADDED = 40
HALF = 128
PLACES = 512
F32 = jnp.float32
BF16 = jnp.bfloat16
NT = (((1,), (1,)), ((), ()))


def split(value):
    high = value.astype(BF16)
    low = (value - high.astype(F32)).astype(BF16)
    return high, low


def at(row, count=16):
    return pl.ds(pl.multiple_of(row, 8), count)


def window(ref, start, size):
    return ref.at[pl.ds(pl.multiple_of(start, 8), size)]


def kept_rows(load):
    rows = {}

    def get(layer, y):
        if (layer, y) not in rows:
            rows[layer, y] = load(layer, y)
        return rows[layer, y]

    return get


def spread(ref, row, fields):
    return jnp.broadcast_to(ref[pl.ds(row, 1), :], (fields, HALF))


def clear_margins(ref, layers, fields):
    margin = jnp.zeros((REACH * fields, HALF), F32)
    for layer in range(layers):
        start = layer * PADDED * fields
        ref[start : start + REACH * fields, :] = margin
        start += (PADDED - REACH) * fields
        ref[start : start + REACH * fields, :] = margin


def along_z(ref, first, layers, fields, band_ref, out_ref, row=0):
    pieces = [ref[at(((first + x) * PADDED + REACH) * fields, 32 * fields), :] for x in range(layers)]
    high, low = split(jnp.concatenate(pieces, axis=0))
    both = jnp.dot(jnp.concatenate([high, low], axis=1), band_ref[...], preferred_element_type=F32)
    out_ref[at(row, layers * 32 * fields), :] = both[:, :HALF] + both[:, HALF:]


def laplacian(get, x, y, z_term, lowest, highest):
    total = z_term
    for k in range(1, REACH + 1):
        ring = get(x, y + k) + get(x, y - k)
        if x + k <= highest:
            ring = ring + get(x + k, y)
        if x - k >= lowest:
            ring = ring + get(x - k, y)
        total = total + STENCIL[k] * ring
    return total


def pack(
    count, me, probes, sources, prior, kappa, cell, owner, slot, weight, scale,
    statics, probes_out, sources_out, prior_out, lent, band_ref, small_int, small_float, sem,
):
    rows = cell.shape[0]
    cells = kappa.shape[0]
    half = probes_out.shape[0]
    mine = me[0] % 2
    other = probes.at[pl.ds(pl.multiple_of((1 - mine) * half, 8), half)]
    small = [
        pltpu.make_async_copy(kappa, statics.at[pl.ds(0, cells)], sem.at[0]),
        pltpu.make_async_copy(cell, small_int.at[0], sem.at[1]),
        pltpu.make_async_copy(owner, small_int.at[1], sem.at[2]),
        pltpu.make_async_copy(slot, small_int.at[2], sem.at[3]),
        pltpu.make_async_copy(weight, small_float.at[pl.ds(0, rows)], sem.at[4]),
        pltpu.make_async_copy(scale, small_float.at[pl.ds(8, 1)], sem.at[5]),
    ]
    large = [
        pltpu.make_async_copy(other, lent.at[pl.ds(0, half)], sem.at[6]),
        pltpu.make_async_copy(sources, lent.at[pl.ds(half, 3 * cells)], sem.at[7]),
        pltpu.make_async_copy(prior, lent.at[pl.ds(half + 3 * cells, cells)], sem.at[8]),
        pltpu.make_async_copy(probes.at[pl.ds(pl.multiple_of(mine * half, 8), half)], probes_out, sem.at[9]),
        pltpu.make_async_copy(sources, sources_out, sem.at[10]),
        pltpu.make_async_copy(prior, prior_out, sem.at[11]),
    ]
    for copy in small + large:
        copy.start()
    apart = lax.broadcasted_iota(jnp.int32, (HALF, HALF), 0) - lax.broadcasted_iota(jnp.int32, (HALF, HALF), 1)
    full = jnp.where(apart == 0, CENTER, jnp.zeros((HALF, HALF), F32))
    for reach in range(1, REACH + 1):
        full = jnp.where(jnp.abs(apart) == reach, STENCIL[reach], full)
    high, low = split(full)
    band_ref[0:HALF, 0:HALF] = high
    band_ref[HALF:, 0:HALF] = high
    band_ref[0:HALF, HALF:] = low
    band_ref[HALF:, HALF:] = jnp.zeros_like(low)
    for copy in small:
        copy.wait()
    for i in range(3):
        statics[cells + i * rows : cells + (i + 1) * rows, :] = small_int[i].astype(F32)
    place = lax.broadcasted_iota(jnp.int32, (rows, HALF), 0) * HALF
    place = place + lax.broadcasted_iota(jnp.int32, (rows, HALF), 1)
    live = jnp.where(place < count[0], small_float[0:rows, :], 0.0)
    statics[cells + 3 * rows : cells + 4 * rows, :] = live
    statics[cells + 4 * rows : cells + 4 * rows + 8, :] = jnp.broadcast_to(small_float[8:9, :], (8, HALF))
    for copy in large:
        copy.wait()


def forward_own(
    fields, me, probes, sources, prior, own, partner, borrowed, band_ref,
    turned, first, second, third, push_ref, prior_ref, z_term, speed_ref,
):
    slab, flat, cells = PADDED * fields, 32 * fields, LAYERS * 32
    ahead = 24 * fields
    half = probes.shape[0]
    mine = me[0] % 2
    clear_margins(first, PAIR, fields)
    clear_margins(second, PAIR, fields)
    lent = borrowed.at[pl.ds(half, 4 * cells)]
    for side, pushes, damping, statics in ((mine, sources, prior, own), (1 - mine, lent, None, partner)):
        for i in range(3):
            push_ref[at(i * 2 * cells + side * cells, cells), :] = pushes[i * cells : (i + 1) * cells, :]
        place = at(side * cells, cells)
        prior_ref[place, :] = lent[3 * cells :, :] if damping is None else damping[...]
        speed_ref[place, :] = statics[0:cells, :]

    def load(chunk, carry):
        for side, ref in ((mine, probes), (1 - mine, borrowed)):
            there = window(turned, side * LAYERS * flat + chunk * 8 * fields, LAYERS * flat - ahead)
            padded = window(first, side * LAYERS * slab + chunk * 8 * fields, LAYERS * slab - ahead)
            here = window(ref, chunk * 8, half - 24)
            push = window(push_ref, side * cells + chunk * 8, cells - 24)
            for x in range(LAYERS):
                rows = [here[p * cells + x * 32 : p * cells + x * 32 + 8, :] for p in range(fields)]
                values = jnp.swapaxes(jnp.stack(rows, axis=0), 0, 1)
                for y in range(8):
                    cell = x * 32 + y
                    there[cell * fields : (cell + 1) * fields, :] = values[y]
                    row = x * slab + (REACH + y) * fields
                    padded[row : row + fields, :] = values[y] * spread(push, cell, fields)
        return carry

    lax.fori_loop(0, 4, load, 0)

    def sweep(field, emit):
        along_z(field, 0, PAIR, fields, band_ref, z_term)

        def body(chunk, carry):
            padded = window(field, chunk * 8 * fields, PAIR * slab - ahead)
            z_part = window(z_term, chunk * 8 * fields, PAIR * flat - ahead)
            speed = window(speed_ref, chunk * 8, 2 * cells - 24)
            push = window(push_ref, chunk * 8, 6 * cells - 24)
            there = window(turned, chunk * 8 * fields, PAIR * flat - ahead)
            put = emit(chunk)

            def load(layer, y):
                row = layer * slab + (REACH + y) * fields
                return padded[row : row + fields, :]

            for side in range(2):
                get = kept_rows(load)
                for y in range(8):
                    for x in range(side * LAYERS, (side + 1) * LAYERS):
                        cell = x * 32 + y
                        row = slice(cell * fields, (cell + 1) * fields)
                        change = spread(speed, cell, fields) * laplacian(get, x, y, z_part[row, :], 0, PAIR - 1)
                        put(x, y, get(x, y), change, there[row, :], push)
            return carry

        lax.fori_loop(0, 4, body, 0)

    def step_one(chunk):
        out = window(second, chunk * 8 * fields, PAIR * slab - ahead)

        def put(x, y, now, change, probe, push):
            change = change + probe * spread(push, 2 * cells + x * 32 + y, fields)
            row = x * slab + (REACH + y) * fields
            out[row : row + fields, :] = 2.0 * now + change

        return put

    sweep(first, step_one)

    def step_two(chunk):
        before = window(first, chunk * 8 * fields, PAIR * slab - ahead)
        out = window(third, chunk * 8 * fields, PAIR * flat - ahead)

        def put(x, y, now, change, probe, push):
            row = x * slab + (REACH + y) * fields
            change = change - before[row : row + fields, :]
            cell = x * 32 + y
            change = change + probe * spread(push, 4 * cells + cell, fields)
            out[cell * fields : (cell + 1) * fields, :] = 2.0 * now + change

        return put

    sweep(second, step_two)


def entry_row(value, row):
    return jnp.concatenate([value[row + i : row + i + 1, :] for i in range(4)], axis=1)


def forward_window(
    fields, peers, me, first, second, third, own, partner, passed, across, band_ref,
    table, place_ref, slot_ref, speed_ref, line_ref, owner_ref, weight_ref,
    cell_ref, below, above, z_term, total_ref, *samples,
):
    entries = line_ref.shape[1]
    cells = LAYERS * 32
    length = own.shape[0]
    odd = me[0] % 2 == 1
    slab, flat = PADDED * fields, 32 * fields
    clear_margins(below, LAYERS, fields)
    clear_margins(above, LAYERS, fields)
    total_ref[...] = jnp.zeros_like(total_ref)
    mine, theirs = own[...], partner[...]
    low = jnp.where(odd, across[...], passed[...])
    high = jnp.where(odd, passed[...], across[...])
    tiles = (
        low[length:, :],
        low[0:length, :],
        jnp.where(odd, theirs, mine),
        jnp.where(odd, mine, theirs),
        high[0:length, :],
        high[length:, :],
    )
    place = lax.broadcasted_iota(jnp.int32, (PLACES, entries), 0)
    slot_place = lax.broadcasted_iota(jnp.int32, (HALF, entries), 0)
    for tile, value in enumerate(tiles):
        speed_ref[tile * cells : (tile + 1) * cells, :] = value[0:cells, :]
        cell = entry_row(value, cells).astype(jnp.int32)
        owner = entry_row(value, cells + 4).astype(jnp.int32)
        slot = entry_row(value, cells + 8).astype(jnp.int32)
        weight = entry_row(value, cells + 12)
        hot = jnp.where(place == jnp.bitwise_and(cell, PLACES - 1), 1.0, 0.0)
        cell_ref[tile * PLACES : (tile + 1) * PLACES, :] = hot.astype(BF16)
        hot = jnp.where(slot_place == slot, 1.0, 0.0)
        slot_ref[tile * HALF : (tile + 1) * HALF, :] = hot.astype(BF16)
        rows = slice(tile * fields, (tile + 1) * fields)
        line_ref[rows, :] = jnp.broadcast_to(lax.shift_right_logical(cell, 9), (fields, entries))
        place_ref[rows, :] = jnp.broadcast_to(jnp.bitwise_and(cell, PLACES - 1), (fields, entries)).astype(F32)
        owner_ref[rows, :] = jnp.broadcast_to(owner, (fields, entries))
        weight_ref[rows, :] = jnp.broadcast_to(weight, (fields, entries))

    def outward(chunk, carry):
        ahead = 24 * fields
        speed = window(speed_ref, chunk * 8, TILES * cells - 24)
        here = window(first, chunk * 8 * fields, PAIR * slab - ahead)
        down_out, up_out = (window(ref, chunk * 8 * fields, LAYERS * slab - ahead) for ref in (below, above))
        for y in range(8):
            rows = [slice(x * slab + (REACH + y) * fields, x * slab + (REACH + y + 1) * fields) for x in range(PAIR)]
            field = [here[row, :] for row in rows]
            for x in range(LAYERS):
                up = sum(STENCIL[4 + x - other] * field[4 + other] for other in range(x, LAYERS))
                down = sum(STENCIL[4 + other - x] * field[other] for other in range(x + 1))
                up_out[rows[x], :] = spread(speed, 4 * cells + x * 32 + y, fields) * up
                down_out[rows[x], :] = spread(speed, cells + x * 32 + y, fields) * down
        return carry

    lax.fori_loop(0, 4, outward, 0)
    along_z(below, 0, LAYERS, fields, band_ref, z_term, 0)
    along_z(above, 0, LAYERS, fields, band_ref, z_term, cells * fields)

    def far(read, x, y, lowest, highest):
        total = None
        for other in range(lowest, highest + 1):
            if 1 <= abs(x - other) <= REACH:
                term = STENCIL[abs(x - other)] * read(other, y)
                total = term if total is None else total + term
        return total

    def respond(chunk, carry):
        ahead = 16 * fields
        speeds = window(speed_ref, chunk * 16, TILES * cells - 16)
        low_side, high_side = (window(ref, chunk * 16 * fields, LAYERS * slab - ahead) for ref in (below, above))
        inside = window(second, chunk * 16 * fields, PAIR * slab - ahead)
        base = window(third, chunk * 16 * fields, PAIR * flat - ahead)
        z_parts = window(z_term, chunk * 16 * fields, PAIR * flat - ahead)

        def load(layer, y):
            if layer < 0:
                ref, layer = low_side, layer + LAYERS
            elif layer >= PAIR:
                ref, layer = high_side, layer - PAIR
            else:
                ref = inside
            row = layer * slab + (REACH + y) * fields
            return ref[row : row + fields, :]

        for tile in range(TILES):
            sample = samples[tile]
            read = kept_rows(load)
            for y in range(16):
                for x in range(LAYERS):
                    cell = x * 32 + y
                    layer = (tile - 2) * LAYERS + x
                    speed = spread(speeds, tile * cells + cell, fields)
                    if tile in (0, 5):
                        value = speed * far(read, layer, y, -4, 11)
                    elif tile in (2, 3):
                        outside = far(read, layer, y, -4, -1) if tile == 2 else far(read, layer, y, 8, 11)
                        row = ((tile - 2) * cells + cell) * fields
                        value = base[row : row + fields, :] + speed * outside
                    else:
                        row = (tile // 4 * cells + cell) * fields
                        lap = laplacian(read, layer, y, z_parts[row : row + fields, :], -4, 11)
                        value = 2.0 * read(layer, y) + speed * lap
                    row = (x * 4 + y // 4) * fields
                    side = y % 4 * HALF
                    sample[row : row + fields, side : side + HALF] = value
            hot = cell_ref[tile * PLACES : (tile + 1) * PLACES, :]
            picked = jnp.dot(jnp.concatenate(split(sample[...]), axis=0), hot, preferred_element_type=F32)
            picked = picked[: 16 * fields, :] + picked[16 * fields :, :]
            rows = slice(tile * fields, (tile + 1) * fields)
            line = line_ref[rows, :]
            total = total_ref[rows, :]
            for i in range(16):
                chosen = line == i // 4 * 8 + chunk * 4 + i % 4
                total = total + jnp.where(chosen, picked[i * fields : (i + 1) * fields, :], 0.0)
            total_ref[rows, :] = total
        return carry

    lax.fori_loop(0, 2, respond, 0)

    for group in range(peers // 16):
        lefts, rights = [], []
        for tile in range(TILES):
            rows = slice(tile * fields, (tile + 1) * fields)
            value = total_ref[rows, :] * weight_ref[rows, :]
            high = value.astype(BF16).astype(F32)
            owner = owner_ref[rows, :]
            for part in (high, value - high):
                pieces = [jnp.where(owner == group * 16 + i, part, 0.0) for i in range(16)]
                lefts.append(jnp.concatenate(pieces, axis=0).astype(BF16))
                rights.append(slot_ref[tile * HALF : (tile + 1) * HALF, :])
        result = lax.dot_general(
            jnp.concatenate(lefts, axis=1), jnp.concatenate(rights, axis=1), NT, preferred_element_type=F32
        )
        table[group * 16 * fields : (group + 1) * 16 * fields, :] = result
    place = lax.broadcasted_iota(jnp.int32, (peers, HALF), 0)
    scales = jnp.zeros((peers, HALF), F32)
    for position, value in ((me[0], mine), (me[0] + 1 - 2 * (me[0] % 2), theirs)):
        scale = jnp.broadcast_to(value[cells + 16 : cells + 17, :], (peers, HALF))
        scales = jnp.where(place == position, scale, scales)
    table[peers * fields :, :] = scales


def basis_parts(first, basis, when, out):
    rank = basis.shape[0] // HALF

    def body(group, carry):
        here = window(basis, (first + group) * 8, basis.shape[0] - 15 * 8)
        there = window(out, group * rank, rank)
        for start in range(0, rank, 16):
            blocks = []
            for block in (start, start + 8):
                rows = [here[k * HALF : k * HALF + 8, :] for k in range(block, block + 8)]
                blocks.append(jnp.swapaxes(jnp.stack(rows, axis=0), 0, 1))
            for step in range(8):
                high, low = split(jnp.concatenate([block[step] for block in blocks], axis=0))
                there[start : start + 16, step * 256 : step * 256 + HALF] = high
                there[start : start + 16, step * 256 + HALF : (step + 1) * 256] = low
        return carry

    lax.fori_loop(0, 8, body, 0)


def turn_places(fields, place_ref, when, hot_ref):
    entries = place_ref.shape[1]
    lane = lax.broadcasted_iota(jnp.int32, (entries, HALF), 1)
    for tile in range(TILES):
        row = place_ref[tile * fields : tile * fields + 1, :]
        column = jnp.transpose(jnp.broadcast_to(row, (HALF, entries))).astype(jnp.int32)
        for part in range(PLACES // HALF):
            hot = jnp.where(column == lane + part * HALF, 1.0, 0.0).astype(BF16)
            hot_ref[tile * entries : (tile + 1) * entries, part * HALF : (part + 1) * HALF] = hot


def adjoint(
    fields, peers, me, table, hot_ref, slot_ref, speed_ref, line_ref, owner_ref, weight_ref, turned, push_ref,
    prior_ref, band_ref, own_basis, own_basis_two, other_basis, other_basis_two, kept, lent, coeffs,
    high_ref, low_ref, inner_two, outer_two, inner_one, outer_one, z_term, image, scaled, *scratch,
):
    *lefts, image_parts = scratch
    entries = line_ref.shape[1]
    cells = LAYERS * 32
    rank = own_basis.shape[0] // 8
    slab, flat = PADDED * fields, 32 * fields
    ahead = 24 * fields
    clear_margins(inner_two, TILES * LAYERS, fields)
    clear_margins(inner_one, 2 * PAIR, fields)
    for owner in range(peers):
        rows = slice(owner * fields, (owner + 1) * fields)
        scaled[rows, :] = table[rows, :] * table[peers * fields + owner : peers * fields + owner + 1, :]
    for tile in range(TILES):
        rows = slice(tile * fields, (tile + 1) * fields)
        owner = owner_ref[rows, :]
        hot = slot_ref[tile * HALF : (tile + 1) * HALF, :]
        hot = jnp.concatenate([hot, hot], axis=0)
        total = jnp.zeros((fields, entries), F32)
        for group in range(peers // 16):
            parts = split(scaled[group * 16 * fields : (group + 1) * 16 * fields, :])
            found = jnp.dot(jnp.concatenate(parts, axis=1), hot, preferred_element_type=F32)
            for i in range(16):
                total = total + jnp.where(owner == group * 16 + i, found[i * fields : (i + 1) * fields, :], 0.0)
        value = total * weight_ref[rows, :]
        high = value.astype(BF16).astype(F32)
        high_ref[rows, :] = high
        low_ref[rows, :] = value - high

    def product(tile):
        left = lefts[tile]
        rows = slice(tile * fields, (tile + 1) * fields)
        line, high, low = line_ref[rows, :], high_ref[rows, :], low_ref[rows, :]
        for i in range(0, 32, 2):
            chosen = [line == i, line == i + 1]
            row = slice(i * fields, (i + 2) * fields)
            for part, side in ((high, slice(0, entries)), (low, slice(entries, 2 * entries))):
                both = [jnp.where(which, part, 0.0) for which in chosen]
                left[row, side] = jnp.concatenate(both, axis=0).astype(BF16)
        hot = hot_ref[tile * entries : (tile + 1) * entries, :]
        return jnp.dot(left[...], jnp.concatenate([hot, hot], axis=0), preferred_element_type=F32)

    def inject(tile, value):
        for i in range(32):
            for step in range(4):
                layer, y = tile * LAYERS + i // 8, i % 8 * 4 + step
                now = value[i * fields : (i + 1) * fields, step * HALF : (step + 1) * HALF]
                if 1 <= tile <= 4:
                    row = ((layer - LAYERS) * 32 + y) * fields
                    outer_two[row : row + fields, :] = now
                speed = spread(speed_ref, layer * 32 + y, fields)
                row = layer * slab + (REACH + y) * fields
                inner_two[row : row + fields, :] = speed * now
        if 1 <= tile <= 4:
            along_z(inner_two, tile * LAYERS, LAYERS, fields, band_ref, z_term, (tile - 1) * cells * fields)

    values = product(0)
    for tile in range(TILES):
        after = product(tile + 1) if tile + 1 < TILES else None
        inject(tile, values)
        values = after

    def step_one(index, carry):
        pair, chunk = index // 4, index % 4
        start, skip = pair * PAIR * slab + chunk * 8 * fields, pair * PAIR * flat + chunk * 8 * fields
        here = window(inner_two, start, 2 * PAIR * slab - ahead)
        two, one, z_part = (window(ref, skip, PAIR * flat - ahead) for ref in (outer_two, outer_one, z_term))
        out = window(inner_one, start, PAIR * slab - ahead)
        speed = window(speed_ref, cells + pair * 2 * cells + chunk * 8, 2 * cells - 24)

        def load(layer, y):
            row = (layer + LAYERS) * slab + (REACH + y) * fields
            return here[row : row + fields, :]

        for side in range(2):
            get = kept_rows(load)
            for y in range(8):
                for x in range(side * LAYERS, (side + 1) * LAYERS):
                    cell = x * 32 + y
                    row = slice(cell * fields, (cell + 1) * fields)
                    now = 2.0 * two[row, :] + laplacian(get, x, y, z_part[row, :], -4, 11)
                    one[row, :] = now
                    row = x * slab + (REACH + y) * fields
                    out[row : row + fields, :] = spread(speed, cell, fields) * now
        return carry

    lax.fori_loop(0, 8, step_one, 0)
    along_z(inner_one, LAYERS, PAIR, fields, band_ref, z_term)
    mine = me[0] % 2

    def step_two(chunk, total):
        skip = chunk * 8 * fields
        here = window(inner_one, skip, 2 * PAIR * slab - ahead)
        two_rows, one_rows = (window(ref, LAYERS * flat + skip, PAIR * flat - ahead) for ref in (outer_two, outer_one))
        z_part, there, out = (window(ref, skip, PAIR * flat - ahead) for ref in (z_term, turned, image))
        push = window(push_ref, chunk * 8, 6 * cells - 24)
        damping = window(prior_ref, chunk * 8, 2 * cells - 24)

        def load(layer, y):
            row = (layer + LAYERS) * slab + (REACH + y) * fields
            return here[row : row + fields, :]

        nothing = jnp.zeros((fields, HALF), F32)
        for side in range(2):
            get = kept_rows(load)
            for y in range(8):
                for x in range(side * LAYERS, (side + 1) * LAYERS):
                    cell = x * 32 + y
                    row = slice(cell * fields, (cell + 1) * fields)
                    two, one = two_rows[row, :], one_rows[row, :]
                    zero = 2.0 * one - two + laplacian(get, x, y, z_part[row, :], -4, 11)
                    value = spread(push, cell, fields) * zero
                    value = value + spread(push, 2 * cells + cell, fields) * one
                    value = value + spread(push, 4 * cells + cell, fields) * two
                    value = value + spread(damping, cell, fields) * there[row, :]
                    out[row, :] = value
                    high = value.astype(BF16).astype(F32)
                    rows, lane = slice(x * 2 * fields, (x + 1) * 2 * fields), y * 256
                    image_parts[rows, lane : lane + HALF] = jnp.concatenate([high, value - high], axis=0).astype(BF16)
                    image_parts[rows, lane + HALF : lane + 256] = jnp.concatenate([high, nothing], axis=0).astype(BF16)
        for side, pieces in ((mine, (own_basis, own_basis_two)), (1 - mine, (other_basis, other_basis_two))):
            for x in range(LAYERS):
                columns = pieces[x // 2][at((x % 2 * 4 + chunk) * rank, rank), :]
                parts = image_parts[at((side * LAYERS + x) * 2 * fields, 2 * fields), :]
                total = total + lax.dot_general(parts, columns, NT, preferred_element_type=F32)
        return total

    total = lax.fori_loop(0, 4, step_two, jnp.zeros((2 * fields, rank), F32))
    coeffs[...] = total[:fields, :] + total[fields:, :]
    kept[...] = image[at(mine * LAYERS * flat, LAYERS * flat), :]
    lent[...] = image[at((1 - mine) * LAYERS * flat, LAYERS * flat), :]


def remainder(fields, me, image, borrowed, basis, basis_two, found, told, out, coeffs, natural, sem):
    rank = coeffs.shape[1]
    half = fields // 2
    mine = me[0] % 2
    total = jnp.where(mine == 1, found[...], told[...])
    coeffs[half:, :] = total[:half, :]
    coeffs[:half, :] = total[half:, :]
    ordered = jnp.where(mine == 1, total, jnp.concatenate([total[half:, :], total[:half, :]], axis=0))
    parts = jnp.concatenate(split(ordered), axis=0)
    whole = natural.reshape(out.shape)
    first, second = (window(natural, side * half * HALF, half * HALF) for side in (mine, 1 - mine))

    def leave(x):
        return pltpu.make_async_copy(whole.at[:, x], out.at[:, x], sem.at[x])

    for x in range(LAYERS):
        for part in range(4):
            columns = (basis, basis_two)[x // 2][(x % 2 * 4 + part) * rank : (x % 2 * 4 + part + 1) * rank, :]
            both = jnp.dot(parts, columns, preferred_element_type=F32)
            cell = x * 32 + part * 8
            results = ([], [])
            for step in range(8):
                side = step * 256
                along = both[:fields, side : side + HALF] + both[:fields, side + HALF : side + 256]
                along = along + both[fields:, side : side + HALF]
                row = slice((cell + step) * half, (cell + step + 1) * half)
                results[0].append(image[row, :] - along[:half, :])
                results[1].append(borrowed[row, :] - along[half:, :])
            for ref, values in zip((first, second), results):
                values = jnp.swapaxes(jnp.stack(values, axis=0), 0, 1)
                for p in range(half):
                    ref[p * HALF + cell : p * HALF + cell + 8, :] = values[p]
        leave(x).start()
    for x in range(LAYERS):
        leave(x).wait()


def call(kernel, inputs, out_shape, scratch, flops, size, scalars=0, far=0, far_out=0, room=16):
    smem = pl.BlockSpec(memory_space=pltpu.SMEM)
    vmem = pl.BlockSpec(memory_space=pltpu.VMEM)
    hbm = pl.BlockSpec(memory_space=pltpu.HBM)
    inputs = [
        pltpu.with_memory_space_constraint(array, pltpu.HBM) if scalars <= i < scalars + far else array
        for i, array in enumerate(inputs)
    ]
    return pl.pallas_call(
        kernel,
        out_shape=out_shape,
        in_specs=[smem] * scalars + [hbm] * far + [vmem] * (len(inputs) - scalars - far),
        out_specs=[hbm] * far_out + [vmem] * (len(out_shape) - far_out),
        scratch_shapes=scratch,
        cost_estimate=pl.CostEstimate(flops=flops, bytes_accessed=size, transcendentals=0),
        compiler_params=pltpu.CompilerParams(vmem_limit_bytes=room * 2**20),
    )(*inputs)


def struct(*shape, dtype=F32):
    return jax.ShapeDtypeStruct(shape, dtype)


def odd_swapped(array, axis, bits):
    count = lax.axis_size(axis)
    return lax.ppermute(array, axis, [(i, i ^ bits) for i in range(1, count, 2)])


def swapped(array, axis, bits):
    count = lax.axis_size(axis)
    return lax.ppermute(array, axis, [(i, i ^ bits) for i in range(count)])


def local(
    probes,
    sources,
    kappa,
    prior,
    basis,
    entry_cell,
    entry_owner,
    entry_slot,
    entry_weight,
    entry_count,
    trace_weight,
):
    rank = basis.shape[0]
    fields = probes.shape[0] // 2
    entries = entry_cell.shape[0]
    peers = lax.axis_size("space")
    slab, flat = PADDED * fields, 32 * fields
    cells = LAYERS * 32
    rows = entries // HALF
    basis = basis.reshape(rank * cells, HALF)
    me = lax.axis_index("space").astype(jnp.int32).reshape(1)

    own, probes_near, sources_near, prior_near, lent, matrix = call(
        pack,
        (
            entry_count,
            me,
            probes.reshape(2 * fields * cells, HALF),
            sources.reshape(3 * cells, HALF),
            prior.reshape(cells, HALF),
            kappa.reshape(cells, HALF),
            entry_cell.reshape(rows, HALF),
            entry_owner.reshape(rows, HALF),
            entry_slot.reshape(rows, HALF),
            entry_weight.reshape(rows, HALF),
            trace_weight.reshape(1, HALF),
        ),
        [
            struct(cells + 4 * rows + 8, HALF),
            struct(fields * cells, HALF),
            struct(3 * cells, HALF),
            struct(cells, HALF),
            struct((fields + 4) * cells, HALF),
            struct(256, 256, dtype=BF16),
        ],
        [pltpu.VMEM((3, rows, HALF), jnp.int32), pltpu.VMEM((16, HALF), F32), pltpu.SemaphoreType.DMA((12,))],
        100_000,
        2 * 2**20,
        scalars=2,
        far=9,
    )
    partner = swapped(own, "space", 1)
    lent, partner = lax.optimization_barrier((lent, partner))
    borrowed = swapped(lent, "space", 1)
    passed = lax.ppermute(
        jnp.concatenate([own, partner], axis=0),
        "space",
        [pair for i in range(1, peers - 1, 2) for pair in ((i, i + 1), (i + 1, i))],
    )

    turned, first, second, third, push, damping = call(
        functools.partial(forward_own, fields),
        (me, probes_near, sources_near, prior_near, own, partner, borrowed, matrix),
        [
            struct(PAIR * flat, HALF),
            struct(PAIR * slab, HALF),
            struct(PAIR * slab, HALF),
            struct(PAIR * flat, HALF),
            struct(6 * cells, HALF),
            struct(2 * cells, HALF),
        ],
        [pltpu.VMEM((PAIR * flat, HALF), F32), pltpu.VMEM((2 * cells, HALF), F32)],
        600_000_000,
        6 * 2**20,
        scalars=1,
    )
    passed, second = lax.optimization_barrier((passed, second))
    across = swapped(passed, "space", 1)
    across, basis_there = lax.optimization_barrier((across, basis))
    basis_there = swapped(basis_there, "space", 1)
    table, place, slot_hot, speed, line, owner, weight = call(
        functools.partial(forward_window, fields, peers),
        (me, first, second, third, own, partner, passed, across, matrix),
        [
            struct(peers * (fields + 1), HALF),
            struct(TILES * fields, entries),
            struct(TILES * HALF, entries, dtype=BF16),
            struct(TILES * cells, HALF),
            struct(TILES * fields, entries, dtype=jnp.int32),
            struct(TILES * fields, entries, dtype=jnp.int32),
            struct(TILES * fields, entries),
        ],
        [
            pltpu.VMEM((TILES * PLACES, entries), BF16),
            pltpu.VMEM((LAYERS * slab, HALF), F32),
            pltpu.VMEM((LAYERS * slab, HALF), F32),
            pltpu.VMEM((PAIR * flat, HALF), F32),
            pltpu.VMEM((TILES * fields, entries), F32),
        ]
        + [pltpu.VMEM((16 * fields, PLACES), F32)] * TILES,
        3_000_000_000,
        6 * 2**20,
        scalars=1,
        room=20,
    )
    columns = []
    bits = 2
    while bits < peers:
        arrived = swapped(table, "space", bits)
        for i in ((0,), (1,), (2, 3))[len(columns)] if len(columns) < 3 else ():
            (some,) = call(
                functools.partial(basis_parts, 8 * (i % 2)),
                ((basis, basis_there)[i // 2], table),
                [struct(8 * rank, 2048, dtype=BF16)],
                [],
                10_000_000,
                4 * 2**20,
            )
            columns.append(some)
        if bits == 2:
            (turned_hot,) = call(
                functools.partial(turn_places, fields),
                (place, table),
                [struct(TILES * entries, PLACES, dtype=BF16)],
                [],
                10_000_000,
                4 * 2**20,
            )
            arrived, turned_hot = lax.optimization_barrier((arrived, turned_hot))
        arrived, columns = lax.optimization_barrier((arrived, columns))
        table = table + arrived
        bits *= 2
    kept, lent, coeffs = call(
        functools.partial(adjoint, fields, peers),
        (me, table, turned_hot, slot_hot, speed, line, owner, weight, turned, push, damping, matrix, *columns),
        [struct(LAYERS * flat, HALF), struct(LAYERS * flat, HALF), struct(fields, rank)],
        [
            pltpu.VMEM((TILES * fields, entries), F32),
            pltpu.VMEM((TILES * fields, entries), F32),
            pltpu.VMEM((TILES * LAYERS * slab, HALF), F32),
            pltpu.VMEM((2 * PAIR * flat, HALF), F32),
            pltpu.VMEM((2 * PAIR * slab, HALF), F32),
            pltpu.VMEM((2 * PAIR * flat, HALF), F32),
            pltpu.VMEM((2 * PAIR * flat, HALF), F32),
            pltpu.VMEM((PAIR * flat, HALF), F32),
            pltpu.VMEM((peers * fields, HALF), F32),
        ]
        + [pltpu.VMEM((32 * fields, 2 * entries), BF16)] * TILES
        + [pltpu.VMEM((2 * PAIR * fields, 2048), BF16)],
        5_000_000_000,
        10 * 2**20,
        scalars=1,
        room=30,
    )
    even = [(i, i + 1) for i in range(0, peers, 2)]
    coeffs = jnp.concatenate([coeffs, lax.ppermute(coeffs, "space", even)], axis=0)
    lent, coeffs = lax.optimization_barrier((lent, coeffs))
    borrowed = swapped(lent, "space", 1)
    bits = 2
    while bits * 4 < peers:
        coeffs = coeffs + odd_swapped(coeffs, "space", bits)
        bits *= 2
    shares = [odd_swapped(coeffs, "space", bits * i) for i in (3, 2, 1)] + [coeffs]
    coeffs = (shares[0] + shares[1]) + (shares[2] + shares[3])
    told = lax.ppermute(coeffs, "space", [(j, i) for i, j in even])
    hess_probe, coeffs = call(
        functools.partial(remainder, 2 * fields),
        (me, kept, borrowed, *columns[:2], coeffs, told),
        [struct(*probes.shape), struct(2 * fields, rank)],
        [pltpu.VMEM((2 * fields * cells, HALF), F32), pltpu.SemaphoreType.DMA((LAYERS,))],
        200_000_000,
        6 * 2**20,
        scalars=1,
        far_out=1,
    )
    return hess_probe, coeffs.T


def solution(mesh):
    return jax.shard_map(
        local,
        mesh=mesh,
        in_specs=(
            P("group", "space", None, None),
            P(None, ("group", "space"), None, None),
            P(("group", "space"), None, None),
            P(("group", "space"), None, None),
            P("group", "space", None, None),
            P(("group", "space")),
            P(("group", "space")),
            P(("group", "space")),
            P(("group", "space")),
            P(("group", "space")),
            P(("group", "space")),
        ),
        out_specs=(P("group", "space", None, None), P("group", None)),
        check_vma=False,
    )
```

```python
import functools

import jax
import jax.numpy as jnp
from jax import lax
from jax.experimental import pallas as pl
from jax.experimental.pallas import tpu as pltpu
from jax.sharding import PartitionSpec as P

STENCIL = (-205.0 / 72.0, 8.0 / 5.0, -1.0 / 5.0, 8.0 / 315.0, -1.0 / 560.0)
CENTER = 3.0 * STENCIL[0]
REACH = 4
LAYERS = 4
PAIR = 8
TILES = 6
PADDED = 40
HALF = 128
PLACES = 512
F32 = jnp.float32
BF16 = jnp.bfloat16
NT = (((1,), (1,)), ((), ()))


def split(value):
    high = value.astype(BF16)
    low = (value - high.astype(F32)).astype(BF16)
    return high, low


def at(row, count=16):
    return pl.ds(pl.multiple_of(row, 8), count)


def window(ref, start, size):
    return ref.at[pl.ds(pl.multiple_of(start, 8), size)]


def kept_rows(load):
    rows = {}

    def get(layer, y):
        if (layer, y) not in rows:
            rows[layer, y] = load(layer, y)
        return rows[layer, y]

    return get


def spread(ref, row, fields):
    return jnp.broadcast_to(ref[pl.ds(row, 1), :], (fields, HALF))


def clear_margins(ref, layers, fields):
    margin = jnp.zeros((REACH * fields, HALF), F32)
    for layer in range(layers):
        start = layer * PADDED * fields
        ref[start : start + REACH * fields, :] = margin
        start += (PADDED - REACH) * fields
        ref[start : start + REACH * fields, :] = margin


def along_z(ref, first, layers, fields, band_ref, out_ref, row=0):
    pieces = [ref[at(((first + x) * PADDED + REACH) * fields, 32 * fields), :] for x in range(layers)]
    high, low = split(jnp.concatenate(pieces, axis=0))
    both = jnp.dot(jnp.concatenate([high, low], axis=1), band_ref[...], preferred_element_type=F32)
    out_ref[at(row, layers * 32 * fields), :] = both[:, :HALF] + both[:, HALF:]


def laplacian(get, x, y, z_term, lowest, highest):
    total = z_term
    for k in range(1, REACH + 1):
        ring = get(x, y + k) + get(x, y - k)
        if x + k <= highest:
            ring = ring + get(x + k, y)
        if x - k >= lowest:
            ring = ring + get(x - k, y)
        total = total + STENCIL[k] * ring
    return total


def pack(
    count, me, probes, sources, prior, kappa, cell, owner, slot, weight, scale,
    statics, probes_out, sources_out, prior_out, lent, band_ref, small_int, small_float, sem,
):
    rows = cell.shape[0]
    cells = kappa.shape[0]
    half = probes_out.shape[0]
    mine = me[0] % 2
    other = probes.at[pl.ds(pl.multiple_of((1 - mine) * half, 8), half)]
    small = [
        pltpu.make_async_copy(kappa, statics.at[pl.ds(0, cells)], sem.at[0]),
        pltpu.make_async_copy(cell, small_int.at[0], sem.at[1]),
        pltpu.make_async_copy(owner, small_int.at[1], sem.at[2]),
        pltpu.make_async_copy(slot, small_int.at[2], sem.at[3]),
        pltpu.make_async_copy(weight, small_float.at[pl.ds(0, rows)], sem.at[4]),
        pltpu.make_async_copy(scale, small_float.at[pl.ds(8, 1)], sem.at[5]),
    ]
    large = [
        pltpu.make_async_copy(other, lent.at[pl.ds(0, half)], sem.at[6]),
        pltpu.make_async_copy(sources, lent.at[pl.ds(half, 3 * cells)], sem.at[7]),
        pltpu.make_async_copy(prior, lent.at[pl.ds(half + 3 * cells, cells)], sem.at[8]),
        pltpu.make_async_copy(probes.at[pl.ds(pl.multiple_of(mine * half, 8), half)], probes_out, sem.at[9]),
        pltpu.make_async_copy(sources, sources_out, sem.at[10]),
        pltpu.make_async_copy(prior, prior_out, sem.at[11]),
    ]
    for copy in small + large:
        copy.start()
    apart = lax.broadcasted_iota(jnp.int32, (HALF, HALF), 0) - lax.broadcasted_iota(jnp.int32, (HALF, HALF), 1)
    full = jnp.where(apart == 0, CENTER, jnp.zeros((HALF, HALF), F32))
    for reach in range(1, REACH + 1):
        full = jnp.where(jnp.abs(apart) == reach, STENCIL[reach], full)
    high, low = split(full)
    band_ref[0:HALF, 0:HALF] = high
    band_ref[HALF:, 0:HALF] = high
    band_ref[0:HALF, HALF:] = low
    band_ref[HALF:, HALF:] = jnp.zeros_like(low)
    for copy in small:
        copy.wait()
    for i in range(3):
        statics[cells + i * rows : cells + (i + 1) * rows, :] = small_int[i].astype(F32)
    place = lax.broadcasted_iota(jnp.int32, (rows, HALF), 0) * HALF
    place = place + lax.broadcasted_iota(jnp.int32, (rows, HALF), 1)
    live = jnp.where(place < count[0], small_float[0:rows, :], 0.0)
    statics[cells + 3 * rows : cells + 4 * rows, :] = live
    statics[cells + 4 * rows : cells + 4 * rows + 8, :] = jnp.broadcast_to(small_float[8:9, :], (8, HALF))
    for copy in large:
        copy.wait()


def forward_own(
    fields, me, probes, sources, prior, own, partner, borrowed, band_ref,
    turned, first, second, third, push_ref, prior_ref, z_term, speed_ref,
):
    slab, flat, cells = PADDED * fields, 32 * fields, LAYERS * 32
    ahead = 24 * fields
    half = probes.shape[0]
    mine = me[0] % 2
    clear_margins(first, PAIR, fields)
    clear_margins(second, PAIR, fields)
    lent = borrowed.at[pl.ds(half, 4 * cells)]
    for side, pushes, damping, statics in ((mine, sources, prior, own), (1 - mine, lent, None, partner)):
        for i in range(3):
            push_ref[at(i * 2 * cells + side * cells, cells), :] = pushes[i * cells : (i + 1) * cells, :]
        place = at(side * cells, cells)
        prior_ref[place, :] = lent[3 * cells :, :] if damping is None else damping[...]
        speed_ref[place, :] = statics[0:cells, :]

    def load(chunk, carry):
        for side, ref in ((mine, probes), (1 - mine, borrowed)):
            there = window(turned, side * LAYERS * flat + chunk * 8 * fields, LAYERS * flat - ahead)
            padded = window(first, side * LAYERS * slab + chunk * 8 * fields, LAYERS * slab - ahead)
            here = window(ref, chunk * 8, half - 24)
            push = window(push_ref, side * cells + chunk * 8, cells - 24)
            for x in range(LAYERS):
                rows = [here[p * cells + x * 32 : p * cells + x * 32 + 8, :] for p in range(fields)]
                values = jnp.swapaxes(jnp.stack(rows, axis=0), 0, 1)
                for y in range(8):
                    cell = x * 32 + y
                    there[cell * fields : (cell + 1) * fields, :] = values[y]
                    row = x * slab + (REACH + y) * fields
                    padded[row : row + fields, :] = values[y] * spread(push, cell, fields)
        return carry

    lax.fori_loop(0, 4, load, 0)

    def sweep(field, emit):
        along_z(field, 0, PAIR, fields, band_ref, z_term)

        def body(chunk, carry):
            padded = window(field, chunk * 8 * fields, PAIR * slab - ahead)
            z_part = window(z_term, chunk * 8 * fields, PAIR * flat - ahead)
            speed = window(speed_ref, chunk * 8, 2 * cells - 24)
            push = window(push_ref, chunk * 8, 6 * cells - 24)
            there = window(turned, chunk * 8 * fields, PAIR * flat - ahead)
            put = emit(chunk)

            def load(layer, y):
                row = layer * slab + (REACH + y) * fields
                return padded[row : row + fields, :]

            for side in range(2):
                get = kept_rows(load)
                for y in range(8):
                    for x in range(side * LAYERS, (side + 1) * LAYERS):
                        cell = x * 32 + y
                        row = slice(cell * fields, (cell + 1) * fields)
                        change = spread(speed, cell, fields) * laplacian(get, x, y, z_part[row, :], 0, PAIR - 1)
                        put(x, y, get(x, y), change, there[row, :], push)
            return carry

        lax.fori_loop(0, 4, body, 0)

    def step_one(chunk):
        out = window(second, chunk * 8 * fields, PAIR * slab - ahead)

        def put(x, y, now, change, probe, push):
            change = change + probe * spread(push, 2 * cells + x * 32 + y, fields)
            row = x * slab + (REACH + y) * fields
            out[row : row + fields, :] = 2.0 * now + change

        return put

    sweep(first, step_one)

    def step_two(chunk):
        before = window(first, chunk * 8 * fields, PAIR * slab - ahead)
        out = window(third, chunk * 8 * fields, PAIR * flat - ahead)

        def put(x, y, now, change, probe, push):
            row = x * slab + (REACH + y) * fields
            change = change - before[row : row + fields, :]
            cell = x * 32 + y
            change = change + probe * spread(push, 4 * cells + cell, fields)
            out[cell * fields : (cell + 1) * fields, :] = 2.0 * now + change

        return put

    sweep(second, step_two)


def entry_row(value, row):
    return jnp.concatenate([value[row + i : row + i + 1, :] for i in range(4)], axis=1)


def forward_window(
    fields, peers, me, first, second, third, own, partner, passed, across, band_ref,
    table, place_ref, slot_ref, speed_ref, line_ref, owner_ref, weight_ref,
    cell_ref, wide_ref, below, above, z_term, total_ref, *samples,
):
    entries = line_ref.shape[1]
    cells = LAYERS * 32
    length = own.shape[0]
    odd = me[0] % 2 == 1
    slab, flat = PADDED * fields, 32 * fields
    clear_margins(below, LAYERS, fields)
    clear_margins(above, LAYERS, fields)
    total_ref[...] = jnp.zeros_like(total_ref)
    mine, theirs = own[...], partner[...]
    low = jnp.where(me[0] < 2, 0.0, jnp.where(odd, across[...], passed[...]))
    high = jnp.where(me[0] >= peers - 2, 0.0, jnp.where(odd, passed[...], across[...]))
    tiles = (
        low[length:, :],
        low[0:length, :],
        jnp.where(odd, theirs, mine),
        jnp.where(odd, mine, theirs),
        high[0:length, :],
        high[length:, :],
    )
    place = lax.broadcasted_iota(jnp.int32, (PLACES, entries), 0)
    slot_place = lax.broadcasted_iota(jnp.int32, (HALF, entries), 0)
    for tile, value in enumerate(tiles):
        speed_ref[tile * cells : (tile + 1) * cells, :] = value[0:cells, :]
        cell = entry_row(value, cells).astype(jnp.int32)
        owner = entry_row(value, cells + 4).astype(jnp.int32)
        slot = entry_row(value, cells + 8).astype(jnp.int32)
        weight = entry_row(value, cells + 12)
        hot = jnp.where(place == jnp.bitwise_and(cell, PLACES - 1), 1.0, 0.0)
        cell_ref[tile * PLACES : (tile + 1) * PLACES, :] = hot.astype(BF16)
        hot = jnp.where(slot_place == slot, 1.0, 0.0)
        slot_ref[tile * HALF : (tile + 1) * HALF, :] = hot.astype(BF16)
        rows = slice(tile * fields, (tile + 1) * fields)
        line_ref[rows, :] = jnp.broadcast_to(lax.shift_right_logical(cell, 8), (fields, entries))
        wide_ref[rows, :] = jnp.broadcast_to(lax.shift_right_logical(cell, 9), (fields, entries))
        place_ref[rows, :] = jnp.broadcast_to(jnp.bitwise_and(cell, 255), (fields, entries)).astype(F32)
        owner_ref[rows, :] = jnp.broadcast_to(owner, (fields, entries))
        weight_ref[rows, :] = jnp.broadcast_to(weight, (fields, entries))

    def outward(chunk, carry):
        ahead = 24 * fields
        speed = window(speed_ref, chunk * 8, TILES * cells - 24)
        here = window(first, chunk * 8 * fields, PAIR * slab - ahead)
        down_out, up_out = (window(ref, chunk * 8 * fields, LAYERS * slab - ahead) for ref in (below, above))
        for y in range(8):
            rows = [slice(x * slab + (REACH + y) * fields, x * slab + (REACH + y + 1) * fields) for x in range(PAIR)]
            field = [here[row, :] for row in rows]
            for x in range(LAYERS):
                up = sum(STENCIL[4 + x - other] * field[4 + other] for other in range(x, LAYERS))
                down = sum(STENCIL[4 + other - x] * field[other] for other in range(x + 1))
                up_out[rows[x], :] = spread(speed, 4 * cells + x * 32 + y, fields) * up
                down_out[rows[x], :] = spread(speed, cells + x * 32 + y, fields) * down
        return carry

    lax.fori_loop(0, 4, outward, 0)
    along_z(below, 0, LAYERS, fields, band_ref, z_term, 0)
    along_z(above, 0, LAYERS, fields, band_ref, z_term, cells * fields)

    def far(read, x, y, lowest, highest):
        total = None
        for other in range(lowest, highest + 1):
            if 1 <= abs(x - other) <= REACH:
                term = STENCIL[abs(x - other)] * read(other, y)
                total = term if total is None else total + term
        return total

    def respond(chunk, carry):
        ahead = 16 * fields
        speeds = window(speed_ref, chunk * 16, TILES * cells - 16)
        low_side, high_side = (window(ref, chunk * 16 * fields, LAYERS * slab - ahead) for ref in (below, above))
        inside = window(second, chunk * 16 * fields, PAIR * slab - ahead)
        base = window(third, chunk * 16 * fields, PAIR * flat - ahead)
        z_parts = window(z_term, chunk * 16 * fields, PAIR * flat - ahead)

        def load(layer, y):
            if layer < 0:
                ref, layer = low_side, layer + LAYERS
            elif layer >= PAIR:
                ref, layer = high_side, layer - PAIR
            else:
                ref = inside
            row = layer * slab + (REACH + y) * fields
            return ref[row : row + fields, :]

        for tile in range(TILES):
            sample = samples[tile]
            read = kept_rows(load)
            for y in range(16):
                for x in range(LAYERS):
                    cell = x * 32 + y
                    layer = (tile - 2) * LAYERS + x
                    speed = spread(speeds, tile * cells + cell, fields)
                    if tile in (0, 5):
                        value = speed * far(read, layer, y, -4, 11)
                    elif tile in (2, 3):
                        outside = far(read, layer, y, -4, -1) if tile == 2 else far(read, layer, y, 8, 11)
                        row = ((tile - 2) * cells + cell) * fields
                        value = base[row : row + fields, :] + speed * outside
                    else:
                        row = (tile // 4 * cells + cell) * fields
                        lap = laplacian(read, layer, y, z_parts[row : row + fields, :], -4, 11)
                        value = 2.0 * read(layer, y) + speed * lap
                    row = (x * 4 + y // 4) * fields
                    side = y % 4 * HALF
                    sample[row : row + fields, side : side + HALF] = value
            hot = cell_ref[tile * PLACES : (tile + 1) * PLACES, :]
            picked = jnp.dot(jnp.concatenate(split(sample[...]), axis=0), hot, preferred_element_type=F32)
            picked = picked[: 16 * fields, :] + picked[16 * fields :, :]
            rows = slice(tile * fields, (tile + 1) * fields)
            line = wide_ref[rows, :]
            total = total_ref[rows, :]
            for i in range(16):
                chosen = line == i // 4 * 8 + chunk * 4 + i % 4
                total = total + jnp.where(chosen, picked[i * fields : (i + 1) * fields, :], 0.0)
            total_ref[rows, :] = total
        return carry

    lax.fori_loop(0, 2, respond, 0)

    for group in range(peers // 16):
        lefts, rights = [], []
        for tile in range(TILES):
            rows = slice(tile * fields, (tile + 1) * fields)
            value = total_ref[rows, :] * weight_ref[rows, :]
            high = value.astype(BF16).astype(F32)
            owner = owner_ref[rows, :]
            for part in (high, value - high):
                pieces = [jnp.where(owner == group * 16 + i, part, 0.0) for i in range(16)]
                lefts.append(jnp.concatenate(pieces, axis=0).astype(BF16))
                rights.append(slot_ref[tile * HALF : (tile + 1) * HALF, :])
        result = lax.dot_general(
            jnp.concatenate(lefts, axis=1), jnp.concatenate(rights, axis=1), NT, preferred_element_type=F32
        )
        table[group * 16 * fields : (group + 1) * 16 * fields, :] = result
    place = lax.broadcasted_iota(jnp.int32, (peers, HALF), 0)
    scales = jnp.zeros((peers, HALF), F32)
    for position, value in ((me[0], mine), (me[0] + 1 - 2 * (me[0] % 2), theirs)):
        scale = jnp.broadcast_to(value[cells + 16 : cells + 17, :], (peers, HALF))
        scales = jnp.where(place == position, scale, scales)
    table[peers * fields :, :] = scales


def basis_parts(first, basis, when, out):
    rank = basis.shape[0] // HALF

    def body(group, carry):
        here = window(basis, (first + group) * 8, basis.shape[0] - 15 * 8)
        there = window(out, group * rank, rank)
        for start in range(0, rank, 16):
            blocks = []
            for block in (start, start + 8):
                rows = [here[k * HALF : k * HALF + 8, :] for k in range(block, block + 8)]
                blocks.append(jnp.swapaxes(jnp.stack(rows, axis=0), 0, 1))
            for step in range(8):
                high, low = split(jnp.concatenate([block[step] for block in blocks], axis=0))
                there[start : start + 16, step * 256 : step * 256 + HALF] = high
                there[start : start + 16, step * 256 + HALF : (step + 1) * 256] = low
        return carry

    lax.fori_loop(0, 8, body, 0)


def turn_places(fields, place_ref, when, hot_ref):
    entries = place_ref.shape[1]
    lane = lax.broadcasted_iota(jnp.int32, (entries, HALF), 1)
    for tile in range(TILES):
        row = place_ref[tile * fields : tile * fields + 1, :]
        column = jnp.transpose(jnp.broadcast_to(row, (HALF, entries))).astype(jnp.int32)
        for part in range(2):
            hot = jnp.where(column == lane + part * HALF, 1.0, 0.0).astype(BF16)
            hot_ref[tile * entries : (tile + 1) * entries, part * HALF : (part + 1) * HALF] = hot


def adjoint(
    fields, peers, me, table, hot_ref, slot_ref, speed_ref, line_ref, owner_ref, weight_ref, turned, push_ref,
    prior_ref, band_ref, own_basis, own_basis_two, other_basis, other_basis_two, kept, lent, coeffs,
    high_ref, low_ref, inner_two, outer_two, inner_one, outer_one, z_term, image, scaled, *scratch,
):
    *lefts, image_parts = scratch
    entries = line_ref.shape[1]
    cells = LAYERS * 32
    rank = own_basis.shape[0] // 8
    slab, flat = PADDED * fields, 32 * fields
    ahead = 24 * fields
    clear_margins(inner_two, TILES * LAYERS, fields)
    clear_margins(inner_one, 2 * PAIR, fields)
    for owner in range(peers):
        rows = slice(owner * fields, (owner + 1) * fields)
        scaled[rows, :] = table[rows, :] * table[peers * fields + owner : peers * fields + owner + 1, :]
    for tile in range(TILES):
        rows = slice(tile * fields, (tile + 1) * fields)
        owner = owner_ref[rows, :]
        hot = slot_ref[tile * HALF : (tile + 1) * HALF, :]
        hot = jnp.concatenate([hot, hot], axis=0)
        total = jnp.zeros((fields, entries), F32)
        for group in range(peers // 16):
            parts = split(scaled[group * 16 * fields : (group + 1) * 16 * fields, :])
            found = jnp.dot(jnp.concatenate(parts, axis=1), hot, preferred_element_type=F32)
            for i in range(16):
                total = total + jnp.where(owner == group * 16 + i, found[i * fields : (i + 1) * fields, :], 0.0)
        value = total * weight_ref[rows, :]
        high = value.astype(BF16).astype(F32)
        high_ref[rows, :] = high
        low_ref[rows, :] = value - high

    def product(tile):
        left = lefts[tile]
        rows = slice(tile * fields, (tile + 1) * fields)
        line, high, low = line_ref[rows, :], high_ref[rows, :], low_ref[rows, :]
        for i in range(0, 64, 2):
            chosen = [line == i, line == i + 1]
            row = slice(i * fields, (i + 2) * fields)
            for part, side in ((high, slice(0, entries)), (low, slice(entries, 2 * entries))):
                both = [jnp.where(which, part, 0.0) for which in chosen]
                left[row, side] = jnp.concatenate(both, axis=0).astype(BF16)
        hot = hot_ref[tile * entries : (tile + 1) * entries, :]
        return jnp.dot(left[...], jnp.concatenate([hot, hot], axis=0), preferred_element_type=F32)

    def inject(tile, value):
        for i in range(64):
            for step in range(2):
                layer, y = tile * LAYERS + i // 16, i % 16 * 2 + step
                now = value[i * fields : (i + 1) * fields, step * HALF : (step + 1) * HALF]
                if 1 <= tile <= 4:
                    row = ((layer - LAYERS) * 32 + y) * fields
                    outer_two[row : row + fields, :] = now
                speed = spread(speed_ref, layer * 32 + y, fields)
                row = layer * slab + (REACH + y) * fields
                inner_two[row : row + fields, :] = speed * now
        if 1 <= tile <= 4:
            along_z(inner_two, tile * LAYERS, LAYERS, fields, band_ref, z_term, (tile - 1) * cells * fields)

    values = product(0)
    for tile in range(TILES):
        after = product(tile + 1) if tile + 1 < TILES else None
        inject(tile, values)
        values = after

    def step_one(index, carry):
        pair, chunk = index // 4, index % 4
        start, skip = pair * PAIR * slab + chunk * 8 * fields, pair * PAIR * flat + chunk * 8 * fields
        here = window(inner_two, start, 2 * PAIR * slab - ahead)
        two, one, z_part = (window(ref, skip, PAIR * flat - ahead) for ref in (outer_two, outer_one, z_term))
        out = window(inner_one, start, PAIR * slab - ahead)
        speed = window(speed_ref, cells + pair * 2 * cells + chunk * 8, 2 * cells - 24)

        def load(layer, y):
            row = (layer + LAYERS) * slab + (REACH + y) * fields
            return here[row : row + fields, :]

        for side in range(2):
            get = kept_rows(load)
            for y in range(8):
                for x in range(side * LAYERS, (side + 1) * LAYERS):
                    cell = x * 32 + y
                    row = slice(cell * fields, (cell + 1) * fields)
                    now = 2.0 * two[row, :] + laplacian(get, x, y, z_part[row, :], -4, 11)
                    one[row, :] = now
                    row = x * slab + (REACH + y) * fields
                    out[row : row + fields, :] = spread(speed, cell, fields) * now
        return carry

    lax.fori_loop(0, 8, step_one, 0)
    along_z(inner_one, LAYERS, PAIR, fields, band_ref, z_term)
    mine = me[0] % 2

    def step_two(chunk, total):
        skip = chunk * 8 * fields
        here = window(inner_one, skip, 2 * PAIR * slab - ahead)
        two_rows, one_rows = (window(ref, LAYERS * flat + skip, PAIR * flat - ahead) for ref in (outer_two, outer_one))
        z_part, there, out = (window(ref, skip, PAIR * flat - ahead) for ref in (z_term, turned, image))
        push = window(push_ref, chunk * 8, 6 * cells - 24)
        damping = window(prior_ref, chunk * 8, 2 * cells - 24)

        def load(layer, y):
            row = (layer + LAYERS) * slab + (REACH + y) * fields
            return here[row : row + fields, :]

        nothing = jnp.zeros((fields, HALF), F32)
        for side in range(2):
            get = kept_rows(load)
            for y in range(8):
                for x in range(side * LAYERS, (side + 1) * LAYERS):
                    cell = x * 32 + y
                    row = slice(cell * fields, (cell + 1) * fields)
                    two, one = two_rows[row, :], one_rows[row, :]
                    zero = 2.0 * one - two + laplacian(get, x, y, z_part[row, :], -4, 11)
                    value = spread(push, cell, fields) * zero
                    value = value + spread(push, 2 * cells + cell, fields) * one
                    value = value + spread(push, 4 * cells + cell, fields) * two
                    value = value + spread(damping, cell, fields) * there[row, :]
                    out[row, :] = value
                    high = value.astype(BF16).astype(F32)
                    rows, lane = slice(x * 2 * fields, (x + 1) * 2 * fields), y * 256
                    image_parts[rows, lane : lane + HALF] = jnp.concatenate([high, value - high], axis=0).astype(BF16)
                    image_parts[rows, lane + HALF : lane + 256] = jnp.concatenate([high, nothing], axis=0).astype(BF16)
        for side, pieces in ((mine, (own_basis, own_basis_two)), (1 - mine, (other_basis, other_basis_two))):
            for x in range(LAYERS):
                columns = pieces[x // 2][at((x % 2 * 4 + chunk) * rank, rank), :]
                parts = image_parts[at((side * LAYERS + x) * 2 * fields, 2 * fields), :]
                total = total + lax.dot_general(parts, columns, NT, preferred_element_type=F32)
        return total

    total = lax.fori_loop(0, 4, step_two, jnp.zeros((2 * fields, rank), F32))
    coeffs[...] = total[:fields, :] + total[fields:, :]
    kept[...] = image[at(mine * LAYERS * flat, LAYERS * flat), :]
    lent[...] = image[at((1 - mine) * LAYERS * flat, LAYERS * flat), :]


def remainder(fields, me, image, borrowed, basis, basis_two, *rest):
    *shares, out, coeffs, natural, sem = rest
    rank = coeffs.shape[1]
    half = fields // 2
    mine = me[0] % 2
    while len(shares) > 1:
        shares = [shares[i][...] + shares[i + 1][...] for i in range(0, len(shares), 2)]
    total = shares[0][...]
    coeffs[at(mine * half, half), :] = total[:half, :]
    coeffs[at((1 - mine) * half, half), :] = total[half:, :]
    parts = jnp.concatenate(split(total), axis=0)
    whole = natural.reshape(out.shape)
    first, second = (window(natural, side * half * HALF, half * HALF) for side in (mine, 1 - mine))

    def leave(x):
        return pltpu.make_async_copy(whole.at[:, x], out.at[:, x], sem.at[x])

    for x in range(LAYERS):
        for part in range(4):
            columns = (basis, basis_two)[x // 2][(x % 2 * 4 + part) * rank : (x % 2 * 4 + part + 1) * rank, :]
            both = jnp.dot(parts, columns, preferred_element_type=F32)
            cell = x * 32 + part * 8
            results = ([], [])
            for step in range(8):
                side = step * 256
                along = both[:fields, side : side + HALF] + both[:fields, side + HALF : side + 256]
                along = along + both[fields:, side : side + HALF]
                row = slice((cell + step) * half, (cell + step + 1) * half)
                results[0].append(image[row, :] - along[:half, :])
                results[1].append(borrowed[row, :] - along[half:, :])
            for ref, values in zip((first, second), results):
                values = jnp.swapaxes(jnp.stack(values, axis=0), 0, 1)
                for p in range(half):
                    ref[p * HALF + cell : p * HALF + cell + 8, :] = values[p]
        leave(x).start()
    for x in range(LAYERS):
        leave(x).wait()


def call(kernel, inputs, out_shape, scratch, flops, size, scalars=0, far=0, far_out=0, room=16):
    smem = pl.BlockSpec(memory_space=pltpu.SMEM)
    vmem = pl.BlockSpec(memory_space=pltpu.VMEM)
    hbm = pl.BlockSpec(memory_space=pltpu.HBM)
    inputs = [
        pltpu.with_memory_space_constraint(array, pltpu.HBM) if scalars <= i < scalars + far else array
        for i, array in enumerate(inputs)
    ]
    return pl.pallas_call(
        kernel,
        out_shape=out_shape,
        in_specs=[smem] * scalars + [hbm] * far + [vmem] * (len(inputs) - scalars - far),
        out_specs=[hbm] * far_out + [vmem] * (len(out_shape) - far_out),
        scratch_shapes=scratch,
        cost_estimate=pl.CostEstimate(flops=flops, bytes_accessed=size, transcendentals=0),
        compiler_params=pltpu.CompilerParams(vmem_limit_bytes=room * 2**20),
    )(*inputs)


def struct(*shape, dtype=F32):
    return jax.ShapeDtypeStruct(shape, dtype)


def swapped(array, axis, bits):
    count = lax.axis_size(axis)
    return lax.ppermute(array, axis, [(i, i ^ bits) for i in range(count)])


def local(
    probes,
    sources,
    kappa,
    prior,
    basis,
    entry_cell,
    entry_owner,
    entry_slot,
    entry_weight,
    entry_count,
    trace_weight,
):
    rank = basis.shape[0]
    fields = probes.shape[0] // 2
    entries = entry_cell.shape[0]
    peers = lax.axis_size("space")
    slab, flat = PADDED * fields, 32 * fields
    cells = LAYERS * 32
    rows = entries // HALF
    basis = basis.reshape(rank * cells, HALF)
    me = lax.axis_index("space").astype(jnp.int32).reshape(1)

    own, probes_near, sources_near, prior_near, lent, matrix = call(
        pack,
        (
            entry_count,
            me,
            probes.reshape(2 * fields * cells, HALF),
            sources.reshape(3 * cells, HALF),
            prior.reshape(cells, HALF),
            kappa.reshape(cells, HALF),
            entry_cell.reshape(rows, HALF),
            entry_owner.reshape(rows, HALF),
            entry_slot.reshape(rows, HALF),
            entry_weight.reshape(rows, HALF),
            trace_weight.reshape(1, HALF),
        ),
        [
            struct(cells + 4 * rows + 8, HALF),
            struct(fields * cells, HALF),
            struct(3 * cells, HALF),
            struct(cells, HALF),
            struct((fields + 4) * cells, HALF),
            struct(256, 256, dtype=BF16),
        ],
        [pltpu.VMEM((3, rows, HALF), jnp.int32), pltpu.VMEM((16, HALF), F32), pltpu.SemaphoreType.DMA((12,))],
        100_000,
        2 * 2**20,
        scalars=2,
        far=9,
    )
    partner = swapped(own, "space", 1)
    lent, partner = lax.optimization_barrier((lent, partner))
    borrowed = swapped(lent, "space", 1)
    passed = lax.ppermute(
        jnp.concatenate([own, partner], axis=0),
        "space",
        [pair for i in range(1, peers - 1, 2) for pair in ((i, i + 1), (i + 1, i))] + [(0, 0), (peers - 1, peers - 1)],
    )

    turned, first, second, third, push, damping = call(
        functools.partial(forward_own, fields),
        (me, probes_near, sources_near, prior_near, own, partner, borrowed, matrix),
        [
            struct(PAIR * flat, HALF),
            struct(PAIR * slab, HALF),
            struct(PAIR * slab, HALF),
            struct(PAIR * flat, HALF),
            struct(6 * cells, HALF),
            struct(2 * cells, HALF),
        ],
        [pltpu.VMEM((PAIR * flat, HALF), F32), pltpu.VMEM((2 * cells, HALF), F32)],
        600_000_000,
        6 * 2**20,
        scalars=1,
    )
    passed, second = lax.optimization_barrier((passed, second))
    across = swapped(passed, "space", 1)
    across, basis_there = lax.optimization_barrier((across, basis))
    basis_there = swapped(basis_there, "space", 1)
    table, place, slot_hot, speed, line, owner, weight = call(
        functools.partial(forward_window, fields, peers),
        (me, first, second, third, own, partner, passed, across, matrix),
        [
            struct(peers * (fields + 1), HALF),
            struct(TILES * fields, entries),
            struct(TILES * HALF, entries, dtype=BF16),
            struct(TILES * cells, HALF),
            struct(TILES * fields, entries, dtype=jnp.int32),
            struct(TILES * fields, entries, dtype=jnp.int32),
            struct(TILES * fields, entries),
        ],
        [
            pltpu.VMEM((TILES * PLACES, entries), BF16),
            pltpu.VMEM((TILES * fields, entries), jnp.int32),
            pltpu.VMEM((LAYERS * slab, HALF), F32),
            pltpu.VMEM((LAYERS * slab, HALF), F32),
            pltpu.VMEM((PAIR * flat, HALF), F32),
            pltpu.VMEM((TILES * fields, entries), F32),
        ]
        + [pltpu.VMEM((16 * fields, PLACES), F32)] * TILES,
        3_000_000_000,
        6 * 2**20,
        scalars=1,
        room=20,
    )
    columns = []
    bits = 2
    while bits < peers:
        arrived = swapped(table, "space", bits)
        for i in ((0,), (1,), (2, 3))[len(columns)] if len(columns) < 3 else ():
            (some,) = call(
                functools.partial(basis_parts, 8 * (i % 2)),
                ((basis, basis_there)[i // 2], table),
                [struct(8 * rank, 2048, dtype=BF16)],
                [],
                10_000_000,
                4 * 2**20,
            )
            columns.append(some)
        if bits == 2:
            (turned_hot,) = call(
                functools.partial(turn_places, fields),
                (place, table),
                [struct(TILES * entries, 256, dtype=BF16)],
                [],
                10_000_000,
                4 * 2**20,
            )
            arrived, turned_hot = lax.optimization_barrier((arrived, turned_hot))
        arrived, columns = lax.optimization_barrier((arrived, columns))
        table = table + arrived
        bits *= 2
    kept, lent, coeffs = call(
        functools.partial(adjoint, fields, peers),
        (me, table, turned_hot, slot_hot, speed, line, owner, weight, turned, push, damping, matrix, *columns),
        [struct(LAYERS * flat, HALF), struct(LAYERS * flat, HALF), struct(fields, rank)],
        [
            pltpu.VMEM((TILES * fields, entries), F32),
            pltpu.VMEM((TILES * fields, entries), F32),
            pltpu.VMEM((TILES * LAYERS * slab, HALF), F32),
            pltpu.VMEM((2 * PAIR * flat, HALF), F32),
            pltpu.VMEM((2 * PAIR * slab, HALF), F32),
            pltpu.VMEM((2 * PAIR * flat, HALF), F32),
            pltpu.VMEM((2 * PAIR * flat, HALF), F32),
            pltpu.VMEM((PAIR * flat, HALF), F32),
            pltpu.VMEM((peers * fields, HALF), F32),
        ]
        + [pltpu.VMEM((64 * fields, 2 * entries), BF16)] * TILES
        + [pltpu.VMEM((2 * PAIR * fields, 2048), BF16)],
        5_000_000_000,
        10 * 2**20,
        scalars=1,
        room=30,
    )
    coeffs = jnp.concatenate([coeffs, swapped(coeffs, "space", 1)], axis=0)
    lent, coeffs = lax.optimization_barrier((lent, coeffs))
    borrowed = swapped(lent, "space", 1)
    bits = 2
    while bits * 4 < peers:
        coeffs = coeffs + swapped(coeffs, "space", bits)
        bits *= 2
    shares = [swapped(coeffs, "space", bits * i) for i in (3, 2, 1)] + [coeffs]
    hess_probe, coeffs = call(
        functools.partial(remainder, 2 * fields),
        (me, kept, borrowed, *columns[:2], *shares),
        [struct(*probes.shape), struct(2 * fields, rank)],
        [pltpu.VMEM((2 * fields * cells, HALF), F32), pltpu.SemaphoreType.DMA((LAYERS,))],
        200_000_000,
        6 * 2**20,
        scalars=1,
        far_out=1,
    )
    return hess_probe, coeffs.T


def solution(mesh):
    return jax.shard_map(
        local,
        mesh=mesh,
        in_specs=(
            P("group", "space", None, None),
            P(None, ("group", "space"), None, None),
            P(("group", "space"), None, None),
            P(("group", "space"), None, None),
            P("group", "space", None, None),
            P(("group", "space")),
            P(("group", "space")),
            P(("group", "space")),
            P(("group", "space")),
            P(("group", "space")),
            P(("group", "space")),
        ),
        out_specs=(P("group", "space", None, None), P("group", None)),
        check_vma=False,
    )
```

```python
import functools

import jax
import jax.numpy as jnp
from jax import lax
from jax.experimental import pallas as pl
from jax.experimental.pallas import tpu as pltpu
from jax.sharding import PartitionSpec as P

STENCIL = (-205.0 / 72.0, 8.0 / 5.0, -1.0 / 5.0, 8.0 / 315.0, -1.0 / 560.0)
CENTER = 3.0 * STENCIL[0]
REACH = 4
LAYERS = 4
PAIR = 8
TILES = 6
PADDED = 40
HALF = 128
PLACES = 512
F32 = jnp.float32
BF16 = jnp.bfloat16
NT = (((1,), (1,)), ((), ()))


def split(value):
    high = value.astype(BF16)
    low = (value - high.astype(F32)).astype(BF16)
    return high, low


def at(row, count=16):
    return pl.ds(pl.multiple_of(row, 8), count)


def window(ref, start, size):
    return ref.at[pl.ds(pl.multiple_of(start, 8), size)]


def kept_rows(load):
    rows = {}

    def get(layer, y):
        if (layer, y) not in rows:
            rows[layer, y] = load(layer, y)
        return rows[layer, y]

    return get


def half_of(me):
    value = me[0]
    for by in (4, 2, 1):
        value = jnp.bitwise_xor(value, lax.shift_right_logical(value, by))
    return jnp.bitwise_and(value, 1)


def spread(ref, row, fields):
    return jnp.broadcast_to(ref[pl.ds(row, 1), :], (fields, HALF))


def clear_margins(ref, layers, fields):
    margin = jnp.zeros((REACH * fields, HALF), F32)
    for layer in range(layers):
        start = layer * PADDED * fields
        ref[start : start + REACH * fields, :] = margin
        start += (PADDED - REACH) * fields
        ref[start : start + REACH * fields, :] = margin


def along_z(ref, first, layers, fields, band_ref, out_ref, row=0):
    pieces = [ref[at(((first + x) * PADDED + REACH) * fields, 32 * fields), :] for x in range(layers)]
    high, low = split(jnp.concatenate(pieces, axis=0))
    both = jnp.dot(jnp.concatenate([high, low], axis=1), band_ref[...], preferred_element_type=F32)
    out_ref[at(row, layers * 32 * fields), :] = both[:, :HALF] + both[:, HALF:]


def laplacian(get, x, y, z_term, lowest, highest):
    total = z_term
    for k in range(1, REACH + 1):
        ring = get(x, y + k) + get(x, y - k)
        if x + k <= highest:
            ring = ring + get(x + k, y)
        if x - k >= lowest:
            ring = ring + get(x - k, y)
        total = total + STENCIL[k] * ring
    return total


def pack(
    count, me, probes, sources, prior, kappa, cell, owner, slot, weight, scale,
    statics, probes_out, sources_out, prior_out, lent, band_ref, small_int, small_float, sem,
):
    rows = cell.shape[0]
    cells = kappa.shape[0]
    half = probes_out.shape[0]
    mine = half_of(me)
    other = probes.at[pl.ds(pl.multiple_of((1 - mine) * half, 8), half)]
    small = [
        pltpu.make_async_copy(kappa, statics.at[pl.ds(0, cells)], sem.at[0]),
        pltpu.make_async_copy(cell, small_int.at[0], sem.at[1]),
        pltpu.make_async_copy(owner, small_int.at[1], sem.at[2]),
        pltpu.make_async_copy(slot, small_int.at[2], sem.at[3]),
        pltpu.make_async_copy(weight, small_float.at[pl.ds(0, rows)], sem.at[4]),
        pltpu.make_async_copy(scale, small_float.at[pl.ds(8, 1)], sem.at[5]),
    ]
    large = [
        pltpu.make_async_copy(other, lent.at[pl.ds(0, half)], sem.at[6]),
        pltpu.make_async_copy(sources, lent.at[pl.ds(half, 3 * cells)], sem.at[7]),
        pltpu.make_async_copy(prior, lent.at[pl.ds(half + 3 * cells, cells)], sem.at[8]),
        pltpu.make_async_copy(probes.at[pl.ds(pl.multiple_of(mine * half, 8), half)], probes_out, sem.at[9]),
        pltpu.make_async_copy(sources, sources_out, sem.at[10]),
        pltpu.make_async_copy(prior, prior_out, sem.at[11]),
    ]
    for copy in small + large:
        copy.start()
    apart = lax.broadcasted_iota(jnp.int32, (HALF, HALF), 0) - lax.broadcasted_iota(jnp.int32, (HALF, HALF), 1)
    full = jnp.where(apart == 0, CENTER, jnp.zeros((HALF, HALF), F32))
    for reach in range(1, REACH + 1):
        full = jnp.where(jnp.abs(apart) == reach, STENCIL[reach], full)
    high, low = split(full)
    band_ref[0:HALF, 0:HALF] = high
    band_ref[HALF:, 0:HALF] = high
    band_ref[0:HALF, HALF:] = low
    band_ref[HALF:, HALF:] = jnp.zeros_like(low)
    for copy in small:
        copy.wait()
    for i in range(3):
        statics[cells + i * rows : cells + (i + 1) * rows, :] = small_int[i].astype(F32)
    place = lax.broadcasted_iota(jnp.int32, (rows, HALF), 0) * HALF
    place = place + lax.broadcasted_iota(jnp.int32, (rows, HALF), 1)
    live = jnp.where(place < count[0], small_float[0:rows, :], 0.0)
    statics[cells + 3 * rows : cells + 4 * rows, :] = live
    statics[cells + 4 * rows : cells + 4 * rows + 8, :] = jnp.broadcast_to(small_float[8:9, :], (8, HALF))
    for copy in large:
        copy.wait()


def forward_own(
    fields, me, probes, sources, prior, own, partner, borrowed, band_ref,
    turned, first, second, third, push_ref, prior_ref, z_term, speed_ref,
):
    slab, flat, cells = PADDED * fields, 32 * fields, LAYERS * 32
    ahead = 24 * fields
    half = probes.shape[0]
    mine = me[0] % 2
    clear_margins(first, PAIR, fields)
    clear_margins(second, PAIR, fields)
    lent = borrowed.at[pl.ds(half, 4 * cells)]
    for side, pushes, damping, statics in ((mine, sources, prior, own), (1 - mine, lent, None, partner)):
        for i in range(3):
            push_ref[at(i * 2 * cells + side * cells, cells), :] = pushes[i * cells : (i + 1) * cells, :]
        place = at(side * cells, cells)
        prior_ref[place, :] = lent[3 * cells :, :] if damping is None else damping[...]
        speed_ref[place, :] = statics[0:cells, :]

    def load(chunk, carry):
        for side, ref in ((mine, probes), (1 - mine, borrowed)):
            there = window(turned, side * LAYERS * flat + chunk * 8 * fields, LAYERS * flat - ahead)
            padded = window(first, side * LAYERS * slab + chunk * 8 * fields, LAYERS * slab - ahead)
            here = window(ref, chunk * 8, half - 24)
            push = window(push_ref, side * cells + chunk * 8, cells - 24)
            for x in range(LAYERS):
                rows = [here[p * cells + x * 32 : p * cells + x * 32 + 8, :] for p in range(fields)]
                values = jnp.swapaxes(jnp.stack(rows, axis=0), 0, 1)
                for y in range(8):
                    cell = x * 32 + y
                    there[cell * fields : (cell + 1) * fields, :] = values[y]
                    row = x * slab + (REACH + y) * fields
                    padded[row : row + fields, :] = values[y] * spread(push, cell, fields)
        return carry

    lax.fori_loop(0, 4, load, 0)

    def sweep(field, emit):
        along_z(field, 0, PAIR, fields, band_ref, z_term)

        def body(chunk, carry):
            padded = window(field, chunk * 8 * fields, PAIR * slab - ahead)
            z_part = window(z_term, chunk * 8 * fields, PAIR * flat - ahead)
            speed = window(speed_ref, chunk * 8, 2 * cells - 24)
            push = window(push_ref, chunk * 8, 6 * cells - 24)
            there = window(turned, chunk * 8 * fields, PAIR * flat - ahead)
            put = emit(chunk)

            def load(layer, y):
                row = layer * slab + (REACH + y) * fields
                return padded[row : row + fields, :]

            for side in range(2):
                get = kept_rows(load)
                for y in range(8):
                    for x in range(side * LAYERS, (side + 1) * LAYERS):
                        cell = x * 32 + y
                        row = slice(cell * fields, (cell + 1) * fields)
                        change = spread(speed, cell, fields) * laplacian(get, x, y, z_part[row, :], 0, PAIR - 1)
                        put(x, y, get(x, y), change, there[row, :], push)
            return carry

        lax.fori_loop(0, 4, body, 0)

    def step_one(chunk):
        out = window(second, chunk * 8 * fields, PAIR * slab - ahead)

        def put(x, y, now, change, probe, push):
            change = change + probe * spread(push, 2 * cells + x * 32 + y, fields)
            row = x * slab + (REACH + y) * fields
            out[row : row + fields, :] = 2.0 * now + change

        return put

    sweep(first, step_one)

    def step_two(chunk):
        before = window(first, chunk * 8 * fields, PAIR * slab - ahead)
        out = window(third, chunk * 8 * fields, PAIR * flat - ahead)

        def put(x, y, now, change, probe, push):
            row = x * slab + (REACH + y) * fields
            change = change - before[row : row + fields, :]
            cell = x * 32 + y
            change = change + probe * spread(push, 4 * cells + cell, fields)
            out[cell * fields : (cell + 1) * fields, :] = 2.0 * now + change

        return put

    sweep(second, step_two)


def entry_row(value, row):
    return jnp.concatenate([value[row + i : row + i + 1, :] for i in range(4)], axis=1)


def forward_window(
    fields, peers, me, first, second, third, own, partner, passed, across, band_ref,
    table, place_ref, slot_ref, speed_ref, line_ref, owner_ref, weight_ref,
    cell_ref, wide_ref, below, above, z_term, total_ref, *samples,
):
    entries = line_ref.shape[1]
    cells = LAYERS * 32
    length = own.shape[0]
    odd = me[0] % 2 == 1
    slab, flat = PADDED * fields, 32 * fields
    clear_margins(below, LAYERS, fields)
    clear_margins(above, LAYERS, fields)
    total_ref[...] = jnp.zeros_like(total_ref)
    mine, theirs = own[...], partner[...]
    low = jnp.where(me[0] < 2, 0.0, jnp.where(odd, across[...], passed[...]))
    high = jnp.where(me[0] >= peers - 2, 0.0, jnp.where(odd, passed[...], across[...]))
    tiles = (
        low[length:, :],
        low[0:length, :],
        jnp.where(odd, theirs, mine),
        jnp.where(odd, mine, theirs),
        high[0:length, :],
        high[length:, :],
    )
    place = lax.broadcasted_iota(jnp.int32, (PLACES, entries), 0)
    slot_place = lax.broadcasted_iota(jnp.int32, (HALF, entries), 0)
    for tile, value in enumerate(tiles):
        speed_ref[tile * cells : (tile + 1) * cells, :] = value[0:cells, :]
        cell = entry_row(value, cells).astype(jnp.int32)
        owner = entry_row(value, cells + 4).astype(jnp.int32)
        slot = entry_row(value, cells + 8).astype(jnp.int32)
        weight = entry_row(value, cells + 12)
        hot = jnp.where(place == jnp.bitwise_and(cell, PLACES - 1), 1.0, 0.0)
        cell_ref[tile * PLACES : (tile + 1) * PLACES, :] = hot.astype(BF16)
        hot = jnp.where(slot_place == slot, 1.0, 0.0)
        slot_ref[tile * HALF : (tile + 1) * HALF, :] = hot.astype(BF16)
        rows = slice(tile * fields, (tile + 1) * fields)
        line_ref[rows, :] = jnp.broadcast_to(lax.shift_right_logical(cell, 8), (fields, entries))
        wide_ref[rows, :] = jnp.broadcast_to(lax.shift_right_logical(cell, 9), (fields, entries))
        place_ref[rows, :] = jnp.broadcast_to(jnp.bitwise_and(cell, 255), (fields, entries)).astype(F32)
        owner_ref[rows, :] = jnp.broadcast_to(owner, (fields, entries))
        weight_ref[rows, :] = jnp.broadcast_to(weight, (fields, entries))

    def outward(chunk, carry):
        ahead = 24 * fields
        speed = window(speed_ref, chunk * 8, TILES * cells - 24)
        here = window(first, chunk * 8 * fields, PAIR * slab - ahead)
        down_out, up_out = (window(ref, chunk * 8 * fields, LAYERS * slab - ahead) for ref in (below, above))
        for y in range(8):
            rows = [slice(x * slab + (REACH + y) * fields, x * slab + (REACH + y + 1) * fields) for x in range(PAIR)]
            field = [here[row, :] for row in rows]
            for x in range(LAYERS):
                up = sum(STENCIL[4 + x - other] * field[4 + other] for other in range(x, LAYERS))
                down = sum(STENCIL[4 + other - x] * field[other] for other in range(x + 1))
                up_out[rows[x], :] = spread(speed, 4 * cells + x * 32 + y, fields) * up
                down_out[rows[x], :] = spread(speed, cells + x * 32 + y, fields) * down
        return carry

    lax.fori_loop(0, 4, outward, 0)
    along_z(below, 0, LAYERS, fields, band_ref, z_term, 0)
    along_z(above, 0, LAYERS, fields, band_ref, z_term, cells * fields)

    def far(read, x, y, lowest, highest):
        total = None
        for other in range(lowest, highest + 1):
            if 1 <= abs(x - other) <= REACH:
                term = STENCIL[abs(x - other)] * read(other, y)
                total = term if total is None else total + term
        return total

    def respond(chunk, carry):
        ahead = 16 * fields
        speeds = window(speed_ref, chunk * 16, TILES * cells - 16)
        low_side, high_side = (window(ref, chunk * 16 * fields, LAYERS * slab - ahead) for ref in (below, above))
        inside = window(second, chunk * 16 * fields, PAIR * slab - ahead)
        base = window(third, chunk * 16 * fields, PAIR * flat - ahead)
        z_parts = window(z_term, chunk * 16 * fields, PAIR * flat - ahead)

        def load(layer, y):
            if layer < 0:
                ref, layer = low_side, layer + LAYERS
            elif layer >= PAIR:
                ref, layer = high_side, layer - PAIR
            else:
                ref = inside
            row = layer * slab + (REACH + y) * fields
            return ref[row : row + fields, :]

        for tile in range(TILES):
            sample = samples[tile]
            read = kept_rows(load)
            for y in range(16):
                for x in range(LAYERS):
                    cell = x * 32 + y
                    layer = (tile - 2) * LAYERS + x
                    speed = spread(speeds, tile * cells + cell, fields)
                    if tile in (0, 5):
                        value = speed * far(read, layer, y, -4, 11)
                    elif tile in (2, 3):
                        outside = far(read, layer, y, -4, -1) if tile == 2 else far(read, layer, y, 8, 11)
                        row = ((tile - 2) * cells + cell) * fields
                        value = base[row : row + fields, :] + speed * outside
                    else:
                        row = (tile // 4 * cells + cell) * fields
                        lap = laplacian(read, layer, y, z_parts[row : row + fields, :], -4, 11)
                        value = 2.0 * read(layer, y) + speed * lap
                    row = (x * 4 + y // 4) * fields
                    side = y % 4 * HALF
                    sample[row : row + fields, side : side + HALF] = value
            hot = cell_ref[tile * PLACES : (tile + 1) * PLACES, :]
            picked = jnp.dot(jnp.concatenate(split(sample[...]), axis=0), hot, preferred_element_type=F32)
            picked = picked[: 16 * fields, :] + picked[16 * fields :, :]
            rows = slice(tile * fields, (tile + 1) * fields)
            line = wide_ref[rows, :]
            total = total_ref[rows, :]
            for i in range(16):
                chosen = line == i // 4 * 8 + chunk * 4 + i % 4
                total = total + jnp.where(chosen, picked[i * fields : (i + 1) * fields, :], 0.0)
            total_ref[rows, :] = total
        return carry

    lax.fori_loop(0, 2, respond, 0)

    for group in range(peers // 16):
        lefts, rights = [], []
        for tile in range(TILES):
            rows = slice(tile * fields, (tile + 1) * fields)
            value = total_ref[rows, :] * weight_ref[rows, :]
            high = value.astype(BF16).astype(F32)
            owner = owner_ref[rows, :]
            for part in (high, value - high):
                pieces = [jnp.where(owner == group * 16 + i, part, 0.0) for i in range(16)]
                lefts.append(jnp.concatenate(pieces, axis=0).astype(BF16))
                rights.append(slot_ref[tile * HALF : (tile + 1) * HALF, :])
        result = lax.dot_general(
            jnp.concatenate(lefts, axis=1), jnp.concatenate(rights, axis=1), NT, preferred_element_type=F32
        )
        table[group * 16 * fields : (group + 1) * 16 * fields, :] = result
    place = lax.broadcasted_iota(jnp.int32, (peers, HALF), 0)
    scales = jnp.zeros((peers, HALF), F32)
    for position, value in ((me[0], mine), (me[0] + 1 - 2 * (me[0] % 2), theirs)):
        scale = jnp.broadcast_to(value[cells + 16 : cells + 17, :], (peers, HALF))
        scales = jnp.where(place == position, scale, scales)
    table[peers * fields :, :] = scales


def basis_parts(first, basis, when, out):
    rank = basis.shape[0] // HALF

    def body(group, carry):
        here = window(basis, (first + group) * 8, basis.shape[0] - 15 * 8)
        there = window(out, group * rank, rank)
        for start in range(0, rank, 16):
            blocks = []
            for block in (start, start + 8):
                rows = [here[k * HALF : k * HALF + 8, :] for k in range(block, block + 8)]
                blocks.append(jnp.swapaxes(jnp.stack(rows, axis=0), 0, 1))
            for step in range(8):
                high, low = split(jnp.concatenate([block[step] for block in blocks], axis=0))
                there[start : start + 16, step * 256 : step * 256 + HALF] = high
                there[start : start + 16, step * 256 + HALF : (step + 1) * 256] = low
        return carry

    lax.fori_loop(0, 8, body, 0)


def turn_places(fields, place_ref, when, hot_ref):
    entries = place_ref.shape[1]
    lane = lax.broadcasted_iota(jnp.int32, (entries, HALF), 1)
    for tile in range(TILES):
        row = place_ref[tile * fields : tile * fields + 1, :]
        column = jnp.transpose(jnp.broadcast_to(row, (HALF, entries))).astype(jnp.int32)
        for part in range(2):
            hot = jnp.where(column == lane + part * HALF, 1.0, 0.0).astype(BF16)
            hot_ref[tile * entries : (tile + 1) * entries, part * HALF : (part + 1) * HALF] = hot


def adjoint(
    fields, peers, me, table, hot_ref, slot_ref, speed_ref, line_ref, owner_ref, weight_ref, turned, push_ref,
    prior_ref, band_ref, own_basis, own_basis_two, other_basis, other_basis_two, kept, lent, coeffs,
    high_ref, low_ref, inner_two, outer_two, inner_one, outer_one, z_term, image, scaled, *scratch,
):
    *lefts, image_parts = scratch
    entries = line_ref.shape[1]
    cells = LAYERS * 32
    rank = own_basis.shape[0] // 8
    slab, flat = PADDED * fields, 32 * fields
    ahead = 24 * fields
    clear_margins(inner_two, TILES * LAYERS, fields)
    clear_margins(inner_one, 2 * PAIR, fields)
    for owner in range(peers):
        rows = slice(owner * fields, (owner + 1) * fields)
        scaled[rows, :] = table[rows, :] * table[peers * fields + owner : peers * fields + owner + 1, :]
    for tile in range(TILES):
        rows = slice(tile * fields, (tile + 1) * fields)
        owner = owner_ref[rows, :]
        hot = slot_ref[tile * HALF : (tile + 1) * HALF, :]
        hot = jnp.concatenate([hot, hot], axis=0)
        total = jnp.zeros((fields, entries), F32)
        for group in range(peers // 16):
            parts = split(scaled[group * 16 * fields : (group + 1) * 16 * fields, :])
            found = jnp.dot(jnp.concatenate(parts, axis=1), hot, preferred_element_type=F32)
            for i in range(16):
                total = total + jnp.where(owner == group * 16 + i, found[i * fields : (i + 1) * fields, :], 0.0)
        value = total * weight_ref[rows, :]
        high = value.astype(BF16).astype(F32)
        high_ref[rows, :] = high
        low_ref[rows, :] = value - high

    def product(tile):
        left = lefts[tile]
        rows = slice(tile * fields, (tile + 1) * fields)
        line, high, low = line_ref[rows, :], high_ref[rows, :], low_ref[rows, :]
        for i in range(0, 64, 2):
            chosen = [line == i, line == i + 1]
            row = slice(i * fields, (i + 2) * fields)
            for part, side in ((high, slice(0, entries)), (low, slice(entries, 2 * entries))):
                both = [jnp.where(which, part, 0.0) for which in chosen]
                left[row, side] = jnp.concatenate(both, axis=0).astype(BF16)
        hot = hot_ref[tile * entries : (tile + 1) * entries, :]
        return jnp.dot(left[...], jnp.concatenate([hot, hot], axis=0), preferred_element_type=F32)

    def inject(tile, value):
        for i in range(64):
            for step in range(2):
                layer, y = tile * LAYERS + i // 16, i % 16 * 2 + step
                now = value[i * fields : (i + 1) * fields, step * HALF : (step + 1) * HALF]
                if 1 <= tile <= 4:
                    row = ((layer - LAYERS) * 32 + y) * fields
                    outer_two[row : row + fields, :] = now
                speed = spread(speed_ref, layer * 32 + y, fields)
                row = layer * slab + (REACH + y) * fields
                inner_two[row : row + fields, :] = speed * now
        if 1 <= tile <= 4:
            along_z(inner_two, tile * LAYERS, LAYERS, fields, band_ref, z_term, (tile - 1) * cells * fields)

    values = product(0)
    for tile in range(TILES):
        after = product(tile + 1) if tile + 1 < TILES else None
        inject(tile, values)
        values = after

    def step_one(index, carry):
        pair, chunk = index // 4, index % 4
        start, skip = pair * PAIR * slab + chunk * 8 * fields, pair * PAIR * flat + chunk * 8 * fields
        here = window(inner_two, start, 2 * PAIR * slab - ahead)
        two, one, z_part = (window(ref, skip, PAIR * flat - ahead) for ref in (outer_two, outer_one, z_term))
        out = window(inner_one, start, PAIR * slab - ahead)
        speed = window(speed_ref, cells + pair * 2 * cells + chunk * 8, 2 * cells - 24)

        def load(layer, y):
            row = (layer + LAYERS) * slab + (REACH + y) * fields
            return here[row : row + fields, :]

        for side in range(2):
            get = kept_rows(load)
            for y in range(8):
                for x in range(side * LAYERS, (side + 1) * LAYERS):
                    cell = x * 32 + y
                    row = slice(cell * fields, (cell + 1) * fields)
                    now = 2.0 * two[row, :] + laplacian(get, x, y, z_part[row, :], -4, 11)
                    one[row, :] = now
                    row = x * slab + (REACH + y) * fields
                    out[row : row + fields, :] = spread(speed, cell, fields) * now
        return carry

    lax.fori_loop(0, 8, step_one, 0)
    along_z(inner_one, LAYERS, PAIR, fields, band_ref, z_term)
    mine = me[0] % 2

    def step_two_chunk(chunk, which):
        skip = chunk * 8 * fields
        here = window(inner_one, skip, 2 * PAIR * slab - ahead)
        two_rows, one_rows = (window(ref, LAYERS * flat + skip, PAIR * flat - ahead) for ref in (outer_two, outer_one))
        z_part, there, out = (window(ref, skip, PAIR * flat - ahead) for ref in (z_term, turned, image))
        push = window(push_ref, chunk * 8, 6 * cells - 24)
        damping = window(prior_ref, chunk * 8, 2 * cells - 24)

        def load(layer, y):
            row = (layer + LAYERS) * slab + (REACH + y) * fields
            return here[row : row + fields, :]

        nothing = jnp.zeros((fields, HALF), F32)
        for side in range(2):
            get = kept_rows(load)
            for y in range(8):
                for x in range(side * LAYERS, (side + 1) * LAYERS):
                    cell = x * 32 + y
                    row = slice(cell * fields, (cell + 1) * fields)
                    two, one = two_rows[row, :], one_rows[row, :]
                    zero = 2.0 * one - two + laplacian(get, x, y, z_part[row, :], -4, 11)
                    value = spread(push, cell, fields) * zero
                    value = value + spread(push, 2 * cells + cell, fields) * one
                    value = value + spread(push, 4 * cells + cell, fields) * two
                    value = value + spread(damping, cell, fields) * there[row, :]
                    out[row, :] = value
                    high = value.astype(BF16).astype(F32)
                    start, lane = (x * 2 + which) * 2 * fields, y * 256
                    rows = slice(start, start + 2 * fields)
                    image_parts[rows, lane : lane + HALF] = jnp.concatenate([high, value - high], axis=0).astype(BF16)
                    image_parts[rows, lane + HALF : lane + 256] = jnp.concatenate([high, nothing], axis=0).astype(BF16)

    def step_two(pair, total):
        for which in range(2):
            step_two_chunk(pair * 2 + which, which)
        for side, pieces in ((mine, (own_basis, own_basis_two)), (1 - mine, (other_basis, other_basis_two))):
            for x in range(LAYERS):
                columns = pieces[x // 2][at((x % 2 * 4 + pair * 2) * rank, 2 * rank), :]
                parts = image_parts[at((side * LAYERS + x) * 4 * fields, 4 * fields), :]
                total = total + lax.dot_general(parts, columns, NT, preferred_element_type=F32)
        return total

    total = lax.fori_loop(0, 2, step_two, jnp.zeros((4 * fields, 2 * rank), F32))
    total = total[: 2 * fields, :rank] + total[2 * fields :, rank:]
    coeffs[...] = total[:fields, :] + total[fields:, :]
    kept[...] = image[at(mine * LAYERS * flat, LAYERS * flat), :]
    lent[...] = image[at((1 - mine) * LAYERS * flat, LAYERS * flat), :]


def remainder(fields, me, image, borrowed, basis, basis_two, *rest):
    *shares, out, coeffs, natural, sem = rest
    rank = coeffs.shape[1]
    half = fields // 2
    mine = half_of(me)
    while len(shares) > 1:
        shares = [shares[i][...] + shares[i + 1][...] for i in range(0, len(shares), 2)]
    total = shares[0][...]
    coeffs[at(mine * half, half), :] = total[:half, :]
    coeffs[at((1 - mine) * half, half), :] = total[half:, :]
    parts = jnp.concatenate(split(total), axis=0)
    whole = natural.reshape(out.shape)
    first, second = (window(natural, side * half * HALF, half * HALF) for side in (mine, 1 - mine))

    def leave(x):
        return pltpu.make_async_copy(whole.at[:, x], out.at[:, x], sem.at[x])

    for x in range(LAYERS):
        for part in range(4):
            columns = (basis, basis_two)[x // 2][(x % 2 * 4 + part) * rank : (x % 2 * 4 + part + 1) * rank, :]
            both = jnp.dot(parts, columns, preferred_element_type=F32)
            cell = x * 32 + part * 8
            results = ([], [])
            for step in range(8):
                side = step * 256
                along = both[:fields, side : side + HALF] + both[:fields, side + HALF : side + 256]
                along = along + both[fields:, side : side + HALF]
                row = slice((cell + step) * half, (cell + step + 1) * half)
                results[0].append(image[row, :] - along[:half, :])
                results[1].append(borrowed[row, :] - along[half:, :])
            for ref, values in zip((first, second), results):
                values = jnp.swapaxes(jnp.stack(values, axis=0), 0, 1)
                for p in range(half):
                    ref[p * HALF + cell : p * HALF + cell + 8, :] = values[p]
        leave(x).start()
    for x in range(LAYERS):
        leave(x).wait()


def call(kernel, inputs, out_shape, scratch, flops, size, scalars=0, far=0, far_out=0, room=16):
    smem = pl.BlockSpec(memory_space=pltpu.SMEM)
    vmem = pl.BlockSpec(memory_space=pltpu.VMEM)
    hbm = pl.BlockSpec(memory_space=pltpu.HBM)
    inputs = [
        pltpu.with_memory_space_constraint(array, pltpu.HBM) if scalars <= i < scalars + far else array
        for i, array in enumerate(inputs)
    ]
    return pl.pallas_call(
        kernel,
        out_shape=out_shape,
        in_specs=[smem] * scalars + [hbm] * far + [vmem] * (len(inputs) - scalars - far),
        out_specs=[hbm] * far_out + [vmem] * (len(out_shape) - far_out),
        scratch_shapes=scratch,
        cost_estimate=pl.CostEstimate(flops=flops, bytes_accessed=size, transcendentals=0),
        compiler_params=pltpu.CompilerParams(vmem_limit_bytes=room * 2**20),
    )(*inputs)


def struct(*shape, dtype=F32):
    return jax.ShapeDtypeStruct(shape, dtype)


def swapped(array, axis, bits):
    count = lax.axis_size(axis)
    return lax.ppermute(array, axis, [(i, i ^ bits) for i in range(count)])


def local(
    probes,
    sources,
    kappa,
    prior,
    basis,
    entry_cell,
    entry_owner,
    entry_slot,
    entry_weight,
    entry_count,
    trace_weight,
):
    rank = basis.shape[0]
    fields = probes.shape[0] // 2
    entries = entry_cell.shape[0]
    peers = lax.axis_size("space")
    slab, flat = PADDED * fields, 32 * fields
    cells = LAYERS * 32
    rows = entries // HALF
    basis = basis.reshape(rank * cells, HALF)
    me = lax.axis_index("space").astype(jnp.int32).reshape(1)

    own, probes_near, sources_near, prior_near, lent, matrix = call(
        pack,
        (
            entry_count,
            me,
            probes.reshape(2 * fields * cells, HALF),
            sources.reshape(3 * cells, HALF),
            prior.reshape(cells, HALF),
            kappa.reshape(cells, HALF),
            entry_cell.reshape(rows, HALF),
            entry_owner.reshape(rows, HALF),
            entry_slot.reshape(rows, HALF),
            entry_weight.reshape(rows, HALF),
            trace_weight.reshape(1, HALF),
        ),
        [
            struct(cells + 4 * rows + 8, HALF),
            struct(fields * cells, HALF),
            struct(3 * cells, HALF),
            struct(cells, HALF),
            struct((fields + 4) * cells, HALF),
            struct(256, 256, dtype=BF16),
        ],
        [pltpu.VMEM((3, rows, HALF), jnp.int32), pltpu.VMEM((16, HALF), F32), pltpu.SemaphoreType.DMA((12,))],
        100_000,
        2 * 2**20,
        scalars=2,
        far=9,
    )
    partner = swapped(own, "space", 1)
    lent, partner = lax.optimization_barrier((lent, partner))
    borrowed = swapped(lent, "space", 1)
    passed = lax.ppermute(
        jnp.concatenate([own, partner], axis=0),
        "space",
        [pair for i in range(1, peers - 1, 2) for pair in ((i, i + 1), (i + 1, i))] + [(0, 0), (peers - 1, peers - 1)],
    )

    turned, first, second, third, push, damping = call(
        functools.partial(forward_own, fields),
        (me, probes_near, sources_near, prior_near, own, partner, borrowed, matrix),
        [
            struct(PAIR * flat, HALF),
            struct(PAIR * slab, HALF),
            struct(PAIR * slab, HALF),
            struct(PAIR * flat, HALF),
            struct(6 * cells, HALF),
            struct(2 * cells, HALF),
        ],
        [pltpu.VMEM((PAIR * flat, HALF), F32), pltpu.VMEM((2 * cells, HALF), F32)],
        600_000_000,
        6 * 2**20,
        scalars=1,
    )
    passed, second = lax.optimization_barrier((passed, second))
    across = swapped(passed, "space", 1)
    across, basis_there = lax.optimization_barrier((across, basis))
    basis_there = swapped(basis_there, "space", 1)
    table, place, slot_hot, speed, line, owner, weight = call(
        functools.partial(forward_window, fields, peers),
        (me, first, second, third, own, partner, passed, across, matrix),
        [
            struct(peers * (fields + 1), HALF),
            struct(TILES * fields, entries),
            struct(TILES * HALF, entries, dtype=BF16),
            struct(TILES * cells, HALF),
            struct(TILES * fields, entries, dtype=jnp.int32),
            struct(TILES * fields, entries, dtype=jnp.int32),
            struct(TILES * fields, entries),
        ],
        [
            pltpu.VMEM((TILES * PLACES, entries), BF16),
            pltpu.VMEM((TILES * fields, entries), jnp.int32),
            pltpu.VMEM((LAYERS * slab, HALF), F32),
            pltpu.VMEM((LAYERS * slab, HALF), F32),
            pltpu.VMEM((PAIR * flat, HALF), F32),
            pltpu.VMEM((TILES * fields, entries), F32),
        ]
        + [pltpu.VMEM((16 * fields, PLACES), F32)] * TILES,
        3_000_000_000,
        6 * 2**20,
        scalars=1,
        room=20,
    )
    columns = []
    bits = 2
    while bits < peers:
        arrived = swapped(table, "space", bits + 1)
        for i in ((0,), (1,), (2, 3))[len(columns)] if len(columns) < 3 else ():
            (some,) = call(
                functools.partial(basis_parts, 8 * (i % 2)),
                ((basis, basis_there)[i // 2], table),
                [struct(8 * rank, 2048, dtype=BF16)],
                [],
                10_000_000,
                4 * 2**20,
            )
            columns.append(some)
        if bits == 2:
            (turned_hot,) = call(
                functools.partial(turn_places, fields),
                (place, table),
                [struct(TILES * entries, 256, dtype=BF16)],
                [],
                10_000_000,
                4 * 2**20,
            )
            arrived, turned_hot = lax.optimization_barrier((arrived, turned_hot))
        arrived, columns = lax.optimization_barrier((arrived, columns))
        table = table + arrived
        bits *= 2
    kept, lent, coeffs = call(
        functools.partial(adjoint, fields, peers),
        (me, table, turned_hot, slot_hot, speed, line, owner, weight, turned, push, damping, matrix, *columns),
        [struct(LAYERS * flat, HALF), struct(LAYERS * flat, HALF), struct(fields, rank)],
        [
            pltpu.VMEM((TILES * fields, entries), F32),
            pltpu.VMEM((TILES * fields, entries), F32),
            pltpu.VMEM((TILES * LAYERS * slab, HALF), F32),
            pltpu.VMEM((2 * PAIR * flat, HALF), F32),
            pltpu.VMEM((2 * PAIR * slab, HALF), F32),
            pltpu.VMEM((2 * PAIR * flat, HALF), F32),
            pltpu.VMEM((2 * PAIR * flat, HALF), F32),
            pltpu.VMEM((PAIR * flat, HALF), F32),
            pltpu.VMEM((peers * fields, HALF), F32),
        ]
        + [pltpu.VMEM((64 * fields, 2 * entries), BF16)] * TILES
        + [pltpu.VMEM((4 * PAIR * fields, 2048), BF16)],
        5_000_000_000,
        10 * 2**20,
        scalars=1,
        room=30,
    )
    coeffs = jnp.concatenate([coeffs, swapped(coeffs, "space", 1)], axis=0)
    lent, coeffs = lax.optimization_barrier((lent, coeffs))
    borrowed = swapped(lent, "space", 1)
    bits = 2
    while bits * 2 < peers:
        coeffs = coeffs + swapped(coeffs, "space", bits + 1)
        bits *= 2
    shares = [coeffs, swapped(coeffs, "space", bits + 1)]
    hess_probe, coeffs = call(
        functools.partial(remainder, 2 * fields),
        (me, kept, borrowed, *columns[:2], *shares),
        [struct(*probes.shape), struct(2 * fields, rank)],
        [pltpu.VMEM((2 * fields * cells, HALF), F32), pltpu.SemaphoreType.DMA((LAYERS,))],
        200_000_000,
        6 * 2**20,
        scalars=1,
        far_out=1,
    )
    return hess_probe, coeffs.T


def solution(mesh):
    return jax.shard_map(
        local,
        mesh=mesh,
        in_specs=(
            P("group", "space", None, None),
            P(None, ("group", "space"), None, None),
            P(("group", "space"), None, None),
            P(("group", "space"), None, None),
            P("group", "space", None, None),
            P(("group", "space")),
            P(("group", "space")),
            P(("group", "space")),
            P(("group", "space")),
            P(("group", "space")),
            P(("group", "space")),
        ),
        out_specs=(P("group", "space", None, None), P("group", None)),
        check_vma=False,
    )
```

```python
import functools

import jax
import jax.numpy as jnp
from jax import lax
from jax.experimental import pallas as pl
from jax.experimental.pallas import tpu as pltpu
from jax.sharding import PartitionSpec as P

STENCIL = (-205.0 / 72.0, 8.0 / 5.0, -1.0 / 5.0, 8.0 / 315.0, -1.0 / 560.0)
CENTER = 3.0 * STENCIL[0]
REACH = 4
LAYERS = 4
PAIR = 8
TILES = 6
PADDED = 40
HALF = 128
PLACES = 512
F32 = jnp.float32
BF16 = jnp.bfloat16
NT = (((1,), (1,)), ((), ()))


def split(value):
    high = value.astype(BF16)
    low = (value - high.astype(F32)).astype(BF16)
    return high, low


def at(row, count=16):
    return pl.ds(pl.multiple_of(row, 8), count)


def window(ref, start, size):
    return ref.at[pl.ds(pl.multiple_of(start, 8), size)]


def kept_rows(load):
    rows = {}

    def get(layer, y):
        if (layer, y) not in rows:
            rows[layer, y] = load(layer, y)
        return rows[layer, y]

    return get


def half_of(me):
    value = me[0]
    for by in (4, 2, 1):
        value = jnp.bitwise_xor(value, lax.shift_right_logical(value, by))
    return jnp.bitwise_and(value, 1)


def spread(ref, row, fields):
    return jnp.broadcast_to(ref[pl.ds(row, 1), :], (fields, HALF))


def clear_margins(ref, layers, fields):
    margin = jnp.zeros((REACH * fields, HALF), F32)
    for layer in range(layers):
        start = layer * PADDED * fields
        ref[start : start + REACH * fields, :] = margin
        start += (PADDED - REACH) * fields
        ref[start : start + REACH * fields, :] = margin


def along_z(ref, first, layers, fields, band_ref, out_ref, row=0):
    pieces = [ref[at(((first + x) * PADDED + REACH) * fields, 32 * fields), :] for x in range(layers)]
    high, low = split(jnp.concatenate(pieces, axis=0))
    both = jnp.dot(jnp.concatenate([high, low], axis=1), band_ref[...], preferred_element_type=F32)
    out_ref[at(row, layers * 32 * fields), :] = both[:, :HALF] + both[:, HALF:]


def laplacian(get, x, y, z_term, lowest, highest):
    total = z_term
    for k in range(1, REACH + 1):
        ring = get(x, y + k) + get(x, y - k)
        if x + k <= highest:
            ring = ring + get(x + k, y)
        if x - k >= lowest:
            ring = ring + get(x - k, y)
        total = total + STENCIL[k] * ring
    return total


def pack(
    count, me, probes, sources, prior, kappa, cell, owner, slot, weight, scale,
    statics, probes_out, sources_out, prior_out, lent, band_ref, small_int, small_float, sem,
):
    rows = cell.shape[0]
    cells = kappa.shape[0]
    half = probes_out.shape[0]
    mine = half_of(me)
    other = probes.at[pl.ds(pl.multiple_of((1 - mine) * half, 8), half)]
    small = [
        pltpu.make_async_copy(kappa, statics.at[pl.ds(0, cells)], sem.at[0]),
        pltpu.make_async_copy(cell, small_int.at[0], sem.at[1]),
        pltpu.make_async_copy(owner, small_int.at[1], sem.at[2]),
        pltpu.make_async_copy(slot, small_int.at[2], sem.at[3]),
        pltpu.make_async_copy(weight, small_float.at[pl.ds(0, rows)], sem.at[4]),
        pltpu.make_async_copy(scale, small_float.at[pl.ds(8, 1)], sem.at[5]),
    ]
    large = [
        pltpu.make_async_copy(other, lent.at[pl.ds(0, half)], sem.at[6]),
        pltpu.make_async_copy(sources, lent.at[pl.ds(half, 3 * cells)], sem.at[7]),
        pltpu.make_async_copy(prior, lent.at[pl.ds(half + 3 * cells, cells)], sem.at[8]),
        pltpu.make_async_copy(probes.at[pl.ds(pl.multiple_of(mine * half, 8), half)], probes_out, sem.at[9]),
        pltpu.make_async_copy(sources, sources_out, sem.at[10]),
        pltpu.make_async_copy(prior, prior_out, sem.at[11]),
    ]
    for copy in small + large:
        copy.start()
    apart = lax.broadcasted_iota(jnp.int32, (HALF, HALF), 0) - lax.broadcasted_iota(jnp.int32, (HALF, HALF), 1)
    full = jnp.where(apart == 0, CENTER, jnp.zeros((HALF, HALF), F32))
    for reach in range(1, REACH + 1):
        full = jnp.where(jnp.abs(apart) == reach, STENCIL[reach], full)
    high, low = split(full)
    band_ref[0:HALF, 0:HALF] = high
    band_ref[HALF:, 0:HALF] = high
    band_ref[0:HALF, HALF:] = low
    band_ref[HALF:, HALF:] = jnp.zeros_like(low)
    for copy in small:
        copy.wait()
    for i in range(3):
        statics[cells + i * rows : cells + (i + 1) * rows, :] = small_int[i].astype(F32)
    place = lax.broadcasted_iota(jnp.int32, (rows, HALF), 0) * HALF
    place = place + lax.broadcasted_iota(jnp.int32, (rows, HALF), 1)
    live = jnp.where(place < count[0], small_float[0:rows, :], 0.0)
    statics[cells + 3 * rows : cells + 4 * rows, :] = live
    statics[cells + 4 * rows : cells + 4 * rows + 8, :] = jnp.broadcast_to(small_float[8:9, :], (8, HALF))
    for copy in large:
        copy.wait()


def forward_own(
    fields, me, probes, sources, prior, own, partner, borrowed, band_ref,
    turned, first, second, third, push_ref, prior_ref, z_term, speed_ref,
):
    slab, flat, cells = PADDED * fields, 32 * fields, LAYERS * 32
    ahead = 24 * fields
    half = probes.shape[0]
    mine = me[0] % 2
    clear_margins(first, PAIR, fields)
    clear_margins(second, PAIR, fields)
    lent = borrowed.at[pl.ds(half, 4 * cells)]
    for side, pushes, damping, statics in ((mine, sources, prior, own), (1 - mine, lent, None, partner)):
        for i in range(3):
            push_ref[at(i * 2 * cells + side * cells, cells), :] = pushes[i * cells : (i + 1) * cells, :]
        place = at(side * cells, cells)
        prior_ref[place, :] = lent[3 * cells :, :] if damping is None else damping[...]
        speed_ref[place, :] = statics[0:cells, :]

    def load(chunk, carry):
        for side, ref in ((mine, probes), (1 - mine, borrowed)):
            there = window(turned, side * LAYERS * flat + chunk * 8 * fields, LAYERS * flat - ahead)
            padded = window(first, side * LAYERS * slab + chunk * 8 * fields, LAYERS * slab - ahead)
            here = window(ref, chunk * 8, half - 24)
            push = window(push_ref, side * cells + chunk * 8, cells - 24)
            for x in range(LAYERS):
                rows = [here[p * cells + x * 32 : p * cells + x * 32 + 8, :] for p in range(fields)]
                values = jnp.swapaxes(jnp.stack(rows, axis=0), 0, 1)
                for y in range(8):
                    cell = x * 32 + y
                    there[cell * fields : (cell + 1) * fields, :] = values[y]
                    row = x * slab + (REACH + y) * fields
                    padded[row : row + fields, :] = values[y] * spread(push, cell, fields)
        return carry

    lax.fori_loop(0, 4, load, 0)

    def sweep(field, emit):
        along_z(field, 0, PAIR, fields, band_ref, z_term)

        def body(chunk, carry):
            padded = window(field, chunk * 8 * fields, PAIR * slab - ahead)
            z_part = window(z_term, chunk * 8 * fields, PAIR * flat - ahead)
            speed = window(speed_ref, chunk * 8, 2 * cells - 24)
            push = window(push_ref, chunk * 8, 6 * cells - 24)
            there = window(turned, chunk * 8 * fields, PAIR * flat - ahead)
            put = emit(chunk)

            def load(layer, y):
                row = layer * slab + (REACH + y) * fields
                return padded[row : row + fields, :]

            for side in range(2):
                get = kept_rows(load)
                for y in range(8):
                    for x in range(side * LAYERS, (side + 1) * LAYERS):
                        cell = x * 32 + y
                        row = slice(cell * fields, (cell + 1) * fields)
                        change = spread(speed, cell, fields) * laplacian(get, x, y, z_part[row, :], 0, PAIR - 1)
                        put(x, y, get(x, y), change, there[row, :], push)
            return carry

        lax.fori_loop(0, 4, body, 0)

    def step_one(chunk):
        out = window(second, chunk * 8 * fields, PAIR * slab - ahead)

        def put(x, y, now, change, probe, push):
            change = change + probe * spread(push, 2 * cells + x * 32 + y, fields)
            row = x * slab + (REACH + y) * fields
            out[row : row + fields, :] = 2.0 * now + change

        return put

    sweep(first, step_one)

    def step_two(chunk):
        before = window(first, chunk * 8 * fields, PAIR * slab - ahead)
        out = window(third, chunk * 8 * fields, PAIR * flat - ahead)

        def put(x, y, now, change, probe, push):
            row = x * slab + (REACH + y) * fields
            change = change - before[row : row + fields, :]
            cell = x * 32 + y
            change = change + probe * spread(push, 4 * cells + cell, fields)
            out[cell * fields : (cell + 1) * fields, :] = 2.0 * now + change

        return put

    sweep(second, step_two)


def entry_row(value, row):
    return jnp.concatenate([value[row + i : row + i + 1, :] for i in range(4)], axis=1)


def forward_window(
    fields, peers, me, first, second, third, own, partner, passed, across, band_ref,
    table, place_ref, slot_ref, speed_ref, line_ref, owner_ref, weight_ref,
    cell_ref, wide_ref, below, above, z_term, total_ref, *samples,
):
    entries = line_ref.shape[1]
    cells = LAYERS * 32
    length = own.shape[0]
    odd = me[0] % 2 == 1
    slab, flat = PADDED * fields, 32 * fields
    clear_margins(below, LAYERS, fields)
    clear_margins(above, LAYERS, fields)
    total_ref[...] = jnp.zeros_like(total_ref)
    mine, theirs = own[...], partner[...]
    low = jnp.where(me[0] < 2, 0.0, jnp.where(odd, across[...], passed[...]))
    high = jnp.where(me[0] >= peers - 2, 0.0, jnp.where(odd, passed[...], across[...]))
    tiles = (
        low[length:, :],
        low[0:length, :],
        jnp.where(odd, theirs, mine),
        jnp.where(odd, mine, theirs),
        high[0:length, :],
        high[length:, :],
    )
    place = lax.broadcasted_iota(jnp.int32, (PLACES, entries), 0)
    slot_place = lax.broadcasted_iota(jnp.int32, (HALF, entries), 0)
    for tile, value in enumerate(tiles):
        speed_ref[tile * cells : (tile + 1) * cells, :] = value[0:cells, :]
        cell = entry_row(value, cells).astype(jnp.int32)
        owner = entry_row(value, cells + 4).astype(jnp.int32)
        slot = entry_row(value, cells + 8).astype(jnp.int32)
        weight = entry_row(value, cells + 12)
        hot = jnp.where(place == jnp.bitwise_and(cell, PLACES - 1), 1.0, 0.0)
        cell_ref[tile * PLACES : (tile + 1) * PLACES, :] = hot.astype(BF16)
        hot = jnp.where(slot_place == slot, 1.0, 0.0)
        slot_ref[tile * HALF : (tile + 1) * HALF, :] = hot.astype(BF16)
        rows = slice(tile * fields, (tile + 1) * fields)
        line_ref[rows, :] = jnp.broadcast_to(lax.shift_right_logical(cell, 8), (fields, entries))
        wide_ref[rows, :] = jnp.broadcast_to(lax.shift_right_logical(cell, 9), (fields, entries))
        place_ref[rows, :] = jnp.broadcast_to(jnp.bitwise_and(cell, 255), (fields, entries)).astype(F32)
        owner_ref[rows, :] = jnp.broadcast_to(owner, (fields, entries))
        weight_ref[rows, :] = jnp.broadcast_to(weight, (fields, entries))

    def outward(chunk, carry):
        ahead = 24 * fields
        speed = window(speed_ref, chunk * 8, TILES * cells - 24)
        here = window(first, chunk * 8 * fields, PAIR * slab - ahead)
        down_out, up_out = (window(ref, chunk * 8 * fields, LAYERS * slab - ahead) for ref in (below, above))
        for y in range(8):
            rows = [slice(x * slab + (REACH + y) * fields, x * slab + (REACH + y + 1) * fields) for x in range(PAIR)]
            field = [here[row, :] for row in rows]
            for x in range(LAYERS):
                up = sum(STENCIL[4 + x - other] * field[4 + other] for other in range(x, LAYERS))
                down = sum(STENCIL[4 + other - x] * field[other] for other in range(x + 1))
                up_out[rows[x], :] = spread(speed, 4 * cells + x * 32 + y, fields) * up
                down_out[rows[x], :] = spread(speed, cells + x * 32 + y, fields) * down
        return carry

    lax.fori_loop(0, 4, outward, 0)
    along_z(below, 0, LAYERS, fields, band_ref, z_term, 0)
    along_z(above, 0, LAYERS, fields, band_ref, z_term, cells * fields)

    def far(read, x, y, lowest, highest):
        total = None
        for other in range(lowest, highest + 1):
            if 1 <= abs(x - other) <= REACH:
                term = STENCIL[abs(x - other)] * read(other, y)
                total = term if total is None else total + term
        return total

    def respond(chunk, carry):
        ahead = 16 * fields
        speeds = window(speed_ref, chunk * 16, TILES * cells - 16)
        low_side, high_side = (window(ref, chunk * 16 * fields, LAYERS * slab - ahead) for ref in (below, above))
        inside = window(second, chunk * 16 * fields, PAIR * slab - ahead)
        base = window(third, chunk * 16 * fields, PAIR * flat - ahead)
        z_parts = window(z_term, chunk * 16 * fields, PAIR * flat - ahead)

        def load(layer, y):
            if layer < 0:
                ref, layer = low_side, layer + LAYERS
            elif layer >= PAIR:
                ref, layer = high_side, layer - PAIR
            else:
                ref = inside
            row = layer * slab + (REACH + y) * fields
            return ref[row : row + fields, :]

        for tile in range(TILES):
            sample = samples[tile]
            read = kept_rows(load)
            for y in range(16):
                for x in range(LAYERS):
                    cell = x * 32 + y
                    layer = (tile - 2) * LAYERS + x
                    speed = spread(speeds, tile * cells + cell, fields)
                    if tile in (0, 5):
                        value = speed * far(read, layer, y, -4, 11)
                    elif tile in (2, 3):
                        outside = far(read, layer, y, -4, -1) if tile == 2 else far(read, layer, y, 8, 11)
                        row = ((tile - 2) * cells + cell) * fields
                        value = base[row : row + fields, :] + speed * outside
                    else:
                        row = (tile // 4 * cells + cell) * fields
                        lap = laplacian(read, layer, y, z_parts[row : row + fields, :], -4, 11)
                        value = 2.0 * read(layer, y) + speed * lap
                    row = (x * 4 + y // 4) * fields
                    side = y % 4 * HALF
                    sample[row : row + fields, side : side + HALF] = value
            hot = cell_ref[tile * PLACES : (tile + 1) * PLACES, :]
            picked = jnp.dot(jnp.concatenate(split(sample[...]), axis=0), hot, preferred_element_type=F32)
            picked = picked[: 16 * fields, :] + picked[16 * fields :, :]
            rows = slice(tile * fields, (tile + 1) * fields)
            line = wide_ref[rows, :]
            total = total_ref[rows, :]
            for i in range(16):
                chosen = line == i // 4 * 8 + chunk * 4 + i % 4
                total = total + jnp.where(chosen, picked[i * fields : (i + 1) * fields, :], 0.0)
            total_ref[rows, :] = total
        return carry

    lax.fori_loop(0, 2, respond, 0)

    for group in range(peers // 16):
        lefts, rights = [], []
        for tile in range(TILES):
            rows = slice(tile * fields, (tile + 1) * fields)
            value = total_ref[rows, :] * weight_ref[rows, :]
            high = value.astype(BF16).astype(F32)
            owner = owner_ref[rows, :]
            for part in (high, value - high):
                pieces = [jnp.where(owner == group * 16 + i, part, 0.0) for i in range(16)]
                lefts.append(jnp.concatenate(pieces, axis=0).astype(BF16))
                rights.append(slot_ref[tile * HALF : (tile + 1) * HALF, :])
        result = lax.dot_general(
            jnp.concatenate(lefts, axis=1), jnp.concatenate(rights, axis=1), NT, preferred_element_type=F32
        )
        table[group * 16 * fields : (group + 1) * 16 * fields, :] = result
    place = lax.broadcasted_iota(jnp.int32, (peers, HALF), 0)
    scales = jnp.zeros((peers, HALF), F32)
    for position, value in ((me[0], mine), (me[0] + 1 - 2 * (me[0] % 2), theirs)):
        scale = jnp.broadcast_to(value[cells + 16 : cells + 17, :], (peers, HALF))
        scales = jnp.where(place == position, scale, scales)
    table[peers * fields :, :] = scales


def basis_parts(first, basis, when, out):
    rank = basis.shape[0] // HALF

    def body(group, carry):
        here = window(basis, (first + group) * 8, basis.shape[0] - 15 * 8)
        there = window(out, group * rank, rank)
        for start in range(0, rank, 16):
            blocks = []
            for block in (start, start + 8):
                rows = [here[k * HALF : k * HALF + 8, :] for k in range(block, block + 8)]
                blocks.append(jnp.swapaxes(jnp.stack(rows, axis=0), 0, 1))
            for step in range(8):
                high, low = split(jnp.concatenate([block[step] for block in blocks], axis=0))
                there[start : start + 16, step * 256 : step * 256 + HALF] = high
                there[start : start + 16, step * 256 + HALF : (step + 1) * 256] = low
        return carry

    lax.fori_loop(0, 8, body, 0)


def turn_places(fields, place_ref, when, hot_ref):
    entries = place_ref.shape[1]
    lane = lax.broadcasted_iota(jnp.int32, (entries, HALF), 1)
    for tile in range(TILES):
        row = place_ref[tile * fields : tile * fields + 1, :]
        column = jnp.transpose(jnp.broadcast_to(row, (HALF, entries))).astype(jnp.int32)
        for part in range(2):
            hot = jnp.where(column == lane + part * HALF, 1.0, 0.0).astype(BF16)
            hot_ref[tile * entries : (tile + 1) * entries, part * HALF : (part + 1) * HALF] = hot


def adjoint(
    fields, peers, me, table, hot_ref, slot_ref, speed_ref, line_ref, owner_ref, weight_ref, turned, push_ref,
    prior_ref, band_ref, own_basis, own_basis_two, other_basis, other_basis_two, kept, lent, coeffs,
    high_ref, low_ref, inner_two, outer_two, inner_one, outer_one, z_term, image, scaled, *scratch,
):
    left, image_parts = scratch
    entries = line_ref.shape[1]
    cells = LAYERS * 32
    rank = own_basis.shape[0] // 8
    slab, flat = PADDED * fields, 32 * fields
    ahead = 24 * fields
    clear_margins(inner_two, TILES * LAYERS, fields)
    clear_margins(inner_one, 2 * PAIR, fields)
    for owner in range(peers):
        rows = slice(owner * fields, (owner + 1) * fields)
        scaled[rows, :] = table[rows, :] * table[peers * fields + owner : peers * fields + owner + 1, :]
    def weigh(tile, carry):
        rows = at(tile * fields, fields)
        owner = owner_ref[rows, :]
        hot = slot_ref[at(tile * HALF, HALF), :]
        hot = jnp.concatenate([hot, hot], axis=0)
        total = jnp.zeros((fields, entries), F32)
        for group in range(peers // 16):
            parts = split(scaled[group * 16 * fields : (group + 1) * 16 * fields, :])
            found = jnp.dot(jnp.concatenate(parts, axis=1), hot, preferred_element_type=F32)
            for i in range(16):
                total = total + jnp.where(owner == group * 16 + i, found[i * fields : (i + 1) * fields, :], 0.0)
        value = total * weight_ref[rows, :]
        high = value.astype(BF16).astype(F32)
        high_ref[rows, :] = high
        low_ref[rows, :] = value - high
        return carry

    lax.fori_loop(0, TILES, weigh, 0)

    def inject(tile, carry):
        rows = at(tile * fields, fields)
        line, high, low = line_ref[rows, :], high_ref[rows, :], low_ref[rows, :]
        for i in range(0, 64, 2):
            chosen = [line == i, line == i + 1]
            row = slice(i * fields, (i + 2) * fields)
            for part, side in ((high, slice(0, entries)), (low, slice(entries, 2 * entries))):
                both = [jnp.where(which, part, 0.0) for which in chosen]
                left[row, side] = jnp.concatenate(both, axis=0).astype(BF16)
        hot = hot_ref[at(tile * entries, entries), :]
        value = jnp.dot(left[...], jnp.concatenate([hot, hot], axis=0), preferred_element_type=F32)
        two = window(outer_two, tile * LAYERS * flat, LAYERS * flat)
        out = window(inner_two, tile * LAYERS * slab, LAYERS * slab)
        speed = window(speed_ref, tile * cells, cells)
        for i in range(64):
            for step in range(2):
                x, y = i // 16, i % 16 * 2 + step
                now = value[i * fields : (i + 1) * fields, step * HALF : (step + 1) * HALF]
                cell = x * 32 + y
                two[cell * fields : (cell + 1) * fields, :] = now
                row = x * slab + (REACH + y) * fields
                out[row : row + fields, :] = spread(speed, cell, fields) * now
        return carry

    lax.fori_loop(0, TILES, inject, 0)

    def terms(tile, carry):
        along_z(inner_two, (tile + 1) * LAYERS, LAYERS, fields, band_ref, z_term, tile * cells * fields)
        return carry

    lax.fori_loop(0, 4, terms, 0)

    def step_one(index, carry):
        pair, chunk = index // 4, index % 4
        start, skip = pair * PAIR * slab + chunk * 8 * fields, pair * PAIR * flat + chunk * 8 * fields
        here = window(inner_two, start, 2 * PAIR * slab - ahead)
        one, z_part = (window(ref, skip, PAIR * flat - ahead) for ref in (outer_one, z_term))
        two = window(outer_two, LAYERS * flat + skip, PAIR * flat - ahead)
        out = window(inner_one, start, PAIR * slab - ahead)
        speed = window(speed_ref, cells + pair * 2 * cells + chunk * 8, 2 * cells - 24)

        def load(layer, y):
            row = (layer + LAYERS) * slab + (REACH + y) * fields
            return here[row : row + fields, :]

        for side in range(2):
            get = kept_rows(load)
            for y in range(8):
                for x in range(side * LAYERS, (side + 1) * LAYERS):
                    cell = x * 32 + y
                    row = slice(cell * fields, (cell + 1) * fields)
                    now = 2.0 * two[row, :] + laplacian(get, x, y, z_part[row, :], -4, 11)
                    one[row, :] = now
                    row = x * slab + (REACH + y) * fields
                    out[row : row + fields, :] = spread(speed, cell, fields) * now
        return carry

    lax.fori_loop(0, 8, step_one, 0)
    along_z(inner_one, LAYERS, PAIR, fields, band_ref, z_term)
    mine = me[0] % 2

    def step_two(chunk, total):
        skip = chunk * 8 * fields
        here = window(inner_one, skip, 2 * PAIR * slab - ahead)
        two_rows = window(outer_two, 2 * LAYERS * flat + skip, PAIR * flat - ahead)
        one_rows = window(outer_one, LAYERS * flat + skip, PAIR * flat - ahead)
        z_part, there, out = (window(ref, skip, PAIR * flat - ahead) for ref in (z_term, turned, image))
        push = window(push_ref, chunk * 8, 6 * cells - 24)
        damping = window(prior_ref, chunk * 8, 2 * cells - 24)

        def load(layer, y):
            row = (layer + LAYERS) * slab + (REACH + y) * fields
            return here[row : row + fields, :]

        nothing = jnp.zeros((fields, HALF), F32)
        for side in range(2):
            get = kept_rows(load)
            for y in range(8):
                for x in range(side * LAYERS, (side + 1) * LAYERS):
                    cell = x * 32 + y
                    row = slice(cell * fields, (cell + 1) * fields)
                    two, one = two_rows[row, :], one_rows[row, :]
                    zero = 2.0 * one - two + laplacian(get, x, y, z_part[row, :], -4, 11)
                    value = spread(push, cell, fields) * zero
                    value = value + spread(push, 2 * cells + cell, fields) * one
                    value = value + spread(push, 4 * cells + cell, fields) * two
                    value = value + spread(damping, cell, fields) * there[row, :]
                    out[row, :] = value
                    high = value.astype(BF16).astype(F32)
                    rows, lane = slice(x * 2 * fields, (x + 1) * 2 * fields), y * 256
                    image_parts[rows, lane : lane + HALF] = jnp.concatenate([high, value - high], axis=0).astype(BF16)
                    image_parts[rows, lane + HALF : lane + 256] = jnp.concatenate([high, nothing], axis=0).astype(BF16)
        for side, pieces in ((mine, (own_basis, own_basis_two)), (1 - mine, (other_basis, other_basis_two))):
            for x in range(LAYERS):
                columns = pieces[x // 2][at((x % 2 * 4 + chunk) * rank, rank), :]
                parts = image_parts[at((side * LAYERS + x) * 2 * fields, 2 * fields), :]
                total = total + lax.dot_general(parts, columns, NT, preferred_element_type=F32)
        return total

    total = lax.fori_loop(0, 4, step_two, jnp.zeros((2 * fields, rank), F32))
    coeffs[...] = total[:fields, :] + total[fields:, :]
    kept[...] = image[at(mine * LAYERS * flat, LAYERS * flat), :]
    lent[...] = image[at((1 - mine) * LAYERS * flat, LAYERS * flat), :]


def remainder(fields, me, image, borrowed, basis, basis_two, *rest):
    *shares, out, coeffs, natural, sem = rest
    rank = coeffs.shape[1]
    half = fields // 2
    mine = half_of(me)
    while len(shares) > 1:
        shares = [shares[i][...] + shares[i + 1][...] for i in range(0, len(shares), 2)]
    total = shares[0][...]
    coeffs[at(mine * half, half), :] = total[:half, :]
    coeffs[at((1 - mine) * half, half), :] = total[half:, :]
    parts = jnp.concatenate(split(total), axis=0)
    whole = natural.reshape(out.shape)
    first, second = (window(natural, side * half * HALF, half * HALF) for side in (mine, 1 - mine))

    def leave(x):
        return pltpu.make_async_copy(whole.at[:, x], out.at[:, x], sem.at[x])

    for x in range(LAYERS):
        for part in range(4):
            columns = (basis, basis_two)[x // 2][(x % 2 * 4 + part) * rank : (x % 2 * 4 + part + 1) * rank, :]
            both = jnp.dot(parts, columns, preferred_element_type=F32)
            cell = x * 32 + part * 8
            results = ([], [])
            for step in range(8):
                side = step * 256
                along = both[:fields, side : side + HALF] + both[:fields, side + HALF : side + 256]
                along = along + both[fields:, side : side + HALF]
                row = slice((cell + step) * half, (cell + step + 1) * half)
                results[0].append(image[row, :] - along[:half, :])
                results[1].append(borrowed[row, :] - along[half:, :])
            for ref, values in zip((first, second), results):
                values = jnp.swapaxes(jnp.stack(values, axis=0), 0, 1)
                for p in range(half):
                    ref[p * HALF + cell : p * HALF + cell + 8, :] = values[p]
        leave(x).start()
    for x in range(LAYERS):
        leave(x).wait()


def call(kernel, inputs, out_shape, scratch, flops, size, scalars=0, far=0, far_out=0, room=16):
    smem = pl.BlockSpec(memory_space=pltpu.SMEM)
    vmem = pl.BlockSpec(memory_space=pltpu.VMEM)
    hbm = pl.BlockSpec(memory_space=pltpu.HBM)
    inputs = [
        pltpu.with_memory_space_constraint(array, pltpu.HBM) if scalars <= i < scalars + far else array
        for i, array in enumerate(inputs)
    ]
    return pl.pallas_call(
        kernel,
        out_shape=out_shape,
        in_specs=[smem] * scalars + [hbm] * far + [vmem] * (len(inputs) - scalars - far),
        out_specs=[hbm] * far_out + [vmem] * (len(out_shape) - far_out),
        scratch_shapes=scratch,
        cost_estimate=pl.CostEstimate(flops=flops, bytes_accessed=size, transcendentals=0),
        compiler_params=pltpu.CompilerParams(vmem_limit_bytes=room * 2**20),
    )(*inputs)


def struct(*shape, dtype=F32):
    return jax.ShapeDtypeStruct(shape, dtype)


def swapped(array, axis, bits):
    count = lax.axis_size(axis)
    return lax.ppermute(array, axis, [(i, i ^ bits) for i in range(count)])


def local(
    probes,
    sources,
    kappa,
    prior,
    basis,
    entry_cell,
    entry_owner,
    entry_slot,
    entry_weight,
    entry_count,
    trace_weight,
):
    rank = basis.shape[0]
    fields = probes.shape[0] // 2
    entries = entry_cell.shape[0]
    peers = lax.axis_size("space")
    slab, flat = PADDED * fields, 32 * fields
    cells = LAYERS * 32
    rows = entries // HALF
    basis = basis.reshape(rank * cells, HALF)
    me = lax.axis_index("space").astype(jnp.int32).reshape(1)

    own, probes_near, sources_near, prior_near, lent, matrix = call(
        pack,
        (
            entry_count,
            me,
            probes.reshape(2 * fields * cells, HALF),
            sources.reshape(3 * cells, HALF),
            prior.reshape(cells, HALF),
            kappa.reshape(cells, HALF),
            entry_cell.reshape(rows, HALF),
            entry_owner.reshape(rows, HALF),
            entry_slot.reshape(rows, HALF),
            entry_weight.reshape(rows, HALF),
            trace_weight.reshape(1, HALF),
        ),
        [
            struct(cells + 4 * rows + 8, HALF),
            struct(fields * cells, HALF),
            struct(3 * cells, HALF),
            struct(cells, HALF),
            struct((fields + 4) * cells, HALF),
            struct(256, 256, dtype=BF16),
        ],
        [pltpu.VMEM((3, rows, HALF), jnp.int32), pltpu.VMEM((16, HALF), F32), pltpu.SemaphoreType.DMA((12,))],
        100_000,
        2 * 2**20,
        scalars=2,
        far=9,
    )
    partner = swapped(own, "space", 1)
    lent, partner = lax.optimization_barrier((lent, partner))
    borrowed = swapped(lent, "space", 1)
    passed = lax.ppermute(
        jnp.concatenate([own, partner], axis=0),
        "space",
        [pair for i in range(1, peers - 1, 2) for pair in ((i, i + 1), (i + 1, i))] + [(0, 0), (peers - 1, peers - 1)],
    )

    turned, first, second, third, push, damping = call(
        functools.partial(forward_own, fields),
        (me, probes_near, sources_near, prior_near, own, partner, borrowed, matrix),
        [
            struct(PAIR * flat, HALF),
            struct(PAIR * slab, HALF),
            struct(PAIR * slab, HALF),
            struct(PAIR * flat, HALF),
            struct(6 * cells, HALF),
            struct(2 * cells, HALF),
        ],
        [pltpu.VMEM((PAIR * flat, HALF), F32), pltpu.VMEM((2 * cells, HALF), F32)],
        600_000_000,
        6 * 2**20,
        scalars=1,
    )
    passed, second = lax.optimization_barrier((passed, second))
    across = swapped(passed, "space", 1)
    across, basis_there = lax.optimization_barrier((across, basis))
    basis_there = swapped(basis_there, "space", 1)
    table, place, slot_hot, speed, line, owner, weight = call(
        functools.partial(forward_window, fields, peers),
        (me, first, second, third, own, partner, passed, across, matrix),
        [
            struct(peers * (fields + 1), HALF),
            struct(TILES * fields, entries),
            struct(TILES * HALF, entries, dtype=BF16),
            struct(TILES * cells, HALF),
            struct(TILES * fields, entries, dtype=jnp.int32),
            struct(TILES * fields, entries, dtype=jnp.int32),
            struct(TILES * fields, entries),
        ],
        [
            pltpu.VMEM((TILES * PLACES, entries), BF16),
            pltpu.VMEM((TILES * fields, entries), jnp.int32),
            pltpu.VMEM((LAYERS * slab, HALF), F32),
            pltpu.VMEM((LAYERS * slab, HALF), F32),
            pltpu.VMEM((PAIR * flat, HALF), F32),
            pltpu.VMEM((TILES * fields, entries), F32),
        ]
        + [pltpu.VMEM((16 * fields, PLACES), F32)] * TILES,
        3_000_000_000,
        6 * 2**20,
        scalars=1,
        room=20,
    )
    columns = []
    bits = 2
    while bits < peers:
        arrived = swapped(table, "space", bits + 1)
        for i in ((0,), (1,), (2, 3))[len(columns)] if len(columns) < 3 else ():
            (some,) = call(
                functools.partial(basis_parts, 8 * (i % 2)),
                ((basis, basis_there)[i // 2], table),
                [struct(8 * rank, 2048, dtype=BF16)],
                [],
                10_000_000,
                4 * 2**20,
            )
            columns.append(some)
        if bits == 2:
            (turned_hot,) = call(
                functools.partial(turn_places, fields),
                (place, table),
                [struct(TILES * entries, 256, dtype=BF16)],
                [],
                10_000_000,
                4 * 2**20,
            )
            arrived, turned_hot = lax.optimization_barrier((arrived, turned_hot))
        arrived, columns = lax.optimization_barrier((arrived, columns))
        table = table + arrived
        bits *= 2
    kept, lent, coeffs = call(
        functools.partial(adjoint, fields, peers),
        (me, table, turned_hot, slot_hot, speed, line, owner, weight, turned, push, damping, matrix, *columns),
        [struct(LAYERS * flat, HALF), struct(LAYERS * flat, HALF), struct(fields, rank)],
        [
            pltpu.VMEM((TILES * fields, entries), F32),
            pltpu.VMEM((TILES * fields, entries), F32),
            pltpu.VMEM((TILES * LAYERS * slab, HALF), F32),
            pltpu.VMEM((TILES * LAYERS * flat, HALF), F32),
            pltpu.VMEM((2 * PAIR * slab, HALF), F32),
            pltpu.VMEM((2 * PAIR * flat, HALF), F32),
            pltpu.VMEM((2 * PAIR * flat, HALF), F32),
            pltpu.VMEM((PAIR * flat, HALF), F32),
            pltpu.VMEM((peers * fields, HALF), F32),
        ]
        + [pltpu.VMEM((64 * fields, 2 * entries), BF16)]
        + [pltpu.VMEM((2 * PAIR * fields, 2048), BF16)],
        5_000_000_000,
        10 * 2**20,
        scalars=1,
        room=30,
    )
    coeffs = jnp.concatenate([coeffs, swapped(coeffs, "space", 1)], axis=0)
    lent, coeffs = lax.optimization_barrier((lent, coeffs))
    borrowed = swapped(lent, "space", 1)
    bits = 2
    while bits * 2 < peers:
        coeffs = coeffs + swapped(coeffs, "space", bits + 1)
        bits *= 2
    shares = [coeffs, swapped(coeffs, "space", bits + 1)]
    hess_probe, coeffs = call(
        functools.partial(remainder, 2 * fields),
        (me, kept, borrowed, *columns[:2], *shares),
        [struct(*probes.shape), struct(2 * fields, rank)],
        [pltpu.VMEM((2 * fields * cells, HALF), F32), pltpu.SemaphoreType.DMA((LAYERS,))],
        200_000_000,
        6 * 2**20,
        scalars=1,
        far_out=1,
    )
    return hess_probe, coeffs.T


def solution(mesh):
    return jax.shard_map(
        local,
        mesh=mesh,
        in_specs=(
            P("group", "space", None, None),
            P(None, ("group", "space"), None, None),
            P(("group", "space"), None, None),
            P(("group", "space"), None, None),
            P("group", "space", None, None),
            P(("group", "space")),
            P(("group", "space")),
            P(("group", "space")),
            P(("group", "space")),
            P(("group", "space")),
            P(("group", "space")),
        ),
        out_specs=(P("group", "space", None, None), P("group", None)),
        check_vma=False,
    )
```

```python
import functools

import jax
import jax.numpy as jnp
from jax import lax
from jax.experimental import pallas as pl
from jax.experimental.pallas import tpu as pltpu
from jax.sharding import PartitionSpec as P

STENCIL = (-205.0 / 72.0, 8.0 / 5.0, -1.0 / 5.0, 8.0 / 315.0, -1.0 / 560.0)
CENTER = 3.0 * STENCIL[0]
REACH = 4
LAYERS = 4
PAIR = 8
TILES = 6
PADDED = 40
HALF = 128
PLACES = 512
F32 = jnp.float32
BF16 = jnp.bfloat16
NT = (((1,), (1,)), ((), ()))


def split(value):
    high = value.astype(BF16)
    low = (value - high.astype(F32)).astype(BF16)
    return high, low


def at(row, count=16):
    return pl.ds(pl.multiple_of(row, 8), count)


def window(ref, start, size):
    return ref.at[pl.ds(pl.multiple_of(start, 8), size)]


def kept_rows(load):
    rows = {}

    def get(layer, y):
        if (layer, y) not in rows:
            rows[layer, y] = load(layer, y)
        return rows[layer, y]

    return get


def half_of(me):
    value = me[0]
    for by in (4, 2, 1):
        value = jnp.bitwise_xor(value, lax.shift_right_logical(value, by))
    return jnp.bitwise_and(value, 1)


def spread(ref, row, fields):
    return jnp.broadcast_to(ref[pl.ds(row, 1), :], (fields, HALF))


def clear_margins(ref, layers, fields):
    margin = jnp.zeros((REACH * fields, HALF), F32)
    for layer in range(layers):
        start = layer * PADDED * fields
        ref[start : start + REACH * fields, :] = margin
        start += (PADDED - REACH) * fields
        ref[start : start + REACH * fields, :] = margin


def along_z(ref, first, layers, fields, band_ref, out_ref, row=0):
    pieces = [ref[at(((first + x) * PADDED + REACH) * fields, 32 * fields), :] for x in range(layers)]
    high, low = split(jnp.concatenate(pieces, axis=0))
    both = jnp.dot(jnp.concatenate([high, low], axis=1), band_ref[...], preferred_element_type=F32)
    out_ref[at(row, layers * 32 * fields), :] = both[:, :HALF] + both[:, HALF:]


def laplacian(get, x, y, z_term, lowest, highest):
    total = z_term
    for k in range(1, REACH + 1):
        ring = get(x, y + k) + get(x, y - k)
        if x + k <= highest:
            ring = ring + get(x + k, y)
        if x - k >= lowest:
            ring = ring + get(x - k, y)
        total = total + STENCIL[k] * ring
    return total


def pack(
    count, me, probes, sources, prior, kappa, cell, owner, slot, weight, scale,
    statics, probes_out, sources_out, prior_out, lent, band_ref, small_int, small_float, sem,
):
    rows = cell.shape[0]
    cells = kappa.shape[0]
    half = probes_out.shape[0]
    mine = half_of(me)
    other = probes.at[pl.ds(pl.multiple_of((1 - mine) * half, 8), half)]
    small = [
        pltpu.make_async_copy(kappa, statics.at[pl.ds(0, cells)], sem.at[0]),
        pltpu.make_async_copy(cell, small_int.at[0], sem.at[1]),
        pltpu.make_async_copy(owner, small_int.at[1], sem.at[2]),
        pltpu.make_async_copy(slot, small_int.at[2], sem.at[3]),
        pltpu.make_async_copy(weight, small_float.at[pl.ds(0, rows)], sem.at[4]),
        pltpu.make_async_copy(scale, small_float.at[pl.ds(8, 1)], sem.at[5]),
    ]
    large = [
        pltpu.make_async_copy(other, lent.at[pl.ds(0, half)], sem.at[6]),
        pltpu.make_async_copy(sources, lent.at[pl.ds(half, 3 * cells)], sem.at[7]),
        pltpu.make_async_copy(prior, lent.at[pl.ds(half + 3 * cells, cells)], sem.at[8]),
        pltpu.make_async_copy(probes.at[pl.ds(pl.multiple_of(mine * half, 8), half)], probes_out, sem.at[9]),
        pltpu.make_async_copy(sources, sources_out, sem.at[10]),
        pltpu.make_async_copy(prior, prior_out, sem.at[11]),
    ]
    for copy in small + large:
        copy.start()
    apart = lax.broadcasted_iota(jnp.int32, (HALF, HALF), 0) - lax.broadcasted_iota(jnp.int32, (HALF, HALF), 1)
    full = jnp.where(apart == 0, CENTER, jnp.zeros((HALF, HALF), F32))
    for reach in range(1, REACH + 1):
        full = jnp.where(jnp.abs(apart) == reach, STENCIL[reach], full)
    high, low = split(full)
    band_ref[0:HALF, 0:HALF] = high
    band_ref[HALF:, 0:HALF] = high
    band_ref[0:HALF, HALF:] = low
    band_ref[HALF:, HALF:] = jnp.zeros_like(low)
    for copy in small:
        copy.wait()
    for i in range(3):
        statics[cells + i * rows : cells + (i + 1) * rows, :] = small_int[i].astype(F32)
    place = lax.broadcasted_iota(jnp.int32, (rows, HALF), 0) * HALF
    place = place + lax.broadcasted_iota(jnp.int32, (rows, HALF), 1)
    live = jnp.where(place < count[0], small_float[0:rows, :], 0.0)
    statics[cells + 3 * rows : cells + 4 * rows, :] = live
    statics[cells + 4 * rows : cells + 4 * rows + 8, :] = jnp.broadcast_to(small_float[8:9, :], (8, HALF))
    for copy in large:
        copy.wait()


def forward_own(
    fields, me, probes, sources, prior, own, partner, borrowed, band_ref,
    turned, first, second, third, push_ref, prior_ref, z_term, speed_ref,
):
    slab, flat, cells = PADDED * fields, 32 * fields, LAYERS * 32
    ahead = 24 * fields
    half = probes.shape[0]
    mine = me[0] % 2
    clear_margins(first, PAIR, fields)
    clear_margins(second, PAIR, fields)
    lent = borrowed.at[pl.ds(half, 4 * cells)]
    for side, pushes, damping, statics in ((mine, sources, prior, own), (1 - mine, lent, None, partner)):
        for i in range(3):
            push_ref[at(i * 2 * cells + side * cells, cells), :] = pushes[i * cells : (i + 1) * cells, :]
        place = at(side * cells, cells)
        prior_ref[place, :] = lent[3 * cells :, :] if damping is None else damping[...]
        speed_ref[place, :] = statics[0:cells, :]

    def load(chunk, carry):
        for side, ref in ((mine, probes), (1 - mine, borrowed)):
            there = window(turned, side * LAYERS * flat + chunk * 8 * fields, LAYERS * flat - ahead)
            padded = window(first, side * LAYERS * slab + chunk * 8 * fields, LAYERS * slab - ahead)
            here = window(ref, chunk * 8, half - 24)
            push = window(push_ref, side * cells + chunk * 8, cells - 24)
            for x in range(LAYERS):
                rows = [here[p * cells + x * 32 : p * cells + x * 32 + 8, :] for p in range(fields)]
                values = jnp.swapaxes(jnp.stack(rows, axis=0), 0, 1)
                for y in range(8):
                    cell = x * 32 + y
                    there[cell * fields : (cell + 1) * fields, :] = values[y]
                    row = x * slab + (REACH + y) * fields
                    padded[row : row + fields, :] = values[y] * spread(push, cell, fields)
        return carry

    lax.fori_loop(0, 4, load, 0)

    def sweep(field, emit):
        along_z(field, 0, PAIR, fields, band_ref, z_term)

        def body(chunk, carry):
            padded = window(field, chunk * 8 * fields, PAIR * slab - ahead)
            z_part = window(z_term, chunk * 8 * fields, PAIR * flat - ahead)
            speed = window(speed_ref, chunk * 8, 2 * cells - 24)
            push = window(push_ref, chunk * 8, 6 * cells - 24)
            there = window(turned, chunk * 8 * fields, PAIR * flat - ahead)
            put = emit(chunk)

            def load(layer, y):
                row = layer * slab + (REACH + y) * fields
                return padded[row : row + fields, :]

            for side in range(2):
                get = kept_rows(load)
                for y in range(8):
                    for x in range(side * LAYERS, (side + 1) * LAYERS):
                        cell = x * 32 + y
                        row = slice(cell * fields, (cell + 1) * fields)
                        change = spread(speed, cell, fields) * laplacian(get, x, y, z_part[row, :], 0, PAIR - 1)
                        put(x, y, get(x, y), change, there[row, :], push)
            return carry

        lax.fori_loop(0, 4, body, 0)

    def step_one(chunk):
        out = window(second, chunk * 8 * fields, PAIR * slab - ahead)

        def put(x, y, now, change, probe, push):
            change = change + probe * spread(push, 2 * cells + x * 32 + y, fields)
            row = x * slab + (REACH + y) * fields
            out[row : row + fields, :] = 2.0 * now + change

        return put

    sweep(first, step_one)

    def step_two(chunk):
        before = window(first, chunk * 8 * fields, PAIR * slab - ahead)
        out = window(third, chunk * 8 * fields, PAIR * flat - ahead)

        def put(x, y, now, change, probe, push):
            row = x * slab + (REACH + y) * fields
            change = change - before[row : row + fields, :]
            cell = x * 32 + y
            change = change + probe * spread(push, 4 * cells + cell, fields)
            out[cell * fields : (cell + 1) * fields, :] = 2.0 * now + change

        return put

    sweep(second, step_two)


def entry_row(value, row):
    return jnp.concatenate([value[row + i : row + i + 1, :] for i in range(4)], axis=1)


def forward_window(
    fields, peers, me, first, second, third, own, partner, passed, across, band_ref,
    table, place_ref, slot_ref, speed_ref, line_ref, owner_ref, weight_ref,
    cell_ref, wide_ref, statics, below, above, z_term, total_ref, *samples,
):
    entries = line_ref.shape[1]
    cells = LAYERS * 32
    length = own.shape[0]
    odd = me[0] % 2 == 1
    slab, flat = PADDED * fields, 32 * fields
    clear_margins(below, LAYERS, fields)
    clear_margins(above, LAYERS, fields)
    total_ref[...] = jnp.zeros_like(total_ref)
    mine, theirs = own[...], partner[...]
    low = jnp.where(me[0] < 2, 0.0, jnp.where(odd, across[...], passed[...]))
    high = jnp.where(me[0] >= peers - 2, 0.0, jnp.where(odd, passed[...], across[...]))
    tiles = (
        low[length:, :],
        low[0:length, :],
        jnp.where(odd, theirs, mine),
        jnp.where(odd, mine, theirs),
        high[0:length, :],
        high[length:, :],
    )
    place = lax.broadcasted_iota(jnp.int32, (PLACES, entries), 0)
    slot_place = lax.broadcasted_iota(jnp.int32, (HALF, entries), 0)
    for tile, value in enumerate(tiles):
        speed_ref[tile * cells : (tile + 1) * cells, :] = value[0:cells, :]
        statics[tile * 16 : (tile + 1) * 16, :] = value[cells : cells + 16, :]

    def describe(tile, carry):
        value = statics[at(tile * 16), :]
        cell, owner, slot = (entry_row(value, i * 4).astype(jnp.int32) for i in range(3))
        weight = entry_row(value, 12)
        hot = jnp.where(place == jnp.bitwise_and(cell, PLACES - 1), 1.0, 0.0)
        cell_ref[at(tile * PLACES, PLACES), :] = hot.astype(BF16)
        hot = jnp.where(slot_place == slot, 1.0, 0.0)
        slot_ref[at(tile * HALF, HALF), :] = hot.astype(BF16)
        rows = at(tile * fields, fields)
        line_ref[rows, :] = jnp.broadcast_to(lax.shift_right_logical(cell, 8), (fields, entries))
        wide_ref[rows, :] = jnp.broadcast_to(lax.shift_right_logical(cell, 9), (fields, entries))
        place_ref[rows, :] = jnp.broadcast_to(jnp.bitwise_and(cell, 255), (fields, entries)).astype(F32)
        owner_ref[rows, :] = jnp.broadcast_to(owner, (fields, entries))
        weight_ref[rows, :] = jnp.broadcast_to(weight, (fields, entries))
        return carry

    lax.fori_loop(0, TILES, describe, 0)

    def outward(chunk, carry):
        ahead = 24 * fields
        speed = window(speed_ref, chunk * 8, TILES * cells - 24)
        here = window(first, chunk * 8 * fields, PAIR * slab - ahead)
        down_out, up_out = (window(ref, chunk * 8 * fields, LAYERS * slab - ahead) for ref in (below, above))
        for y in range(8):
            rows = [slice(x * slab + (REACH + y) * fields, x * slab + (REACH + y + 1) * fields) for x in range(PAIR)]
            field = [here[row, :] for row in rows]
            for x in range(LAYERS):
                up = sum(STENCIL[4 + x - other] * field[4 + other] for other in range(x, LAYERS))
                down = sum(STENCIL[4 + other - x] * field[other] for other in range(x + 1))
                up_out[rows[x], :] = spread(speed, 4 * cells + x * 32 + y, fields) * up
                down_out[rows[x], :] = spread(speed, cells + x * 32 + y, fields) * down
        return carry

    lax.fori_loop(0, 4, outward, 0)
    along_z(below, 0, LAYERS, fields, band_ref, z_term, 0)
    along_z(above, 0, LAYERS, fields, band_ref, z_term, cells * fields)

    def far(read, x, y, lowest, highest):
        total = None
        for other in range(lowest, highest + 1):
            if 1 <= abs(x - other) <= REACH:
                term = STENCIL[abs(x - other)] * read(other, y)
                total = term if total is None else total + term
        return total

    def respond(chunk, carry):
        ahead = 16 * fields
        speeds = window(speed_ref, chunk * 16, TILES * cells - 16)
        low_side, high_side = (window(ref, chunk * 16 * fields, LAYERS * slab - ahead) for ref in (below, above))
        inside = window(second, chunk * 16 * fields, PAIR * slab - ahead)
        base = window(third, chunk * 16 * fields, PAIR * flat - ahead)
        z_parts = window(z_term, chunk * 16 * fields, PAIR * flat - ahead)

        def load(layer, y):
            if layer < 0:
                ref, layer = low_side, layer + LAYERS
            elif layer >= PAIR:
                ref, layer = high_side, layer - PAIR
            else:
                ref = inside
            row = layer * slab + (REACH + y) * fields
            return ref[row : row + fields, :]

        for tile in range(TILES):
            sample = samples[tile]
            read = kept_rows(load)
            for y in range(16):
                for x in range(LAYERS):
                    cell = x * 32 + y
                    layer = (tile - 2) * LAYERS + x
                    speed = spread(speeds, tile * cells + cell, fields)
                    if tile in (0, 5):
                        value = speed * far(read, layer, y, -4, 11)
                    elif tile in (2, 3):
                        outside = far(read, layer, y, -4, -1) if tile == 2 else far(read, layer, y, 8, 11)
                        row = ((tile - 2) * cells + cell) * fields
                        value = base[row : row + fields, :] + speed * outside
                    else:
                        row = (tile // 4 * cells + cell) * fields
                        lap = laplacian(read, layer, y, z_parts[row : row + fields, :], -4, 11)
                        value = 2.0 * read(layer, y) + speed * lap
                    row = (x * 4 + y // 4) * fields
                    side = y % 4 * HALF
                    sample[row : row + fields, side : side + HALF] = value
            hot = cell_ref[tile * PLACES : (tile + 1) * PLACES, :]
            picked = jnp.dot(jnp.concatenate(split(sample[...]), axis=0), hot, preferred_element_type=F32)
            picked = picked[: 16 * fields, :] + picked[16 * fields :, :]
            rows = slice(tile * fields, (tile + 1) * fields)
            line = wide_ref[rows, :]
            total = total_ref[rows, :]
            for i in range(16):
                chosen = line == i // 4 * 8 + chunk * 4 + i % 4
                total = total + jnp.where(chosen, picked[i * fields : (i + 1) * fields, :], 0.0)
            total_ref[rows, :] = total
        return carry

    lax.fori_loop(0, 2, respond, 0)

    for group in range(peers // 16):
        lefts, rights = [], []
        for tile in range(TILES):
            rows = slice(tile * fields, (tile + 1) * fields)
            value = total_ref[rows, :] * weight_ref[rows, :]
            high = value.astype(BF16).astype(F32)
            owner = owner_ref[rows, :]
            for part in (high, value - high):
                pieces = [jnp.where(owner == group * 16 + i, part, 0.0) for i in range(16)]
                lefts.append(jnp.concatenate(pieces, axis=0).astype(BF16))
                rights.append(slot_ref[tile * HALF : (tile + 1) * HALF, :])
        result = lax.dot_general(
            jnp.concatenate(lefts, axis=1), jnp.concatenate(rights, axis=1), NT, preferred_element_type=F32
        )
        table[group * 16 * fields : (group + 1) * 16 * fields, :] = result
    place = lax.broadcasted_iota(jnp.int32, (peers, HALF), 0)
    scales = jnp.zeros((peers, HALF), F32)
    for position, value in ((me[0], mine), (me[0] + 1 - 2 * (me[0] % 2), theirs)):
        scale = jnp.broadcast_to(value[cells + 16 : cells + 17, :], (peers, HALF))
        scales = jnp.where(place == position, scale, scales)
    table[peers * fields :, :] = scales


def basis_parts(first, basis, when, out):
    rank = basis.shape[0] // HALF

    def body(group, carry):
        here = window(basis, (first + group) * 8, basis.shape[0] - 15 * 8)
        there = window(out, group * rank, rank)
        for start in range(0, rank, 16):
            blocks = []
            for block in (start, start + 8):
                rows = [here[k * HALF : k * HALF + 8, :] for k in range(block, block + 8)]
                blocks.append(jnp.swapaxes(jnp.stack(rows, axis=0), 0, 1))
            for step in range(8):
                high, low = split(jnp.concatenate([block[step] for block in blocks], axis=0))
                there[start : start + 16, step * 256 : step * 256 + HALF] = high
                there[start : start + 16, step * 256 + HALF : (step + 1) * 256] = low
        return carry

    lax.fori_loop(0, 8, body, 0)


def turn_places(fields, place_ref, when, hot_ref):
    entries = place_ref.shape[1]
    lane = lax.broadcasted_iota(jnp.int32, (entries, HALF), 1)
    for tile in range(TILES):
        row = place_ref[tile * fields : tile * fields + 1, :]
        column = jnp.transpose(jnp.broadcast_to(row, (HALF, entries))).astype(jnp.int32)
        for part in range(2):
            hot = jnp.where(column == lane + part * HALF, 1.0, 0.0).astype(BF16)
            hot_ref[tile * entries : (tile + 1) * entries, part * HALF : (part + 1) * HALF] = hot


def adjoint(
    fields, peers, me, table, hot_ref, slot_ref, speed_ref, line_ref, owner_ref, weight_ref, turned, push_ref,
    prior_ref, band_ref, own_basis, own_basis_two, other_basis, other_basis_two, kept, lent, coeffs,
    high_ref, low_ref, inner_two, outer_two, inner_one, outer_one, z_term, image, scaled, *scratch,
):
    *lefts, image_parts = scratch
    entries = line_ref.shape[1]
    cells = LAYERS * 32
    rank = own_basis.shape[0] // 8
    slab, flat = PADDED * fields, 32 * fields
    ahead = 24 * fields
    clear_margins(inner_two, TILES * LAYERS, fields)
    clear_margins(inner_one, 2 * PAIR, fields)
    for owner in range(peers):
        rows = slice(owner * fields, (owner + 1) * fields)
        scaled[rows, :] = table[rows, :] * table[peers * fields + owner : peers * fields + owner + 1, :]
    for tile in range(TILES):
        rows = slice(tile * fields, (tile + 1) * fields)
        owner = owner_ref[rows, :]
        hot = slot_ref[tile * HALF : (tile + 1) * HALF, :]
        hot = jnp.concatenate([hot, hot], axis=0)
        total = jnp.zeros((fields, entries), F32)
        for group in range(peers // 16):
            parts = split(scaled[group * 16 * fields : (group + 1) * 16 * fields, :])
            found = jnp.dot(jnp.concatenate(parts, axis=1), hot, preferred_element_type=F32)
            for i in range(16):
                total = total + jnp.where(owner == group * 16 + i, found[i * fields : (i + 1) * fields, :], 0.0)
        value = total * weight_ref[rows, :]
        high = value.astype(BF16).astype(F32)
        high_ref[rows, :] = high
        low_ref[rows, :] = value - high

    def product(tile):
        left = lefts[tile]
        rows = slice(tile * fields, (tile + 1) * fields)
        line, high, low = line_ref[rows, :], high_ref[rows, :], low_ref[rows, :]
        for i in range(0, 64, 2):
            chosen = [line == i, line == i + 1]
            row = slice(i * fields, (i + 2) * fields)
            for part, side in ((high, slice(0, entries)), (low, slice(entries, 2 * entries))):
                both = [jnp.where(which, part, 0.0) for which in chosen]
                left[row, side] = jnp.concatenate(both, axis=0).astype(BF16)
        hot = hot_ref[tile * entries : (tile + 1) * entries, :]
        return jnp.dot(left[...], jnp.concatenate([hot, hot], axis=0), preferred_element_type=F32)

    def inject(tile, value):
        for i in range(64):
            for step in range(2):
                layer, y = tile * LAYERS + i // 16, i % 16 * 2 + step
                now = value[i * fields : (i + 1) * fields, step * HALF : (step + 1) * HALF]
                if 1 <= tile <= 4:
                    row = ((layer - LAYERS) * 32 + y) * fields
                    outer_two[row : row + fields, :] = now
                speed = spread(speed_ref, layer * 32 + y, fields)
                row = layer * slab + (REACH + y) * fields
                inner_two[row : row + fields, :] = speed * now
        if 2 <= tile:
            along_z(inner_two, (tile - 1) * LAYERS, LAYERS, fields, band_ref, z_term, (tile - 2) * cells * fields)

    values = product(0)
    for tile in range(TILES):
        after = product(tile + 1) if tile + 1 < TILES else None
        inject(tile, values)
        values = after

    def step_one(index, carry):
        pair, chunk = index // 4, index % 4
        start, skip = pair * PAIR * slab + chunk * 8 * fields, pair * PAIR * flat + chunk * 8 * fields
        here = window(inner_two, start, 2 * PAIR * slab - ahead)
        two, one, z_part = (window(ref, skip, PAIR * flat - ahead) for ref in (outer_two, outer_one, z_term))
        out = window(inner_one, start, PAIR * slab - ahead)
        speed = window(speed_ref, cells + pair * 2 * cells + chunk * 8, 2 * cells - 24)

        def load(layer, y):
            row = (layer + LAYERS) * slab + (REACH + y) * fields
            return here[row : row + fields, :]

        for side in range(2):
            get = kept_rows(load)
            for y in range(8):
                for x in range(side * LAYERS, (side + 1) * LAYERS):
                    cell = x * 32 + y
                    row = slice(cell * fields, (cell + 1) * fields)
                    now = 2.0 * two[row, :] + laplacian(get, x, y, z_part[row, :], -4, 11)
                    one[row, :] = now
                    row = x * slab + (REACH + y) * fields
                    out[row : row + fields, :] = spread(speed, cell, fields) * now
        return carry

    lax.fori_loop(0, 8, step_one, 0)
    along_z(inner_one, LAYERS, PAIR, fields, band_ref, z_term)
    mine = me[0] % 2

    def step_two(chunk, total):
        skip = chunk * 8 * fields
        here = window(inner_one, skip, 2 * PAIR * slab - ahead)
        two_rows, one_rows = (window(ref, LAYERS * flat + skip, PAIR * flat - ahead) for ref in (outer_two, outer_one))
        z_part, there, out = (window(ref, skip, PAIR * flat - ahead) for ref in (z_term, turned, image))
        push = window(push_ref, chunk * 8, 6 * cells - 24)
        damping = window(prior_ref, chunk * 8, 2 * cells - 24)

        def load(layer, y):
            row = (layer + LAYERS) * slab + (REACH + y) * fields
            return here[row : row + fields, :]

        nothing = jnp.zeros((fields, HALF), F32)
        for side in range(2):
            get = kept_rows(load)
            for y in range(8):
                for x in range(side * LAYERS, (side + 1) * LAYERS):
                    cell = x * 32 + y
                    row = slice(cell * fields, (cell + 1) * fields)
                    two, one = two_rows[row, :], one_rows[row, :]
                    zero = 2.0 * one - two + laplacian(get, x, y, z_part[row, :], -4, 11)
                    value = spread(push, cell, fields) * zero
                    value = value + spread(push, 2 * cells + cell, fields) * one
                    value = value + spread(push, 4 * cells + cell, fields) * two
                    value = value + spread(damping, cell, fields) * there[row, :]
                    out[row, :] = value
                    high = value.astype(BF16).astype(F32)
                    rows, lane = slice(x * 2 * fields, (x + 1) * 2 * fields), y * 256
                    image_parts[rows, lane : lane + HALF] = jnp.concatenate([high, value - high], axis=0).astype(BF16)
                    image_parts[rows, lane + HALF : lane + 256] = jnp.concatenate([high, nothing], axis=0).astype(BF16)
        for side, pieces in ((mine, (own_basis, own_basis_two)), (1 - mine, (other_basis, other_basis_two))):
            for x in range(LAYERS):
                columns = pieces[x // 2][at((x % 2 * 4 + chunk) * rank, rank), :]
                parts = image_parts[at((side * LAYERS + x) * 2 * fields, 2 * fields), :]
                total = total + lax.dot_general(parts, columns, NT, preferred_element_type=F32)
        return total

    total = lax.fori_loop(0, 4, step_two, jnp.zeros((2 * fields, rank), F32))
    coeffs[...] = total[:fields, :] + total[fields:, :]
    kept[...] = image[at(mine * LAYERS * flat, LAYERS * flat), :]
    lent[...] = image[at((1 - mine) * LAYERS * flat, LAYERS * flat), :]


def remainder(fields, me, image, borrowed, basis, basis_two, *rest):
    *shares, out, coeffs, natural, sem = rest
    rank = coeffs.shape[1]
    half = fields // 2
    mine = half_of(me)
    while len(shares) > 1:
        shares = [shares[i][...] + shares[i + 1][...] for i in range(0, len(shares), 2)]
    total = shares[0][...]
    coeffs[at(mine * half, half), :] = total[:half, :]
    coeffs[at((1 - mine) * half, half), :] = total[half:, :]
    parts = jnp.concatenate(split(total), axis=0)
    whole = natural.reshape(out.shape)
    first, second = (window(natural, side * half * HALF, half * HALF) for side in (mine, 1 - mine))

    def leave(x):
        return pltpu.make_async_copy(whole.at[:, x], out.at[:, x], sem.at[x])

    for x in range(LAYERS):
        for part in range(4):
            columns = (basis, basis_two)[x // 2][(x % 2 * 4 + part) * rank : (x % 2 * 4 + part + 1) * rank, :]
            both = jnp.dot(parts, columns, preferred_element_type=F32)
            cell = x * 32 + part * 8
            results = ([], [])
            for step in range(8):
                side = step * 256
                along = both[:fields, side : side + HALF] + both[:fields, side + HALF : side + 256]
                along = along + both[fields:, side : side + HALF]
                row = slice((cell + step) * half, (cell + step + 1) * half)
                results[0].append(image[row, :] - along[:half, :])
                results[1].append(borrowed[row, :] - along[half:, :])
            for ref, values in zip((first, second), results):
                values = jnp.swapaxes(jnp.stack(values, axis=0), 0, 1)
                for p in range(half):
                    ref[p * HALF + cell : p * HALF + cell + 8, :] = values[p]
        leave(x).start()
    for x in range(LAYERS):
        leave(x).wait()


def call(kernel, inputs, out_shape, scratch, flops, size, scalars=0, far=0, far_out=0, room=16):
    smem = pl.BlockSpec(memory_space=pltpu.SMEM)
    vmem = pl.BlockSpec(memory_space=pltpu.VMEM)
    hbm = pl.BlockSpec(memory_space=pltpu.HBM)
    inputs = [
        pltpu.with_memory_space_constraint(array, pltpu.HBM) if scalars <= i < scalars + far else array
        for i, array in enumerate(inputs)
    ]
    return pl.pallas_call(
        kernel,
        out_shape=out_shape,
        in_specs=[smem] * scalars + [hbm] * far + [vmem] * (len(inputs) - scalars - far),
        out_specs=[hbm] * far_out + [vmem] * (len(out_shape) - far_out),
        scratch_shapes=scratch,
        cost_estimate=pl.CostEstimate(flops=flops, bytes_accessed=size, transcendentals=0),
        compiler_params=pltpu.CompilerParams(vmem_limit_bytes=room * 2**20),
    )(*inputs)


def struct(*shape, dtype=F32):
    return jax.ShapeDtypeStruct(shape, dtype)


def swapped(array, axis, bits):
    count = lax.axis_size(axis)
    return lax.ppermute(array, axis, [(i, i ^ bits) for i in range(count)])


def local(
    probes,
    sources,
    kappa,
    prior,
    basis,
    entry_cell,
    entry_owner,
    entry_slot,
    entry_weight,
    entry_count,
    trace_weight,
):
    rank = basis.shape[0]
    fields = probes.shape[0] // 2
    entries = entry_cell.shape[0]
    peers = lax.axis_size("space")
    slab, flat = PADDED * fields, 32 * fields
    cells = LAYERS * 32
    rows = entries // HALF
    basis = basis.reshape(rank * cells, HALF)
    me = lax.axis_index("space").astype(jnp.int32).reshape(1)

    own, probes_near, sources_near, prior_near, lent, matrix = call(
        pack,
        (
            entry_count,
            me,
            probes.reshape(2 * fields * cells, HALF),
            sources.reshape(3 * cells, HALF),
            prior.reshape(cells, HALF),
            kappa.reshape(cells, HALF),
            entry_cell.reshape(rows, HALF),
            entry_owner.reshape(rows, HALF),
            entry_slot.reshape(rows, HALF),
            entry_weight.reshape(rows, HALF),
            trace_weight.reshape(1, HALF),
        ),
        [
            struct(cells + 4 * rows + 8, HALF),
            struct(fields * cells, HALF),
            struct(3 * cells, HALF),
            struct(cells, HALF),
            struct((fields + 4) * cells, HALF),
            struct(256, 256, dtype=BF16),
        ],
        [pltpu.VMEM((3, rows, HALF), jnp.int32), pltpu.VMEM((16, HALF), F32), pltpu.SemaphoreType.DMA((12,))],
        100_000,
        2 * 2**20,
        scalars=2,
        far=9,
    )
    partner = swapped(own, "space", 1)
    lent, partner = lax.optimization_barrier((lent, partner))
    borrowed = swapped(lent, "space", 1)
    passed = lax.ppermute(
        jnp.concatenate([own, partner], axis=0),
        "space",
        [pair for i in range(1, peers - 1, 2) for pair in ((i, i + 1), (i + 1, i))] + [(0, 0), (peers - 1, peers - 1)],
    )

    turned, first, second, third, push, damping = call(
        functools.partial(forward_own, fields),
        (me, probes_near, sources_near, prior_near, own, partner, borrowed, matrix),
        [
            struct(PAIR * flat, HALF),
            struct(PAIR * slab, HALF),
            struct(PAIR * slab, HALF),
            struct(PAIR * flat, HALF),
            struct(6 * cells, HALF),
            struct(2 * cells, HALF),
        ],
        [pltpu.VMEM((PAIR * flat, HALF), F32), pltpu.VMEM((2 * cells, HALF), F32)],
        600_000_000,
        6 * 2**20,
        scalars=1,
    )
    passed, second = lax.optimization_barrier((passed, second))
    across = swapped(passed, "space", 1)
    across, basis_there = lax.optimization_barrier((across, basis))
    basis_there = swapped(basis_there, "space", 1)
    table, place, slot_hot, speed, line, owner, weight = call(
        functools.partial(forward_window, fields, peers),
        (me, first, second, third, own, partner, passed, across, matrix),
        [
            struct(peers * (fields + 1), HALF),
            struct(TILES * fields, entries),
            struct(TILES * HALF, entries, dtype=BF16),
            struct(TILES * cells, HALF),
            struct(TILES * fields, entries, dtype=jnp.int32),
            struct(TILES * fields, entries, dtype=jnp.int32),
            struct(TILES * fields, entries),
        ],
        [
            pltpu.VMEM((TILES * PLACES, entries), BF16),
            pltpu.VMEM((TILES * fields, entries), jnp.int32),
            pltpu.VMEM((TILES * 16, HALF), F32),
            pltpu.VMEM((LAYERS * slab, HALF), F32),
            pltpu.VMEM((LAYERS * slab, HALF), F32),
            pltpu.VMEM((PAIR * flat, HALF), F32),
            pltpu.VMEM((TILES * fields, entries), F32),
        ]
        + [pltpu.VMEM((16 * fields, PLACES), F32)] * TILES,
        3_000_000_000,
        6 * 2**20,
        scalars=1,
        room=20,
    )
    columns = []
    bits = 2
    while bits < peers:
        arrived = swapped(table, "space", bits + 1)
        for i in ((0,), (1,), (2, 3))[len(columns)] if len(columns) < 3 else ():
            (some,) = call(
                functools.partial(basis_parts, 8 * (i % 2)),
                ((basis, basis_there)[i // 2], table),
                [struct(8 * rank, 2048, dtype=BF16)],
                [],
                10_000_000,
                4 * 2**20,
            )
            columns.append(some)
        if bits == 2:
            (turned_hot,) = call(
                functools.partial(turn_places, fields),
                (place, table),
                [struct(TILES * entries, 256, dtype=BF16)],
                [],
                10_000_000,
                4 * 2**20,
            )
            arrived, turned_hot = lax.optimization_barrier((arrived, turned_hot))
        arrived, columns = lax.optimization_barrier((arrived, columns))
        table = table + arrived
        bits *= 2
    kept, lent, coeffs = call(
        functools.partial(adjoint, fields, peers),
        (me, table, turned_hot, slot_hot, speed, line, owner, weight, turned, push, damping, matrix, *columns),
        [struct(LAYERS * flat, HALF), struct(LAYERS * flat, HALF), struct(fields, rank)],
        [
            pltpu.VMEM((TILES * fields, entries), F32),
            pltpu.VMEM((TILES * fields, entries), F32),
            pltpu.VMEM((TILES * LAYERS * slab, HALF), F32),
            pltpu.VMEM((2 * PAIR * flat, HALF), F32),
            pltpu.VMEM((2 * PAIR * slab, HALF), F32),
            pltpu.VMEM((2 * PAIR * flat, HALF), F32),
            pltpu.VMEM((2 * PAIR * flat, HALF), F32),
            pltpu.VMEM((PAIR * flat, HALF), F32),
            pltpu.VMEM((peers * fields, HALF), F32),
        ]
        + [pltpu.VMEM((64 * fields, 2 * entries), BF16)] * TILES
        + [pltpu.VMEM((2 * PAIR * fields, 2048), BF16)],
        5_000_000_000,
        10 * 2**20,
        scalars=1,
        room=30,
    )
    coeffs = jnp.concatenate([coeffs, swapped(coeffs, "space", 1)], axis=0)
    lent, coeffs = lax.optimization_barrier((lent, coeffs))
    borrowed = swapped(lent, "space", 1)
    bits = 2
    while bits * 2 < peers:
        coeffs = coeffs + swapped(coeffs, "space", bits + 1)
        bits *= 2
    shares = [coeffs, swapped(coeffs, "space", bits + 1)]
    hess_probe, coeffs = call(
        functools.partial(remainder, 2 * fields),
        (me, kept, borrowed, *columns[:2], *shares),
        [struct(*probes.shape), struct(2 * fields, rank)],
        [pltpu.VMEM((2 * fields * cells, HALF), F32), pltpu.SemaphoreType.DMA((LAYERS,))],
        200_000_000,
        6 * 2**20,
        scalars=1,
        far_out=1,
    )
    return hess_probe, coeffs.T


def solution(mesh):
    return jax.shard_map(
        local,
        mesh=mesh,
        in_specs=(
            P("group", "space", None, None),
            P(None, ("group", "space"), None, None),
            P(("group", "space"), None, None),
            P(("group", "space"), None, None),
            P("group", "space", None, None),
            P(("group", "space")),
            P(("group", "space")),
            P(("group", "space")),
            P(("group", "space")),
            P(("group", "space")),
            P(("group", "space")),
        ),
        out_specs=(P("group", "space", None, None), P("group", None)),
        check_vma=False,
    )
```
